32 devices in a mesh: section: 2 (over y), tensor: 4 (over x, core), dp: 4 (over z).
Axes of the slice: x: 2, y: 2, z: 4, core: 2. Of those that a mesh axis runs over, the one named last changes fastest.
Arguments:
- tokens: bfloat16 [12288, 768], P('dp'), may hold values from -6 to 6
- doc_lengths: int32 [8, 4], P('dp'), may hold values from 1 to 1152, 1536 in all within a row
- routes: int32 [2, 12288, 2], P('section', 'dp'), may hold values from 0 to 7, all different within a row; in each aligned block of 1536 rows (0 to 1535, 1536 to 3071, ..., all dimensions but the last counted through in order) at most 480 rows name the same one
- gain_attn: bfloat16 [2, 768], P('section'), may hold values from 0.5 to 1.5
- w_query: bfloat16 [2, 768, 768], P('section', None, 'tensor'), may hold values from -0.21875 to 0.21875
- w_key: bfloat16 [2, 768, 768], P('section', None, 'tensor'), may hold values from -0.21875 to 0.21875
- w_value: bfloat16 [2, 768, 768], P('section', None, 'tensor'), may hold values from -0.21875 to 0.21875
- w_output: bfloat16 [2, 768, 768], P('section', 'tensor'), may hold values from -0.875 to 0.875
- gain_ffn: bfloat16 [2, 768], P('section'), may hold values from 0.5 to 1.5
- w_router: bfloat16 [2, 768, 8], P('section'), may hold values from -0.15625 to 0.15625
- w_gate_exp: bfloat16 [2, 8, 768, 2048], P('section', None, None, 'tensor'), may hold values from -0.21875 to 0.21875
- w_up_exp: bfloat16 [2, 8, 768, 2048], P('section', None, None, 'tensor'), may hold values from -0.21875 to 0.21875
- w_down_exp: bfloat16 [2, 8, 2048, 768], P('section', None, 'tensor'), may hold values from -0.5 to 0.5
- w_gate_sh: bfloat16 [2, 768, 2048], P('section', None, 'tensor'), may hold values from -0.21875 to 0.21875
- w_up_sh: bfloat16 [2, 768, 2048], P('section', None, 'tensor'), may hold values from -0.21875 to 0.21875
- w_down_sh: bfloat16 [2, 2048, 768], P('section', 'tensor'), may hold values from -0.25 to 0.25
- cotangent: bfloat16 [12288, 768], P('dp'), may hold values from -6 to 6
Outputs:
- layer_out: bfloat16 [2, 12288, 768], P('section', 'dp')
- input_grad: float32 [2, 12288, 768], P('section', 'dp')
- grad_gain_attn: float32 [2, 768], P('section', 'dp')
- grad_query: float32 [2, 768, 768], P('section', 'dp', 'tensor')
- grad_key: float32 [2, 768, 768], P('section', 'dp', 'tensor')
- grad_value: float32 [2, 768, 768], P('section', 'dp', 'tensor')
- grad_output: float32 [2, 768, 768], P('section', 'tensor', 'dp')
- grad_gain_ffn: float32 [2, 768], P('section', 'dp')
- grad_router: float32 [2, 768, 8], P('section', 'dp')
- grad_gate_exp: float32 [2, 8, 768, 2048], P('section', None, 'dp', 'tensor')
- grad_up_exp: float32 [2, 8, 768, 2048], P('section', None, 'dp', 'tensor')
- grad_down_exp: float32 [2, 8, 2048, 768], P('section', None, 'tensor', 'dp')
- grad_gate_sh: float32 [2, 768, 2048], P('section', 'dp', 'tensor')
- grad_up_sh: float32 [2, 768, 2048], P('section', 'dp', 'tensor')
- grad_down_sh: float32 [2, 2048, 768], P('section', 'tensor', 'dp')
The draws below stay inside these ranges and needn't reach their ends.
Inputs may be any that keep to these rules, and one draw needn't show every extreme that they name: `doc_lengths`: each row holds the lengths of 4 documents that fill one sequence of 1536 tokens. `routes`: each token names two different experts in each layer; within each sequence's 1536 tokens no expert is named by more than 480 tokens, and in some sequence one is named by exactly that many.
All inputs are finite; a program needn't handle non-finite values.
Results may differ from the reference program's by a relative error of at most 0.035.
Values may be sent and summed in bfloat16 or wider, within the bound.
A program may use at most 512 MiB of HBM per device.

```python
import math
import jax
import jax.numpy as jnp
import numpy as np
from jax import lax

D = 768
HEADS = 12
HEAD_DIM = 64
FF = 2048
SHARED_FF = 2048
EXPERTS = 8
SEQ_LEN = 1536
WINDOW = 1024
Q_BLOCK = 512
DOCS = 4
CAPACITY = 480
SEQUENCES = 8
TOKENS = 12288


def block_levels(own_key, dims, cuts, least, high):
    level, own = 1.0, jax.random.fold_in(own_key, 6)
    for dim, blocks in cuts:
        steps = jnp.exp(jax.random.uniform(jax.random.fold_in(own, dim), (blocks,), jnp.float32, least / len(cuts), high / len(cuts)))
        level = level * jnp.repeat(steps, dims[dim] // blocks).reshape([-1 if axis == dim else 1 for axis in range(len(dims))])
    return level


def split_up(amount, total, bound, slope):
    weights = [(1 << 20) // math.isqrt(rank ** slope) + 1 for rank in range(2, amount + 1)]
    rest, given = total - bound - (amount - 1), [1] * (amount - 1)
    while rest > 0:
        free = [i for i in range(amount - 1) if given[i] < bound]
        whole, remaining = sum([weights[i] for i in free]), rest
        for i in free:
            addition = min(bound - given[i], max(1, remaining * weights[i] // whole), rest)
            given[i] = given[i] + addition
            rest = rest - addition
    return np.array([bound] + given)


def ragged(rng, count, total, most, lean):
    if count == 2:
        one = jax.random.randint(rng, (), max(1, total - most), min(most, total - 1) + 1)
        return jnp.stack([one, total - one])
    sizes = jnp.asarray(split_up(count, total, most, lean), jnp.int32)
    couples = (count - 1) // 2
    source_of, taker = sizes[1:1 + 2 * couples:2], sizes[2:2 + 2 * couples:2]
    room = jnp.minimum(source_of - 1, most - taker)
    shifted = jax.random.randint(jax.random.fold_in(rng, 1), (couples,), 0, 1 << 20) % (room + 1)
    sizes = sizes.at[1:1 + 2 * couples:2].set(source_of - shifted).at[2:2 + 2 * couples:2].set(taker + shifted)
    return sizes[jax.random.permutation(jax.random.fold_in(rng, 2), count)]


def deal_out(own_key, own, number, rows, number_of, top, bound, slope):
    order = jax.random.permutation(own_key, number_of)
    heavy_load, common = load_shares(number_of, rows * top, bound, slope, True), load_shares(number_of, rows * top, bound, slope, False)
    places = jnp.arange(number_of)

    def named(sizes, offset_by):
        used = int((sizes > 0).sum())
        fixed = max(1, used // 4)
        moved = fixed + (places - fixed + offset_by * (used - fixed)) % max(1, number_of - fixed)
        return jnp.zeros((number_of,), jnp.int32).at[order[jnp.where(places < fixed, places, moved)]].set(jnp.asarray(sizes, jnp.int32))

    sizes = jnp.where(number % 4 == 0, named(heavy_load, number // 4), named(common, number - number // 4 - 1))
    mixed = jax.random.permutation(jax.random.fold_in(own, 3), number_of)
    giver, taker = mixed[0:number_of // 2 * 2:2], mixed[1:number_of // 2 * 2:2]
    room = jnp.minimum(sizes[giver] - 1, bound - sizes[taker]) // 2
    room = jnp.where((giver == order[0]) | (taker == order[0]) | (sizes[taker] == 0), 0, jnp.maximum(room, 0))
    moved = jax.random.randint(jax.random.fold_in(own, 4), (number_of // 2,), 0, 1 << 20) % (room + 1)
    sizes = sizes.at[giver].add(-moved).at[taker].add(moved)
    labels = jnp.searchsorted(jnp.cumsum(sizes), jnp.arange(rows * top), side="right").astype(jnp.int32)
    listing = labels.reshape(top, rows).T
    listing = listing[jax.random.permutation(jax.random.fold_in(own, 1), rows)]
    offset_by = jax.random.randint(jax.random.fold_in(own, 2), (rows, 1), 0, top)
    return jnp.take_along_axis(listing, (jnp.arange(top)[None, :] + offset_by) % top, axis=1)


def load_shares(count, total, bound, skew, full):
    portions = [(1 << 20) // math.isqrt(rank ** skew) + 1 for rank in range(1, count + 1)]
    largest = bound if full else min(bound, max(-(-total // count), total * portions[0] // sum(portions)))
    least = 1 if total - largest >= count - 1 else 0
    holding, rest = [largest] + [least] * (count - 1), total - largest - least * (count - 1)
    while rest > 0:
        free = [i for i in range(1, count) if holding[i] < largest] or [i for i in range(1, count) if holding[i] < bound]
        whole, budget = sum([portions[i] for i in free]), rest
        for i in free:
            extra = min(bound - holding[i], max(1, budget * portions[i] // whole), rest)
            holding[i] = holding[i] + extra
            rest = rest - extra
    return np.array(holding)


def bell_draw(stream_key, shape, spread, bound, shards=(), kind=jnp.bfloat16):
    loudness = block_levels(stream_key, shape, shards, -0.22, 0.18) if shards else 1.0
    values = jax.random.normal(stream_key, shape, jnp.float32) * spread * loudness
    return jnp.minimum(jnp.maximum(values, -bound), bound).astype(kind)


def setup_inputs(seed: int = 0) -> dict:
    key_of = jax.random.split(jax.random.key(seed), 18)
    tokens = bell_draw(key_of[0], (TOKENS, D), 1.0, 6.0, ((0, 4),))
    doc_lengths = jax.vmap(lambda own: ragged(own, DOCS, SEQ_LEN, SEQ_LEN * 3 // 4, 2))(jax.random.split(key_of[1], SEQUENCES)).reshape((SEQUENCES, DOCS)).astype(jnp.int32)
    routes_keys = jax.random.split(jax.random.fold_in(key_of[2], 1), 2 * TOKENS // SEQ_LEN)
    routes_turns = jax.random.permutation(jax.random.fold_in(key_of[2], 3), 2 * TOKENS // SEQ_LEN)
    routes = jax.vmap(lambda own, number: deal_out(jax.random.fold_in(key_of[2], 2), own, number, SEQ_LEN, EXPERTS, 2, CAPACITY, 2))(routes_keys, routes_turns).reshape((2, TOKENS, 2))
    gain_attn = jnp.clip(1.0 + 0.1 * jax.random.normal(key_of[3], (2, D), jnp.float32), 0.5, 1.5).astype(jnp.bfloat16)
    w_query = bell_draw(key_of[4], (2, D, HEADS * HEAD_DIM), D ** -0.5, 0.21875, ((0, 2), (2, 4)))
    w_key = bell_draw(key_of[5], (2, D, HEADS * HEAD_DIM), D ** -0.5, 0.21875, ((0, 2), (2, 4)))
    w_value = bell_draw(key_of[6], (2, D, HEADS * HEAD_DIM), D ** -0.5, 0.21875, ((0, 2), (2, 4)))
    w_output = bell_draw(key_of[7], (2, HEADS * HEAD_DIM, D), (HEADS * HEAD_DIM // 16) ** -0.5, 0.875, ((0, 2), (1, 4)))
    gain_ffn = jnp.clip(1.0 + 0.1 * jax.random.normal(key_of[8], (2, D), jnp.float32), 0.5, 1.5).astype(jnp.bfloat16)
    w_router = bell_draw(key_of[9], (2, D, EXPERTS), (2 * D) ** -0.5, 0.15625, ((0, 2),))
    w_gate_exp = bell_draw(key_of[10], (2, EXPERTS, D, FF), D ** -0.5, 0.21875, ((0, 2), (3, 4)))
    w_up_exp = bell_draw(key_of[11], (2, EXPERTS, D, FF), D ** -0.5, 0.21875, ((0, 2), (3, 4)))
    w_down_exp = bell_draw(key_of[12], (2, EXPERTS, FF, D), (FF // 16) ** -0.5, 0.5, ((0, 2), (2, 4)))
    w_gate_sh = bell_draw(key_of[13], (2, D, SHARED_FF), D ** -0.5, 0.21875, ((0, 2), (2, 4)))
    w_up_sh = bell_draw(key_of[14], (2, D, SHARED_FF), D ** -0.5, 0.21875, ((0, 2), (2, 4)))
    w_down_sh = bell_draw(key_of[15], (2, SHARED_FF, D), (SHARED_FF // 4) ** -0.5, 0.25, ((0, 2), (1, 4)))
    cotangent = bell_draw(key_of[16], (TOKENS, D), 1.0, 6.0, ((0, 4),))
    return dict(tokens=tokens, doc_lengths=doc_lengths, routes=routes, gain_attn=gain_attn, w_query=w_query, w_key=w_key, w_value=w_value, w_output=w_output, gain_ffn=gain_ffn, w_router=w_router, w_gate_exp=w_gate_exp, w_up_exp=w_up_exp, w_down_exp=w_down_exp, w_gate_sh=w_gate_sh, w_up_sh=w_up_sh, w_down_sh=w_down_sh, cotangent=cotangent)


highest = lax.Precision.HIGHEST

@jax.custom_vjp
def low(v):
    return lax.optimization_barrier(v.astype(jnp.bfloat16)).astype(jnp.float32)

@jax.custom_vjp
def low_back(v):
    return v

def low_keep(v):
    return (low(v), None)

def low_pass(kept, grad):
    return (grad,)

def back_keep(v):
    return (v, None)

def back_low(kept, grad):
    return (low(grad),)
low.defvjp(low_keep, low_pass)
low_back.defvjp(back_keep, back_low)

def rms_norm(values, gain):
    return gain * values * lax.rsqrt(lax.optimization_barrier(jnp.mean(values * values, axis=-1, keepdims=True)) + 1e-06)

def rotary_tables():
    half = HEAD_DIM // 2
    rates = jnp.exp(-jnp.log(10000.0) * jnp.arange(half, dtype=jnp.float32) * 2.0 / HEAD_DIM)
    angles = jnp.arange(SEQ_LEN, dtype=jnp.float32)[:, None] * rates[None, :]
    return (jnp.cos(angles)[:, None, :], jnp.sin(angles)[:, None, :])

def rotate(values, cosine, sine):
    half = HEAD_DIM // 2
    first = values[..., :half]
    second = values[..., half:]
    return jnp.concatenate([first * cosine - second * sine, second * cosine + first * sine], axis=-1)

def document_ids(lengths):
    ends = jnp.cumsum(lengths).astype(jnp.int32)
    positions = jnp.arange(SEQ_LEN, dtype=jnp.int32)
    return lax.optimization_barrier(jnp.sum((positions[:, None] >= ends[None, :]).astype(jnp.int32), axis=1))

def allowed_keys(index, padded):
    starting = index * Q_BLOCK
    query_pos = starting + jnp.arange(Q_BLOCK, dtype=jnp.int32)
    key_pos = starting - WINDOW + jnp.arange(WINDOW + Q_BLOCK, dtype=jnp.int32)
    query_doc = lax.dynamic_slice_in_dim(padded, starting + WINDOW, Q_BLOCK, 0)
    key_doc = lax.dynamic_slice_in_dim(padded, starting, WINDOW + Q_BLOCK, 0)
    causal = key_pos[None, :] <= query_pos[:, None]
    inside = query_pos[:, None] - key_pos[None, :] < WINDOW
    return causal & inside & (query_doc[:, None] == key_doc[None, :])

def routing(routes):
    flat = routes.reshape(-1)
    onehot = (flat[:, None] == jnp.arange(EXPERTS, dtype=jnp.int32)[None, :]).astype(jnp.int32)
    before = jnp.cumsum(onehot, axis=0) - onehot
    rank = lax.optimization_barrier(jnp.sum(before * onehot, axis=1))
    slot = flat * CAPACITY + rank
    order = jnp.arange(2 * SEQ_LEN, dtype=jnp.int32)
    source_route = jnp.full((EXPERTS * CAPACITY,), 2 * SEQ_LEN, jnp.int32).at[slot].set(order)
    return (slot.reshape(SEQ_LEN, 2), source_route)

def attend(query, keys, values, doc_ids):
    heads = query.shape[1]
    scale = HEAD_DIM ** (-0.5)
    blank = jnp.zeros((WINDOW, heads, HEAD_DIM), jnp.float32)
    key_pad = jnp.concatenate([blank, keys], axis=0)
    value_pad = jnp.concatenate([blank, values], axis=0)
    padded = jnp.concatenate([jnp.full((WINDOW,), -1, jnp.int32), doc_ids])

    def block(index):
        starting = index * Q_BLOCK
        query_block = lax.dynamic_slice_in_dim(query, starting, Q_BLOCK, 0)
        key_block = lax.dynamic_slice_in_dim(key_pad, starting, WINDOW + Q_BLOCK, 0)
        value_block = lax.dynamic_slice_in_dim(value_pad, starting, WINDOW + Q_BLOCK, 0)
        scores = low_back(jnp.einsum('qhd,khd->hqk', query_block, key_block, precision=highest) * scale)
        masked = jnp.where(allowed_keys(index, padded)[None], scores, -1e+30)
        probs = low(jax.nn.softmax(masked, axis=-1))
        return jnp.einsum('hqk,khd->qhd', probs, value_block, precision=highest)
    mixed = lax.map(jax.checkpoint(block), jnp.arange(SEQ_LEN // Q_BLOCK, dtype=jnp.int32))
    return mixed.reshape(SEQ_LEN, heads, HEAD_DIM)

def layer(inputs, params, routes, doc_ids, cosine, sine):
    gain_attn, w_query, w_key, w_value, w_output, gain_ffn, w_router, w_gate_exp, w_up_exp, w_down_exp, w_gate_sh, w_up_sh, w_down_sh = params
    heads = w_query.shape[1] // HEAD_DIM
    normed = low(rms_norm(inputs, gain_attn))

    def project(weight):
        return low_back(jnp.dot(normed, weight, precision=highest)).reshape(SEQ_LEN, heads, HEAD_DIM)
    query = low(rotate(project(w_query), cosine, sine))
    keys = low(rotate(project(w_key), cosine, sine))
    values = low(project(w_value))
    mixed = low(low_back(attend(query, keys, values, doc_ids).reshape(SEQ_LEN, heads * HEAD_DIM)))
    state = inputs + low_back(jnp.dot(mixed, w_output, precision=highest))
    normed_ffn = low(rms_norm(state, gain_ffn))
    probs = jax.nn.softmax(low_back(jnp.dot(normed_ffn, w_router, precision=highest)), axis=-1)
    gates = jnp.take_along_axis(probs, routes, axis=1)
    slot, source_route = routing(routes)
    padded = jnp.concatenate([normed_ffn, jnp.zeros((1, normed_ffn.shape[1]), jnp.float32)], axis=0)
    expert_in = padded[source_route // 2].reshape(EXPERTS, CAPACITY, normed_ffn.shape[1])
    gate_value = low_back(jnp.einsum('ecd,edf->ecf', expert_in, w_gate_exp, precision=highest))
    lift_value = low_back(jnp.einsum('ecd,edf->ecf', expert_in, w_up_exp, precision=highest))
    hidden = low(jax.nn.silu(gate_value) * lift_value)
    expert_out = low_back(jnp.einsum('ecf,efd->ecd', hidden, w_down_exp, precision=highest))
    expert_out = expert_out.reshape(EXPERTS * CAPACITY, normed_ffn.shape[1])
    routed = gates[:, 0:1] * expert_out[slot[:, 0]] + gates[:, 1:2] * expert_out[slot[:, 1]]
    shared_gate = low_back(jnp.dot(normed_ffn, w_gate_sh, precision=highest))
    shared_lift = low_back(jnp.dot(normed_ffn, w_up_sh, precision=highest))
    shared_hidden = low(jax.nn.silu(shared_gate) * shared_lift)
    shared_out = low_back(jnp.dot(shared_hidden, w_down_sh, precision=highest))
    return state + (routed + shared_out)

def reference(tokens, doc_lengths, routes, gain_attn, w_query, w_key, w_value, w_output, gain_ffn, w_router, w_gate_exp, w_up_exp, w_down_exp, w_gate_sh, w_up_sh, w_down_sh, cotangent):
    weights = tuple((weight.astype(jnp.float32) for weight in (gain_attn, w_query, w_key, w_value, w_output, gain_ffn, w_router, w_gate_exp, w_up_exp, w_down_exp, w_gate_sh, w_up_sh, w_down_sh)))
    sequences = doc_lengths.shape[0]
    width = tokens.shape[1]
    inputs = tokens.astype(jnp.float32).reshape(sequences, SEQ_LEN, width)
    route_seq = routes.reshape(2, sequences, SEQ_LEN, 2)
    doc_ids = jax.vmap(document_ids)(doc_lengths)
    cosine, sine = rotary_tables()
    probes = jnp.zeros((2, sequences, SEQ_LEN, width), jnp.float32)
    checked = jax.checkpoint(layer)

    def forward(params, probe):
        first = tuple((weight[0] for weight in params))
        second = tuple((weight[1] for weight in params))

        def one(carry, items):
            seq_in, seq_ids, route_first, route_second, probe_first, probe_second = items
            lower = low(checked(seq_in + probe_first, first, route_first, seq_ids, cosine, sine))
            upper = low(checked(low_back(lower) + probe_second, second, route_second, seq_ids, cosine, sine))
            return (carry, (lower, upper))
        unused, pair = lax.scan(one, jnp.zeros((), jnp.float32), (inputs, doc_ids, route_seq[0], route_seq[1], probe[0], probe[1]))
        return pair
    (lower, upper), pullback = jax.vjp(forward, weights, probes)
    grads, grad_probes = pullback((jnp.zeros_like(lower), cotangent.astype(jnp.float32).reshape(sequences, SEQ_LEN, width)))
    layer_out = jnp.stack([lower, upper]).reshape(2, sequences * SEQ_LEN, width).astype(jnp.bfloat16)
    input_grad = grad_probes.reshape(2, sequences * SEQ_LEN, width)
    return (layer_out, input_grad, grads[0], grads[1], grads[2], grads[3], grads[4], grads[5], grads[6], grads[7], grads[8], grads[9], grads[10], grads[11], grads[12])
```

```python
import functools

import jax
import jax.numpy as jnp
import numpy as np
from jax import lax
from jax.experimental import pallas as pl
from jax.experimental.pallas import tpu as pltpu
from jax.sharding import PartitionSpec as P

HEAD_DIM = 64
EXPERTS = 8
SEQ_LEN = 1536
WINDOW = 1024
CAPACITY = 480
BLOCK = 256
BLOCKS = SEQ_LEN // BLOCK
LANES = 128
SLOTS = 3
VMEM_BYTES = 60 * 2**20
MESH = pl.DeviceIdType.MESH
F32 = jnp.float32
BF16 = jnp.bfloat16
NT = (((1,), (1,)), ((), ()))
TN = (((0,), (0,)), ((), ()))


def shape_of(shape, dtype):
    return jax.ShapeDtypeStruct(shape, dtype)


def dot(left, right):
    return jnp.dot(left, right, preferred_element_type=F32)


def dot_nt(left, right):
    return lax.dot_general(left, right, NT, preferred_element_type=F32)


def dot_tn(left, right):
    return lax.dot_general(left, right, TN, preferred_element_type=F32)


def once(shape, index):
    return pl.BlockSpec(shape, index, pipeline_mode=pl.Buffered(1))


def loop(count, body):
    lax.fori_loop(0, count, lambda step, none: (body(step), none)[1], 0)


def rows_of(step, size):
    return pl.ds(pl.multiple_of(step * size, size), size)


def greet(partners):
    barrier = pltpu.get_barrier_semaphore()
    for partner in partners:
        pl.semaphore_signal(barrier, inc=1, device_id=partner, device_id_type=MESH)
    pl.semaphore_wait(barrier, len(partners))


def remote(source, target, send, recv, device):
    return pltpu.make_async_remote_copy(
        src_ref=source,
        dst_ref=target,
        send_sem=send,
        recv_sem=recv,
        device_id=device,
        device_id_type=MESH,
    )


def partners_of():
    place = lax.axis_index("tensor")
    core = lax.rem(place, 2)
    near = {"tensor": place + 1 - 2 * core}
    far = {"tensor": lax.rem(place + 2, 4)}
    return core, near, far


def halves(rows, pieces):
    size = rows // 2
    part = size // pieces
    return [(size, step * part, part) for step in range(pieces)]


def sum_kernel(counts, *refs):
    arrays = len(counts)
    ins, outs = refs[:arrays], refs[arrays : 2 * arrays]
    first, kept, second = (refs[(2 + k) * arrays : (3 + k) * arrays] for k in range(3))
    send1, recv1, send2, recv2, send3, recv3 = refs[5 * arrays :]
    core, near, far = partners_of()
    greet([near, far])
    steps = []
    for which, count in enumerate(counts):
        for size, offset, part in halves(ins[which].shape[0], count):
            steps.append((which, size, offset, part))
    copies = []
    for number, (which, size, offset, part) in enumerate(steps):
        other = pl.ds(pl.multiple_of((1 - core) * size + offset, 16), part)
        copies.append(
            remote(
                ins[which].at[other],
                first[which].at[pl.ds(offset, part)],
                send1.at[number],
                recv1.at[number],
                near,
            )
        )
        copies[-1].start()
    crossing = []
    for number, (which, size, offset, part) in enumerate(steps):
        mine = pl.ds(pl.multiple_of(core * size + offset, 16), part)
        local = pl.ds(offset, part)
        copies[number].wait_recv()
        kept[which][local, :] = (
            ins[which][mine, :].astype(F32) + first[which][local, :].astype(F32)
        ).astype(BF16)
        crossing.append(
            remote(
                kept[which].at[local],
                second[which].at[local],
                send2.at[number],
                recv2.at[number],
                far,
            )
        )
        crossing[-1].start()
    back = []
    for number, (which, size, offset, part) in enumerate(steps):
        mine = pl.ds(pl.multiple_of(core * size + offset, 16), part)
        local = pl.ds(offset, part)
        crossing[number].wait_recv()
        outs[which][mine, :] = (
            kept[which][local, :].astype(F32) + second[which][local, :].astype(F32)
        ).astype(BF16)
        back.append(
            remote(
                outs[which].at[mine],
                outs[which].at[mine],
                send3.at[number],
                recv3.at[number],
                near,
            )
        )
        back[-1].start()
    for copy in back:
        copy.wait_recv()
    for copy in copies + crossing + back:
        copy.wait_send()


def tensor_sum(arrays, counts, identity):
    scratch = []
    for copy in range(3):
        scratch += [pltpu.VMEM((a.shape[0] // 2, a.shape[1]), BF16) for a in arrays]
    total = sum(counts)
    scratch += [pltpu.SemaphoreType.DMA((total,))] * 6
    return pl.pallas_call(
        functools.partial(sum_kernel, counts),
        out_shape=[shape_of(a.shape, BF16) for a in arrays],
        in_specs=[pl.BlockSpec(memory_space=pltpu.VMEM)] * len(arrays),
        out_specs=[pl.BlockSpec(memory_space=pltpu.VMEM)] * len(arrays),
        scratch_shapes=scratch,
        compiler_params=pltpu.CompilerParams(
            collective_id=identity, has_side_effects=True, vmem_limit_bytes=VMEM_BYTES
        ),
        name="tensor_sum",
    )(*arrays)


def relay_kernel(
    pieces,
    finish,
    part_ref,
    extra_refs,
    full_ref,
    next_ref,
    first,
    kept,
    second,
    sends,
    recvs,
):
    core, near, far = partners_of()
    across = {"section": 1 - lax.axis_index("section")}
    greet([near, far, across])
    steps = halves(part_ref.shape[0], pieces)

    def place(size, offset, part, side):
        return pl.ds(pl.multiple_of(side * size + offset, 16), part)

    copies = []
    for number, (size, offset, part) in enumerate(steps):
        copies.append(
            remote(
                part_ref.at[place(size, offset, part, 1 - core)],
                first.at[pl.ds(offset, part)],
                sends.at[0, number],
                recvs.at[0, number],
                near,
            )
        )
        copies[-1].start()
    crossing = []
    for number, (size, offset, part) in enumerate(steps):
        local = pl.ds(offset, part)
        copies[number].wait_recv()
        kept[local, :] = (
            part_ref[place(size, offset, part, core), :].astype(F32)
            + first[local, :].astype(F32)
        ).astype(BF16)
        crossing.append(
            remote(
                kept.at[local],
                second.at[local],
                sends.at[1, number],
                recvs.at[1, number],
                far,
            )
        )
        crossing[-1].start()
    back, passed = [], []
    for number, (size, offset, part) in enumerate(steps):
        local = pl.ds(offset, part)
        mine = place(size, offset, part, core)
        crossing[number].wait_recv()
        total = (kept[local, :].astype(F32) + second[local, :].astype(F32)).astype(BF16)
        source, given = finish(total, mine, local, True)
        back.append(
            remote(
                source,
                source,
                sends.at[2, number],
                recvs.at[2, number],
                near,
            )
        )
        back[-1].start()
        passed.append(
            remote(
                given,
                next_ref.at[mine],
                sends.at[3, number],
                recvs.at[3, number],
                across,
            )
        )
        passed[-1].start()
    spread = []
    for number, (size, offset, part) in enumerate(steps):
        mine = place(size, offset, part, core)
        passed[number].wait_recv()
        spread.append(
            remote(
                next_ref.at[mine],
                next_ref.at[mine],
                sends.at[4, number],
                recvs.at[4, number],
                near,
            )
        )
        spread[-1].start()
    for number, (size, offset, part) in enumerate(steps):
        back[number].wait_recv()
        finish(None, place(size, offset, part, 1 - core), pl.ds(offset, part), False)
    for copy in spread:
        copy.wait_recv()
    for copy in copies + crossing + back + passed + spread:
        copy.wait_send()


def output_kernel(pieces, part_ref, state_ref, out_ref, next_ref, first, kept, second, sends, recvs):
    def finish(total, rows, local, own):
        if own:
            out_ref[rows, :] = (state_ref[rows, :] + total.astype(F32)).astype(BF16)
            return out_ref.at[rows], out_ref.at[rows]

    relay_kernel(
        pieces, finish, part_ref, None, out_ref, next_ref, first, kept, second, sends, recvs
    )


def input_kernel(
    pieces,
    part_ref,
    layer_in_ref,
    grad_state_ref,
    gain_ref,
    grad_ref,
    next_ref,
    grad_gain_ref,
    first,
    kept,
    second,
    full,
    given,
    gains,
    sends,
    recvs,
):
    gains[...] = jnp.zeros_like(gains)

    def rows_back(rows, side):
        grad_normed = full[rows, :].astype(F32)
        values = layer_in_ref[rows, :].astype(F32)
        scale = lax.rsqrt(jnp.mean(values * values, axis=-1, keepdims=True) + 1e-06)
        normed = values * scale
        scaled = gain_ref[...] * grad_normed
        inner = jnp.mean(normed * scaled, axis=-1, keepdims=True)
        grad = grad_state_ref[rows, :] + scale * (scaled - normed * inner)
        grad_ref[rows, :] = grad
        gains[side : side + 1, :] += jnp.sum(grad_normed * normed, axis=0, keepdims=True)
        return grad

    def finish(total, rows, local, own):
        if own:
            full[rows, :] = total
            given[local, :] = rows_back(rows, 0).astype(BF16)
            return full.at[rows], given.at[local]
        rows_back(rows, 1)

    relay_kernel(
        pieces, finish, part_ref, None, full, next_ref, first, kept, second, sends, recvs
    )
    grad_gain_ref[...] = gains[0:1, :] + gains[1:2, :]


def relay_scratch(rows, width, pieces):
    half = [pltpu.VMEM((rows // 2, width), BF16)] * 3
    return half, [pltpu.SemaphoreType.DMA((5, pieces))] * 2


def output_relay(part, state, identity, pieces=6):
    rows, width = part.shape
    half, semaphores = relay_scratch(rows, width, pieces)
    whole = pl.BlockSpec(memory_space=pltpu.VMEM)
    return pl.pallas_call(
        functools.partial(output_kernel, pieces),
        out_shape=[shape_of((rows, width), BF16)] * 2,
        in_specs=[whole] * 2,
        out_specs=[whole] * 2,
        scratch_shapes=half + semaphores,
        compiler_params=pltpu.CompilerParams(
            collective_id=identity, has_side_effects=True, vmem_limit_bytes=VMEM_BYTES
        ),
        name="output_relay",
    )(part, state)


def input_relay(part, layer_in, grad_state, gain, identity, pieces=6):
    rows, width = part.shape
    half, semaphores = relay_scratch(rows, width, pieces)
    whole = pl.BlockSpec(memory_space=pltpu.VMEM)
    return pl.pallas_call(
        functools.partial(input_kernel, pieces),
        out_shape=[
            shape_of((rows, width), F32),
            shape_of((rows, width), BF16),
            shape_of((1, width), F32),
        ],
        in_specs=[whole] * 4,
        out_specs=[whole] * 3,
        scratch_shapes=half
        + [
            pltpu.VMEM((rows, width), BF16),
            pltpu.VMEM((rows // 2, width), BF16),
            pltpu.VMEM((8, width), F32),
        ]
        + semaphores,
        compiler_params=pltpu.CompilerParams(
            collective_id=identity, has_side_effects=True, vmem_limit_bytes=VMEM_BYTES
        ),
        name="input_relay",
    )(part, layer_in, grad_state, gain)


def attention_forward_kernel(
    stored,
    meta,
    first_block,
    tok_ref,
    rec_ref,
    gain_ref,
    wall_ref,
    wo_ref,
    cos_ref,
    sin_ref,
    low_ref,
    *rest,
):
    rest = rest[stored:]
    part_ref, x_ref, a_ref, qkv_ref, o_ref, lse_ref = rest[:6]
    keys, values, scores, tops, sums, mixed = rest[6:]
    index = pl.program_id(0)
    heads = wo_ref.shape[0] // LANES
    wide = heads * LANES
    x = jnp.where(meta[0] == 0, tok_ref[...], rec_ref[...])
    x_ref[0] = x
    x = x.astype(F32)
    normed = gain_ref[...] * x * lax.rsqrt(jnp.mean(x * x, axis=-1, keepdims=True) + 1e-06)
    normed = normed.astype(BF16)
    a_ref[0] = normed
    cosine, sine = cos_ref[...], sin_ref[...]
    here = rows_of(index, BLOCK)
    for group in range(2 * heads):
        columns = slice(group * LANES, (group + 1) * LANES)
        pre = dot(normed, wall_ref[:, columns])
        turned = pre * cosine + pltpu.roll(pre, HEAD_DIM, 1) * sine
        if group < heads:
            turned = turned * 0.0625
        qkv_ref[0, :, columns] = turned.astype(BF16)
    qkv_ref[0, :, 2 * wide :] = dot(normed, wall_ref[:, 2 * wide :]).astype(BF16)
    keys[here, :] = qkv_ref[0, :, wide : 2 * wide]
    values[here, :] = qkv_ref[0, :, 2 * wide :]
    low = low_ref[0]
    query_at = index * BLOCK + lax.broadcasted_iota(jnp.int32, (BLOCK, BLOCK), 0)
    key_at = lax.broadcasted_iota(jnp.int32, (BLOCK, BLOCK), 1)
    tops[...] = jnp.full_like(tops, -1e30)
    sums[...] = jnp.zeros_like(sums)
    mixed[...] = jnp.zeros_like(mixed)
    begin = first_block[meta[2] * BLOCKS + index]

    def score(block, none):
        at = key_at + block * BLOCK
        valid = (at >= low) & (at <= query_at)
        there = rows_of(block, BLOCK)
        for head in range(heads):
            columns = slice(head * LANES, (head + 1) * LANES)
            raw = dot_nt(qkv_ref[0, :, columns], keys[there, columns])
            raw = jnp.where(valid, raw, -1e30)
            scores[head, block] = raw
            tops[head] = jnp.maximum(
                tops[head], jnp.maximum(raw[:, :LANES], raw[:, LANES:])
            )
        return none

    lax.fori_loop(begin, index + 1, score, 0)
    top = [jnp.max(tops[head], axis=1, keepdims=True) for head in range(heads)]

    def mix(block, none):
        there = rows_of(block, BLOCK)
        for head in range(heads):
            columns = slice(head * LANES, (head + 1) * LANES)
            weights = jnp.exp(scores[head, block] - top[head])
            sums[head] += weights[:, :LANES] + weights[:, LANES:]
            mixed[:, columns] += dot(weights.astype(BF16), values[there, columns])
        return none

    lax.fori_loop(begin, index + 1, mix, 0)
    for head in range(heads):
        columns = slice(head * LANES, (head + 1) * LANES)
        total = jnp.sum(sums[head], axis=1, keepdims=True)
        o_ref[0, :, columns] = (mixed[:, columns] / total).astype(BF16)
        logsum = jnp.broadcast_to(top[head] + jnp.log(total), (BLOCK, LANES))
        lse_ref[0, head : head + 1, :] = logsum.T[0:1, :]
    part_ref[...] = dot(o_ref[0], wo_ref[...]).astype(BF16)


def attention_forward(meta, first_block, tokens, received, gain, wall, wo, cosine, sine, low, kept):
    width = tokens.shape[1]
    wide = wo.shape[0]
    heads = wide // LANES
    stored = 0 if kept is None else 5
    saved = [
        shape_of((SLOTS, SEQ_LEN, width), BF16),
        shape_of((SLOTS, SEQ_LEN, width), BF16),
        shape_of((SLOTS, SEQ_LEN, 3 * wide), BF16),
        shape_of((SLOTS, SEQ_LEN, wide), BF16),
        shape_of((SLOTS, 8, SEQ_LEN), F32),
    ]

    def slot_rows(columns):
        return pl.BlockSpec((1, BLOCK, columns), lambda i, m, f: (m[1], i, 0))

    grid_spec = pltpu.PrefetchScalarGridSpec(
        num_scalar_prefetch=2,
        grid=(BLOCKS,),
        in_specs=[
            pl.BlockSpec((BLOCK, width), lambda i, m, f: (m[2] * BLOCKS + i, 0)),
            pl.BlockSpec((BLOCK, width), lambda i, m, f: (i, 0)),
            once((1, width), lambda i, m, f: (0, 0)),
            once(wall.shape, lambda i, m, f: (0, 0)),
            once(wo.shape, lambda i, m, f: (0, 0)),
            pl.BlockSpec((BLOCK, LANES), lambda i, m, f: (i, 0)),
            pl.BlockSpec((BLOCK, LANES), lambda i, m, f: (i, 0)),
            pl.BlockSpec((1, BLOCK, 1), lambda i, m, f: (m[2], i, 0)),
        ]
        + [pl.BlockSpec(memory_space=pl.ANY)] * stored,
        out_specs=[
            pl.BlockSpec((BLOCK, width), lambda i, m, f: (i, 0)),
            slot_rows(width),
            slot_rows(width),
            slot_rows(3 * wide),
            slot_rows(wide),
            pl.BlockSpec((1, 8, BLOCK), lambda i, m, f: (m[1], 0, i)),
        ],
        scratch_shapes=[
            pltpu.VMEM((SEQ_LEN, wide), BF16),
            pltpu.VMEM((SEQ_LEN, wide), BF16),
            pltpu.VMEM((heads, BLOCKS, BLOCK, BLOCK), F32),
            pltpu.VMEM((heads, BLOCK, LANES), F32),
            pltpu.VMEM((heads, BLOCK, LANES), F32),
            pltpu.VMEM((BLOCK, wide), F32),
        ],
    )
    outs = pl.pallas_call(
        functools.partial(attention_forward_kernel, stored),
        grid_spec=grid_spec,
        out_shape=[shape_of((SEQ_LEN, width), BF16)] + saved,
        input_output_aliases={10 + k: 1 + k for k in range(stored)},
        compiler_params=pltpu.CompilerParams(vmem_limit_bytes=VMEM_BYTES),
        name="attention_forward",
    )(
        meta,
        first_block,
        tokens,
        received,
        gain,
        wall,
        wo,
        cosine,
        sine,
        low,
        *(kept or ()),
    )
    return outs[0], outs[1:]


CHUNK = 96
ROW_CHUNK = 128


def pick_matrices(expert, post_ref, pos_ref, pick, put):
    def by_slot(step):
        slot_at = step * CHUNK + lax.broadcasted_iota(jnp.int32, (CHUNK, SEQ_LEN), 0)
        pick[rows_of(step, CHUNK), :] = jnp.where(
            slot_at == post_ref[0, pl.ds(expert, 1), :], 1.0, 0.0
        ).astype(BF16)

    loop(CAPACITY // CHUNK, by_slot)

    def by_token(step):
        rows = rows_of(step, ROW_CHUNK)
        places = pos_ref[0, rows, :]
        lane = lax.broadcasted_iota(jnp.int32, places.shape, 1)
        place = jnp.sum(jnp.where(lane == expert, places, 0), axis=1, keepdims=True)
        slot_at = lax.broadcasted_iota(jnp.int32, (ROW_CHUNK, CAPACITY), 1)
        put[rows, :] = jnp.where(slot_at == place, 1.0, 0.0).astype(BF16)

    loop(SEQ_LEN // ROW_CHUNK, by_token)


def slot_gates(expert, post_ref, probs_ref, gates):
    def body(step):
        slot_at = step * CHUNK + lax.broadcasted_iota(jnp.int32, (CHUNK, SEQ_LEN), 0)
        chosen = jnp.where(
            slot_at == post_ref[0, pl.ds(expert, 1), :], probs_ref[0, pl.ds(expert, 1), :], 0.0
        )
        gates[rows_of(step, CHUNK), :] = jnp.broadcast_to(
            jnp.sum(chosen, axis=1, keepdims=True), (CHUNK, LANES)
        )

    loop(CAPACITY // CHUNK, body)


def put_back(put, rows_in, total):
    def body(step):
        rows = rows_of(step, 2 * BLOCK)
        total[rows, :] += dot(put[rows, :], rows_in[...])

    loop(SEQ_LEN // (2 * BLOCK), body)


def feed_forward_kernel(
    stored,
    meta,
    x_ref,
    ar_ref,
    gain_ref,
    router_ref,
    post_ref,
    pos_ref,
    wg_ref,
    wu_ref,
    wd_ref,
    wgs_ref,
    wus_ref,
    wds_ref,
    *rest,
):
    rest = rest[stored:]
    part_ref, state_ref, h_ref, b_ref, xe_ref, g_ref, u_ref, gs_ref, us_ref, probs_ref = rest[:10]
    total, pick, put, gates, gate_value, lift_value, hidden, scaled = rest[10:]
    expert = pl.program_id(0)

    @pl.when(expert == 0)
    def _():
        def body(step):
            rows = rows_of(step, ROW_CHUNK)
            state = x_ref[0, rows, :].astype(F32) + ar_ref[rows, :].astype(F32)
            state_ref[rows, :] = state
            h_ref[0, rows, :] = state
            scale = lax.rsqrt(jnp.mean(state * state, axis=-1, keepdims=True) + 1e-06)
            b_ref[0, rows, :] = (gain_ref[...] * state * scale).astype(BF16)
            total[rows, :] = jnp.zeros((ROW_CHUNK, total.shape[1]), F32)

        loop(SEQ_LEN // ROW_CHUNK, body)
        logits = dot_nt(router_ref[...], b_ref[0])
        weights = jnp.exp(logits - jnp.max(logits, axis=0, keepdims=True))
        probs_ref[0] = weights / jnp.sum(weights, axis=0, keepdims=True)

    def activate(gate_in, lift_in, gate_out, lift_out, out, count):
        def body(step):
            rows = rows_of(step, CHUNK)
            gate, lift = gate_in[rows, :], lift_in[rows, :]
            gate_out[rows, :] = gate.astype(BF16)
            lift_out[rows, :] = lift.astype(BF16)
            out[rows, :] = (gate / (1.0 + jnp.exp(-gate)) * lift).astype(BF16)

        loop(count // CHUNK, body)

    @pl.when(expert < EXPERTS)
    def _():
        pick_matrices(expert, post_ref, pos_ref, pick, put)
        slot_gates(expert, post_ref, probs_ref, gates)
        xe_ref[0, 0] = dot(pick[...], b_ref[0]).astype(BF16)
        gate_value[:CAPACITY, :] = dot(xe_ref[0, 0], wg_ref[0])
        lift_value[:CAPACITY, :] = dot(xe_ref[0, 0], wu_ref[0])
        activate(
            gate_value, lift_value, g_ref.at[0, 0], u_ref.at[0, 0], hidden, CAPACITY
        )
        scaled[...] = (dot(hidden[:CAPACITY, :], wd_ref[0]) * gates[:, 0:1]).astype(BF16)
        put_back(put, scaled, total)

    @pl.when(expert == EXPERTS)
    def _():
        gate_value[...] = dot(b_ref[0], wgs_ref[...])
        lift_value[...] = dot(b_ref[0], wus_ref[...])
        activate(gate_value, lift_value, gs_ref.at[0], us_ref.at[0], hidden, SEQ_LEN)

        def body(step):
            rows = rows_of(step, 2 * BLOCK)
            part_ref[rows, :] = (total[rows, :] + dot(hidden[rows, :], wds_ref[...])).astype(BF16)

        loop(SEQ_LEN // (2 * BLOCK), body)


def feed_forward(meta, layer_in, ar, gain, router, post, pos, weights, kept):
    width = ar.shape[1]
    wg, wu, wd, wgs, wus, wds = weights
    hidden = wg.shape[2]
    stored = 0 if kept is None else 8
    saved = [
        shape_of((SLOTS, SEQ_LEN, width), F32),
        shape_of((SLOTS, SEQ_LEN, width), BF16),
        shape_of((SLOTS, EXPERTS, CAPACITY, width), BF16),
        shape_of((SLOTS, EXPERTS, CAPACITY, hidden), BF16),
        shape_of((SLOTS, EXPERTS, CAPACITY, hidden), BF16),
        shape_of((SLOTS, SEQ_LEN, hidden), BF16),
        shape_of((SLOTS, SEQ_LEN, hidden), BF16),
        shape_of((SLOTS, EXPERTS, SEQ_LEN), F32),
    ]

    def slot_whole(columns):
        return once((1, SEQ_LEN, columns), lambda e, m: (m[1], 0, 0))

    def slot_expert(columns):
        return pl.BlockSpec(
            (1, 1, CAPACITY, columns), lambda e, m: (m[1], jnp.minimum(e, EXPERTS - 1), 0, 0)
        )

    def fixed(shape):
        return once(shape, lambda e, m: (0,) * len(shape))

    def of_expert(array):
        return pl.BlockSpec(
            (1,) + array.shape[1:], lambda e, m: (jnp.minimum(e, EXPERTS - 1), 0, 0)
        )

    grid_spec = pltpu.PrefetchScalarGridSpec(
        num_scalar_prefetch=1,
        grid=(EXPERTS + 1,),
        in_specs=[
            slot_whole(width),
            fixed(ar.shape),
            fixed(gain.shape),
            fixed(router.shape),
            once((1, EXPERTS, SEQ_LEN), lambda e, m: (m[2], 0, 0)),
            once((1, SEQ_LEN, EXPERTS), lambda e, m: (m[2], 0, 0)),
            of_expert(wg),
            of_expert(wu),
            of_expert(wd),
            fixed(wgs.shape),
            fixed(wus.shape),
            fixed(wds.shape),
        ]
        + [pl.BlockSpec(memory_space=pl.ANY)] * stored,
        out_specs=[
            fixed((SEQ_LEN, width)),
            fixed((SEQ_LEN, width)),
            slot_whole(width),
            slot_whole(width),
            slot_expert(width),
            slot_expert(hidden),
            slot_expert(hidden),
            slot_whole(hidden),
            slot_whole(hidden),
            once((1, EXPERTS, SEQ_LEN), lambda e, m: (m[1], 0, 0)),
        ],
        scratch_shapes=[
            pltpu.VMEM((SEQ_LEN, width), F32),
            pltpu.VMEM((CAPACITY, SEQ_LEN), BF16),
            pltpu.VMEM((SEQ_LEN, CAPACITY), BF16),
            pltpu.VMEM((CAPACITY, LANES), F32),
            pltpu.VMEM((SEQ_LEN, hidden), F32),
            pltpu.VMEM((SEQ_LEN, hidden), F32),
            pltpu.VMEM((SEQ_LEN, hidden), BF16),
            pltpu.VMEM((CAPACITY, width), BF16),
        ],
    )
    outs = pl.pallas_call(
        functools.partial(feed_forward_kernel, stored),
        grid_spec=grid_spec,
        out_shape=[shape_of((SEQ_LEN, width), BF16), shape_of((SEQ_LEN, width), F32)] + saved,
        input_output_aliases={13 + k: 2 + k for k in range(stored)},
        compiler_params=pltpu.CompilerParams(vmem_limit_bytes=VMEM_BYTES),
        name="feed_forward",
    )(meta, layer_in, ar, gain, router, post, pos, wg, wu, wd, wgs, wus, wds, *(kept or ()))
    return outs[0], outs[1], outs[2:]


def feed_backward_kernel(
    stored,
    meta,
    cot_ref,
    rec_ref,
    post_ref,
    pos_ref,
    g_ref,
    u_ref,
    gs_ref,
    us_ref,
    probs_ref,
    wg_ref,
    wu_ref,
    wd_ref,
    wgs_ref,
    wus_ref,
    wds_ref,
    *rest,
):
    rest = rest[stored:]
    part_ref, choice_ref = rest[:2]
    dy_ref, hid_ref, dg_ref, du_ref, de_ref, hids_ref, dgs_ref, dus_ref = rest[2:10]
    total, pick, put, gates, back, rows_in, choice = rest[10:]
    expert = pl.program_id(0)

    @pl.when(expert == 0)
    def _():
        def body(step):
            rows = rows_of(step, ROW_CHUNK)
            given = jnp.where(meta[0] == 1, cot_ref[rows, :], rec_ref[rows, :])
            dy_ref[0, rows, :] = jnp.where(meta[0] == 0, jnp.zeros_like(given), given)
            total[rows, :] = jnp.zeros((ROW_CHUNK, total.shape[1]), F32)

        loop(SEQ_LEN // ROW_CHUNK, body)
        choice[...] = jnp.zeros_like(choice)

    def pull(gate_in, lift_in, weight, rows, hid, grad_gate, grad_lift):
        gate, lift = gate_in[rows, :].astype(F32), lift_in[rows, :].astype(F32)
        sigma = 1.0 / (1.0 + jnp.exp(-gate))
        swish = gate * sigma
        hidden = (swish * lift).astype(BF16)
        hid[rows, :] = hidden
        grad = back[rows, :]
        inner = jnp.sum(hidden.astype(F32) * grad, axis=1, keepdims=True)
        if weight is not None:
            grad = grad * weight
        grad_gate[rows, :] = (grad * lift * sigma * (1.0 + gate * (1.0 - sigma))).astype(BF16)
        grad_lift[rows, :] = (grad * swish).astype(BF16)
        return inner

    @pl.when(expert < EXPERTS)
    def _():
        pick_matrices(expert, post_ref, pos_ref, pick, put)
        slot_gates(expert, post_ref, probs_ref, gates)
        rows_in[...] = dot(pick[...], dy_ref[0]).astype(BF16)
        back[:CAPACITY, :] = dot_nt(rows_in[...], wd_ref[0])

        def body(step):
            rows = rows_of(step, CHUNK)
            weight = gates[rows, 0:1]
            inner = pull(
                g_ref.at[0, 0],
                u_ref.at[0, 0],
                weight,
                rows,
                hid_ref.at[0, 0],
                dg_ref.at[0, 0],
                du_ref.at[0, 0],
            )
            de_ref[0, 0, rows, :] = (weight * rows_in[rows, :].astype(F32)).astype(BF16)
            slot_at = step * CHUNK + lax.broadcasted_iota(jnp.int32, (CHUNK, SEQ_LEN), 0)
            mine = slot_at == post_ref[0, pl.ds(expert, 1), :]
            choice[pl.ds(expert, 1), :] += jnp.sum(
                jnp.where(mine, inner, 0.0), axis=0, keepdims=True
            )

        loop(CAPACITY // CHUNK, body)
        rows_in[...] = (
            dot_nt(dg_ref[0, 0], wg_ref[0]) + dot_nt(du_ref[0, 0], wu_ref[0])
        ).astype(BF16)
        put_back(put, rows_in, total)

    @pl.when(expert == EXPERTS)
    def _():
        back[...] = dot_nt(dy_ref[0], wds_ref[...])

        def body(step):
            pull(
                gs_ref.at[0],
                us_ref.at[0],
                None,
                rows_of(step, CHUNK),
                hids_ref.at[0],
                dgs_ref.at[0],
                dus_ref.at[0],
            )

        loop(SEQ_LEN // CHUNK, body)

        def finish(step):
            rows = rows_of(step, 2 * BLOCK)
            part_ref[rows, :] = (
                total[rows, :]
                + dot_nt(dgs_ref[0, rows, :], wgs_ref[...])
                + dot_nt(dus_ref[0, rows, :], wus_ref[...])
            ).astype(BF16)

        loop(SEQ_LEN // (2 * BLOCK), finish)
        half = SEQ_LEN // 2
        blank = jnp.zeros((8, half), F32)
        choice_ref[...] = jnp.concatenate(
            [choice[:, :half], blank, choice[:, half:], blank], axis=0
        ).astype(BF16)


def feed_backward(meta, cotangent, received, post, pos, forward_kept, weights, kept):
    width = cotangent.shape[1]
    wg, wu, wd, wgs, wus, wds = weights
    hidden = wg.shape[2]
    stored = 0 if kept is None else 8
    unused_h, unused_b, unused_x, gate, lift, gate_sh, lift_sh, probs = forward_kept
    saved = [
        shape_of((SLOTS, SEQ_LEN, width), BF16),
        shape_of((SLOTS, EXPERTS, CAPACITY, hidden), BF16),
        shape_of((SLOTS, EXPERTS, CAPACITY, hidden), BF16),
        shape_of((SLOTS, EXPERTS, CAPACITY, hidden), BF16),
        shape_of((SLOTS, EXPERTS, CAPACITY, width), BF16),
        shape_of((SLOTS, SEQ_LEN, hidden), BF16),
        shape_of((SLOTS, SEQ_LEN, hidden), BF16),
        shape_of((SLOTS, SEQ_LEN, hidden), BF16),
    ]

    def slot_whole(columns, which):
        return once((1, SEQ_LEN, columns), lambda e, m: (m[which], 0, 0))

    def slot_expert(columns, which):
        return pl.BlockSpec(
            (1, 1, CAPACITY, columns), lambda e, m: (m[which], jnp.minimum(e, EXPERTS - 1), 0, 0)
        )

    def fixed(shape):
        return once(shape, lambda e, m: (0,) * len(shape))

    def of_expert(array):
        return pl.BlockSpec(
            (1,) + array.shape[1:], lambda e, m: (jnp.minimum(e, EXPERTS - 1), 0, 0)
        )

    grid_spec = pltpu.PrefetchScalarGridSpec(
        num_scalar_prefetch=1,
        grid=(EXPERTS + 1,),
        in_specs=[
            once((SEQ_LEN, width), lambda e, m: (m[2], 0)),
            fixed((SEQ_LEN, width)),
            once((1, EXPERTS, SEQ_LEN), lambda e, m: (m[2], 0, 0)),
            once((1, SEQ_LEN, EXPERTS), lambda e, m: (m[2], 0, 0)),
            slot_expert(hidden, 3),
            slot_expert(hidden, 3),
            slot_whole(hidden, 3),
            slot_whole(hidden, 3),
            once((1, EXPERTS, SEQ_LEN), lambda e, m: (m[3], 0, 0)),
            of_expert(wg),
            of_expert(wu),
            of_expert(wd),
            fixed(wgs.shape),
            fixed(wus.shape),
            fixed(wds.shape),
        ]
        + [pl.BlockSpec(memory_space=pl.ANY)] * stored,
        out_specs=[
            fixed((SEQ_LEN, width)),
            fixed((32, SEQ_LEN // 2)),
            slot_whole(width, 1),
            slot_expert(hidden, 1),
            slot_expert(hidden, 1),
            slot_expert(hidden, 1),
            slot_expert(width, 1),
            slot_whole(hidden, 1),
            slot_whole(hidden, 1),
            slot_whole(hidden, 1),
        ],
        scratch_shapes=[
            pltpu.VMEM((SEQ_LEN, width), F32),
            pltpu.VMEM((CAPACITY, SEQ_LEN), BF16),
            pltpu.VMEM((SEQ_LEN, CAPACITY), BF16),
            pltpu.VMEM((CAPACITY, LANES), F32),
            pltpu.VMEM((SEQ_LEN, hidden), F32),
            pltpu.VMEM((CAPACITY, width), BF16),
            pltpu.VMEM((EXPERTS, SEQ_LEN), F32),
        ],
    )
    outs = pl.pallas_call(
        functools.partial(feed_backward_kernel, stored),
        grid_spec=grid_spec,
        out_shape=[shape_of((SEQ_LEN, width), BF16), shape_of((32, SEQ_LEN // 2), BF16)] + saved,
        input_output_aliases={16 + k: 2 + k for k in range(stored)},
        compiler_params=pltpu.CompilerParams(vmem_limit_bytes=VMEM_BYTES),
        name="feed_backward",
    )(
        meta,
        cotangent,
        received,
        post,
        pos,
        gate,
        lift,
        gate_sh,
        lift_sh,
        probs,
        wg,
        wu,
        wd,
        wgs,
        wus,
        wds,
        *(kept or ()),
    )
    return outs[0], outs[1], outs[2:]


def attention_backward_kernel(
    stored,
    meta,
    first_block,
    sum_ref,
    choice_ref,
    probs_ref,
    dy_ref,
    h_ref,
    b_ref,
    gain_ref,
    router_ref,
    wall_ref,
    wo_ref,
    cos_ref,
    sin_ref,
    qkv_ref,
    o_ref,
    lse_ref,
    low_ref,
    *rest,
):
    rest = rest[stored:]
    part_ref, dh_ref, gain_grad_ref, router_grad_ref, dqkv_ref, dattn_ref = rest[:6]
    dk_all, dv_all, dq_all, do_all, inner_all = rest[6:]
    step = pl.program_id(0)
    index = BLOCKS - 1 - step
    heads = wo_ref.shape[0] // LANES
    wide = heads * LANES

    @pl.when(step == 0)
    def _():
        gain_grad_ref[...] = jnp.zeros_like(gain_grad_ref)
        router_grad_ref[...] = jnp.zeros_like(router_grad_ref)
        dk_all[...] = jnp.zeros_like(dk_all)
        dv_all[...] = jnp.zeros_like(dv_all)

    probs = probs_ref[0]
    chosen = choice_ref[0:8, :].astype(F32)
    logit_grads = probs * (chosen - jnp.sum(probs * chosen, axis=0, keepdims=True))
    logit_grads = logit_grads.astype(BF16)
    router_grad_ref[...] += dot(logit_grads, b_ref[0])
    grad_normed = sum_ref[...].astype(F32) + dot_tn(logit_grads, router_ref[...])
    state = h_ref[0]
    scale = lax.rsqrt(jnp.mean(state * state, axis=-1, keepdims=True) + 1e-06)
    normed = state * scale
    gain_grad_ref[...] += jnp.sum(grad_normed * normed, axis=0, keepdims=True)
    scaled = gain_ref[...] * grad_normed
    inner = jnp.mean(normed * scaled, axis=-1, keepdims=True)
    grad_state = dy_ref[0].astype(F32) + scale * (scaled - normed * inner)
    dh_ref[...] = grad_state
    dattn = grad_state.astype(BF16)
    dattn_ref[0] = dattn
    do = dot_nt(dattn, wo_ref[...]).astype(BF16)
    do_all[...] = do
    products = do.astype(F32) * o_ref[0].astype(F32)
    for head in range(heads):
        columns = slice(head * LANES, (head + 1) * LANES)
        row = jnp.sum(products[:, columns], axis=1, keepdims=True)
        inner_all[head : head + 1, :] = jnp.broadcast_to(row, (BLOCK, LANES)).T[0:1, :]
    dq_all[...] = jnp.zeros_like(dq_all)
    here = rows_of(index, BLOCK)
    low = low_ref[0]
    query_at = index * BLOCK + lax.broadcasted_iota(jnp.int32, (BLOCK, BLOCK), 1)
    key_at = lax.broadcasted_iota(jnp.int32, (BLOCK, BLOCK), 0)

    def body(block, none):
        at = key_at + block * BLOCK
        valid = (at >= low) & (at <= query_at)
        there = rows_of(block, BLOCK)
        for head in range(heads):
            columns = slice(head * LANES, (head + 1) * LANES)
            key_columns = slice(wide + head * LANES, wide + (head + 1) * LANES)
            value_columns = slice(2 * wide + head * LANES, 2 * wide + (head + 1) * LANES)
            query = qkv_ref[0, here, columns]
            keys = qkv_ref[0, there, key_columns]
            scores = jnp.where(valid, dot_nt(keys, query), -1e30)
            probs = jnp.exp(scores - lse_ref[0, head : head + 1, :])
            grad_probs = dot_nt(qkv_ref[0, there, value_columns], do_all[:, columns])
            grad_scores = (probs * (grad_probs - inner_all[head : head + 1, :])).astype(BF16)
            dv_all[there, columns] += dot(probs.astype(BF16), do_all[:, columns])
            dk_all[there, columns] += dot(grad_scores, query)
            dq_all[:, columns] += dot_tn(grad_scores, keys)
        return none

    lax.fori_loop(first_block[meta[2] * BLOCKS + index], index + 1, body, 0)
    cosine, sine = cos_ref[...], sin_ref[...]
    for head in range(heads):
        columns = slice(head * LANES, (head + 1) * LANES)
        key_columns = slice(wide + head * LANES, wide + (head + 1) * LANES)
        value_columns = slice(2 * wide + head * LANES, 2 * wide + (head + 1) * LANES)
        dq = dq_all[:, columns] * 0.0625
        dk = dk_all[here, columns]
        dqkv_ref[0, :, columns] = (dq * cosine - pltpu.roll(dq, HEAD_DIM, 1) * sine).astype(BF16)
        dqkv_ref[0, :, key_columns] = (
            dk * cosine - pltpu.roll(dk, HEAD_DIM, 1) * sine
        ).astype(BF16)
        dqkv_ref[0, :, value_columns] = dv_all[here, columns].astype(BF16)
    part_ref[...] = dot_nt(dqkv_ref[0], wall_ref[...]).astype(BF16)


def attention_backward(
    meta, first_block, summed, choice, forward_kept, attention_kept, dy, gain, router, wall, wo, cosine, sine, low, kept
):
    width = summed.shape[1]
    wide = wo.shape[0]
    stored = 0 if kept is None else 2
    h, b, probs = forward_kept[0], forward_kept[1], forward_kept[7]
    unused_x, unused_a, qkv, o, lse = attention_kept
    saved = [
        shape_of((SLOTS, SEQ_LEN, 3 * wide), BF16),
        shape_of((SLOTS, SEQ_LEN, width), BF16),
    ]

    def at(step):
        return BLOCKS - 1 - step

    def slot_rows(columns, which):
        return pl.BlockSpec((1, BLOCK, columns), lambda s, m, f: (m[which], at(s), 0))

    def fixed(shape):
        return once(shape, lambda s, m, f: (0,) * len(shape))

    halves_of = BLOCKS // 2
    grid_spec = pltpu.PrefetchScalarGridSpec(
        num_scalar_prefetch=2,
        grid=(BLOCKS,),
        in_specs=[
            pl.BlockSpec((BLOCK, width), lambda s, m, f: (at(s), 0)),
            pl.BlockSpec((16, BLOCK), lambda s, m, f: (at(s) // halves_of, at(s) % halves_of)),
            pl.BlockSpec((1, EXPERTS, BLOCK), lambda s, m, f: (m[3], 0, at(s))),
            slot_rows(width, 1),
            slot_rows(width, 3),
            slot_rows(width, 3),
            fixed(gain.shape),
            fixed(router.shape),
            fixed(wall.shape),
            fixed(wo.shape),
            pl.BlockSpec((BLOCK, LANES), lambda s, m, f: (at(s), 0)),
            pl.BlockSpec((BLOCK, LANES), lambda s, m, f: (at(s), 0)),
            once((1, SEQ_LEN, 3 * wide), lambda s, m, f: (m[3], 0, 0)),
            slot_rows(wide, 3),
            pl.BlockSpec((1, 8, BLOCK), lambda s, m, f: (m[3], 0, at(s))),
            pl.BlockSpec((1, 1, BLOCK), lambda s, m, f: (m[2], 0, at(s))),
        ]
        + [pl.BlockSpec(memory_space=pl.ANY)] * stored,
        out_specs=[
            pl.BlockSpec((BLOCK, width), lambda s, m, f: (at(s), 0)),
            pl.BlockSpec((BLOCK, width), lambda s, m, f: (at(s), 0)),
            fixed((1, width)),
            fixed((8, width)),
            slot_rows(3 * wide, 1),
            slot_rows(width, 1),
        ],
        scratch_shapes=[
            pltpu.VMEM((SEQ_LEN, wide), F32),
            pltpu.VMEM((SEQ_LEN, wide), F32),
            pltpu.VMEM((BLOCK, wide), F32),
            pltpu.VMEM((BLOCK, wide), BF16),
            pltpu.VMEM((8, BLOCK), F32),
        ],
    )
    outs = pl.pallas_call(
        functools.partial(attention_backward_kernel, stored),
        grid_spec=grid_spec,
        out_shape=[
            shape_of((SEQ_LEN, width), BF16),
            shape_of((SEQ_LEN, width), F32),
            shape_of((1, width), F32),
            shape_of((8, width), F32),
        ]
        + saved,
        input_output_aliases={18 + k: 4 + k for k in range(stored)},
        compiler_params=pltpu.CompilerParams(vmem_limit_bytes=VMEM_BYTES),
        name="attention_backward",
    )(
        meta,
        first_block,
        summed,
        choice,
        probs,
        dy,
        h,
        b,
        gain,
        router,
        wall,
        wo,
        cosine,
        sine,
        qkv,
        o,
        lse,
        low,
        *(kept or ()),
    )
    return outs[:4], outs[4:]


def expert_grads_kernel(*refs):
    ins, out_ref = refs[:-1], refs[-1]
    (xa, xb), (ga, gb), (ua, ub), (ea, eb), (ha, hb) = (ins[2 * k : 2 * k + 2] for k in range(5))
    devices, unused, rows, unused = out_ref.shape
    pairs = [((xa, xb), (ga, gb)), ((xa, xb), (ua, ub)), ((ea, eb), (ha, hb))]
    for number, (left, right) in enumerate(pairs):
        for device in range(devices):
            columns = slice(device * rows, (device + 1) * rows)
            out_ref[device, number] = (
                dot_tn(left[0][0, 0, :, columns], right[0][0, 0])
                + dot_tn(left[1][0, 0, :, columns], right[1][0, 0])
            ).astype(BF16)


def expert_grads(first, count, devices, picked, hid, grad_gate, grad_lift, grad_expert):
    width, hidden = picked.shape[3], hid.shape[3]
    rows = width // devices

    def pair(columns):
        return [
            pl.BlockSpec(
                (1, 1, CAPACITY, columns), functools.partial(lambda slot, e: (slot, first + e, 0, 0), slot)
            )
            for slot in (1, 2)
        ]

    return pl.pallas_call(
        expert_grads_kernel,
        grid=(count,),
        in_specs=pair(width) + pair(hidden) + pair(hidden) + pair(width) + pair(hidden),
        out_specs=pl.BlockSpec((devices, 3, rows, hidden), lambda e: (0, e, 0, 0)),
        out_shape=shape_of((devices, 3 * count, rows, hidden), BF16),
        compiler_params=pltpu.CompilerParams(vmem_limit_bytes=VMEM_BYTES),
        name="expert_grads",
    )(
        *(picked, picked, grad_gate, grad_gate, grad_lift, grad_lift),
        *(grad_expert, grad_expert, hid, hid),
    )


def token_grads_kernel(count, *refs):
    lefts, rights = refs[:count], refs[count : 2 * count]
    outs, totals = refs[2 * count : 3 * count], refs[3 * count :]
    step = pl.program_id(0)

    @pl.when(step == 0)
    def _():
        for total in totals:
            total[...] = jnp.zeros_like(total)

    for left, right, total in zip(lefts, rights, totals):
        total[...] += dot_tn(left[0], right[0])

    @pl.when(step == pl.num_programs(0) - 1)
    def _():
        for out, total in zip(outs, totals):
            out[...] = total[...].astype(BF16)


def token_grads(lefts, rights):
    count = len(lefts)
    rows = 2 * BLOCK
    steps = SEQ_LEN // rows

    def spec(array):
        return pl.BlockSpec((1, rows, array.shape[2]), lambda s: (1 + s // steps, s % steps, 0))

    shapes = [(left.shape[2], right.shape[2]) for left, right in zip(lefts, rights)]
    return pl.pallas_call(
        functools.partial(token_grads_kernel, count),
        grid=(2 * steps,),
        in_specs=[spec(a) for a in lefts] + [spec(a) for a in rights],
        out_specs=[once(shape, lambda s: (0, 0)) for shape in shapes],
        out_shape=[shape_of(shape, BF16) for shape in shapes],
        scratch_shapes=[pltpu.VMEM(shape, F32) for shape in shapes],
        compiler_params=pltpu.CompilerParams(vmem_limit_bytes=VMEM_BYTES),
        name="token_grads",
    )(*lefts, *rights)


def rotary_tables():
    half = HEAD_DIM // 2
    rates = np.exp(-np.log(10000.0) * np.arange(half) * 2.0 / HEAD_DIM)
    angles = np.arange(SEQ_LEN)[:, None] * rates[None, :]
    cosine, sine = np.cos(angles), np.sin(angles)
    cosine = np.concatenate([cosine] * 4, axis=1)
    sine = np.concatenate([sine, sine, -sine, -sine], axis=1)
    return jnp.asarray(cosine, F32), jnp.asarray(sine, F32)


def paired(weight):
    rows = weight.shape[0]
    heads = weight.shape[1] // HEAD_DIM
    half = HEAD_DIM // 2
    split = weight.reshape(rows, heads, HEAD_DIM)
    swapped = jnp.concatenate([-split[:, :, half:], split[:, :, :half]], axis=2)
    return jnp.concatenate([split, swapped], axis=2).reshape(rows, heads * LANES)


def padded(weight):
    rows = weight.shape[0]
    heads = weight.shape[1] // HEAD_DIM
    split = weight.reshape(rows, heads, HEAD_DIM)
    return jnp.concatenate([split, jnp.zeros_like(split)], axis=2).reshape(rows, heads * LANES)


def unpadded(grads):
    rows = grads.shape[0]
    return grads.reshape(rows, -1, LANES)[:, :, :HEAD_DIM].reshape(rows, -1)


def places(routes):
    experts = jnp.arange(EXPERTS, dtype=jnp.int32)
    named = jnp.any(routes[:, :, :, None] == experts, axis=2)
    before = (
        jnp.arange(SEQ_LEN, dtype=jnp.int32)[:, None] > jnp.arange(SEQ_LEN, dtype=jnp.int32)
    ).astype(BF16)
    rank = jnp.einsum("ts,nse->nte", before, named.astype(BF16), preferred_element_type=F32)
    by_token = jnp.where(named, rank.astype(jnp.int32), -1)
    return by_token, jnp.swapaxes(by_token, 1, 2)


def first_allowed(lengths):
    ends = jnp.cumsum(lengths, axis=1)
    at = jnp.arange(SEQ_LEN, dtype=jnp.int32)
    starts = jnp.max(jnp.where(ends[:, None, :] <= at[None, :, None], ends[:, None, :], 0), axis=2)
    return jnp.maximum(starts, at[None, :] - (WINDOW - 1)).astype(jnp.int32)


def on_device(
    tokens,
    doc_lengths,
    routes,
    gain_attn,
    w_query,
    w_key,
    w_value,
    w_output,
    gain_ffn,
    w_router,
    w_gate_exp,
    w_up_exp,
    w_down_exp,
    w_gate_sh,
    w_up_sh,
    w_down_sh,
    cotangent,
):
    section = lax.axis_index("section")
    devices = lax.axis_size("dp")
    count = doc_lengths.shape[0]
    width = tokens.shape[1]
    cosine, sine = rotary_tables()
    wall = jnp.concatenate([paired(w_query[0]), paired(w_key[0]), padded(w_value[0])], axis=1)
    wo = padded(w_output[0].T).T
    router = w_router[0].T
    gain_a, gain_f = gain_attn.astype(F32), gain_ffn.astype(F32)
    feed_weights = (
        w_gate_exp[0],
        w_up_exp[0],
        w_down_exp[0],
        w_gate_sh[0],
        w_up_sh[0],
        w_down_sh[0],
    )
    pos, post = places(routes[0].reshape(count, SEQ_LEN, 2))
    low = first_allowed(doc_lengths)
    first_block = (low[:, ::BLOCK] // BLOCK).reshape(-1)
    low_column, low_row = low[:, :, None], low[:, None, :]

    received = jnp.zeros((SEQ_LEN, width), BF16)
    attention_kept, feed_kept, results = None, None, []
    for tick in range(count + 1):
        raw = tick - section
        active = (raw >= 0) & (raw < count)
        sequence = jnp.clip(raw, 0, count - 1)
        meta = jnp.stack([section, jnp.where(active, sequence + 1, 0), sequence]).astype(jnp.int32)
        part, attention_kept = attention_forward(
            meta,
            first_block,
            tokens,
            received,
            gain_a,
            wall,
            wo,
            cosine,
            sine,
            low_column,
            attention_kept,
        )
        (summed,) = tensor_sum([part], (6,), 0)
        part, state, feed_kept = feed_forward(
            meta, attention_kept[0], summed, gain_f, router, post, pos, feed_weights, feed_kept
        )
        result, received = output_relay(part, state, 1)
        results.append(result)

    received = jnp.zeros((SEQ_LEN, width), BF16)
    grads_kept, attention_grads_kept, inputs = None, None, []
    small = jnp.zeros((10, width), F32)
    for tick in range(count + 1):
        raw = tick - 1 + section
        active = (raw >= 0) & (raw < count)
        sequence = jnp.clip(raw, 0, count - 1)
        source = jnp.where(active, 2 - section, 0)
        meta = jnp.stack(
            [source, jnp.where(active, sequence + 1, 0), sequence, sequence + 1]
        ).astype(jnp.int32)
        part, choice, grads_kept = feed_backward(
            meta, cotangent, received, post, pos, feed_kept, feed_weights, grads_kept
        )
        summed, choice = tensor_sum([part, choice], (6, 1), 2)
        (part, grad_state, gain_grad, router_grad), attention_grads_kept = attention_backward(
            meta,
            first_block,
            summed,
            choice,
            feed_kept,
            attention_kept,
            grads_kept[0],
            gain_f,
            router,
            wall,
            wo,
            cosine,
            sine,
            low_row,
            attention_grads_kept,
        )
        layer_in = lax.dynamic_index_in_dim(attention_kept[0], sequence + 1, 0, False)
        grad_input, received, gain_attn_grad = input_relay(part, layer_in, grad_state, gain_a, 3)
        inputs.append(grad_input)
        small = small + jnp.concatenate([gain_attn_grad, gain_grad, router_grad], axis=0)

    def spread(array):
        return lax.psum_scatter(array, "dp", scatter_dimension=0, tiled=False)

    dy, hid, grad_gate, grad_lift, grad_expert, hid_sh, grad_gate_sh, grad_lift_sh = grads_kept
    groups = 4
    size = EXPERTS // groups
    expert_parts = [
        spread(
            expert_grads(
                group * size, size, devices, feed_kept[2], hid, grad_gate, grad_lift, grad_expert
            )
        )
        for group in range(groups)
    ]
    rows = width // devices
    shared = token_grads([feed_kept[1], feed_kept[1], dy], [grad_gate_sh, grad_lift_sh, hid_sh])
    shared = spread(jnp.stack(shared).reshape(3, devices, rows, -1).swapaxes(0, 1))
    projections, outward = token_grads(
        [attention_kept[1], attention_grads_kept[1]], [attention_grads_kept[0], attention_kept[3]]
    )
    wide = wo.shape[0]
    columns = w_query.shape[2]
    packed = jnp.concatenate(
        [
            2.0 * unpadded(projections[:, : 2 * wide]),
            unpadded(projections[:, 2 * wide :]),
            unpadded(outward),
            jnp.pad(small, ((0, 6), (0, 0))).T.astype(BF16),
        ],
        axis=1,
    )
    packed = spread(packed.reshape(devices, rows, -1)).astype(F32)
    shared = shared.astype(F32)
    experts = jnp.concatenate(expert_parts, axis=0).astype(F32)
    experts = experts.reshape(EXPERTS, 3, rows, -1)

    def choose(items):
        return jnp.concatenate(
            [jnp.where(section == 0, items[k], items[k + 1]) for k in range(count)], axis=0
        )

    layer_out = choose(results)
    input_grad = jnp.concatenate(
        [jnp.where(section == 0, inputs[k + 1], inputs[k]) for k in range(count)], axis=0
    )
    extra = 4 * columns
    return (
        layer_out[None],
        input_grad[None],
        packed[None, :, extra],
        packed[None, :, :columns],
        packed[None, :, columns : 2 * columns],
        packed[None, :, 2 * columns : 3 * columns],
        packed[:, 3 * columns : extra].T[None],
        packed[None, :, extra + 1],
        packed[None, :, extra + 2 : extra + 10],
        experts[None, :, 0],
        experts[None, :, 1],
        jnp.swapaxes(experts[:, 2], 1, 2)[None],
        shared[None, 0],
        shared[None, 1],
        shared[2].T[None],
    )


def solution(mesh):
    return jax.shard_map(
        on_device,
        mesh=mesh,
        in_specs=(
            P("dp", None),
            P("dp", None),
            P("section", "dp", None),
            P("section", None),
            P("section", None, "tensor"),
            P("section", None, "tensor"),
            P("section", None, "tensor"),
            P("section", "tensor", None),
            P("section", None),
            P("section", None, None),
            P("section", None, None, "tensor"),
            P("section", None, None, "tensor"),
            P("section", None, "tensor", None),
            P("section", None, "tensor"),
            P("section", None, "tensor"),
            P("section", "tensor", None),
            P("dp", None),
        ),
        out_specs=(
            P("section", "dp", None),
            P("section", "dp", None),
            P("section", "dp"),
            P("section", "dp", "tensor"),
            P("section", "dp", "tensor"),
            P("section", "dp", "tensor"),
            P("section", "tensor", "dp"),
            P("section", "dp"),
            P("section", "dp", None),
            P("section", None, "dp", "tensor"),
            P("section", None, "dp", "tensor"),
            P("section", None, "tensor", "dp"),
            P("section", "dp", "tensor"),
            P("section", "dp", "tensor"),
            P("section", "tensor", "dp"),
        ),
        check_vma=False,
    )
```

```python
import functools

import jax
import jax.numpy as jnp
import numpy as np
from jax import lax
from jax.experimental import pallas as pl
from jax.experimental.pallas import tpu as pltpu
from jax.sharding import PartitionSpec as P

HEAD_DIM = 64
EXPERTS = 8
SEQ_LEN = 1536
WINDOW = 1024
CAPACITY = 480
BLOCK = 256
BLOCKS = SEQ_LEN // BLOCK
LANES = 128
SLOTS = 3
VMEM_BYTES = 60 * 2**20
MESH = pl.DeviceIdType.MESH
F32 = jnp.float32
BF16 = jnp.bfloat16
NT = (((1,), (1,)), ((), ()))
TN = (((0,), (0,)), ((), ()))


def shape_of(shape, dtype):
    return jax.ShapeDtypeStruct(shape, dtype)


def dot(left, right):
    return jnp.dot(left, right, preferred_element_type=F32)


def dot_nt(left, right):
    return lax.dot_general(left, right, NT, preferred_element_type=F32)


def dot_tn(left, right):
    return lax.dot_general(left, right, TN, preferred_element_type=F32)


def once(shape, index):
    return pl.BlockSpec(shape, index, pipeline_mode=pl.Buffered(1))


def loop(count, body):
    lax.fori_loop(0, count, lambda step, none: (body(step), none)[1], 0)


def rows_of(step, size):
    return pl.ds(pl.multiple_of(step * size, size), size)


def greet(partners):
    barrier = pltpu.get_barrier_semaphore()
    for partner in partners:
        pl.semaphore_signal(barrier, inc=1, device_id=partner, device_id_type=MESH)
    pl.semaphore_wait(barrier, len(partners))


def remote(source, target, send, recv, device):
    return pltpu.make_async_remote_copy(
        src_ref=source,
        dst_ref=target,
        send_sem=send,
        recv_sem=recv,
        device_id=device,
        device_id_type=MESH,
    )


def partners_of():
    place = lax.axis_index("tensor")
    core = lax.rem(place, 2)
    near = {"tensor": place + 1 - 2 * core}
    far = {"tensor": lax.rem(place + 2, 4)}
    return core, near, far


def halves(rows, pieces):
    size = rows // 2
    part = size // pieces
    return [(size, step * part, part) for step in range(pieces)]


def sum_kernel(counts, *refs):
    arrays = len(counts)
    ins, outs = refs[:arrays], refs[arrays : 2 * arrays]
    first, kept, second = (refs[(2 + k) * arrays : (3 + k) * arrays] for k in range(3))
    send1, recv1, send2, recv2, send3, recv3 = refs[5 * arrays :]
    core, near, far = partners_of()
    greet([near, far])
    steps = []
    for which, count in enumerate(counts):
        for size, offset, part in halves(ins[which].shape[0], count):
            steps.append((which, size, offset, part))
    copies = []
    for number, (which, size, offset, part) in enumerate(steps):
        other = pl.ds(pl.multiple_of((1 - core) * size + offset, 16), part)
        copies.append(
            remote(
                ins[which].at[other],
                first[which].at[pl.ds(offset, part)],
                send1.at[number],
                recv1.at[number],
                near,
            )
        )
        copies[-1].start()
    crossing = []
    for number, (which, size, offset, part) in enumerate(steps):
        mine = pl.ds(pl.multiple_of(core * size + offset, 16), part)
        local = pl.ds(offset, part)
        copies[number].wait_recv()
        kept[which][local, :] = (
            ins[which][mine, :].astype(F32) + first[which][local, :].astype(F32)
        ).astype(BF16)
        crossing.append(
            remote(
                kept[which].at[local],
                second[which].at[local],
                send2.at[number],
                recv2.at[number],
                far,
            )
        )
        crossing[-1].start()
    back = []
    for number, (which, size, offset, part) in enumerate(steps):
        mine = pl.ds(pl.multiple_of(core * size + offset, 16), part)
        local = pl.ds(offset, part)
        crossing[number].wait_recv()
        outs[which][mine, :] = (
            kept[which][local, :].astype(F32) + second[which][local, :].astype(F32)
        ).astype(BF16)
        back.append(
            remote(
                outs[which].at[mine],
                outs[which].at[mine],
                send3.at[number],
                recv3.at[number],
                near,
            )
        )
        back[-1].start()
    for copy in back:
        copy.wait_recv()
    for copy in copies + crossing + back:
        copy.wait_send()


def tensor_sum(arrays, counts, identity):
    scratch = []
    for copy in range(3):
        scratch += [pltpu.VMEM((a.shape[0] // 2, a.shape[1]), BF16) for a in arrays]
    total = sum(counts)
    scratch += [pltpu.SemaphoreType.DMA((total,))] * 6
    return pl.pallas_call(
        functools.partial(sum_kernel, counts),
        out_shape=[shape_of(a.shape, BF16) for a in arrays],
        in_specs=[pl.BlockSpec(memory_space=pltpu.VMEM)] * len(arrays),
        out_specs=[pl.BlockSpec(memory_space=pltpu.VMEM)] * len(arrays),
        scratch_shapes=scratch,
        compiler_params=pltpu.CompilerParams(
            collective_id=identity, has_side_effects=True, vmem_limit_bytes=VMEM_BYTES
        ),
        name="tensor_sum",
    )(*arrays)


def gather_kernel(pieces, own_ref, out_ref, sends, recvs):
    place = lax.axis_index("tensor")
    core, near, far = partners_of()
    greet([near, far])
    far_place = lax.rem(place + 2, 4)
    size = own_ref.shape[0] // pieces
    first, crossing, passed = [], [], []
    for piece in range(pieces):
        rows = pl.ds(piece * size, size)
        crossing.append(
            remote(
                own_ref.at[rows],
                out_ref.at[place, rows],
                sends.at[0, piece],
                recvs.at[0, piece],
                far,
            )
        )
        crossing[-1].start()
    for piece in range(pieces):
        rows = pl.ds(piece * size, size)
        first.append(
            remote(
                own_ref.at[rows],
                out_ref.at[place, rows],
                sends.at[1, piece],
                recvs.at[1, piece],
                near,
            )
        )
        first[-1].start()
    out_ref[place] = own_ref[...]
    for piece in range(pieces):
        rows = pl.ds(piece * size, size)
        crossing[piece].wait_recv()
        passed.append(
            remote(
                out_ref.at[far_place, rows],
                out_ref.at[far_place, rows],
                sends.at[2, piece],
                recvs.at[2, piece],
                near,
            )
        )
        passed[-1].start()
    for copy in first + passed:
        copy.wait_recv()
    for copy in first + crossing + passed:
        copy.wait_send()


def tensor_gather(own, identity, pieces=6):
    whole = pl.BlockSpec(memory_space=pltpu.VMEM)
    return pl.pallas_call(
        functools.partial(gather_kernel, pieces),
        out_shape=shape_of((4,) + own.shape, BF16),
        in_specs=[whole],
        out_specs=whole,
        scratch_shapes=[pltpu.SemaphoreType.DMA((3, pieces))] * 2,
        compiler_params=pltpu.CompilerParams(
            collective_id=identity, has_side_effects=True, vmem_limit_bytes=VMEM_BYTES
        ),
        name="tensor_gather",
    )(own)


def relay_kernel(
    pieces,
    finish,
    part_ref,
    next_ref,
    first,
    kept,
    second,
    sends,
    recvs,
):
    core, near, far = partners_of()
    across = {"section": 1 - lax.axis_index("section")}
    greet([near, far, across])
    steps = halves(part_ref.shape[0], pieces)

    def place(size, offset, part, side):
        return pl.ds(pl.multiple_of(side * size + offset, 16), part)

    copies = []
    for number, (size, offset, part) in enumerate(steps):
        copies.append(
            remote(
                part_ref.at[place(size, offset, part, 1 - core)],
                first.at[pl.ds(offset, part)],
                sends.at[0, number],
                recvs.at[0, number],
                near,
            )
        )
        copies[-1].start()
    crossing = []
    for number, (size, offset, part) in enumerate(steps):
        local = pl.ds(offset, part)
        copies[number].wait_recv()
        kept[local, :] = (
            part_ref[place(size, offset, part, core), :].astype(F32)
            + first[local, :].astype(F32)
        ).astype(BF16)
        crossing.append(
            remote(
                kept.at[local],
                second.at[local],
                sends.at[1, number],
                recvs.at[1, number],
                far,
            )
        )
        crossing[-1].start()
    back, passed = [], []
    for number, (size, offset, part) in enumerate(steps):
        local = pl.ds(offset, part)
        mine = place(size, offset, part, core)
        crossing[number].wait_recv()
        total = (kept[local, :].astype(F32) + second[local, :].astype(F32)).astype(BF16)
        source, given = finish(total, mine, local, True)
        back.append(
            remote(
                source,
                source,
                sends.at[2, number],
                recvs.at[2, number],
                near,
            )
        )
        back[-1].start()
        passed.append(
            remote(
                given,
                next_ref.at[mine],
                sends.at[3, number],
                recvs.at[3, number],
                across,
            )
        )
        passed[-1].start()
    spread = []
    for number, (size, offset, part) in enumerate(steps):
        mine = place(size, offset, part, core)
        passed[number].wait_recv()
        spread.append(
            remote(
                next_ref.at[mine],
                next_ref.at[mine],
                sends.at[4, number],
                recvs.at[4, number],
                near,
            )
        )
        spread[-1].start()
    for number, (size, offset, part) in enumerate(steps):
        back[number].wait_recv()
        finish(None, place(size, offset, part, 1 - core), pl.ds(offset, part), False)
    for copy in spread:
        copy.wait_recv()
    for copy in copies + crossing + back + passed + spread:
        copy.wait_send()


def output_kernel(
    pieces,
    tick,
    part_ref,
    states_ref,
    out_ref,
    next_ref,
    first,
    kept,
    second,
    state,
    loaded,
    sends,
    recvs,
):
    core = lax.rem(lax.axis_index("tensor"), 2)
    half = part_ref.shape[0] // 2
    slot = lax.rem(tick + 1 - lax.axis_index("section"), states_ref.shape[0])
    load = pltpu.make_async_copy(
        states_ref.at[slot, pl.ds(pl.multiple_of(core * half, 16), half)], state, loaded
    )
    load.start()
    arrived = []

    def finish(total, rows, local, own):
        if own:
            if not arrived:
                load.wait()
                arrived.append(True)
            out_ref[rows, :] = (state[local, :] + total.astype(F32)).astype(BF16)
            return out_ref.at[rows], out_ref.at[rows]

    relay_kernel(pieces, finish, part_ref, next_ref, first, kept, second, sends, recvs)


def input_kernel(
    pieces,
    part_ref,
    layer_in_ref,
    grad_state_ref,
    gain_ref,
    grad_ref,
    next_ref,
    grad_gain_ref,
    first,
    kept,
    second,
    full,
    given,
    gains,
    sends,
    recvs,
):
    gains[...] = jnp.zeros_like(gains)

    def rows_back(rows, side):
        grad_normed = full[rows, :].astype(F32)
        values = layer_in_ref[rows, :].astype(F32)
        scale = lax.rsqrt(jnp.mean(values * values, axis=-1, keepdims=True) + 1e-06)
        normed = values * scale
        scaled = gain_ref[...] * grad_normed
        inner = jnp.mean(normed * scaled, axis=-1, keepdims=True)
        grad = grad_state_ref[rows, :] + scale * (scaled - normed * inner)
        grad_ref[rows, :] = grad
        gains[side : side + 1, :] += jnp.sum(grad_normed * normed, axis=0, keepdims=True)
        return grad

    def finish(total, rows, local, own):
        if own:
            full[rows, :] = total
            given[local, :] = rows_back(rows, 0).astype(BF16)
            return full.at[rows], given.at[local]
        rows_back(rows, 1)

    relay_kernel(pieces, finish, part_ref, next_ref, first, kept, second, sends, recvs)
    grad_gain_ref[...] = gains[0:1, :] + gains[1:2, :]


def relay_scratch(rows, width, pieces):
    half = [pltpu.VMEM((rows // 2, width), BF16)] * 3
    return half, [pltpu.SemaphoreType.DMA((5, pieces))] * 2


def output_relay(part, states, tick, identity, pieces=12):
    rows, width = part.shape
    half, semaphores = relay_scratch(rows, width, pieces)
    whole = pl.BlockSpec(memory_space=pltpu.VMEM)
    return pl.pallas_call(
        functools.partial(output_kernel, pieces, tick),
        out_shape=[shape_of((rows, width), BF16)] * 2,
        in_specs=[whole, pl.BlockSpec(memory_space=pl.ANY)],
        out_specs=[whole] * 2,
        scratch_shapes=half
        + [pltpu.VMEM((rows // 2, width), F32), pltpu.SemaphoreType.DMA]
        + semaphores,
        compiler_params=pltpu.CompilerParams(
            collective_id=identity, has_side_effects=True, vmem_limit_bytes=VMEM_BYTES
        ),
        name="output_relay",
    )(part, states)


def input_relay(part, layer_in, grad_state, gain, identity, pieces=12):
    rows, width = part.shape
    half, semaphores = relay_scratch(rows, width, pieces)
    whole = pl.BlockSpec(memory_space=pltpu.VMEM)
    return pl.pallas_call(
        functools.partial(input_kernel, pieces),
        out_shape=[
            shape_of((rows, width), F32),
            shape_of((rows, width), BF16),
            shape_of((1, width), F32),
        ],
        in_specs=[whole] * 4,
        out_specs=[whole] * 3,
        scratch_shapes=half
        + [
            pltpu.VMEM((rows, width), BF16),
            pltpu.VMEM((rows // 2, width), BF16),
            pltpu.VMEM((8, width), F32),
        ]
        + semaphores,
        compiler_params=pltpu.CompilerParams(
            collective_id=identity, has_side_effects=True, vmem_limit_bytes=VMEM_BYTES
        ),
        name="input_relay",
    )(part, layer_in, grad_state, gain)


def attention_forward_kernel(
    stored,
    meta,
    first_block,
    tok_ref,
    rec_ref,
    gain_ref,
    wall_ref,
    cos_ref,
    sin_ref,
    low_ref,
    *rest,
):
    rest = rest[stored:]
    packed_ref, x_ref, a_ref, qkv_ref, o_ref, lse_ref = rest[:6]
    keys, values, scores, tops, sums, mixed = rest[6:]
    index = pl.program_id(0)
    heads = wall_ref.shape[1] // (3 * LANES)
    wide = heads * LANES
    x = jnp.where(meta[0] == 0, tok_ref[...], rec_ref[...])
    x_ref[0] = x
    x = x.astype(F32)
    normed = gain_ref[...] * x * lax.rsqrt(jnp.mean(x * x, axis=-1, keepdims=True) + 1e-06)
    normed = normed.astype(BF16)
    a_ref[0] = normed
    cosine, sine = cos_ref[...], sin_ref[...]
    here = rows_of(index, BLOCK)
    for group in range(2 * heads):
        columns = slice(group * LANES, (group + 1) * LANES)
        pre = dot(normed, wall_ref[:, columns])
        turned = pre * cosine + pltpu.roll(pre, HEAD_DIM, 1) * sine
        if group < heads:
            turned = turned * 0.0625
        qkv_ref[0, :, columns] = turned.astype(BF16)
    qkv_ref[0, :, 2 * wide :] = dot(normed, wall_ref[:, 2 * wide :]).astype(BF16)
    keys[here, :] = qkv_ref[0, :, wide : 2 * wide]
    values[here, :] = qkv_ref[0, :, 2 * wide :]
    low = low_ref[0]
    query_at = index * BLOCK + lax.broadcasted_iota(jnp.int32, (BLOCK, BLOCK), 0)
    key_at = lax.broadcasted_iota(jnp.int32, (BLOCK, BLOCK), 1)
    tops[...] = jnp.full_like(tops, -1e30)
    sums[...] = jnp.zeros_like(sums)
    mixed[...] = jnp.zeros_like(mixed)
    begin = first_block[meta[2] * BLOCKS + index]

    def score(block, none):
        at = key_at + block * BLOCK
        valid = (at >= low) & (at <= query_at)
        there = rows_of(block, BLOCK)
        for head in range(heads):
            columns = slice(head * LANES, (head + 1) * LANES)
            raw = dot_nt(qkv_ref[0, :, columns], keys[there, columns])
            raw = jnp.where(valid, raw, -1e30)
            scores[head, block] = raw
            tops[head] = jnp.maximum(
                tops[head], jnp.maximum(raw[:, :LANES], raw[:, LANES:])
            )
        return none

    lax.fori_loop(begin, index + 1, score, 0)
    top = [jnp.max(tops[head], axis=1, keepdims=True) for head in range(heads)]

    def mix(block, none):
        there = rows_of(block, BLOCK)
        for head in range(heads):
            columns = slice(head * LANES, (head + 1) * LANES)
            weights = jnp.exp(scores[head, block] - top[head])
            sums[head] += weights[:, :LANES] + weights[:, LANES:]
            mixed[:, columns] += dot(weights.astype(BF16), values[there, columns])
        return none

    lax.fori_loop(begin, index + 1, mix, 0)
    for head in range(heads):
        columns = slice(head * LANES, (head + 1) * LANES)
        total = jnp.sum(sums[head], axis=1, keepdims=True)
        o_ref[0, :, columns] = (mixed[:, columns] / total).astype(BF16)
        logsum = jnp.broadcast_to(top[head] + jnp.log(total), (BLOCK, LANES))
        lse_ref[0, head : head + 1, :] = logsum.T[0:1, :]
    half = BLOCK // 2
    packed_ref[...] = jnp.concatenate(
        [
            o_ref[0, side * half : (side + 1) * half, head * LANES : head * LANES + HEAD_DIM]
            for side in range(2)
            for head in range(heads)
        ],
        axis=1,
    )


def attention_forward(meta, first_block, tokens, received, gain, wall, cosine, sine, low, kept):
    width = tokens.shape[1]
    wide = wall.shape[1] // 3
    heads = wide // LANES
    stored = 0 if kept is None else 5
    saved = [
        shape_of((SLOTS, SEQ_LEN, width), BF16),
        shape_of((SLOTS, SEQ_LEN, width), BF16),
        shape_of((SLOTS, SEQ_LEN, 3 * wide), BF16),
        shape_of((SLOTS, SEQ_LEN, wide), BF16),
        shape_of((SLOTS, 8, SEQ_LEN), F32),
    ]

    def slot_rows(columns):
        return pl.BlockSpec((1, BLOCK, columns), lambda i, m, f: (m[1], i, 0))

    grid_spec = pltpu.PrefetchScalarGridSpec(
        num_scalar_prefetch=2,
        grid=(BLOCKS,),
        in_specs=[
            pl.BlockSpec((BLOCK, width), lambda i, m, f: (m[2] * BLOCKS + i, 0)),
            pl.BlockSpec((BLOCK, width), lambda i, m, f: (i, 0)),
            once((1, width), lambda i, m, f: (0, 0)),
            once(wall.shape, lambda i, m, f: (0, 0)),
            pl.BlockSpec((BLOCK, LANES), lambda i, m, f: (i, 0)),
            pl.BlockSpec((BLOCK, LANES), lambda i, m, f: (i, 0)),
            pl.BlockSpec((1, BLOCK, 1), lambda i, m, f: (m[2], i, 0)),
        ]
        + [pl.BlockSpec(memory_space=pl.ANY)] * stored,
        out_specs=[
            pl.BlockSpec((BLOCK // 2, wide), lambda i, m, f: (i, 0)),
            slot_rows(width),
            slot_rows(width),
            slot_rows(3 * wide),
            slot_rows(wide),
            pl.BlockSpec((1, 8, BLOCK), lambda i, m, f: (m[1], 0, i)),
        ],
        scratch_shapes=[
            pltpu.VMEM((SEQ_LEN, wide), BF16),
            pltpu.VMEM((SEQ_LEN, wide), BF16),
            pltpu.VMEM((heads, BLOCKS, BLOCK, BLOCK), F32),
            pltpu.VMEM((heads, BLOCK, LANES), F32),
            pltpu.VMEM((heads, BLOCK, LANES), F32),
            pltpu.VMEM((BLOCK, wide), F32),
        ],
    )
    outs = pl.pallas_call(
        functools.partial(attention_forward_kernel, stored),
        grid_spec=grid_spec,
        out_shape=[shape_of((SEQ_LEN // 2, wide), BF16)] + saved,
        input_output_aliases={9 + k: 1 + k for k in range(stored)},
        compiler_params=pltpu.CompilerParams(vmem_limit_bytes=VMEM_BYTES),
        name="attention_forward",
    )(
        meta,
        first_block,
        tokens,
        received,
        gain,
        wall,
        cosine,
        sine,
        low,
        *(kept or ()),
    )
    return outs[0], outs[1:]


PAIR = 2
ROWS = 512
ROW_STEPS = SEQ_LEN // ROWS
PAIR_STEPS = EXPERTS // PAIR
SPAN = 512
CHUNK = 96


def build_pick(first, chunks, post_ref, probs, pick, gates):
    for which, step in chunks:
        row = pl.ds(first + which, 1)
        slot_at = step * CHUNK + lax.broadcasted_iota(jnp.int32, (CHUNK, SEQ_LEN), 0)
        here = slot_at == post_ref[0, row, :]
        rows = slice(which * CAPACITY + step * CHUNK, which * CAPACITY + (step + 1) * CHUNK)
        pick[rows, :] = jnp.where(here, 1.0, 0.0).astype(BF16)
        if probs is not None:
            chosen = jnp.sum(jnp.where(here, probs[row, :], 0.0), axis=1, keepdims=True)
            gates[rows, :] = jnp.broadcast_to(chosen, (CHUNK, LANES))


def build_gates(first, post_ref, probs, gates):
    for which in range(PAIR):
        row = pl.ds(first + which, 1)
        for step in range(CAPACITY // CHUNK):
            slot_at = step * CHUNK + lax.broadcasted_iota(jnp.int32, (CHUNK, SEQ_LEN), 0)
            here = slot_at == post_ref[0, row, :]
            rows = slice(which * CAPACITY + step * CHUNK, which * CAPACITY + (step + 1) * CHUNK)
            chosen = jnp.sum(jnp.where(here, probs[row, :], 0.0), axis=1, keepdims=True)
            gates[rows, :] = jnp.broadcast_to(chosen, (CHUNK, LANES))


def build_put(first, rows, pos_ref, put):
    places = pos_ref[0, rows, :]
    lane = lax.broadcasted_iota(jnp.int32, places.shape, 1)
    slot_at = lax.broadcasted_iota(jnp.int32, (places.shape[0], SPAN), 1)
    for which in range(PAIR):
        place = jnp.sum(jnp.where(lane == first + which, places, 0), axis=1, keepdims=True)
        put[rows, which * SPAN : (which + 1) * SPAN] = jnp.where(
            slot_at == place, 1.0, 0.0
        ).astype(BF16)


ALL_CHUNKS = [(which, step) for which in range(PAIR) for step in range(CAPACITY // CHUNK)]


def of_pair(which):
    return slice(which * CAPACITY, (which + 1) * CAPACITY)


def feed_forward_kernel(
    stored,
    meta,
    x_ref,
    ag_ref,
    wo_ref,
    gain_ref,
    router_ref,
    post_ref,
    pos_ref,
    wg_ref,
    wu_ref,
    wd_ref,
    wgs_ref,
    wus_ref,
    wds_ref,
    *rest,
):
    rest = rest[stored:]
    part_ref, h_ref, b_ref, xe_ref, g_ref, u_ref, gs_ref, us_ref, probs_ref = rest[:9]
    total, normed, probs, pick, put, gates, scaled = rest[9:]
    step = pl.program_id(0)
    pair = jnp.maximum(step - ROW_STEPS, 0)

    def activate(gate, lift, gate_out, lift_out):
        gate_out[...] = gate.astype(BF16)
        lift_out[...] = lift.astype(BF16)
        return (gate / (1.0 + jnp.exp(-gate)) * lift).astype(BF16)

    @pl.when(step < ROW_STEPS)
    def _():
        half = BLOCK // 2
        columns = ag_ref.shape[2] // 2
        mixed = jnp.concatenate(
            [
                jnp.concatenate(
                    [
                        ag_ref[device, block : block + half, side * columns : (side + 1) * columns]
                        for device in range(4)
                    ],
                    axis=1,
                )
                for block in range(0, ROWS // 2, half)
                for side in range(2)
            ],
            axis=0,
        )
        state = x_ref[0].astype(F32) + dot(mixed, wo_ref[...])
        h_ref[0] = state
        scale = lax.rsqrt(jnp.mean(state * state, axis=-1, keepdims=True) + 1e-06)
        b = (gain_ref[...] * state * scale).astype(BF16)
        b_ref[0] = b
        here = rows_of(step, ROWS)
        normed[here, :] = b
        logits = dot_nt(router_ref[...], b)
        weights = jnp.exp(logits - jnp.max(logits, axis=0, keepdims=True))
        weights = weights / jnp.sum(weights, axis=0, keepdims=True)
        probs_ref[0] = weights
        probs[:, here] = weights
        hidden = activate(dot(b, wgs_ref[...]), dot(b, wus_ref[...]), gs_ref.at[0], us_ref.at[0])
        total[here, :] = dot(hidden, wds_ref[...])

    @pl.when(step == 0)
    def _():
        build_pick(0, ALL_CHUNKS, post_ref, None, pick, gates)
        scaled[...] = jnp.zeros_like(scaled)

    def experts(combine):
        for start in range(0, SEQ_LEN, ROWS):
            rows = pl.ds(start, ROWS)
            if combine:
                total[rows, :] += dot(put[rows, :], scaled[...])
            build_put(pair * PAIR, rows, pos_ref, put)
        picked = dot(pick[...], normed[...]).astype(BF16)
        build_gates(pair * PAIR, post_ref, probs, gates)
        build_pick(
            jnp.minimum(pair + 1, PAIR_STEPS - 1) * PAIR, ALL_CHUNKS, post_ref, None, pick, gates
        )
        for which in range(PAIR):
            rows = picked[of_pair(which), :]
            xe_ref[0, which] = rows
            hidden = activate(
                dot(rows, wg_ref[which]), dot(rows, wu_ref[which]), g_ref.at[0, which], u_ref.at[0, which]
            )
            scaled[which * SPAN : which * SPAN + CAPACITY, :] = (
                dot(hidden, wd_ref[which]) * gates[of_pair(which), 0:1]
            ).astype(BF16)

    @pl.when(step == ROW_STEPS)
    def _():
        experts(False)

    @pl.when((step > ROW_STEPS) & (step < ROW_STEPS + PAIR_STEPS))
    def _():
        experts(True)

    @pl.when(step == ROW_STEPS + PAIR_STEPS)
    def _():
        for start in range(0, SEQ_LEN, ROWS):
            rows = pl.ds(start, ROWS)
            part_ref[rows, :] = (total[rows, :] + dot(put[rows, :], scaled[...])).astype(BF16)


def step_specs():
    def row_at(step):
        return jnp.minimum(step, ROW_STEPS - 1)

    def pair_at(step):
        return jnp.clip(step - ROW_STEPS, 0, PAIR_STEPS - 1)

    return row_at, pair_at


def feed_forward(
    meta, layer_in, gathered, out_weight, gain, router, post, pos, weights, kept
):
    width = layer_in.shape[2]
    wg, wu, wd, wgs, wus, wds = weights
    hidden = wg.shape[2]
    stored = 0 if kept is None else 8
    saved = [
        shape_of((SLOTS, SEQ_LEN, width), F32),
        shape_of((SLOTS, SEQ_LEN, width), BF16),
        shape_of((SLOTS, EXPERTS, CAPACITY, width), BF16),
        shape_of((SLOTS, EXPERTS, CAPACITY, hidden), BF16),
        shape_of((SLOTS, EXPERTS, CAPACITY, hidden), BF16),
        shape_of((SLOTS, SEQ_LEN, hidden), BF16),
        shape_of((SLOTS, SEQ_LEN, hidden), BF16),
        shape_of((SLOTS, EXPERTS, SEQ_LEN), F32),
    ]
    row_at, pair_at = step_specs()

    def slot_rows(columns):
        return pl.BlockSpec((1, ROWS, columns), lambda s, m: (m[1], row_at(s), 0))

    def slot_pair(columns):
        return pl.BlockSpec((1, PAIR, CAPACITY, columns), lambda s, m: (m[1], pair_at(s), 0, 0))

    def fixed(shape):
        return once(shape, lambda s, m: (0,) * len(shape))

    def of_pairs(array):
        return pl.BlockSpec((PAIR,) + array.shape[1:], lambda s, m: (pair_at(s), 0, 0))

    grid_spec = pltpu.PrefetchScalarGridSpec(
        num_scalar_prefetch=1,
        grid=(ROW_STEPS + PAIR_STEPS + 1,),
        in_specs=[
            slot_rows(width),
            pl.BlockSpec((4, ROWS // 2, gathered.shape[2]), lambda s, m: (0, row_at(s), 0)),
            fixed(out_weight.shape),
            fixed(gain.shape),
            fixed(router.shape),
            once((1, EXPERTS, SEQ_LEN), lambda s, m: (m[2], 0, 0)),
            once((1, SEQ_LEN, EXPERTS), lambda s, m: (m[2], 0, 0)),
            of_pairs(wg),
            of_pairs(wu),
            of_pairs(wd),
            fixed(wgs.shape),
            fixed(wus.shape),
            fixed(wds.shape),
        ]
        + [pl.BlockSpec(memory_space=pl.ANY)] * stored,
        out_specs=[
            fixed((SEQ_LEN, width)),
            slot_rows(width),
            slot_rows(width),
            slot_pair(width),
            slot_pair(hidden),
            slot_pair(hidden),
            slot_rows(hidden),
            slot_rows(hidden),
            pl.BlockSpec((1, EXPERTS, ROWS), lambda s, m: (m[1], 0, row_at(s))),
        ],
        scratch_shapes=[
            pltpu.VMEM((SEQ_LEN, width), F32),
            pltpu.VMEM((SEQ_LEN, width), BF16),
            pltpu.VMEM((EXPERTS, SEQ_LEN), F32),
            pltpu.VMEM((PAIR * CAPACITY, SEQ_LEN), BF16),
            pltpu.VMEM((SEQ_LEN, PAIR * SPAN), BF16),
            pltpu.VMEM((PAIR * CAPACITY, LANES), F32),
            pltpu.VMEM((PAIR * SPAN, width), BF16),
        ],
    )
    outs = pl.pallas_call(
        functools.partial(feed_forward_kernel, stored),
        grid_spec=grid_spec,
        out_shape=[shape_of((SEQ_LEN, width), BF16)] + saved,
        input_output_aliases={14 + k: 1 + k for k in range(stored)},
        compiler_params=pltpu.CompilerParams(vmem_limit_bytes=VMEM_BYTES),
        name="feed_forward",
    )(
        meta,
        layer_in,
        gathered,
        out_weight,
        gain,
        router,
        post,
        pos,
        wg,
        wu,
        wd,
        wgs,
        wus,
        wds,
        *(kept or ()),
    )
    return outs[0], outs[1:]


def feed_backward_kernel(
    stored,
    meta,
    cot_ref,
    rec_ref,
    post_ref,
    pos_ref,
    g_ref,
    u_ref,
    gs_ref,
    us_ref,
    probs_ref,
    wg_ref,
    wu_ref,
    wd_ref,
    wgs_ref,
    wus_ref,
    wds_ref,
    *rest,
):
    rest = rest[stored:]
    part_ref, choice_ref = rest[:2]
    dy_ref, hid_ref, dg_ref, du_ref, de_ref, hids_ref, dgs_ref, dus_ref = rest[2:10]
    total, given, pick, put, gates, slots, choice = rest[10:]
    step = pl.program_id(0)
    pair = jnp.maximum(step - ROW_STEPS, 0)

    def pull(grad, weight, gate, lift):
        gate, lift = gate.astype(F32), lift.astype(F32)
        sigma = 1.0 / (1.0 + jnp.exp(-gate))
        swish = gate * sigma
        hidden = (swish * lift).astype(BF16)
        inner = None
        if weight is not None:
            inner = jnp.sum(hidden.astype(F32) * grad, axis=1, keepdims=True)
            grad = grad * weight
        grad_gate = (grad * lift * (sigma + swish * (1.0 - sigma))).astype(BF16)
        return hidden, grad_gate, (grad * swish).astype(BF16), inner

    @pl.when(step < ROW_STEPS)
    def _():
        dy = jnp.where(meta[0] == 1, cot_ref[...], rec_ref[...])
        dy = jnp.where(meta[0] == 0, jnp.zeros_like(dy), dy)
        dy_ref[0] = dy
        here = rows_of(step, ROWS)
        given[here, :] = dy
        hidden, grad_gate, grad_lift, unused = pull(
            dot_nt(dy, wds_ref[...]), None, gs_ref[0], us_ref[0]
        )
        hids_ref[0] = hidden
        dgs_ref[0] = grad_gate
        dus_ref[0] = grad_lift
        total[here, :] = dot_nt(grad_gate, wgs_ref[...]) + dot_nt(grad_lift, wus_ref[...])

    @pl.when(step == 0)
    def _():
        build_pick(0, ALL_CHUNKS, post_ref, None, pick, gates)
        slots[...] = jnp.zeros_like(slots)

    def experts(combine):
        for start in range(0, SEQ_LEN, ROWS):
            rows = pl.ds(start, ROWS)
            if combine:
                total[rows, :] += dot(put[rows, :], slots[...])
            build_put(pair * PAIR, rows, pos_ref, put)
        picked = dot(pick[...], given[...]).astype(BF16)
        build_gates(pair * PAIR, post_ref, probs_ref.at[0], gates)
        build_pick(
            jnp.minimum(pair + 1, PAIR_STEPS - 1) * PAIR, ALL_CHUNKS, post_ref, None, pick, gates
        )
        for which in range(PAIR):
            rows = picked[of_pair(which), :]
            weight = gates[of_pair(which), 0:1]
            hidden, grad_gate, grad_lift, inner = pull(
                dot_nt(rows, wd_ref[which]), weight, g_ref[0, which], u_ref[0, which]
            )
            hid_ref[0, which] = hidden
            dg_ref[0, which] = grad_gate
            du_ref[0, which] = grad_lift
            de_ref[0, which] = (weight * rows.astype(F32)).astype(BF16)
            row = pl.ds(pair * PAIR + which, 1)
            chosen = jnp.zeros((1, SEQ_LEN), F32)
            for chunk in range(CAPACITY // CHUNK):
                slot_at = chunk * CHUNK + lax.broadcasted_iota(jnp.int32, (CHUNK, SEQ_LEN), 0)
                here = slot_at == post_ref[0, row, :]
                chosen += jnp.sum(
                    jnp.where(here, inner[chunk * CHUNK : (chunk + 1) * CHUNK], 0.0),
                    axis=0,
                    keepdims=True,
                )
            choice[row, :] = chosen
            slots[which * SPAN : which * SPAN + CAPACITY, :] = (
                dot_nt(grad_gate, wg_ref[which]) + dot_nt(grad_lift, wu_ref[which])
            ).astype(BF16)

    @pl.when(step == ROW_STEPS)
    def _():
        experts(False)

    @pl.when((step > ROW_STEPS) & (step < ROW_STEPS + PAIR_STEPS))
    def _():
        experts(True)

    @pl.when(step == ROW_STEPS + PAIR_STEPS)
    def _():
        for start in range(0, SEQ_LEN, ROWS):
            rows = pl.ds(start, ROWS)
            part_ref[rows, :] = (total[rows, :] + dot(put[rows, :], slots[...])).astype(BF16)
        half = SEQ_LEN // 2
        blank = jnp.zeros((8, half), F32)
        choice_ref[...] = jnp.concatenate(
            [choice[:, :half], blank, choice[:, half:], blank], axis=0
        ).astype(BF16)


def feed_backward(meta, cotangent, received, post, pos, forward_kept, weights, kept):
    width = cotangent.shape[1]
    wg, wu, wd, wgs, wus, wds = weights
    hidden = wg.shape[2]
    stored = 0 if kept is None else 8
    unused_h, unused_b, unused_x, gate, lift, gate_sh, lift_sh, probs = forward_kept
    saved = [
        shape_of((SLOTS, SEQ_LEN, width), BF16),
        shape_of((SLOTS, EXPERTS, CAPACITY, hidden), BF16),
        shape_of((SLOTS, EXPERTS, CAPACITY, hidden), BF16),
        shape_of((SLOTS, EXPERTS, CAPACITY, hidden), BF16),
        shape_of((SLOTS, EXPERTS, CAPACITY, width), BF16),
        shape_of((SLOTS, SEQ_LEN, hidden), BF16),
        shape_of((SLOTS, SEQ_LEN, hidden), BF16),
        shape_of((SLOTS, SEQ_LEN, hidden), BF16),
    ]
    row_at, pair_at = step_specs()

    def slot_rows(columns, which):
        return pl.BlockSpec((1, ROWS, columns), lambda s, m: (m[which], row_at(s), 0))

    def slot_pair(columns, which):
        return pl.BlockSpec(
            (1, PAIR, CAPACITY, columns), lambda s, m: (m[which], pair_at(s), 0, 0)
        )

    def fixed(shape):
        return once(shape, lambda s, m: (0,) * len(shape))

    def of_pairs(array):
        return pl.BlockSpec((PAIR,) + array.shape[1:], lambda s, m: (pair_at(s), 0, 0))

    grid_spec = pltpu.PrefetchScalarGridSpec(
        num_scalar_prefetch=1,
        grid=(ROW_STEPS + PAIR_STEPS + 1,),
        in_specs=[
            pl.BlockSpec((ROWS, width), lambda s, m: (m[2] * ROW_STEPS + row_at(s), 0)),
            pl.BlockSpec((ROWS, width), lambda s, m: (row_at(s), 0)),
            once((1, EXPERTS, SEQ_LEN), lambda s, m: (m[2], 0, 0)),
            once((1, SEQ_LEN, EXPERTS), lambda s, m: (m[2], 0, 0)),
            slot_pair(hidden, 3),
            slot_pair(hidden, 3),
            slot_rows(hidden, 3),
            slot_rows(hidden, 3),
            once((1, EXPERTS, SEQ_LEN), lambda s, m: (m[3], 0, 0)),
            of_pairs(wg),
            of_pairs(wu),
            of_pairs(wd),
            fixed(wgs.shape),
            fixed(wus.shape),
            fixed(wds.shape),
        ]
        + [pl.BlockSpec(memory_space=pl.ANY)] * stored,
        out_specs=[
            fixed((SEQ_LEN, width)),
            fixed((32, SEQ_LEN // 2)),
            slot_rows(width, 1),
            slot_pair(hidden, 1),
            slot_pair(hidden, 1),
            slot_pair(hidden, 1),
            slot_pair(width, 1),
            slot_rows(hidden, 1),
            slot_rows(hidden, 1),
            slot_rows(hidden, 1),
        ],
        scratch_shapes=[
            pltpu.VMEM((SEQ_LEN, width), F32),
            pltpu.VMEM((SEQ_LEN, width), BF16),
            pltpu.VMEM((PAIR * CAPACITY, SEQ_LEN), BF16),
            pltpu.VMEM((SEQ_LEN, PAIR * SPAN), BF16),
            pltpu.VMEM((PAIR * CAPACITY, LANES), F32),
            pltpu.VMEM((PAIR * SPAN, width), BF16),
            pltpu.VMEM((EXPERTS, SEQ_LEN), F32),
        ],
    )
    outs = pl.pallas_call(
        functools.partial(feed_backward_kernel, stored),
        grid_spec=grid_spec,
        out_shape=[shape_of((SEQ_LEN, width), BF16), shape_of((32, SEQ_LEN // 2), BF16)] + saved,
        input_output_aliases={16 + k: 2 + k for k in range(stored)},
        compiler_params=pltpu.CompilerParams(vmem_limit_bytes=VMEM_BYTES),
        name="feed_backward",
    )(
        meta,
        cotangent,
        received,
        post,
        pos,
        gate,
        lift,
        gate_sh,
        lift_sh,
        probs,
        wg,
        wu,
        wd,
        wgs,
        wus,
        wds,
        *(kept or ()),
    )
    return outs[0], outs[1], outs[2:]


def attention_backward_kernel(
    stored,
    meta,
    first_block,
    sum_ref,
    choice_ref,
    probs_ref,
    dy_ref,
    h_ref,
    b_ref,
    gain_ref,
    router_ref,
    wall_ref,
    wo_ref,
    cos_ref,
    sin_ref,
    qkv_ref,
    o_ref,
    lse_ref,
    low_ref,
    *rest,
):
    rest = rest[stored:]
    part_ref, dh_ref, gain_grad_ref, router_grad_ref, dqkv_ref, dattn_ref = rest[:6]
    dk_all, dv_all, dq_all, do_all, inner_all = rest[6:]
    step = pl.program_id(0)
    index = BLOCKS - 1 - step
    heads = wo_ref.shape[0] // LANES
    wide = heads * LANES

    @pl.when(step == 0)
    def _():
        gain_grad_ref[...] = jnp.zeros_like(gain_grad_ref)
        router_grad_ref[...] = jnp.zeros_like(router_grad_ref)
        dk_all[...] = jnp.zeros_like(dk_all)
        dv_all[...] = jnp.zeros_like(dv_all)

    probs = probs_ref[0]
    chosen = choice_ref[0:8, :].astype(F32)
    logit_grads = probs * (chosen - jnp.sum(probs * chosen, axis=0, keepdims=True))
    logit_grads = logit_grads.astype(BF16)
    router_grad_ref[...] += dot(logit_grads, b_ref[0])
    grad_normed = sum_ref[...].astype(F32) + dot_tn(logit_grads, router_ref[...])
    state = h_ref[0]
    scale = lax.rsqrt(jnp.mean(state * state, axis=-1, keepdims=True) + 1e-06)
    normed = state * scale
    gain_grad_ref[...] += jnp.sum(grad_normed * normed, axis=0, keepdims=True)
    scaled = gain_ref[...] * grad_normed
    inner = jnp.mean(normed * scaled, axis=-1, keepdims=True)
    grad_state = dy_ref[0].astype(F32) + scale * (scaled - normed * inner)
    dh_ref[...] = grad_state
    dattn = grad_state.astype(BF16)
    dattn_ref[0] = dattn
    do = dot_nt(dattn, wo_ref[...]).astype(BF16)
    do_all[...] = do
    products = do.astype(F32) * o_ref[0].astype(F32)
    for head in range(heads):
        columns = slice(head * LANES, (head + 1) * LANES)
        row = jnp.sum(products[:, columns], axis=1, keepdims=True)
        inner_all[head : head + 1, :] = jnp.broadcast_to(row, (BLOCK, LANES)).T[0:1, :]
    dq_all[...] = jnp.zeros_like(dq_all)
    here = rows_of(index, BLOCK)
    low = low_ref[0]
    query_at = index * BLOCK + lax.broadcasted_iota(jnp.int32, (BLOCK, BLOCK), 1)
    key_at = lax.broadcasted_iota(jnp.int32, (BLOCK, BLOCK), 0)

    def body(block, none):
        at = key_at + block * BLOCK
        valid = (at >= low) & (at <= query_at)
        there = rows_of(block, BLOCK)
        for head in range(heads):
            columns = slice(head * LANES, (head + 1) * LANES)
            key_columns = slice(wide + head * LANES, wide + (head + 1) * LANES)
            value_columns = slice(2 * wide + head * LANES, 2 * wide + (head + 1) * LANES)
            query = qkv_ref[0, here, columns]
            keys = qkv_ref[0, there, key_columns]
            scores = jnp.where(valid, dot_nt(keys, query), -1e30)
            probs = jnp.exp(scores - lse_ref[0, head : head + 1, :])
            grad_probs = dot_nt(qkv_ref[0, there, value_columns], do_all[:, columns])
            grad_scores = (probs * (grad_probs - inner_all[head : head + 1, :])).astype(BF16)
            dv_all[there, columns] += dot(probs.astype(BF16), do_all[:, columns])
            dk_all[there, columns] += dot(grad_scores, query)
            dq_all[:, columns] += dot_tn(grad_scores, keys)
        return none

    lax.fori_loop(first_block[meta[2] * BLOCKS + index], index + 1, body, 0)
    cosine, sine = cos_ref[...], sin_ref[...]
    for head in range(heads):
        columns = slice(head * LANES, (head + 1) * LANES)
        key_columns = slice(wide + head * LANES, wide + (head + 1) * LANES)
        value_columns = slice(2 * wide + head * LANES, 2 * wide + (head + 1) * LANES)
        dq = dq_all[:, columns] * 0.0625
        dk = dk_all[here, columns]
        dqkv_ref[0, :, columns] = (dq * cosine - pltpu.roll(dq, HEAD_DIM, 1) * sine).astype(BF16)
        dqkv_ref[0, :, key_columns] = (
            dk * cosine - pltpu.roll(dk, HEAD_DIM, 1) * sine
        ).astype(BF16)
        dqkv_ref[0, :, value_columns] = dv_all[here, columns].astype(BF16)
    part_ref[...] = dot_nt(dqkv_ref[0], wall_ref[...]).astype(BF16)


def attention_backward(
    meta, first_block, summed, choice, forward_kept, attention_kept, dy, gain, router, wall, wo, cosine, sine, low, kept
):
    width = summed.shape[1]
    wide = wo.shape[0]
    stored = 0 if kept is None else 2
    h, b, probs = forward_kept[0], forward_kept[1], forward_kept[7]
    unused_x, unused_a, qkv, o, lse = attention_kept
    saved = [
        shape_of((SLOTS, SEQ_LEN, 3 * wide), BF16),
        shape_of((SLOTS, SEQ_LEN, width), BF16),
    ]

    def at(step):
        return BLOCKS - 1 - step

    def slot_rows(columns, which):
        return pl.BlockSpec((1, BLOCK, columns), lambda s, m, f: (m[which], at(s), 0))

    def fixed(shape):
        return once(shape, lambda s, m, f: (0,) * len(shape))

    halves_of = BLOCKS // 2
    grid_spec = pltpu.PrefetchScalarGridSpec(
        num_scalar_prefetch=2,
        grid=(BLOCKS,),
        in_specs=[
            pl.BlockSpec((BLOCK, width), lambda s, m, f: (at(s), 0)),
            pl.BlockSpec((16, BLOCK), lambda s, m, f: (at(s) // halves_of, at(s) % halves_of)),
            pl.BlockSpec((1, EXPERTS, BLOCK), lambda s, m, f: (m[3], 0, at(s))),
            slot_rows(width, 1),
            slot_rows(width, 3),
            slot_rows(width, 3),
            fixed(gain.shape),
            fixed(router.shape),
            fixed(wall.shape),
            fixed(wo.shape),
            pl.BlockSpec((BLOCK, LANES), lambda s, m, f: (at(s), 0)),
            pl.BlockSpec((BLOCK, LANES), lambda s, m, f: (at(s), 0)),
            once((1, SEQ_LEN, 3 * wide), lambda s, m, f: (m[3], 0, 0)),
            slot_rows(wide, 3),
            pl.BlockSpec((1, 8, BLOCK), lambda s, m, f: (m[3], 0, at(s))),
            pl.BlockSpec((1, 1, BLOCK), lambda s, m, f: (m[2], 0, at(s))),
        ]
        + [pl.BlockSpec(memory_space=pl.ANY)] * stored,
        out_specs=[
            pl.BlockSpec((BLOCK, width), lambda s, m, f: (at(s), 0)),
            pl.BlockSpec((BLOCK, width), lambda s, m, f: (at(s), 0)),
            fixed((1, width)),
            fixed((8, width)),
            slot_rows(3 * wide, 1),
            slot_rows(width, 1),
        ],
        scratch_shapes=[
            pltpu.VMEM((SEQ_LEN, wide), F32),
            pltpu.VMEM((SEQ_LEN, wide), F32),
            pltpu.VMEM((BLOCK, wide), F32),
            pltpu.VMEM((BLOCK, wide), BF16),
            pltpu.VMEM((8, BLOCK), F32),
        ],
    )
    outs = pl.pallas_call(
        functools.partial(attention_backward_kernel, stored),
        grid_spec=grid_spec,
        out_shape=[
            shape_of((SEQ_LEN, width), BF16),
            shape_of((SEQ_LEN, width), F32),
            shape_of((1, width), F32),
            shape_of((8, width), F32),
        ]
        + saved,
        input_output_aliases={18 + k: 4 + k for k in range(stored)},
        compiler_params=pltpu.CompilerParams(vmem_limit_bytes=VMEM_BYTES),
        name="attention_backward",
    )(
        meta,
        first_block,
        summed,
        choice,
        probs,
        dy,
        h,
        b,
        gain,
        router,
        wall,
        wo,
        cosine,
        sine,
        qkv,
        o,
        lse,
        low,
        *(kept or ()),
    )
    return outs[:4], outs[4:]


def expert_grads_kernel(*refs):
    ins, out_ref = refs[:-1], refs[-1]
    (xa, xb), (ga, gb), (ua, ub), (ea, eb), (ha, hb) = (ins[2 * k : 2 * k + 2] for k in range(5))
    devices, unused, rows, unused = out_ref.shape
    pairs = [((xa, xb), (ga, gb)), ((xa, xb), (ua, ub)), ((ea, eb), (ha, hb))]
    for number, (left, right) in enumerate(pairs):
        for device in range(devices):
            columns = slice(device * rows, (device + 1) * rows)
            out_ref[device, number] = (
                dot_tn(left[0][0, 0, :, columns], right[0][0, 0])
                + dot_tn(left[1][0, 0, :, columns], right[1][0, 0])
            ).astype(BF16)


def expert_grads(first, count, extra, devices, picked, hid, grad_gate, grad_lift, grad_expert):
    width, hidden = picked.shape[3], hid.shape[3]
    rows = width // devices

    def pair(columns):
        return [
            pl.BlockSpec(
                (1, 1, CAPACITY, columns),
                functools.partial(lambda slot, e: (slot, first + e, 0, 0), slot),
            )
            for slot in (1, 2)
        ]

    return pl.pallas_call(
        expert_grads_kernel,
        grid=(count,),
        in_specs=pair(width) + pair(hidden) + pair(hidden) + pair(width) + pair(hidden),
        out_specs=pl.BlockSpec((devices, 3, rows, hidden), lambda e: (0, e, 0, 0)),
        out_shape=shape_of((devices, 3 * count + extra, rows, hidden), BF16),
        compiler_params=pltpu.CompilerParams(vmem_limit_bytes=VMEM_BYTES),
        name="expert_grads",
    )(
        *(picked, picked, grad_gate, grad_gate, grad_lift, grad_lift),
        *(grad_expert, grad_expert, hid, hid),
    )


def shared_grads_kernel(b_ref, dy_ref, gate_ref, lift_ref, hid_ref, before_ref, out_ref, *totals):
    step = pl.program_id(0)
    pairs = [(b_ref, gate_ref), (b_ref, lift_ref), (dy_ref, hid_ref)]

    @pl.when(step == 0)
    def _():
        for total in totals:
            total[...] = jnp.zeros_like(total)

    for (left, right), total in zip(pairs, totals):
        total[...] += dot_tn(left[0], right[0])

    @pl.when(step == pl.num_programs(0) - 1)
    def _():
        devices, unused, rows, unused = out_ref.shape
        for number, total in enumerate(totals):
            for device in range(devices):
                out_ref[device, number] = total[device * rows : (device + 1) * rows, :].astype(
                    BF16
                )


def shared_grads(before, b, dy, grad_gate, grad_lift, hid):
    devices, matrices, width, hidden = before.shape
    rows = 2 * BLOCK
    steps = SEQ_LEN // rows

    def spec(array):
        return pl.BlockSpec((1, rows, array.shape[2]), lambda s: (1 + s // steps, s % steps, 0))

    return pl.pallas_call(
        shared_grads_kernel,
        grid=(2 * steps,),
        in_specs=[spec(array) for array in (b, dy, grad_gate, grad_lift, hid)]
        + [pl.BlockSpec(memory_space=pl.ANY)],
        out_specs=once((devices, 3, width, hidden), lambda s: (0, matrices // 3 - 1, 0, 0)),
        out_shape=shape_of(before.shape, BF16),
        scratch_shapes=[pltpu.VMEM((devices * width, hidden), F32)] * 3,
        input_output_aliases={5: 0},
        compiler_params=pltpu.CompilerParams(vmem_limit_bytes=VMEM_BYTES),
        name="shared_grads",
    )(b, dy, grad_gate, grad_lift, hid, before)


def token_grads_kernel(count, *refs):
    lefts, rights = refs[:count], refs[count : 2 * count]
    outs, totals = refs[2 * count : 3 * count], refs[3 * count :]
    step = pl.program_id(0)

    @pl.when(step == 0)
    def _():
        for total in totals:
            total[...] = jnp.zeros_like(total)

    for left, right, total in zip(lefts, rights, totals):
        total[...] += dot_tn(left[0], right[0])

    @pl.when(step == pl.num_programs(0) - 1)
    def _():
        for out, total in zip(outs, totals):
            out[...] = total[...].astype(BF16)


def token_grads(lefts, rights):
    count = len(lefts)
    rows = 2 * BLOCK
    steps = SEQ_LEN // rows

    def spec(array):
        return pl.BlockSpec((1, rows, array.shape[2]), lambda s: (1 + s // steps, s % steps, 0))

    shapes = [(left.shape[2], right.shape[2]) for left, right in zip(lefts, rights)]
    return pl.pallas_call(
        functools.partial(token_grads_kernel, count),
        grid=(2 * steps,),
        in_specs=[spec(a) for a in lefts] + [spec(a) for a in rights],
        out_specs=[once(shape, lambda s: (0, 0)) for shape in shapes],
        out_shape=[shape_of(shape, BF16) for shape in shapes],
        scratch_shapes=[pltpu.VMEM(shape, F32) for shape in shapes],
        compiler_params=pltpu.CompilerParams(vmem_limit_bytes=VMEM_BYTES),
        name="token_grads",
    )(*lefts, *rights)


def rotary_tables():
    half = HEAD_DIM // 2
    rates = np.exp(-np.log(10000.0) * np.arange(half) * 2.0 / HEAD_DIM)
    angles = np.arange(SEQ_LEN)[:, None] * rates[None, :]
    cosine, sine = np.cos(angles), np.sin(angles)
    cosine = np.concatenate([cosine] * 4, axis=1)
    sine = np.concatenate([sine, sine, -sine, -sine], axis=1)
    return jnp.asarray(cosine, F32), jnp.asarray(sine, F32)


def paired(weight):
    rows = weight.shape[0]
    heads = weight.shape[1] // HEAD_DIM
    half = HEAD_DIM // 2
    split = weight.reshape(rows, heads, HEAD_DIM)
    swapped = jnp.concatenate([-split[:, :, half:], split[:, :, :half]], axis=2)
    return jnp.concatenate([split, swapped], axis=2).reshape(rows, heads * LANES)


def padded(weight):
    rows = weight.shape[0]
    heads = weight.shape[1] // HEAD_DIM
    split = weight.reshape(rows, heads, HEAD_DIM)
    return jnp.concatenate([split, jnp.zeros_like(split)], axis=2).reshape(rows, heads * LANES)


def unpadded(grads):
    rows = grads.shape[0]
    return grads.reshape(rows, -1, LANES)[:, :, :HEAD_DIM].reshape(rows, -1)


def places(routes):
    experts = jnp.arange(EXPERTS, dtype=jnp.int32)
    named = jnp.any(routes[:, :, :, None] == experts, axis=2)
    before = (
        jnp.arange(SEQ_LEN, dtype=jnp.int32)[:, None] > jnp.arange(SEQ_LEN, dtype=jnp.int32)
    ).astype(BF16)
    rank = jnp.einsum("ts,nse->nte", before, named.astype(BF16), preferred_element_type=F32)
    by_token = jnp.where(named, rank.astype(jnp.int32), -1)
    return by_token, jnp.swapaxes(by_token, 1, 2)


def first_allowed(lengths):
    ends = jnp.cumsum(lengths, axis=1)
    at = jnp.arange(SEQ_LEN, dtype=jnp.int32)
    starts = jnp.max(jnp.where(ends[:, None, :] <= at[None, :, None], ends[:, None, :], 0), axis=2)
    return jnp.maximum(starts, at[None, :] - (WINDOW - 1)).astype(jnp.int32)


def on_device(
    tokens,
    doc_lengths,
    routes,
    gain_attn,
    w_query,
    w_key,
    w_value,
    w_output,
    gain_ffn,
    w_router,
    w_gate_exp,
    w_up_exp,
    w_down_exp,
    w_gate_sh,
    w_up_sh,
    w_down_sh,
    cotangent,
):
    section = lax.axis_index("section")
    devices = lax.axis_size("dp")
    count = doc_lengths.shape[0]
    width = tokens.shape[1]
    cosine, sine = rotary_tables()
    wall = jnp.concatenate([paired(w_query[0]), paired(w_key[0]), padded(w_value[0])], axis=1)
    wo = padded(w_output[0].T).T
    out_weight = lax.all_gather(w_output[0], "tensor", axis=0, tiled=True)
    router = w_router[0].T
    gain_a, gain_f = gain_attn.astype(F32), gain_ffn.astype(F32)
    feed_weights = (
        w_gate_exp[0],
        w_up_exp[0],
        w_down_exp[0],
        w_gate_sh[0],
        w_up_sh[0],
        w_down_sh[0],
    )
    pos, post = places(routes[0].reshape(count, SEQ_LEN, 2))
    low = first_allowed(doc_lengths)
    first_block = (low[:, ::BLOCK] // BLOCK).reshape(-1)
    low_column, low_row = low[:, :, None], low[:, None, :]

    received = jnp.zeros((SEQ_LEN, width), BF16)
    attention_kept, feed_kept, results = None, None, []
    for tick in range(count + 1):
        raw = tick - section
        active = (raw >= 0) & (raw < count)
        sequence = jnp.clip(raw, 0, count - 1)
        meta = jnp.stack([section, jnp.where(active, sequence + 1, 0), sequence]).astype(jnp.int32)
        own, attention_kept = attention_forward(
            meta,
            first_block,
            tokens,
            received,
            gain_a,
            wall,
            cosine,
            sine,
            low_column,
            attention_kept,
        )
        gathered = tensor_gather(own, 0)
        part, feed_kept = feed_forward(
            meta,
            attention_kept[0],
            gathered,
            out_weight,
            gain_f,
            router,
            post,
            pos,
            feed_weights,
            feed_kept,
        )
        result, received = output_relay(part, feed_kept[0], tick, 4 + tick)
        results.append(result)

    def spread(array):
        return lax.psum_scatter(array, "dp", scatter_dimension=0, tiled=False)

    received = jnp.zeros((SEQ_LEN, width), BF16)
    grads_kept, attention_grads_kept, inputs = None, None, []
    small = jnp.zeros((10, width), F32)
    for tick in range(count + 1):
        raw = tick - 1 + section
        active = (raw >= 0) & (raw < count)
        sequence = jnp.clip(raw, 0, count - 1)
        source = jnp.where(active, 2 - section, 0)
        meta = jnp.stack(
            [source, jnp.where(active, sequence + 1, 0), sequence, sequence + 1]
        ).astype(jnp.int32)
        part, choice, grads_kept = feed_backward(
            meta, cotangent, received, post, pos, feed_kept, feed_weights, grads_kept
        )
        if tick == count:
            dy, hid, grad_gate, grad_lift, grad_expert, hid_sh, grad_gate_sh, grad_lift_sh = (
                grads_kept
            )
            lead = 2
            picked = feed_kept[2]
            first_grads = expert_grads(
                0, lead, 0, devices, picked, hid, grad_gate, grad_lift, grad_expert
            )
            other_grads = expert_grads(
                lead,
                EXPERTS - lead,
                3,
                devices,
                picked,
                hid,
                grad_gate,
                grad_lift,
                grad_expert,
            )
            other_grads = shared_grads(
                other_grads, feed_kept[1], dy, grad_gate_sh, grad_lift_sh, hid_sh
            )
            part, choice, first_grads, other_grads = lax.optimization_barrier(
                (part, choice, first_grads, other_grads)
            )
            first_grads, other_grads = spread(first_grads), spread(other_grads)
        summed, choice = tensor_sum([part, choice], (12, 1), 2)
        (part, grad_state, gain_grad, router_grad), attention_grads_kept = attention_backward(
            meta,
            first_block,
            summed,
            choice,
            feed_kept,
            attention_kept,
            grads_kept[0],
            gain_f,
            router,
            wall,
            wo,
            cosine,
            sine,
            low_row,
            attention_grads_kept,
        )
        layer_in = lax.dynamic_index_in_dim(attention_kept[0], sequence + 1, 0, False)
        grad_input, received, gain_attn_grad = input_relay(part, layer_in, grad_state, gain_a, 3)
        inputs.append(grad_input)
        small = small + jnp.concatenate([gain_attn_grad, gain_grad, router_grad], axis=0)

    projections, outward = token_grads(
        [attention_kept[1], attention_grads_kept[1]], [attention_grads_kept[0], attention_kept[3]]
    )
    wide = wo.shape[0]
    rows = width // devices
    columns = w_query.shape[2]
    packed = jnp.concatenate(
        [
            2.0 * unpadded(projections[:, : 2 * wide]),
            unpadded(projections[:, 2 * wide :]),
            unpadded(outward),
            jnp.pad(small, ((0, 6), (0, 0))).T.astype(BF16),
        ],
        axis=1,
    )
    packed = spread(packed.reshape(devices, rows, -1)).astype(F32)
    shared = other_grads[-3:].astype(F32)
    experts = jnp.concatenate([first_grads, other_grads[:-3]], axis=0).astype(F32)
    experts = experts.reshape(EXPERTS, 3, rows, -1)

    def choose(items):
        return jnp.concatenate(
            [jnp.where(section == 0, items[k], items[k + 1]) for k in range(count)], axis=0
        )

    layer_out = choose(results)
    input_grad = jnp.concatenate(
        [jnp.where(section == 0, inputs[k + 1], inputs[k]) for k in range(count)], axis=0
    )
    extra = 4 * columns
    return (
        layer_out[None],
        input_grad[None],
        packed[None, :, extra],
        packed[None, :, :columns],
        packed[None, :, columns : 2 * columns],
        packed[None, :, 2 * columns : 3 * columns],
        packed[:, 3 * columns : extra].T[None],
        packed[None, :, extra + 1],
        packed[None, :, extra + 2 : extra + 10],
        experts[None, :, 0],
        experts[None, :, 1],
        jnp.swapaxes(experts[:, 2], 1, 2)[None],
        shared[None, 0],
        shared[None, 1],
        shared[2].T[None],
    )


def solution(mesh):
    return jax.shard_map(
        on_device,
        mesh=mesh,
        in_specs=(
            P("dp", None),
            P("dp", None),
            P("section", "dp", None),
            P("section", None),
            P("section", None, "tensor"),
            P("section", None, "tensor"),
            P("section", None, "tensor"),
            P("section", "tensor", None),
            P("section", None),
            P("section", None, None),
            P("section", None, None, "tensor"),
            P("section", None, None, "tensor"),
            P("section", None, "tensor", None),
            P("section", None, "tensor"),
            P("section", None, "tensor"),
            P("section", "tensor", None),
            P("dp", None),
        ),
        out_specs=(
            P("section", "dp", None),
            P("section", "dp", None),
            P("section", "dp"),
            P("section", "dp", "tensor"),
            P("section", "dp", "tensor"),
            P("section", "dp", "tensor"),
            P("section", "tensor", "dp"),
            P("section", "dp"),
            P("section", "dp", None),
            P("section", None, "dp", "tensor"),
            P("section", None, "dp", "tensor"),
            P("section", None, "tensor", "dp"),
            P("section", "dp", "tensor"),
            P("section", "dp", "tensor"),
            P("section", "tensor", "dp"),
        ),
        check_vma=False,
    )
```

```python
import functools

import jax
import jax.numpy as jnp
import numpy as np
from jax import lax
from jax.experimental import pallas as pl
from jax.experimental.pallas import tpu as pltpu
from jax.sharding import PartitionSpec as P

HEAD_DIM = 64
EXPERTS = 8
SEQ_LEN = 1536
WINDOW = 1024
CAPACITY = 480
BLOCK = 256
BLOCKS = SEQ_LEN // BLOCK
LANES = 128
SLOTS = 3
VMEM_BYTES = 60 * 2**20
MESH = pl.DeviceIdType.MESH
F32 = jnp.float32
BF16 = jnp.bfloat16
NT = (((1,), (1,)), ((), ()))
TN = (((0,), (0,)), ((), ()))


def shape_of(shape, dtype):
    return jax.ShapeDtypeStruct(shape, dtype)


def cost(micros):
    return pl.CostEstimate(
        flops=int(micros * 1.15e9), bytes_accessed=int(micros * 3.6e6), transcendentals=0
    )


def dot(left, right):
    return jnp.dot(left, right, preferred_element_type=F32)


def dot_nt(left, right):
    return lax.dot_general(left, right, NT, preferred_element_type=F32)


def dot_tn(left, right):
    return lax.dot_general(left, right, TN, preferred_element_type=F32)


def once(shape, index):
    return pl.BlockSpec(shape, index, pipeline_mode=pl.Buffered(1))


def loop(count, body):
    lax.fori_loop(0, count, lambda step, none: (body(step), none)[1], 0)


def rows_of(step, size):
    return pl.ds(pl.multiple_of(step * size, size), size)


def greet(partners):
    barrier = pltpu.get_barrier_semaphore()
    for partner in partners:
        pl.semaphore_signal(barrier, inc=1, device_id=partner, device_id_type=MESH)
    pl.semaphore_wait(barrier, len(partners))


def remote(source, target, send, recv, device):
    return pltpu.make_async_remote_copy(
        src_ref=source,
        dst_ref=target,
        send_sem=send,
        recv_sem=recv,
        device_id=device,
        device_id_type=MESH,
    )


def partners_of():
    place = lax.axis_index("tensor")
    core = lax.rem(place, 2)
    return {"tensor": place + 1 - 2 * core}, {"tensor": lax.rem(place + 2, 4)}


def sides(rows):
    core = lax.rem(lax.axis_index("tensor"), 2)
    half = rows // 2
    return core * half, (1 - core) * half


def piece_rows(side, step, size):
    return pl.ds(pl.multiple_of(side + step * size, 16), size)


def cross_kernel(pieces, part_ref, mine, first, kept, second, sends, recvs, loaded, use):
    near, far = partners_of()
    own, other = sides(part_ref.shape[0])
    size = mine.shape[0] // pieces
    copies = []
    for step in range(pieces):
        local = pl.ds(step * size, size)
        copies.append(
            remote(
                part_ref.at[piece_rows(other, step, size)],
                first.at[local],
                sends.at[0, step],
                recvs.at[0, step],
                near,
            )
        )
        copies[-1].start()
    load = pltpu.make_async_copy(
        part_ref.at[pl.ds(pl.multiple_of(own, 16), mine.shape[0])], mine, loaded
    )
    load.start()
    load.wait()
    for step in range(pieces):
        local = pl.ds(step * size, size)
        copies[step].wait_recv()
        kept[local, :] = (mine[local, :].astype(F32) + first[local, :].astype(F32)).astype(BF16)
        copies.append(
            remote(
                kept.at[local], second.at[local], sends.at[1, step], recvs.at[1, step], far
            )
        )
        copies[-1].start()
    for step in range(pieces):
        local = pl.ds(step * size, size)
        copies[pieces + step].wait_recv()
        use(step, local, kept[local, :].astype(F32) + second[local, :].astype(F32))
    return copies


def sum_kernel(
    pieces, part_ref, out_ref, mine, first, kept, second, done, sends, recvs, loaded, stored
):
    near, far = partners_of()
    greet([near, far])
    own, other = sides(part_ref.shape[0])
    size = mine.shape[0] // pieces
    back, local_copies = [], []

    def use(step, local, total):
        done[local, :] = total.astype(BF16)
        rows = piece_rows(own, step, size)
        back.append(
            remote(done.at[local], out_ref.at[rows], sends.at[2, step], recvs.at[2, step], near)
        )
        back[-1].start()
        local_copies.append(
            pltpu.make_async_copy(done.at[local], out_ref.at[rows], stored.at[step])
        )
        local_copies[-1].start()

    copies = cross_kernel(
        pieces, part_ref, mine, first, kept, second, sends, recvs, loaded, use
    )
    for copy in back:
        copy.wait_recv()
    for copy in copies + back:
        copy.wait_send()
    for copy in local_copies:
        copy.wait()


def tensor_sum(part, identity, pieces):
    rows, width = part.shape
    hbm = pl.BlockSpec(memory_space=pl.ANY)
    return pl.pallas_call(
        functools.partial(sum_kernel, pieces),
        out_shape=shape_of((rows, width), BF16),
        in_specs=[hbm],
        out_specs=hbm,
        scratch_shapes=[pltpu.VMEM((rows // 2, width), BF16)] * 5
        + [pltpu.SemaphoreType.DMA((3, pieces))] * 2
        + [pltpu.SemaphoreType.DMA, pltpu.SemaphoreType.DMA((pieces,))],
        compiler_params=pltpu.CompilerParams(
            collective_id=identity, has_side_effects=True, vmem_limit_bytes=VMEM_BYTES
        ),
        cost_estimate=cost(32),
        name="tensor_sum",
    )(part)


def gather_kernel(pieces, own_ref, out_ref, sends, recvs, stored):
    place = lax.axis_index("tensor")
    near, far = partners_of()
    greet([near, far])
    far_place = lax.rem(place + 2, 4)
    size = own_ref.shape[0] // pieces
    first, crossing, passed = [], [], []
    for group, copies, partner in ((0, crossing, far), (1, first, near)):
        for piece in range(pieces):
            rows = pl.ds(piece * size, size)
            copies.append(
                remote(
                    own_ref.at[rows],
                    out_ref.at[place, rows],
                    sends.at[group, piece],
                    recvs.at[group, piece],
                    partner,
                )
            )
            copies[-1].start()
    local = pltpu.make_async_copy(own_ref, out_ref.at[place], stored)
    local.start()
    for piece in range(pieces):
        rows = pl.ds(piece * size, size)
        crossing[piece].wait_recv()
        passed.append(
            remote(
                out_ref.at[far_place, rows],
                out_ref.at[far_place, rows],
                sends.at[2, piece],
                recvs.at[2, piece],
                near,
            )
        )
        passed[-1].start()
    for copy in first + passed:
        copy.wait_recv()
    for copy in first + crossing + passed:
        copy.wait_send()
    local.wait()


def tensor_gather(own, identity, pieces=6):
    hbm = pl.BlockSpec(memory_space=pl.ANY)
    return pl.pallas_call(
        functools.partial(gather_kernel, pieces),
        out_shape=shape_of((4,) + own.shape, BF16),
        in_specs=[hbm],
        out_specs=hbm,
        scratch_shapes=[pltpu.SemaphoreType.DMA((3, pieces))] * 2 + [pltpu.SemaphoreType.DMA],
        compiler_params=pltpu.CompilerParams(
            collective_id=identity, has_side_effects=True, vmem_limit_bytes=VMEM_BYTES
        ),
        cost_estimate=cost(18),
        name="tensor_gather",
    )(own)


def pass_on(step, source, rows, next_ref, sends, recvs, across):
    copy = remote(source, next_ref.at[rows], sends.at[3, step], recvs.at[3, step], across)
    copy.start()
    return copy


def spread_on(pieces, size, own, passed, next_ref, sends, recvs, near):
    spread = []
    for step in range(pieces):
        rows = piece_rows(own, step, size)
        passed[step].wait_recv()
        spread.append(
            remote(next_ref.at[rows], next_ref.at[rows], sends.at[4, step], recvs.at[4, step], near)
        )
        spread[-1].start()
    return spread


def output_kernel(
    pieces,
    tick,
    part_ref,
    states_ref,
    out_ref,
    next_ref,
    mine,
    first,
    kept,
    second,
    done,
    state,
    sends,
    recvs,
    loaded,
    state_loaded,
    stored,
):
    near, far = partners_of()
    section = lax.axis_index("section")
    across = {"section": 1 - section}
    slot = lax.rem(tick + 1 - section, states_ref.shape[0])
    own, other = sides(part_ref.shape[0])
    size = mine.shape[0] // pieces
    load = pltpu.make_async_copy(
        states_ref.at[slot, pl.ds(pl.multiple_of(own, 16), mine.shape[0])], state, state_loaded
    )
    load.start()
    greet([near, far, across])
    back, passed, local_copies = [], [], []

    def use(step, local, total):
        if step == 0:
            load.wait()
        done[local, :] = (state[local, :] + total.astype(BF16).astype(F32)).astype(BF16)
        rows = piece_rows(own, step, size)
        passed.append(pass_on(step, done.at[local], rows, next_ref, sends, recvs, across))
        back.append(
            remote(done.at[local], out_ref.at[rows], sends.at[2, step], recvs.at[2, step], near)
        )
        back[-1].start()
        local_copies.append(
            pltpu.make_async_copy(done.at[local], out_ref.at[rows], stored.at[step])
        )
        local_copies[-1].start()

    copies = cross_kernel(
        pieces, part_ref, mine, first, kept, second, sends, recvs, loaded, use
    )
    spread = spread_on(pieces, size, own, passed, next_ref, sends, recvs, near)
    for copy in back + spread:
        copy.wait_recv()
    for copy in copies + back + passed + spread:
        copy.wait_send()
    for copy in local_copies:
        copy.wait()


def output_relay(part, states, tick, identity, pieces=12):
    rows, width = part.shape
    hbm = pl.BlockSpec(memory_space=pl.ANY)
    return pl.pallas_call(
        functools.partial(output_kernel, pieces, tick),
        out_shape=[shape_of((rows, width), BF16)] * 2,
        in_specs=[hbm] * 2,
        out_specs=[hbm] * 2,
        scratch_shapes=[pltpu.VMEM((rows // 2, width), BF16)] * 5
        + [pltpu.VMEM((rows // 2, width), F32)]
        + [pltpu.SemaphoreType.DMA((5, pieces))] * 2
        + [pltpu.SemaphoreType.DMA] * 2
        + [pltpu.SemaphoreType.DMA((pieces,))],
        compiler_params=pltpu.CompilerParams(
            collective_id=identity, has_side_effects=True, vmem_limit_bytes=VMEM_BYTES
        ),
        cost_estimate=cost(38),
        name="output_relay",
    )(part, states)


def input_kernel(
    pieces,
    tick,
    part_ref,
    layers_ref,
    grad_state_ref,
    gain_ref,
    grad_ref,
    next_ref,
    grad_gain_ref,
    mine,
    first,
    kept,
    second,
    given,
    full,
    layer_in,
    grad_state,
    grad,
    gains,
    sends,
    recvs,
    loaded,
    inputs_loaded,
    stored,
):
    near, far = partners_of()
    section = lax.axis_index("section")
    across = {"section": 1 - section}
    slot = lax.rem(tick + section, layers_ref.shape[0])
    rows = part_ref.shape[0]
    own, other = sides(rows)
    half = rows // 2
    size = half // pieces
    loads = []
    for side, start in ((0, own), (1, other)):
        there = pl.ds(pl.multiple_of(start, 16), half)
        loads.append(
            [
                pltpu.make_async_copy(
                    layers_ref.at[slot, there], layer_in.at[there], inputs_loaded.at[side, 0]
                ),
                pltpu.make_async_copy(
                    grad_state_ref.at[there], grad_state.at[there], inputs_loaded.at[side, 1]
                ),
            ]
        )
        for load in loads[-1]:
            load.start()
    greet([near, far, across])
    gains[...] = jnp.zeros_like(gains)
    back, passed, local_copies = [], [], []

    def rows_back(here, side, step):
        grad_normed = full[here, :].astype(F32)
        values = layer_in[here, :].astype(F32)
        scale = lax.rsqrt(jnp.mean(values * values, axis=-1, keepdims=True) + 1e-06)
        normed = values * scale
        scaled = gain_ref[...] * grad_normed
        inner = jnp.mean(normed * scaled, axis=-1, keepdims=True)
        result = grad_state[here, :] + scale * (scaled - normed * inner)
        grad[here, :] = result
        gains[side : side + 1, :] += jnp.sum(grad_normed * normed, axis=0, keepdims=True)
        local_copies.append(
            pltpu.make_async_copy(grad.at[here], grad_ref.at[here], stored.at[side, step])
        )
        local_copies[-1].start()
        return result

    def use(step, local, total):
        if step == 0:
            for load in loads[0]:
                load.wait()
        here = piece_rows(own, step, size)
        full[here, :] = total.astype(BF16)
        back.append(
            remote(full.at[here], full.at[here], sends.at[2, step], recvs.at[2, step], near)
        )
        back[-1].start()
        given[local, :] = rows_back(here, 0, step).astype(BF16)
        passed.append(pass_on(step, given.at[local], here, next_ref, sends, recvs, across))

    copies = cross_kernel(
        pieces, part_ref, mine, first, kept, second, sends, recvs, loaded, use
    )
    spread = spread_on(pieces, size, own, passed, next_ref, sends, recvs, near)
    for load in loads[1]:
        load.wait()
    for step in range(pieces):
        back[step].wait_recv()
        rows_back(piece_rows(other, step, size), 1, step)
    grad_gain_ref[...] = gains[0:1, :] + gains[1:2, :]
    for copy in spread:
        copy.wait_recv()
    for copy in copies + back + passed + spread:
        copy.wait_send()
    for copy in local_copies:
        copy.wait()


def input_relay(part, layers, grad_state, gain, tick, identity, pieces=12):
    rows, width = part.shape
    hbm = pl.BlockSpec(memory_space=pl.ANY)
    whole = pl.BlockSpec(memory_space=pltpu.VMEM)
    return pl.pallas_call(
        functools.partial(input_kernel, pieces, tick),
        out_shape=[
            shape_of((rows, width), F32),
            shape_of((rows, width), BF16),
            shape_of((1, width), F32),
        ],
        in_specs=[hbm] * 3 + [whole],
        out_specs=[hbm] * 2 + [whole],
        scratch_shapes=[pltpu.VMEM((rows // 2, width), BF16)] * 5
        + [pltpu.VMEM((rows, width), BF16)] * 2
        + [pltpu.VMEM((rows, width), F32)] * 2
        + [pltpu.VMEM((8, width), F32)]
        + [pltpu.SemaphoreType.DMA((5, pieces))] * 2
        + [pltpu.SemaphoreType.DMA]
        + [pltpu.SemaphoreType.DMA((2, 2)), pltpu.SemaphoreType.DMA((2, pieces))],
        compiler_params=pltpu.CompilerParams(
            collective_id=identity, has_side_effects=True, vmem_limit_bytes=VMEM_BYTES
        ),
        cost_estimate=cost(42),
        name="input_relay",
    )(part, layers, grad_state, gain)


def attention_forward_kernel(
    stored,
    meta,
    first_block,
    tok_ref,
    rec_ref,
    gain_ref,
    wall_ref,
    cos_ref,
    sin_ref,
    low_ref,
    *rest,
):
    rest = rest[stored:]
    packed_ref, x_ref, a_ref, qkv_ref, o_ref, lse_ref = rest[:6]
    keys, values, scores, tops, sums, mixed = rest[6:]
    index = pl.program_id(0)
    heads = wall_ref.shape[1] // (3 * LANES)
    wide = heads * LANES
    x = jnp.where(meta[0] == 0, tok_ref[...], rec_ref[...])
    x_ref[0] = x
    x = x.astype(F32)
    normed = gain_ref[...] * x * lax.rsqrt(jnp.mean(x * x, axis=-1, keepdims=True) + 1e-06)
    normed = normed.astype(BF16)
    a_ref[0] = normed
    cosine, sine = cos_ref[...], sin_ref[...]
    here = rows_of(index, BLOCK)
    for group in range(2 * heads):
        columns = slice(group * LANES, (group + 1) * LANES)
        pre = dot(normed, wall_ref[:, columns])
        turned = pre * cosine + pltpu.roll(pre, HEAD_DIM, 1) * sine
        if group < heads:
            turned = turned * 0.0625
        qkv_ref[0, :, columns] = turned.astype(BF16)
    qkv_ref[0, :, 2 * wide :] = dot(normed, wall_ref[:, 2 * wide :]).astype(BF16)
    keys[here, :] = qkv_ref[0, :, wide : 2 * wide]
    values[here, :] = qkv_ref[0, :, 2 * wide :]
    low = low_ref[0]
    query_at = index * BLOCK + lax.broadcasted_iota(jnp.int32, (BLOCK, BLOCK), 0)
    key_at = lax.broadcasted_iota(jnp.int32, (BLOCK, BLOCK), 1)
    tops[...] = jnp.full_like(tops, -1e30)
    sums[...] = jnp.zeros_like(sums)
    mixed[...] = jnp.zeros_like(mixed)
    begin = first_block[meta[2] * BLOCKS + index]

    def score(block, none):
        at = key_at + block * BLOCK
        valid = (at >= low) & (at <= query_at)
        there = rows_of(block, BLOCK)
        for head in range(heads):
            columns = slice(head * LANES, (head + 1) * LANES)
            raw = dot_nt(qkv_ref[0, :, columns], keys[there, columns])
            raw = jnp.where(valid, raw, -1e30)
            scores[head, block] = raw
            tops[head] = jnp.maximum(
                tops[head], jnp.maximum(raw[:, :LANES], raw[:, LANES:])
            )
        return none

    lax.fori_loop(begin, index + 1, score, 0)
    top = [jnp.max(tops[head], axis=1, keepdims=True) for head in range(heads)]

    def mix(block, none):
        there = rows_of(block, BLOCK)
        for head in range(heads):
            columns = slice(head * LANES, (head + 1) * LANES)
            weights = jnp.exp(scores[head, block] - top[head])
            sums[head] += weights[:, :LANES] + weights[:, LANES:]
            mixed[:, columns] += dot(weights.astype(BF16), values[there, columns])
        return none

    lax.fori_loop(begin, index + 1, mix, 0)
    for head in range(heads):
        columns = slice(head * LANES, (head + 1) * LANES)
        total = jnp.sum(sums[head], axis=1, keepdims=True)
        o_ref[0, :, columns] = (mixed[:, columns] / total).astype(BF16)
        logsum = jnp.broadcast_to(top[head] + jnp.log(total), (BLOCK, LANES))
        lse_ref[0, head : head + 1, :] = logsum.T[0:1, :]
    half = BLOCK // 2
    packed_ref[...] = jnp.concatenate(
        [
            o_ref[0, side * half : (side + 1) * half, head * LANES : head * LANES + HEAD_DIM]
            for side in range(2)
            for head in range(heads)
        ],
        axis=1,
    )


def attention_forward(meta, first_block, tokens, received, gain, wall, cosine, sine, low, kept):
    width = tokens.shape[1]
    wide = wall.shape[1] // 3
    heads = wide // LANES
    stored = 0 if kept is None else 5
    saved = [
        shape_of((SLOTS, SEQ_LEN, width), BF16),
        shape_of((SLOTS, SEQ_LEN, width), BF16),
        shape_of((SLOTS, SEQ_LEN, 3 * wide), BF16),
        shape_of((SLOTS, SEQ_LEN, wide), BF16),
        shape_of((SLOTS, 8, SEQ_LEN), F32),
    ]

    def slot_rows(columns):
        return pl.BlockSpec((1, BLOCK, columns), lambda i, m, f: (m[1], i, 0))

    grid_spec = pltpu.PrefetchScalarGridSpec(
        num_scalar_prefetch=2,
        grid=(BLOCKS,),
        in_specs=[
            pl.BlockSpec((BLOCK, width), lambda i, m, f: (m[2] * BLOCKS + i, 0)),
            pl.BlockSpec((BLOCK, width), lambda i, m, f: (i, 0)),
            once((1, width), lambda i, m, f: (0, 0)),
            once(wall.shape, lambda i, m, f: (0, 0)),
            pl.BlockSpec((BLOCK, LANES), lambda i, m, f: (i, 0)),
            pl.BlockSpec((BLOCK, LANES), lambda i, m, f: (i, 0)),
            pl.BlockSpec((1, BLOCK, 1), lambda i, m, f: (m[2], i, 0)),
        ]
        + [pl.BlockSpec(memory_space=pl.ANY)] * stored,
        out_specs=[
            pl.BlockSpec((BLOCK // 2, wide), lambda i, m, f: (i, 0)),
            slot_rows(width),
            slot_rows(width),
            slot_rows(3 * wide),
            slot_rows(wide),
            pl.BlockSpec((1, 8, BLOCK), lambda i, m, f: (m[1], 0, i)),
        ],
        scratch_shapes=[
            pltpu.VMEM((SEQ_LEN, wide), BF16),
            pltpu.VMEM((SEQ_LEN, wide), BF16),
            pltpu.VMEM((heads, BLOCKS, BLOCK, BLOCK), F32),
            pltpu.VMEM((heads, BLOCK, LANES), F32),
            pltpu.VMEM((heads, BLOCK, LANES), F32),
            pltpu.VMEM((BLOCK, wide), F32),
        ],
    )
    outs = pl.pallas_call(
        functools.partial(attention_forward_kernel, stored),
        grid_spec=grid_spec,
        out_shape=[shape_of((SEQ_LEN // 2, wide), BF16)] + saved,
        input_output_aliases={9 + k: 1 + k for k in range(stored)},
        compiler_params=pltpu.CompilerParams(vmem_limit_bytes=VMEM_BYTES),
        cost_estimate=cost(24),
        name="attention_forward",
    )(
        meta,
        first_block,
        tokens,
        received,
        gain,
        wall,
        cosine,
        sine,
        low,
        *(kept or ()),
    )
    return outs[0], outs[1:]


PAIR = 2
ROWS = 512
ROW_STEPS = SEQ_LEN // ROWS
PAIR_STEPS = EXPERTS // PAIR
SPAN = 512
CHUNK = 96


def build_pick(first, chunks, post_ref, probs, pick, gates):
    for which, step in chunks:
        row = pl.ds(first + which, 1)
        slot_at = step * CHUNK + lax.broadcasted_iota(jnp.int32, (CHUNK, SEQ_LEN), 0)
        here = slot_at == post_ref[0, row, :]
        rows = slice(which * CAPACITY + step * CHUNK, which * CAPACITY + (step + 1) * CHUNK)
        pick[rows, :] = jnp.where(here, 1.0, 0.0).astype(BF16)
        if probs is not None:
            chosen = jnp.sum(jnp.where(here, probs[row, :], 0.0), axis=1, keepdims=True)
            gates[rows, :] = jnp.broadcast_to(chosen, (CHUNK, LANES))


def build_gates(first, post_ref, probs, gates):
    for which in range(PAIR):
        row = pl.ds(first + which, 1)
        for step in range(CAPACITY // CHUNK):
            slot_at = step * CHUNK + lax.broadcasted_iota(jnp.int32, (CHUNK, SEQ_LEN), 0)
            here = slot_at == post_ref[0, row, :]
            rows = slice(which * CAPACITY + step * CHUNK, which * CAPACITY + (step + 1) * CHUNK)
            chosen = jnp.sum(jnp.where(here, probs[row, :], 0.0), axis=1, keepdims=True)
            gates[rows, :] = jnp.broadcast_to(chosen, (CHUNK, LANES))


def build_put(first, rows, pos_ref, put):
    places = pos_ref[0, rows, :]
    lane = lax.broadcasted_iota(jnp.int32, places.shape, 1)
    slot_at = lax.broadcasted_iota(jnp.int32, (places.shape[0], SPAN), 1)
    for which in range(PAIR):
        place = jnp.sum(jnp.where(lane == first + which, places, 0), axis=1, keepdims=True)
        put[rows, which * SPAN : (which + 1) * SPAN] = jnp.where(
            slot_at == place, 1.0, 0.0
        ).astype(BF16)


ALL_CHUNKS = [(which, step) for which in range(PAIR) for step in range(CAPACITY // CHUNK)]


def of_pair(which):
    return slice(which * CAPACITY, (which + 1) * CAPACITY)


def feed_forward_kernel(
    stored,
    meta,
    x_ref,
    ag_ref,
    wo_ref,
    gain_ref,
    router_ref,
    post_ref,
    pos_ref,
    wg_ref,
    wu_ref,
    wd_ref,
    wgs_ref,
    wus_ref,
    wds_ref,
    *rest,
):
    rest = rest[stored:]
    part_ref, h_ref, b_ref, xe_ref, g_ref, u_ref, gs_ref, us_ref, probs_ref = rest[:9]
    total, normed, probs, pick, put, gates, scaled = rest[9:]
    step = pl.program_id(0)
    pair = jnp.maximum(step - ROW_STEPS, 0)

    def activate(gate, lift, gate_out, lift_out):
        gate_out[...] = gate.astype(BF16)
        lift_out[...] = lift.astype(BF16)
        return (gate / (1.0 + jnp.exp(-gate)) * lift).astype(BF16)

    @pl.when(step < ROW_STEPS)
    def _():
        half = BLOCK // 2
        columns = ag_ref.shape[2] // 2
        mixed = jnp.concatenate(
            [
                jnp.concatenate(
                    [
                        ag_ref[device, block : block + half, side * columns : (side + 1) * columns]
                        for device in range(4)
                    ],
                    axis=1,
                )
                for block in range(0, ROWS // 2, half)
                for side in range(2)
            ],
            axis=0,
        )
        state = x_ref[0].astype(F32) + dot(mixed, wo_ref[...])
        h_ref[0] = state
        scale = lax.rsqrt(jnp.mean(state * state, axis=-1, keepdims=True) + 1e-06)
        b = (gain_ref[...] * state * scale).astype(BF16)
        b_ref[0] = b
        here = rows_of(step, ROWS)
        normed[here, :] = b
        logits = dot_nt(router_ref[...], b)
        weights = jnp.exp(logits - jnp.max(logits, axis=0, keepdims=True))
        weights = weights / jnp.sum(weights, axis=0, keepdims=True)
        probs_ref[0] = weights
        probs[:, here] = weights
        hidden = activate(dot(b, wgs_ref[...]), dot(b, wus_ref[...]), gs_ref.at[0], us_ref.at[0])
        total[here, :] = dot(hidden, wds_ref[...])

    @pl.when(step == 0)
    def _():
        build_pick(0, ALL_CHUNKS, post_ref, None, pick, gates)
        scaled[...] = jnp.zeros_like(scaled)

    def experts(combine):
        for start in range(0, SEQ_LEN, ROWS):
            rows = pl.ds(start, ROWS)
            if combine:
                total[rows, :] += dot(put[rows, :], scaled[...])
            build_put(pair * PAIR, rows, pos_ref, put)
        picked = dot(pick[...], normed[...]).astype(BF16)
        build_gates(pair * PAIR, post_ref, probs, gates)
        build_pick(
            jnp.minimum(pair + 1, PAIR_STEPS - 1) * PAIR, ALL_CHUNKS, post_ref, None, pick, gates
        )
        for which in range(PAIR):
            rows = picked[of_pair(which), :]
            xe_ref[0, which] = rows
            hidden = activate(
                dot(rows, wg_ref[which]), dot(rows, wu_ref[which]), g_ref.at[0, which], u_ref.at[0, which]
            )
            scaled[which * SPAN : which * SPAN + CAPACITY, :] = (
                dot(hidden, wd_ref[which]) * gates[of_pair(which), 0:1]
            ).astype(BF16)

    @pl.when(step == ROW_STEPS)
    def _():
        experts(False)

    @pl.when((step > ROW_STEPS) & (step < ROW_STEPS + PAIR_STEPS))
    def _():
        experts(True)

    @pl.when(step == ROW_STEPS + PAIR_STEPS)
    def _():
        for start in range(0, SEQ_LEN, ROWS):
            rows = pl.ds(start, ROWS)
            part_ref[rows, :] = (total[rows, :] + dot(put[rows, :], scaled[...])).astype(BF16)


def step_specs():
    def row_at(step):
        return jnp.minimum(step, ROW_STEPS - 1)

    def pair_at(step):
        return jnp.clip(step - ROW_STEPS, 0, PAIR_STEPS - 1)

    return row_at, pair_at


def feed_forward(
    meta, layer_in, gathered, out_weight, gain, router, post, pos, weights, kept
):
    width = layer_in.shape[2]
    wg, wu, wd, wgs, wus, wds = weights
    hidden = wg.shape[2]
    stored = 0 if kept is None else 8
    saved = [
        shape_of((SLOTS, SEQ_LEN, width), F32),
        shape_of((SLOTS, SEQ_LEN, width), BF16),
        shape_of((SLOTS, EXPERTS, CAPACITY, width), BF16),
        shape_of((SLOTS, EXPERTS, CAPACITY, hidden), BF16),
        shape_of((SLOTS, EXPERTS, CAPACITY, hidden), BF16),
        shape_of((SLOTS, SEQ_LEN, hidden), BF16),
        shape_of((SLOTS, SEQ_LEN, hidden), BF16),
        shape_of((SLOTS, EXPERTS, SEQ_LEN), F32),
    ]
    row_at, pair_at = step_specs()

    def slot_rows(columns):
        return pl.BlockSpec((1, ROWS, columns), lambda s, m: (m[1], row_at(s), 0))

    def slot_pair(columns):
        return pl.BlockSpec((1, PAIR, CAPACITY, columns), lambda s, m: (m[1], pair_at(s), 0, 0))

    def fixed(shape):
        return once(shape, lambda s, m: (0,) * len(shape))

    def of_pairs(array):
        return pl.BlockSpec((PAIR,) + array.shape[1:], lambda s, m: (pair_at(s), 0, 0))

    grid_spec = pltpu.PrefetchScalarGridSpec(
        num_scalar_prefetch=1,
        grid=(ROW_STEPS + PAIR_STEPS + 1,),
        in_specs=[
            slot_rows(width),
            pl.BlockSpec((4, ROWS // 2, gathered.shape[2]), lambda s, m: (0, row_at(s), 0)),
            fixed(out_weight.shape),
            fixed(gain.shape),
            fixed(router.shape),
            once((1, EXPERTS, SEQ_LEN), lambda s, m: (m[2], 0, 0)),
            once((1, SEQ_LEN, EXPERTS), lambda s, m: (m[2], 0, 0)),
            of_pairs(wg),
            of_pairs(wu),
            of_pairs(wd),
            fixed(wgs.shape),
            fixed(wus.shape),
            fixed(wds.shape),
        ]
        + [pl.BlockSpec(memory_space=pl.ANY)] * stored,
        out_specs=[
            fixed((SEQ_LEN, width)),
            slot_rows(width),
            slot_rows(width),
            slot_pair(width),
            slot_pair(hidden),
            slot_pair(hidden),
            slot_rows(hidden),
            slot_rows(hidden),
            pl.BlockSpec((1, EXPERTS, ROWS), lambda s, m: (m[1], 0, row_at(s))),
        ],
        scratch_shapes=[
            pltpu.VMEM((SEQ_LEN, width), F32),
            pltpu.VMEM((SEQ_LEN, width), BF16),
            pltpu.VMEM((EXPERTS, SEQ_LEN), F32),
            pltpu.VMEM((PAIR * CAPACITY, SEQ_LEN), BF16),
            pltpu.VMEM((SEQ_LEN, PAIR * SPAN), BF16),
            pltpu.VMEM((PAIR * CAPACITY, LANES), F32),
            pltpu.VMEM((PAIR * SPAN, width), BF16),
        ],
    )
    outs = pl.pallas_call(
        functools.partial(feed_forward_kernel, stored),
        grid_spec=grid_spec,
        out_shape=[shape_of((SEQ_LEN, width), BF16)] + saved,
        input_output_aliases={14 + k: 1 + k for k in range(stored)},
        compiler_params=pltpu.CompilerParams(vmem_limit_bytes=VMEM_BYTES),
        cost_estimate=cost(56),
        name="feed_forward",
    )(
        meta,
        layer_in,
        gathered,
        out_weight,
        gain,
        router,
        post,
        pos,
        wg,
        wu,
        wd,
        wgs,
        wus,
        wds,
        *(kept or ()),
    )
    return outs[0], outs[1:]


def feed_backward_kernel(
    stored,
    meta,
    cot_ref,
    rec_ref,
    post_ref,
    pos_ref,
    g_ref,
    u_ref,
    gs_ref,
    us_ref,
    probs_ref,
    wg_ref,
    wu_ref,
    wd_ref,
    wgs_ref,
    wus_ref,
    wds_ref,
    *rest,
):
    rest = rest[stored:]
    part_ref, dy_ref, hid_ref, dg_ref, du_ref, de_ref, hids_ref, dgs_ref, dus_ref = rest[:9]
    total, given, pick, put, gates, slots, choice = rest[9:]
    step = pl.program_id(0)
    pair = jnp.maximum(step - ROW_STEPS, 0)

    def pull(grad, weight, gate, lift):
        gate, lift = gate.astype(F32), lift.astype(F32)
        sigma = 1.0 / (1.0 + jnp.exp(-gate))
        swish = gate * sigma
        hidden = (swish * lift).astype(BF16)
        inner = None
        if weight is not None:
            inner = jnp.sum(hidden.astype(F32) * grad, axis=1, keepdims=True)
            grad = grad * weight
        grad_gate = (grad * lift * (sigma + swish * (1.0 - sigma))).astype(BF16)
        return hidden, grad_gate, (grad * swish).astype(BF16), inner

    @pl.when(step < ROW_STEPS)
    def _():
        dy = jnp.where(meta[0] == 1, cot_ref[...], rec_ref[...])
        dy = jnp.where(meta[0] == 0, jnp.zeros_like(dy), dy)
        dy_ref[0] = dy
        here = rows_of(step, ROWS)
        given[here, :] = dy
        hidden, grad_gate, grad_lift, unused = pull(
            dot_nt(dy, wds_ref[...]), None, gs_ref[0], us_ref[0]
        )
        hids_ref[0] = hidden
        dgs_ref[0] = grad_gate
        dus_ref[0] = grad_lift
        total[here, :] = dot_nt(grad_gate, wgs_ref[...]) + dot_nt(grad_lift, wus_ref[...])

    @pl.when(step == 0)
    def _():
        build_pick(0, ALL_CHUNKS, post_ref, None, pick, gates)
        slots[...] = jnp.zeros_like(slots)

    def experts(combine):
        for start in range(0, SEQ_LEN, ROWS):
            rows = pl.ds(start, ROWS)
            if combine:
                total[rows, :] += dot(put[rows, :], slots[...])
            build_put(pair * PAIR, rows, pos_ref, put)
        picked = dot(pick[...], given[...]).astype(BF16)
        build_gates(pair * PAIR, post_ref, probs_ref.at[0], gates)
        build_pick(
            jnp.minimum(pair + 1, PAIR_STEPS - 1) * PAIR, ALL_CHUNKS, post_ref, None, pick, gates
        )
        for which in range(PAIR):
            rows = picked[of_pair(which), :]
            weight = gates[of_pair(which), 0:1]
            hidden, grad_gate, grad_lift, inner = pull(
                dot_nt(rows, wd_ref[which]), weight, g_ref[0, which], u_ref[0, which]
            )
            hid_ref[0, which] = hidden
            dg_ref[0, which] = grad_gate
            du_ref[0, which] = grad_lift
            de_ref[0, which] = (weight * rows.astype(F32)).astype(BF16)
            row = pl.ds(pair * PAIR + which, 1)
            chosen = jnp.zeros((1, SEQ_LEN), F32)
            for chunk in range(CAPACITY // CHUNK):
                slot_at = chunk * CHUNK + lax.broadcasted_iota(jnp.int32, (CHUNK, SEQ_LEN), 0)
                here = slot_at == post_ref[0, row, :]
                chosen += jnp.sum(
                    jnp.where(here, inner[chunk * CHUNK : (chunk + 1) * CHUNK], 0.0),
                    axis=0,
                    keepdims=True,
                )
            choice[row, :] = chosen
            slots[which * SPAN : which * SPAN + CAPACITY, :] = (
                dot_nt(grad_gate, wg_ref[which]) + dot_nt(grad_lift, wu_ref[which])
            ).astype(BF16)

    @pl.when(step == ROW_STEPS)
    def _():
        experts(False)

    @pl.when((step > ROW_STEPS) & (step < ROW_STEPS + PAIR_STEPS))
    def _():
        experts(True)

    @pl.when(step == ROW_STEPS + PAIR_STEPS)
    def _():
        for start in range(0, SEQ_LEN, ROWS):
            rows = pl.ds(start, ROWS)
            part_ref[rows, :] = (total[rows, :] + dot(put[rows, :], slots[...])).astype(BF16)
        half = SEQ_LEN // 2
        blank = jnp.zeros((8, half), F32)
        part_ref[SEQ_LEN:, :] = jnp.concatenate(
            [choice[:, :half], blank, choice[:, half:], blank], axis=0
        ).astype(BF16)


def feed_backward(meta, cotangent, received, post, pos, forward_kept, weights, kept):
    width = cotangent.shape[1]
    wg, wu, wd, wgs, wus, wds = weights
    hidden = wg.shape[2]
    stored = 0 if kept is None else 8
    unused_h, unused_b, unused_x, gate, lift, gate_sh, lift_sh, probs = forward_kept
    saved = [
        shape_of((SLOTS, SEQ_LEN, width), BF16),
        shape_of((SLOTS, EXPERTS, CAPACITY, hidden), BF16),
        shape_of((SLOTS, EXPERTS, CAPACITY, hidden), BF16),
        shape_of((SLOTS, EXPERTS, CAPACITY, hidden), BF16),
        shape_of((SLOTS, EXPERTS, CAPACITY, width), BF16),
        shape_of((SLOTS, SEQ_LEN, hidden), BF16),
        shape_of((SLOTS, SEQ_LEN, hidden), BF16),
        shape_of((SLOTS, SEQ_LEN, hidden), BF16),
    ]
    row_at, pair_at = step_specs()

    def slot_rows(columns, which):
        return pl.BlockSpec((1, ROWS, columns), lambda s, m: (m[which], row_at(s), 0))

    def slot_pair(columns, which):
        return pl.BlockSpec(
            (1, PAIR, CAPACITY, columns), lambda s, m: (m[which], pair_at(s), 0, 0)
        )

    def fixed(shape):
        return once(shape, lambda s, m: (0,) * len(shape))

    def of_pairs(array):
        return pl.BlockSpec((PAIR,) + array.shape[1:], lambda s, m: (pair_at(s), 0, 0))

    grid_spec = pltpu.PrefetchScalarGridSpec(
        num_scalar_prefetch=1,
        grid=(ROW_STEPS + PAIR_STEPS + 1,),
        in_specs=[
            pl.BlockSpec((ROWS, width), lambda s, m: (m[2] * ROW_STEPS + row_at(s), 0)),
            pl.BlockSpec((ROWS, width), lambda s, m: (row_at(s), 0)),
            once((1, EXPERTS, SEQ_LEN), lambda s, m: (m[2], 0, 0)),
            once((1, SEQ_LEN, EXPERTS), lambda s, m: (m[2], 0, 0)),
            slot_pair(hidden, 3),
            slot_pair(hidden, 3),
            slot_rows(hidden, 3),
            slot_rows(hidden, 3),
            once((1, EXPERTS, SEQ_LEN), lambda s, m: (m[3], 0, 0)),
            of_pairs(wg),
            of_pairs(wu),
            of_pairs(wd),
            fixed(wgs.shape),
            fixed(wus.shape),
            fixed(wds.shape),
        ]
        + [pl.BlockSpec(memory_space=pl.ANY)] * stored,
        out_specs=[
            fixed((SEQ_LEN + 32, width)),
            slot_rows(width, 1),
            slot_pair(hidden, 1),
            slot_pair(hidden, 1),
            slot_pair(hidden, 1),
            slot_pair(width, 1),
            slot_rows(hidden, 1),
            slot_rows(hidden, 1),
            slot_rows(hidden, 1),
        ],
        scratch_shapes=[
            pltpu.VMEM((SEQ_LEN, width), F32),
            pltpu.VMEM((SEQ_LEN, width), BF16),
            pltpu.VMEM((PAIR * CAPACITY, SEQ_LEN), BF16),
            pltpu.VMEM((SEQ_LEN, PAIR * SPAN), BF16),
            pltpu.VMEM((PAIR * CAPACITY, LANES), F32),
            pltpu.VMEM((PAIR * SPAN, width), BF16),
            pltpu.VMEM((EXPERTS, SEQ_LEN), F32),
        ],
    )
    outs = pl.pallas_call(
        functools.partial(feed_backward_kernel, stored),
        grid_spec=grid_spec,
        out_shape=[shape_of((SEQ_LEN + 32, width), BF16)] + saved,
        input_output_aliases={16 + k: 1 + k for k in range(stored)},
        compiler_params=pltpu.CompilerParams(vmem_limit_bytes=VMEM_BYTES),
        cost_estimate=cost(60),
        name="feed_backward",
    )(
        meta,
        cotangent,
        received,
        post,
        pos,
        gate,
        lift,
        gate_sh,
        lift_sh,
        probs,
        wg,
        wu,
        wd,
        wgs,
        wus,
        wds,
        *(kept or ()),
    )
    return outs[0], outs[1:]


def attention_backward_kernel(
    stored,
    meta,
    first_block,
    sum_ref,
    choice_ref,
    probs_ref,
    dy_ref,
    h_ref,
    b_ref,
    gain_ref,
    router_ref,
    wall_ref,
    wo_ref,
    cos_ref,
    sin_ref,
    qkv_ref,
    o_ref,
    lse_ref,
    low_ref,
    *rest,
):
    rest = rest[stored:]
    part_ref, dh_ref, gain_grad_ref, router_grad_ref, dqkv_ref, dattn_ref = rest[:6]
    dk_all, dv_all, dq_all, do_all, inner_all = rest[6:]
    step = pl.program_id(0)
    index = BLOCKS - 1 - step
    heads = wo_ref.shape[0] // LANES
    wide = heads * LANES

    @pl.when(step == 0)
    def _():
        gain_grad_ref[...] = jnp.zeros_like(gain_grad_ref)
        router_grad_ref[...] = jnp.zeros_like(router_grad_ref)
        dk_all[...] = jnp.zeros_like(dk_all)
        dv_all[...] = jnp.zeros_like(dv_all)

    probs = probs_ref[0]
    chosen = choice_ref[0:8, :].astype(F32)
    logit_grads = probs * (chosen - jnp.sum(probs * chosen, axis=0, keepdims=True))
    logit_grads = logit_grads.astype(BF16)
    router_grad_ref[...] += dot(logit_grads, b_ref[0])
    grad_normed = sum_ref[...].astype(F32) + dot_tn(logit_grads, router_ref[...])
    state = h_ref[0]
    scale = lax.rsqrt(jnp.mean(state * state, axis=-1, keepdims=True) + 1e-06)
    normed = state * scale
    gain_grad_ref[...] += jnp.sum(grad_normed * normed, axis=0, keepdims=True)
    scaled = gain_ref[...] * grad_normed
    inner = jnp.mean(normed * scaled, axis=-1, keepdims=True)
    grad_state = dy_ref[0].astype(F32) + scale * (scaled - normed * inner)
    dh_ref[...] = grad_state
    dattn = grad_state.astype(BF16)
    dattn_ref[0] = dattn
    do = dot_nt(dattn, wo_ref[...]).astype(BF16)
    do_all[...] = do
    products = do.astype(F32) * o_ref[0].astype(F32)
    for head in range(heads):
        columns = slice(head * LANES, (head + 1) * LANES)
        row = jnp.sum(products[:, columns], axis=1, keepdims=True)
        inner_all[head : head + 1, :] = jnp.broadcast_to(row, (BLOCK, LANES)).T[0:1, :]
    dq_all[...] = jnp.zeros_like(dq_all)
    here = rows_of(index, BLOCK)
    low = low_ref[0]
    query_at = index * BLOCK + lax.broadcasted_iota(jnp.int32, (BLOCK, BLOCK), 1)
    key_at = lax.broadcasted_iota(jnp.int32, (BLOCK, BLOCK), 0)

    def body(block, none):
        at = key_at + block * BLOCK
        valid = (at >= low) & (at <= query_at)
        there = rows_of(block, BLOCK)
        for head in range(heads):
            columns = slice(head * LANES, (head + 1) * LANES)
            key_columns = slice(wide + head * LANES, wide + (head + 1) * LANES)
            value_columns = slice(2 * wide + head * LANES, 2 * wide + (head + 1) * LANES)
            query = qkv_ref[0, here, columns]
            keys = qkv_ref[0, there, key_columns]
            scores = jnp.where(valid, dot_nt(keys, query), -1e30)
            probs = jnp.exp(scores - lse_ref[0, head : head + 1, :])
            grad_probs = dot_nt(qkv_ref[0, there, value_columns], do_all[:, columns])
            grad_scores = (probs * (grad_probs - inner_all[head : head + 1, :])).astype(BF16)
            dv_all[there, columns] += dot(probs.astype(BF16), do_all[:, columns])
            dk_all[there, columns] += dot(grad_scores, query)
            dq_all[:, columns] += dot_tn(grad_scores, keys)
        return none

    lax.fori_loop(first_block[meta[2] * BLOCKS + index], index + 1, body, 0)
    cosine, sine = cos_ref[...], sin_ref[...]
    for head in range(heads):
        columns = slice(head * LANES, (head + 1) * LANES)
        key_columns = slice(wide + head * LANES, wide + (head + 1) * LANES)
        value_columns = slice(2 * wide + head * LANES, 2 * wide + (head + 1) * LANES)
        dq = dq_all[:, columns] * 0.0625
        dk = dk_all[here, columns]
        dqkv_ref[0, :, columns] = (dq * cosine - pltpu.roll(dq, HEAD_DIM, 1) * sine).astype(BF16)
        dqkv_ref[0, :, key_columns] = (
            dk * cosine - pltpu.roll(dk, HEAD_DIM, 1) * sine
        ).astype(BF16)
        dqkv_ref[0, :, value_columns] = dv_all[here, columns].astype(BF16)
    part_ref[...] = dot_nt(dqkv_ref[0], wall_ref[...]).astype(BF16)


def attention_backward(
    meta, first_block, summed, forward_kept, attention_kept, dy, gain, router, wall, wo, cosine, sine, low, kept
):
    width = summed.shape[1]
    wide = wo.shape[0]
    stored = 0 if kept is None else 2
    h, b, probs = forward_kept[0], forward_kept[1], forward_kept[7]
    unused_x, unused_a, qkv, o, lse = attention_kept
    saved = [
        shape_of((SLOTS, SEQ_LEN, 3 * wide), BF16),
        shape_of((SLOTS, SEQ_LEN, width), BF16),
    ]

    def at(step):
        return BLOCKS - 1 - step

    def slot_rows(columns, which):
        return pl.BlockSpec((1, BLOCK, columns), lambda s, m, f: (m[which], at(s), 0))

    def fixed(shape):
        return once(shape, lambda s, m, f: (0,) * len(shape))

    halves_of = BLOCKS // 2
    grid_spec = pltpu.PrefetchScalarGridSpec(
        num_scalar_prefetch=2,
        grid=(BLOCKS,),
        in_specs=[
            pl.BlockSpec((BLOCK, width), lambda s, m, f: (at(s), 0)),
            pl.BlockSpec(
                (16, BLOCK), lambda s, m, f: (SEQ_LEN // 16 + at(s) // halves_of, at(s) % halves_of)
            ),
            pl.BlockSpec((1, EXPERTS, BLOCK), lambda s, m, f: (m[3], 0, at(s))),
            slot_rows(width, 1),
            slot_rows(width, 3),
            slot_rows(width, 3),
            fixed(gain.shape),
            fixed(router.shape),
            fixed(wall.shape),
            fixed(wo.shape),
            pl.BlockSpec((BLOCK, LANES), lambda s, m, f: (at(s), 0)),
            pl.BlockSpec((BLOCK, LANES), lambda s, m, f: (at(s), 0)),
            once((1, SEQ_LEN, 3 * wide), lambda s, m, f: (m[3], 0, 0)),
            slot_rows(wide, 3),
            pl.BlockSpec((1, 8, BLOCK), lambda s, m, f: (m[3], 0, at(s))),
            pl.BlockSpec((1, 1, BLOCK), lambda s, m, f: (m[2], 0, at(s))),
        ]
        + [pl.BlockSpec(memory_space=pl.ANY)] * stored,
        out_specs=[
            pl.BlockSpec((BLOCK, width), lambda s, m, f: (at(s), 0)),
            pl.BlockSpec((BLOCK, width), lambda s, m, f: (at(s), 0)),
            fixed((1, width)),
            fixed((8, width)),
            slot_rows(3 * wide, 1),
            slot_rows(width, 1),
        ],
        scratch_shapes=[
            pltpu.VMEM((SEQ_LEN, wide), F32),
            pltpu.VMEM((SEQ_LEN, wide), F32),
            pltpu.VMEM((BLOCK, wide), F32),
            pltpu.VMEM((BLOCK, wide), BF16),
            pltpu.VMEM((8, BLOCK), F32),
        ],
    )
    outs = pl.pallas_call(
        functools.partial(attention_backward_kernel, stored),
        grid_spec=grid_spec,
        out_shape=[
            shape_of((SEQ_LEN, width), BF16),
            shape_of((SEQ_LEN, width), F32),
            shape_of((1, width), F32),
            shape_of((8, width), F32),
        ]
        + saved,
        input_output_aliases={18 + k: 4 + k for k in range(stored)},
        compiler_params=pltpu.CompilerParams(vmem_limit_bytes=VMEM_BYTES),
        cost_estimate=cost(37),
        name="attention_backward",
    )(
        meta,
        first_block,
        summed,
        summed,
        probs,
        dy,
        h,
        b,
        gain,
        router,
        wall,
        wo,
        cosine,
        sine,
        qkv,
        o,
        lse,
        low,
        *(kept or ()),
    )
    return outs[:4], outs[4:]


def expert_grads_kernel(*refs):
    ins, out_ref = refs[:-1], refs[-1]
    (xa, xb), (ga, gb), (ua, ub), (ea, eb), (ha, hb) = (ins[2 * k : 2 * k + 2] for k in range(5))
    devices, unused, rows, unused = out_ref.shape
    pairs = [((xa, xb), (ga, gb)), ((xa, xb), (ua, ub)), ((ea, eb), (ha, hb))]
    for number, (left, right) in enumerate(pairs):
        for device in range(devices):
            columns = slice(device * rows, (device + 1) * rows)
            out_ref[device, number] = (
                dot_tn(left[0][0, 0, :, columns], right[0][0, 0])
                + dot_tn(left[1][0, 0, :, columns], right[1][0, 0])
            ).astype(BF16)


def expert_grads(first, count, extra, devices, picked, hid, grad_gate, grad_lift, grad_expert):
    width, hidden = picked.shape[3], hid.shape[3]
    rows = width // devices

    def pair(columns):
        return [
            pl.BlockSpec(
                (1, 1, CAPACITY, columns),
                functools.partial(lambda slot, e: (slot, first + e, 0, 0), slot),
            )
            for slot in (1, 2)
        ]

    return pl.pallas_call(
        expert_grads_kernel,
        grid=(count,),
        in_specs=pair(width) + pair(hidden) + pair(hidden) + pair(width) + pair(hidden),
        out_specs=pl.BlockSpec((devices, 3, rows, hidden), lambda e: (0, e, 0, 0)),
        out_shape=shape_of((devices, 3 * count + extra, rows, hidden), BF16),
        compiler_params=pltpu.CompilerParams(vmem_limit_bytes=VMEM_BYTES),
        cost_estimate=cost(6 * count),
        name="expert_grads",
    )(
        *(picked, picked, grad_gate, grad_gate, grad_lift, grad_lift),
        *(grad_expert, grad_expert, hid, hid),
    )


def shared_grads_kernel(b_ref, dy_ref, gate_ref, lift_ref, hid_ref, before_ref, out_ref, *totals):
    step = pl.program_id(0)
    pairs = [(b_ref, gate_ref), (b_ref, lift_ref), (dy_ref, hid_ref)]

    @pl.when(step == 0)
    def _():
        for total in totals:
            total[...] = jnp.zeros_like(total)

    for (left, right), total in zip(pairs, totals):
        total[...] += dot_tn(left[0], right[0])

    @pl.when(step == pl.num_programs(0) - 1)
    def _():
        devices, unused, rows, unused = out_ref.shape
        for number, total in enumerate(totals):
            for device in range(devices):
                out_ref[device, number] = total[device * rows : (device + 1) * rows, :].astype(
                    BF16
                )


def shared_grads(before, b, dy, grad_gate, grad_lift, hid):
    devices, matrices, width, hidden = before.shape
    rows = 2 * BLOCK
    steps = SEQ_LEN // rows

    def spec(array):
        return pl.BlockSpec((1, rows, array.shape[2]), lambda s: (1 + s // steps, s % steps, 0))

    return pl.pallas_call(
        shared_grads_kernel,
        grid=(2 * steps,),
        in_specs=[spec(array) for array in (b, dy, grad_gate, grad_lift, hid)]
        + [pl.BlockSpec(memory_space=pl.ANY)],
        out_specs=once((devices, 3, width, hidden), lambda s: (0, matrices // 3 - 1, 0, 0)),
        out_shape=shape_of(before.shape, BF16),
        scratch_shapes=[pltpu.VMEM((devices * width, hidden), F32)] * 3,
        input_output_aliases={5: 0},
        compiler_params=pltpu.CompilerParams(vmem_limit_bytes=VMEM_BYTES),
        cost_estimate=cost(13),
        name="shared_grads",
    )(b, dy, grad_gate, grad_lift, hid, before)


def token_grads_kernel(count, *refs):
    lefts, rights = refs[:count], refs[count : 2 * count]
    outs, totals = refs[2 * count : 3 * count], refs[3 * count :]
    step = pl.program_id(0)

    @pl.when(step == 0)
    def _():
        for total in totals:
            total[...] = jnp.zeros_like(total)

    for left, right, total in zip(lefts, rights, totals):
        total[...] += dot_tn(left[0], right[0])

    @pl.when(step == pl.num_programs(0) - 1)
    def _():
        for out, total in zip(outs, totals):
            out[...] = total[...].astype(BF16)


def token_grads(lefts, rights):
    count = len(lefts)
    rows = 2 * BLOCK
    steps = SEQ_LEN // rows

    def spec(array):
        return pl.BlockSpec((1, rows, array.shape[2]), lambda s: (1 + s // steps, s % steps, 0))

    shapes = [(left.shape[2], right.shape[2]) for left, right in zip(lefts, rights)]
    return pl.pallas_call(
        functools.partial(token_grads_kernel, count),
        grid=(2 * steps,),
        in_specs=[spec(a) for a in lefts] + [spec(a) for a in rights],
        out_specs=[once(shape, lambda s: (0, 0)) for shape in shapes],
        out_shape=[shape_of(shape, BF16) for shape in shapes],
        scratch_shapes=[pltpu.VMEM(shape, F32) for shape in shapes],
        compiler_params=pltpu.CompilerParams(vmem_limit_bytes=VMEM_BYTES),
        cost_estimate=cost(14),
        name="token_grads",
    )(*lefts, *rights)


def rotary_tables():
    half = HEAD_DIM // 2
    rates = np.exp(-np.log(10000.0) * np.arange(half) * 2.0 / HEAD_DIM)
    angles = np.arange(SEQ_LEN)[:, None] * rates[None, :]
    cosine, sine = np.cos(angles), np.sin(angles)
    cosine = np.concatenate([cosine] * 4, axis=1)
    sine = np.concatenate([sine, sine, -sine, -sine], axis=1)
    return jnp.asarray(cosine, F32), jnp.asarray(sine, F32)


def paired(weight):
    rows = weight.shape[0]
    heads = weight.shape[1] // HEAD_DIM
    half = HEAD_DIM // 2
    split = weight.reshape(rows, heads, HEAD_DIM)
    swapped = jnp.concatenate([-split[:, :, half:], split[:, :, :half]], axis=2)
    return jnp.concatenate([split, swapped], axis=2).reshape(rows, heads * LANES)


def padded(weight):
    rows = weight.shape[0]
    heads = weight.shape[1] // HEAD_DIM
    split = weight.reshape(rows, heads, HEAD_DIM)
    return jnp.concatenate([split, jnp.zeros_like(split)], axis=2).reshape(rows, heads * LANES)


def unpadded(grads):
    rows = grads.shape[0]
    return grads.reshape(rows, -1, LANES)[:, :, :HEAD_DIM].reshape(rows, -1)


def places(routes):
    experts = jnp.arange(EXPERTS, dtype=jnp.int32)
    named = jnp.any(routes[:, :, :, None] == experts, axis=2)
    before = (
        jnp.arange(SEQ_LEN, dtype=jnp.int32)[:, None] > jnp.arange(SEQ_LEN, dtype=jnp.int32)
    ).astype(BF16)
    rank = jnp.einsum("ts,nse->nte", before, named.astype(BF16), preferred_element_type=F32)
    by_token = jnp.where(named, rank.astype(jnp.int32), -1)
    return by_token, jnp.swapaxes(by_token, 1, 2)


def first_allowed(lengths):
    ends = jnp.cumsum(lengths, axis=1)
    at = jnp.arange(SEQ_LEN, dtype=jnp.int32)
    starts = jnp.max(jnp.where(ends[:, None, :] <= at[None, :, None], ends[:, None, :], 0), axis=2)
    return jnp.maximum(starts, at[None, :] - (WINDOW - 1)).astype(jnp.int32)


def on_device(
    tokens,
    doc_lengths,
    routes,
    gain_attn,
    w_query,
    w_key,
    w_value,
    w_output,
    gain_ffn,
    w_router,
    w_gate_exp,
    w_up_exp,
    w_down_exp,
    w_gate_sh,
    w_up_sh,
    w_down_sh,
    cotangent,
):
    section = lax.axis_index("section")
    devices = lax.axis_size("dp")
    count = doc_lengths.shape[0]
    width = tokens.shape[1]
    cosine, sine = rotary_tables()
    wall = jnp.concatenate([paired(w_query[0]), paired(w_key[0]), padded(w_value[0])], axis=1)
    wo = padded(w_output[0].T).T
    out_weight = lax.all_gather(w_output[0], "tensor", axis=0, tiled=True)
    router = w_router[0].T
    gain_a, gain_f = gain_attn.astype(F32), gain_ffn.astype(F32)
    feed_weights = (
        w_gate_exp[0],
        w_up_exp[0],
        w_down_exp[0],
        w_gate_sh[0],
        w_up_sh[0],
        w_down_sh[0],
    )
    pos, post = places(routes[0].reshape(count, SEQ_LEN, 2))
    low = first_allowed(doc_lengths)
    first_block = (low[:, ::BLOCK] // BLOCK).reshape(-1)
    low_column, low_row = low[:, :, None], low[:, None, :]

    received = jnp.zeros((SEQ_LEN, width), BF16)
    attention_kept, feed_kept, results = None, None, []
    grads_kept, attention_grads_kept, inputs = None, None, []
    small = jnp.zeros((10, width), F32)

    def spread(array):
        return lax.psum_scatter(array, "dp", scatter_dimension=0, tiled=False)

    def after(meta, array):
        return lax.optimization_barrier((meta, array))

    def forward_meta(tick):
        raw = tick - section
        active = (raw >= 0) & (raw < count)
        sequence = jnp.clip(raw, 0, count - 1)
        return jnp.stack([section, jnp.where(active, sequence + 1, 0), sequence]).astype(jnp.int32)

    def backward_meta(tick):
        raw = tick - 1 + section
        active = (raw >= 0) & (raw < count)
        sequence = jnp.clip(raw, 0, count - 1)
        source = jnp.where(active, 2 - section, 0)
        return jnp.stack(
            [source, jnp.where(active, sequence + 1, 0), sequence, sequence + 1]
        ).astype(jnp.int32)

    def attend(meta, received, kept):
        return attention_forward(
            meta, first_block, tokens, received, gain_a, wall, cosine, sine, low_column, kept
        )

    def feed(meta, gathered, kept):
        return feed_forward(
            meta,
            attention_kept[0],
            gathered,
            out_weight,
            gain_f,
            router,
            post,
            pos,
            feed_weights,
            kept,
        )

    def feed_back(meta, received):
        return feed_backward(
            meta, cotangent, received, post, pos, feed_kept, feed_weights, grads_kept
        )

    def attend_back(meta, summed):
        return attention_backward(
            meta,
            first_block,
            summed,
            feed_kept,
            attention_kept,
            grads_kept[0],
            gain_f,
            router,
            wall,
            wo,
            cosine,
            sine,
            low_row,
            attention_grads_kept,
        )

    for tick in range(count):
        meta = forward_meta(tick)
        own, attention_kept = attend(meta, received, attention_kept)
        gathered = tensor_gather(own, 0)
        part, feed_kept = feed(meta, gathered, feed_kept)
        result, received = output_relay(part, feed_kept[0], tick, 4 + tick)
        results.append(result)

    blank = jnp.zeros((SEQ_LEN, width), BF16)
    meta, back_meta = forward_meta(count), backward_meta(0)
    own, attention_kept = attend(meta, received, attention_kept)
    back_meta, own = after(back_meta, own)
    gathered = lax.all_gather(own, "tensor")
    part, grads_kept = feed_back(back_meta, blank)
    meta, part = after(meta, part)
    summed = lax.psum(part, "tensor")
    last_part, feed_kept = feed(meta, gathered, feed_kept)
    back_meta, last_part = after(back_meta, last_part)

    for tick in range(count + 1):
        if tick > 0:
            back_meta = backward_meta(tick)
            part, grads_kept = feed_back(back_meta, received)
        if tick == count:
            dy, hid, grad_gate, grad_lift, grad_expert, hid_sh, grad_gate_sh, grad_lift_sh = (
                grads_kept
            )
            lead = 2
            picked = feed_kept[2]
            first_grads = expert_grads(
                0, lead, 0, devices, picked, hid, grad_gate, grad_lift, grad_expert
            )
            first_grads, picked, grad_gate = lax.optimization_barrier(
                (first_grads, picked, grad_gate)
            )
            other_grads = expert_grads(
                lead,
                EXPERTS - lead,
                3,
                devices,
                picked,
                hid,
                grad_gate,
                grad_lift,
                grad_expert,
            )
            other_grads = shared_grads(
                other_grads, feed_kept[1], dy, grad_gate_sh, grad_lift_sh, hid_sh
            )
            part, other_grads = lax.optimization_barrier((part, other_grads))
            first_grads, other_grads = spread(first_grads), spread(other_grads)
        if tick > 0:
            summed = tensor_sum(part, 2, 7)
        (part, grad_state, gain_grad, router_grad), attention_grads_kept = attend_back(
            back_meta, summed
        )
        grad_input, received, gain_attn_grad = input_relay(
            part, attention_kept[0], grad_state, gain_a, tick, 4 + count + 1 + tick
        )
        inputs.append(grad_input)
        small = small + jnp.concatenate([gain_attn_grad, gain_grad, router_grad], axis=0)
    result, unused = output_relay(last_part, feed_kept[0], count, 4 + count)
    results.append(result)

    projections, outward = token_grads(
        [attention_kept[1], attention_grads_kept[1]], [attention_grads_kept[0], attention_kept[3]]
    )
    wide = wo.shape[0]
    rows = width // devices
    columns = w_query.shape[2]
    packed = jnp.concatenate(
        [
            2.0 * unpadded(projections[:, : 2 * wide]),
            unpadded(projections[:, 2 * wide :]),
            unpadded(outward),
            jnp.pad(small, ((0, 6), (0, 0))).T.astype(BF16),
        ],
        axis=1,
    )
    packed, first_grads, other_grads = lax.optimization_barrier(
        (packed, first_grads, other_grads)
    )
    packed = spread(packed.reshape(devices, rows, -1)).astype(F32)
    shared = other_grads[-3:].astype(F32)
    experts = jnp.concatenate([first_grads, other_grads[:-3]], axis=0).astype(F32)
    experts = experts.reshape(EXPERTS, 3, rows, -1)

    def choose(items):
        return jnp.concatenate(
            [jnp.where(section == 0, items[k], items[k + 1]) for k in range(count)], axis=0
        )

    layer_out = choose(results)
    input_grad = jnp.concatenate(
        [jnp.where(section == 0, inputs[k + 1], inputs[k]) for k in range(count)], axis=0
    )
    extra = 4 * columns
    return (
        layer_out[None],
        input_grad[None],
        packed[None, :, extra],
        packed[None, :, :columns],
        packed[None, :, columns : 2 * columns],
        packed[None, :, 2 * columns : 3 * columns],
        packed[:, 3 * columns : extra].T[None],
        packed[None, :, extra + 1],
        packed[None, :, extra + 2 : extra + 10],
        experts[None, :, 0],
        experts[None, :, 1],
        jnp.swapaxes(experts[:, 2], 1, 2)[None],
        shared[None, 0],
        shared[None, 1],
        shared[2].T[None],
    )


def solution(mesh):
    return jax.shard_map(
        on_device,
        mesh=mesh,
        in_specs=(
            P("dp", None),
            P("dp", None),
            P("section", "dp", None),
            P("section", None),
            P("section", None, "tensor"),
            P("section", None, "tensor"),
            P("section", None, "tensor"),
            P("section", "tensor", None),
            P("section", None),
            P("section", None, None),
            P("section", None, None, "tensor"),
            P("section", None, None, "tensor"),
            P("section", None, "tensor", None),
            P("section", None, "tensor"),
            P("section", None, "tensor"),
            P("section", "tensor", None),
            P("dp", None),
        ),
        out_specs=(
            P("section", "dp", None),
            P("section", "dp", None),
            P("section", "dp"),
            P("section", "dp", "tensor"),
            P("section", "dp", "tensor"),
            P("section", "dp", "tensor"),
            P("section", "tensor", "dp"),
            P("section", "dp"),
            P("section", "dp", None),
            P("section", None, "dp", "tensor"),
            P("section", None, "dp", "tensor"),
            P("section", None, "tensor", "dp"),
            P("section", "dp", "tensor"),
            P("section", "dp", "tensor"),
            P("section", "tensor", "dp"),
        ),
        check_vma=False,
    )
```

```python
import functools

import jax
import jax.numpy as jnp
import numpy as np
from jax import lax
from jax.experimental import pallas as pl
from jax.experimental.pallas import tpu as pltpu
from jax.sharding import PartitionSpec as P

HEAD_DIM = 64
EXPERTS = 8
SEQ_LEN = 1536
WINDOW = 1024
CAPACITY = 480
BLOCK = 512
PACK = 256
BLOCKS = SEQ_LEN // BLOCK
KEYS = 256
BACK_BLOCK = 384
BACK_BLOCKS = SEQ_LEN // BACK_BLOCK
BACK_KEYS = 384
LANES = 128
SLOTS = 3
VMEM_BYTES = 60 * 2**20
MESH = pl.DeviceIdType.MESH
F32 = jnp.float32
BF16 = jnp.bfloat16
NT = (((1,), (1,)), ((), ()))
TN = (((0,), (0,)), ((), ()))


def shape_of(shape, dtype):
    return jax.ShapeDtypeStruct(shape, dtype)


def cost(micros):
    return pl.CostEstimate(
        flops=int(micros * 1.15e9), bytes_accessed=int(micros * 3.6e6), transcendentals=0
    )


def dot(left, right):
    return jnp.dot(left, right, preferred_element_type=F32)


def dot_nt(left, right):
    return lax.dot_general(left, right, NT, preferred_element_type=F32)


def dot_tn(left, right):
    return lax.dot_general(left, right, TN, preferred_element_type=F32)


def once(shape, index):
    return pl.BlockSpec(shape, index, pipeline_mode=pl.Buffered(1))


def loop(count, body):
    lax.fori_loop(0, count, lambda step, none: (body(step), none)[1], 0)


def rows_of(step, size):
    return pl.ds(pl.multiple_of(step * size, size), size)


def greet(partners):
    barrier = pltpu.get_barrier_semaphore()
    for partner in partners:
        pl.semaphore_signal(barrier, inc=1, device_id=partner, device_id_type=MESH)
    pl.semaphore_wait(barrier, len(partners))


def remote(source, target, send, recv, device):
    return pltpu.make_async_remote_copy(
        src_ref=source,
        dst_ref=target,
        send_sem=send,
        recv_sem=recv,
        device_id=device,
        device_id_type=MESH,
    )


def partners_of():
    place = lax.axis_index("tensor")
    core = lax.rem(place, 2)
    return {"tensor": place + 1 - 2 * core}, {"tensor": lax.rem(place + 2, 4)}


def sides(rows):
    core = lax.rem(lax.axis_index("tensor"), 2)
    half = rows // 2
    return core * half, (1 - core) * half


def piece_rows(side, step, size):
    return pl.ds(pl.multiple_of(side + step * size, 16), size)


def cross_kernel(pieces, part_ref, mine, first, kept, second, sends, recvs, loaded, use):
    near, far = partners_of()
    own, other = sides(part_ref.shape[0])
    size = mine.shape[0] // pieces
    copies = []
    for step in range(pieces):
        local = pl.ds(step * size, size)
        copies.append(
            remote(
                part_ref.at[piece_rows(other, step, size)],
                first.at[local],
                sends.at[0, step],
                recvs.at[0, step],
                near,
            )
        )
        copies[-1].start()
    load = pltpu.make_async_copy(
        part_ref.at[pl.ds(pl.multiple_of(own, 16), mine.shape[0])], mine, loaded
    )
    load.start()
    load.wait()
    for step in range(pieces):
        local = pl.ds(step * size, size)
        copies[step].wait_recv()
        kept[local, :] = (mine[local, :].astype(F32) + first[local, :].astype(F32)).astype(BF16)
        copies.append(
            remote(
                kept.at[local], second.at[local], sends.at[1, step], recvs.at[1, step], far
            )
        )
        copies[-1].start()
    for step in range(pieces):
        local = pl.ds(step * size, size)
        copies[pieces + step].wait_recv()
        use(step, local, kept[local, :].astype(F32) + second[local, :].astype(F32))
    return copies


def sum_kernel(
    pieces, part_ref, out_ref, mine, first, kept, second, done, sends, recvs, loaded, stored
):
    near, far = partners_of()
    greet([near, far])
    own, other = sides(part_ref.shape[0])
    size = mine.shape[0] // pieces
    back, local_copies = [], []

    def use(step, local, total):
        done[local, :] = total.astype(BF16)
        rows = piece_rows(own, step, size)
        back.append(
            remote(done.at[local], out_ref.at[rows], sends.at[2, step], recvs.at[2, step], near)
        )
        back[-1].start()
        local_copies.append(
            pltpu.make_async_copy(done.at[local], out_ref.at[rows], stored.at[step])
        )
        local_copies[-1].start()

    copies = cross_kernel(
        pieces, part_ref, mine, first, kept, second, sends, recvs, loaded, use
    )
    for copy in back:
        copy.wait_recv()
    for copy in copies + back:
        copy.wait_send()
    for copy in local_copies:
        copy.wait()


def tensor_sum(part, identity, pieces):
    rows, width = part.shape
    hbm = pl.BlockSpec(memory_space=pl.ANY)
    return pl.pallas_call(
        functools.partial(sum_kernel, pieces),
        out_shape=shape_of((rows, width), BF16),
        in_specs=[hbm],
        out_specs=hbm,
        scratch_shapes=[pltpu.VMEM((rows // 2, width), BF16)] * 5
        + [pltpu.SemaphoreType.DMA((3, pieces))] * 2
        + [pltpu.SemaphoreType.DMA, pltpu.SemaphoreType.DMA((pieces,))],
        compiler_params=pltpu.CompilerParams(
            collective_id=identity, has_side_effects=True, vmem_limit_bytes=VMEM_BYTES
        ),
        cost_estimate=cost(32),
        name="tensor_sum",
    )(part)


def gather_kernel(pieces, own_ref, out_ref, sends, recvs, stored):
    place = lax.axis_index("tensor")
    near, far = partners_of()
    greet([near, far])
    far_place = lax.rem(place + 2, 4)
    size = own_ref.shape[0] // pieces
    first, crossing, passed = [], [], []
    for group, copies, partner in ((0, crossing, far), (1, first, near)):
        for piece in range(pieces):
            rows = pl.ds(piece * size, size)
            copies.append(
                remote(
                    own_ref.at[rows],
                    out_ref.at[place, rows],
                    sends.at[group, piece],
                    recvs.at[group, piece],
                    partner,
                )
            )
            copies[-1].start()
    local = pltpu.make_async_copy(own_ref, out_ref.at[place], stored)
    local.start()
    for piece in range(pieces):
        rows = pl.ds(piece * size, size)
        crossing[piece].wait_recv()
        passed.append(
            remote(
                out_ref.at[far_place, rows],
                out_ref.at[far_place, rows],
                sends.at[2, piece],
                recvs.at[2, piece],
                near,
            )
        )
        passed[-1].start()
    for copy in first + passed:
        copy.wait_recv()
    for copy in first + crossing + passed:
        copy.wait_send()
    local.wait()


def tensor_gather(own, identity, pieces=6):
    hbm = pl.BlockSpec(memory_space=pl.ANY)
    return pl.pallas_call(
        functools.partial(gather_kernel, pieces),
        out_shape=shape_of((4,) + own.shape, BF16),
        in_specs=[hbm],
        out_specs=hbm,
        scratch_shapes=[pltpu.SemaphoreType.DMA((3, pieces))] * 2 + [pltpu.SemaphoreType.DMA],
        compiler_params=pltpu.CompilerParams(
            collective_id=identity, has_side_effects=True, vmem_limit_bytes=VMEM_BYTES
        ),
        cost_estimate=cost(18),
        name="tensor_gather",
    )(own)


def pass_on(step, source, rows, next_ref, sends, recvs, across):
    copy = remote(source, next_ref.at[rows], sends.at[3, step], recvs.at[3, step], across)
    copy.start()
    return copy


LAG = 3


def spread_on(step, passed, rows, next_ref, sends, recvs, near):
    passed[step].wait_recv()
    copy = remote(next_ref.at[rows], next_ref.at[rows], sends.at[4, step], recvs.at[4, step], near)
    copy.start()
    return copy


def output_kernel(
    pieces,
    tick,
    part_ref,
    states_ref,
    out_ref,
    next_ref,
    mine,
    first,
    kept,
    second,
    done,
    state,
    sends,
    recvs,
    loaded,
    state_loaded,
    stored,
):
    near, far = partners_of()
    section = lax.axis_index("section")
    across = {"section": 1 - section}
    slot = lax.rem(tick + 1 - section, states_ref.shape[0])
    own, other = sides(part_ref.shape[0])
    size = mine.shape[0] // pieces
    load = pltpu.make_async_copy(
        states_ref.at[slot, pl.ds(pl.multiple_of(own, 16), mine.shape[0])], state, state_loaded
    )
    load.start()
    greet([near, far, across])
    back, passed, spread, local_copies = [], [], [], []

    def forward(step):
        rows = piece_rows(own, step, size)
        spread.append(spread_on(step, passed, rows, next_ref, sends, recvs, near))

    def use(step, local, total):
        if step == 0:
            load.wait()
        done[local, :] = (state[local, :] + total.astype(BF16).astype(F32)).astype(BF16)
        rows = piece_rows(own, step, size)
        passed.append(pass_on(step, done.at[local], rows, next_ref, sends, recvs, across))
        back.append(
            remote(done.at[local], out_ref.at[rows], sends.at[2, step], recvs.at[2, step], near)
        )
        back[-1].start()
        local_copies.append(
            pltpu.make_async_copy(done.at[local], out_ref.at[rows], stored.at[step])
        )
        local_copies[-1].start()
        if step >= LAG:
            forward(step - LAG)

    copies = cross_kernel(
        pieces, part_ref, mine, first, kept, second, sends, recvs, loaded, use
    )
    for step in range(pieces - LAG, pieces):
        forward(step)
    for copy in back + spread:
        copy.wait_recv()
    for copy in copies + back + passed + spread:
        copy.wait_send()
    for copy in local_copies:
        copy.wait()


def output_relay(part, states, tick, identity, pieces=12):
    rows, width = part.shape
    hbm = pl.BlockSpec(memory_space=pl.ANY)
    return pl.pallas_call(
        functools.partial(output_kernel, pieces, tick),
        out_shape=[shape_of((rows, width), BF16)] * 2,
        in_specs=[hbm] * 2,
        out_specs=[hbm] * 2,
        scratch_shapes=[pltpu.VMEM((rows // 2, width), BF16)] * 5
        + [pltpu.VMEM((rows // 2, width), F32)]
        + [pltpu.SemaphoreType.DMA((5, pieces))] * 2
        + [pltpu.SemaphoreType.DMA] * 2
        + [pltpu.SemaphoreType.DMA((pieces,))],
        compiler_params=pltpu.CompilerParams(
            collective_id=identity, has_side_effects=True, vmem_limit_bytes=VMEM_BYTES
        ),
        cost_estimate=cost(38),
        name="output_relay",
    )(part, states)


def input_kernel(
    pieces,
    tick,
    part_ref,
    layers_ref,
    grad_state_ref,
    gain_ref,
    grad_ref,
    next_ref,
    grad_gain_ref,
    mine,
    first,
    kept,
    second,
    given,
    full,
    layer_in,
    grad_state,
    grad,
    gains,
    sends,
    recvs,
    loaded,
    inputs_loaded,
    stored,
):
    near, far = partners_of()
    section = lax.axis_index("section")
    across = {"section": 1 - section}
    slot = lax.rem(tick + section, layers_ref.shape[0])
    rows = part_ref.shape[0]
    own, other = sides(rows)
    half = rows // 2
    size = half // pieces
    loads = []
    for side, start in ((0, own), (1, other)):
        there = pl.ds(pl.multiple_of(start, 16), half)
        loads.append(
            [
                pltpu.make_async_copy(
                    layers_ref.at[slot, there], layer_in.at[there], inputs_loaded.at[side, 0]
                ),
                pltpu.make_async_copy(
                    grad_state_ref.at[there], grad_state.at[there], inputs_loaded.at[side, 1]
                ),
            ]
        )
        for load in loads[-1]:
            load.start()
    greet([near, far, across])
    gains[...] = jnp.zeros_like(gains)
    back, passed, spread, local_copies = [], [], [], []

    def rows_back(here, side, step):
        grad_normed = full[here, :].astype(F32)
        values = layer_in[here, :].astype(F32)
        scale = lax.rsqrt(jnp.mean(values * values, axis=-1, keepdims=True) + 1e-06)
        normed = values * scale
        scaled = gain_ref[...] * grad_normed
        inner = jnp.mean(normed * scaled, axis=-1, keepdims=True)
        result = grad_state[here, :] + scale * (scaled - normed * inner)
        grad[here, :] = result
        gains[side : side + 1, :] += jnp.sum(grad_normed * normed, axis=0, keepdims=True)
        local_copies.append(
            pltpu.make_async_copy(grad.at[here], grad_ref.at[here], stored.at[side, step])
        )
        local_copies[-1].start()
        return result

    def partner_rows(step):
        if step == 0:
            for load in loads[1]:
                load.wait()
        back[step].wait_recv()
        rows_back(piece_rows(other, step, size), 1, step)

    def forward(step):
        here = piece_rows(own, step, size)
        spread.append(spread_on(step, passed, here, next_ref, sends, recvs, near))

    def use(step, local, total):
        if step == 0:
            for load in loads[0]:
                load.wait()
        here = piece_rows(own, step, size)
        full[here, :] = total.astype(BF16)
        back.append(
            remote(full.at[here], full.at[here], sends.at[2, step], recvs.at[2, step], near)
        )
        back[-1].start()
        given[local, :] = rows_back(here, 0, step).astype(BF16)
        passed.append(pass_on(step, given.at[local], here, next_ref, sends, recvs, across))
        if step > 0:
            partner_rows(step - 1)
        if step >= LAG:
            forward(step - LAG)

    copies = cross_kernel(
        pieces, part_ref, mine, first, kept, second, sends, recvs, loaded, use
    )
    partner_rows(pieces - 1)
    for step in range(pieces - LAG, pieces):
        forward(step)
    grad_gain_ref[...] = gains[0:1, :] + gains[1:2, :]
    for copy in spread:
        copy.wait_recv()
    for copy in copies + back + passed + spread:
        copy.wait_send()
    for copy in local_copies:
        copy.wait()


def input_relay(part, layers, grad_state, gain, tick, identity, pieces=12):
    rows, width = part.shape
    hbm = pl.BlockSpec(memory_space=pl.ANY)
    whole = pl.BlockSpec(memory_space=pltpu.VMEM)
    return pl.pallas_call(
        functools.partial(input_kernel, pieces, tick),
        out_shape=[
            shape_of((rows, width), F32),
            shape_of((rows, width), BF16),
            shape_of((1, width), F32),
        ],
        in_specs=[hbm] * 3 + [whole],
        out_specs=[hbm] * 2 + [whole],
        scratch_shapes=[pltpu.VMEM((rows // 2, width), BF16)] * 5
        + [pltpu.VMEM((rows, width), BF16)] * 2
        + [pltpu.VMEM((rows, width), F32)] * 2
        + [pltpu.VMEM((8, width), F32)]
        + [pltpu.SemaphoreType.DMA((5, pieces))] * 2
        + [pltpu.SemaphoreType.DMA]
        + [pltpu.SemaphoreType.DMA((2, 2)), pltpu.SemaphoreType.DMA((2, pieces))],
        compiler_params=pltpu.CompilerParams(
            collective_id=identity, has_side_effects=True, vmem_limit_bytes=VMEM_BYTES
        ),
        cost_estimate=cost(42),
        name="input_relay",
    )(part, layers, grad_state, gain)


def attention_forward_kernel(
    stored,
    meta,
    first_block,
    tok_ref,
    rec_ref,
    gain_ref,
    wall_ref,
    cos_ref,
    sin_ref,
    low_ref,
    *rest,
):
    rest = rest[stored:]
    packed_ref, x_ref, a_ref, qkv_ref, o_ref, lse_ref = rest[:6]
    keys, values, scores, tops, sums, mixed = rest[6:]
    index = pl.program_id(0)
    heads = wall_ref.shape[1] // (3 * LANES)
    wide = heads * LANES
    x = jnp.where(meta[0] == 0, tok_ref[...], rec_ref[...])
    x_ref[0] = x
    x = x.astype(F32)
    normed = gain_ref[...] * x * lax.rsqrt(jnp.mean(x * x, axis=-1, keepdims=True) + 1e-06)
    normed = normed.astype(BF16)
    a_ref[0] = normed
    cosine, sine = cos_ref[...], sin_ref[...]
    here = rows_of(index, BLOCK)
    projected = dot(normed, wall_ref[...])
    for group in range(2 * heads):
        columns = slice(group * LANES, (group + 1) * LANES)
        pre = projected[:, columns]
        turned = pre * cosine + pltpu.roll(pre, HEAD_DIM, 1) * sine
        if group < heads:
            turned = turned * 0.0625
        qkv_ref[0, :, columns] = turned.astype(BF16)
    qkv_ref[0, :, 2 * wide :] = projected[:, 2 * wide :].astype(BF16)
    keys[here, :] = qkv_ref[0, :, wide : 2 * wide]
    low = low_ref[0]
    query_at = index * BLOCK + lax.broadcasted_iota(jnp.int32, (BLOCK, KEYS), 0)
    key_at = lax.broadcasted_iota(jnp.int32, (BLOCK, KEYS), 1)

    @pl.when(index * BLOCK % KEYS == 0)
    def _():
        values[rows_of(index * BLOCK // KEYS, KEYS), :] = jnp.zeros((KEYS, wide), BF16)

    values[here, :] = qkv_ref[0, :, 2 * wide :]
    tops[...] = jnp.full_like(tops, -1e30)
    sums[...] = jnp.zeros_like(sums)
    mixed[...] = jnp.zeros_like(mixed)
    begin = first_block[meta[2] * BLOCKS + index]

    def score(block, none):
        at = key_at + block * KEYS
        valid = (at >= low) & (at <= query_at)
        there = rows_of(block, KEYS)
        for head in range(heads):
            columns = slice(head * LANES, (head + 1) * LANES)
            raw = dot_nt(qkv_ref[0, :, columns], keys[there, columns])
            raw = jnp.where(valid, raw, -1e30)
            scores[head, block] = raw
            best = tops[head]
            for start in range(0, KEYS, LANES):
                best = jnp.maximum(best, raw[:, start : start + LANES])
            tops[head] = best
        return none

    end = ((index + 1) * BLOCK - 1) // KEYS + 1
    lax.fori_loop(begin, end, score, 0)
    top = [jnp.max(tops[head], axis=1, keepdims=True) for head in range(heads)]

    def mix(block, none):
        there = rows_of(block, KEYS)
        for head in range(heads):
            columns = slice(head * LANES, (head + 1) * LANES)
            weights = jnp.exp(scores[head, block] - top[head])
            part = weights[:, :LANES]
            for start in range(LANES, KEYS, LANES):
                part = part + weights[:, start : start + LANES]
            sums[head] += part
            mixed[:, columns] += dot(weights.astype(BF16), values[there, columns])
        return none

    lax.fori_loop(begin, end, mix, 0)
    for head in range(heads):
        columns = slice(head * LANES, (head + 1) * LANES)
        total = jnp.sum(sums[head], axis=1, keepdims=True)
        o_ref[0, :, columns] = (mixed[:, columns] / total).astype(BF16)
        logsum = jnp.broadcast_to(top[head] + jnp.log(total), (BLOCK, LANES))
        lse_ref[0, head : head + 1, :] = logsum.T[0:1, :]
    half = PACK // 2
    for start in range(0, BLOCK, PACK):
        packed_ref[start // 2 : start // 2 + half, :] = jnp.concatenate(
            [
                o_ref[
                    0,
                    start + side * half : start + (side + 1) * half,
                    head * LANES : head * LANES + HEAD_DIM,
                ]
                for side in range(2)
                for head in range(heads)
            ],
            axis=1,
        )


def attention_forward(meta, first_block, tokens, received, gain, wall, cosine, sine, low, kept):
    width = tokens.shape[1]
    wide = wall.shape[1] // 3
    heads = wide // LANES
    stored = 0 if kept is None else 5
    saved = [
        shape_of((SLOTS, SEQ_LEN, width), BF16),
        shape_of((SLOTS, SEQ_LEN, width), BF16),
        shape_of((SLOTS, SEQ_LEN, 3 * wide), BF16),
        shape_of((SLOTS, SEQ_LEN, wide), BF16),
        shape_of((SLOTS, 8, SEQ_LEN), F32),
    ]

    def slot_rows(columns):
        return pl.BlockSpec((1, BLOCK, columns), lambda i, m, f: (m[1], i, 0))

    grid_spec = pltpu.PrefetchScalarGridSpec(
        num_scalar_prefetch=2,
        grid=(BLOCKS,),
        in_specs=[
            pl.BlockSpec((BLOCK, width), lambda i, m, f: (m[2] * BLOCKS + i, 0)),
            pl.BlockSpec((BLOCK, width), lambda i, m, f: (i, 0)),
            once((1, width), lambda i, m, f: (0, 0)),
            once(wall.shape, lambda i, m, f: (0, 0)),
            pl.BlockSpec((BLOCK, LANES), lambda i, m, f: (i, 0)),
            pl.BlockSpec((BLOCK, LANES), lambda i, m, f: (i, 0)),
            pl.BlockSpec((1, BLOCK, 1), lambda i, m, f: (m[2], i, 0)),
        ]
        + [pl.BlockSpec(memory_space=pl.ANY)] * stored,
        out_specs=[
            pl.BlockSpec((BLOCK // 2, wide), lambda i, m, f: (i, 0)),
            slot_rows(width),
            slot_rows(width),
            slot_rows(3 * wide),
            slot_rows(wide),
            pl.BlockSpec((1, 8, BLOCK), lambda i, m, f: (m[1], 0, i)),
        ],
        scratch_shapes=[
            pltpu.VMEM((SEQ_LEN, wide), BF16),
            pltpu.VMEM((SEQ_LEN, wide), BF16),
            pltpu.VMEM((heads, SEQ_LEN // KEYS, BLOCK, KEYS), F32),
            pltpu.VMEM((heads, BLOCK, LANES), F32),
            pltpu.VMEM((heads, BLOCK, LANES), F32),
            pltpu.VMEM((BLOCK, wide), F32),
        ],
    )
    outs = pl.pallas_call(
        functools.partial(attention_forward_kernel, stored),
        grid_spec=grid_spec,
        out_shape=[shape_of((SEQ_LEN // 2, wide), BF16)] + saved,
        input_output_aliases={9 + k: 1 + k for k in range(stored)},
        compiler_params=pltpu.CompilerParams(vmem_limit_bytes=VMEM_BYTES),
        cost_estimate=cost(24),
        name="attention_forward",
    )(
        meta,
        first_block,
        tokens,
        received,
        gain,
        wall,
        cosine,
        sine,
        low,
        *(kept or ()),
    )
    return outs[0], outs[1:]


def reserve(shapes):
    return pl.pallas_call(
        lambda *refs: None,
        out_shape=shapes,
        out_specs=[pl.BlockSpec(memory_space=pl.ANY)] * len(shapes),
        compiler_params=pltpu.CompilerParams(has_side_effects=True),
        cost_estimate=cost(1),
        name="reserve",
    )()


PAIR = 2
ROWS = 512
ROW_STEPS = SEQ_LEN // ROWS
PAIR_STEPS = EXPERTS // PAIR
SPAN = 512
CHUNK = 96


def build_pick(first, chunks, post_ref, probs, pick, gates):
    for which, step in chunks:
        row = pl.ds(first + which, 1)
        slot_at = step * CHUNK + lax.broadcasted_iota(jnp.int32, (CHUNK, SEQ_LEN), 0)
        here = slot_at == post_ref[0, row, :]
        rows = slice(which * CAPACITY + step * CHUNK, which * CAPACITY + (step + 1) * CHUNK)
        pick[rows, :] = jnp.where(here, 1.0, 0.0).astype(BF16)
        if probs is not None:
            chosen = jnp.sum(jnp.where(here, probs[row, :], 0.0), axis=1, keepdims=True)
            gates[rows, :] = jnp.broadcast_to(chosen, (CHUNK, LANES))


def build_gates(first, post_ref, probs, gates):
    for which in range(PAIR):
        row = pl.ds(first + which, 1)
        for step in range(CAPACITY // CHUNK):
            slot_at = step * CHUNK + lax.broadcasted_iota(jnp.int32, (CHUNK, SEQ_LEN), 0)
            here = slot_at == post_ref[0, row, :]
            rows = slice(which * CAPACITY + step * CHUNK, which * CAPACITY + (step + 1) * CHUNK)
            chosen = jnp.sum(jnp.where(here, probs[row, :], 0.0), axis=1, keepdims=True)
            gates[rows, :] = jnp.broadcast_to(chosen, (CHUNK, LANES))


def build_put(first, rows, pos_ref, put):
    places = pos_ref[0, rows, :]
    lane = lax.broadcasted_iota(jnp.int32, places.shape, 1)
    slot_at = lax.broadcasted_iota(jnp.int32, (places.shape[0], SPAN), 1)
    for which in range(PAIR):
        place = jnp.sum(jnp.where(lane == first + which, places, 0), axis=1, keepdims=True)
        put[rows, which * SPAN : (which + 1) * SPAN] = jnp.where(
            slot_at == place, 1.0, 0.0
        ).astype(BF16)


ALL_CHUNKS = [(which, step) for which in range(PAIR) for step in range(CAPACITY // CHUNK)]


def of_pair(which):
    return slice(which * CAPACITY, (which + 1) * CAPACITY)


def feed_forward_kernel(
    stored,
    meta,
    x_ref,
    ag_ref,
    wo_ref,
    gain_ref,
    router_ref,
    post_ref,
    pos_ref,
    wg_ref,
    wu_ref,
    wd_ref,
    wgs_ref,
    wus_ref,
    wds_ref,
    *rest,
):
    rest = rest[stored:]
    part_ref, h_ref, b_ref, xe_ref, g_ref, u_ref, gs_ref, us_ref, probs_ref = rest[:9]
    total, normed, probs, pick, put, gates, scaled = rest[9:]
    step = pl.program_id(0)
    pair = jnp.maximum(step - ROW_STEPS, 0)

    def activate(gate, lift, gate_out, lift_out):
        gate_out[...] = gate.astype(BF16)
        lift_out[...] = lift.astype(BF16)
        return (gate / (1.0 + jnp.exp(-gate)) * lift).astype(BF16)

    @pl.when(step < ROW_STEPS)
    def _():
        half = PACK // 2
        columns = ag_ref.shape[2] // 2
        mixed = jnp.concatenate(
            [
                jnp.concatenate(
                    [
                        ag_ref[device, block : block + half, side * columns : (side + 1) * columns]
                        for device in range(4)
                    ],
                    axis=1,
                )
                for block in range(0, ROWS // 2, half)
                for side in range(2)
            ],
            axis=0,
        )
        state = x_ref[0].astype(F32) + dot(mixed, wo_ref[...])
        h_ref[0] = state
        scale = lax.rsqrt(jnp.mean(state * state, axis=-1, keepdims=True) + 1e-06)
        b = (gain_ref[...] * state * scale).astype(BF16)
        b_ref[0] = b
        here = rows_of(step, ROWS)
        normed[here, :] = b
        logits = dot_nt(router_ref[...], b)
        weights = jnp.exp(logits - jnp.max(logits, axis=0, keepdims=True))
        weights = weights / jnp.sum(weights, axis=0, keepdims=True)
        probs_ref[0] = weights
        probs[:, here] = weights
        hidden = activate(dot(b, wgs_ref[...]), dot(b, wus_ref[...]), gs_ref.at[0], us_ref.at[0])
        total[here, :] = dot(hidden, wds_ref[...])

    @pl.when(step == 0)
    def _():
        build_pick(0, ALL_CHUNKS, post_ref, None, pick, gates)
        scaled[...] = jnp.zeros_like(scaled)

    def experts(combine):
        for start in range(0, SEQ_LEN, ROWS):
            rows = pl.ds(start, ROWS)
            if combine:
                total[rows, :] += dot(put[rows, :], scaled[...])
            build_put(pair * PAIR, rows, pos_ref, put)
        picked = dot(pick[...], normed[...]).astype(BF16)
        build_gates(pair * PAIR, post_ref, probs, gates)
        build_pick(
            jnp.minimum(pair + 1, PAIR_STEPS - 1) * PAIR, ALL_CHUNKS, post_ref, None, pick, gates
        )
        for which in range(PAIR):
            rows = picked[of_pair(which), :]
            xe_ref[0, which] = rows
            hidden = activate(
                dot(rows, wg_ref[which]), dot(rows, wu_ref[which]), g_ref.at[0, which], u_ref.at[0, which]
            )
            scaled[which * SPAN : which * SPAN + CAPACITY, :] = (
                dot(hidden, wd_ref[which]) * gates[of_pair(which), 0:1]
            ).astype(BF16)

    @pl.when(step == ROW_STEPS)
    def _():
        experts(False)

    @pl.when((step > ROW_STEPS) & (step < ROW_STEPS + PAIR_STEPS))
    def _():
        experts(True)

    @pl.when(step == ROW_STEPS + PAIR_STEPS)
    def _():
        for start in range(0, SEQ_LEN, ROWS):
            rows = pl.ds(start, ROWS)
            part_ref[rows, :] = (total[rows, :] + dot(put[rows, :], scaled[...])).astype(BF16)


def step_specs():
    def row_at(step):
        return jnp.minimum(step, ROW_STEPS - 1)

    def pair_at(step):
        return jnp.clip(step - ROW_STEPS, 0, PAIR_STEPS - 1)

    return row_at, pair_at


def feed_forward(
    meta, layer_in, gathered, out_weight, gain, router, post, pos, weights, kept
):
    width = layer_in.shape[2]
    wg, wu, wd, wgs, wus, wds = weights
    hidden = wg.shape[2]
    stored = 8
    saved = [
        shape_of((SLOTS, SEQ_LEN, width), F32),
        shape_of((SLOTS, SEQ_LEN, width), BF16),
        shape_of((SLOTS, EXPERTS, CAPACITY, width), BF16),
        shape_of((SLOTS, EXPERTS, CAPACITY, hidden), BF16),
        shape_of((SLOTS, EXPERTS, CAPACITY, hidden), BF16),
        shape_of((SLOTS, SEQ_LEN, hidden), BF16),
        shape_of((SLOTS, SEQ_LEN, hidden), BF16),
        shape_of((SLOTS, EXPERTS, SEQ_LEN), F32),
    ]
    row_at, pair_at = step_specs()

    def slot_rows(columns):
        return pl.BlockSpec((1, ROWS, columns), lambda s, m: (m[1], row_at(s), 0))

    def slot_pair(columns):
        return pl.BlockSpec((1, PAIR, CAPACITY, columns), lambda s, m: (m[1], pair_at(s), 0, 0))

    def fixed(shape):
        return once(shape, lambda s, m: (0,) * len(shape))

    def of_pairs(array):
        return pl.BlockSpec((PAIR,) + array.shape[1:], lambda s, m: (pair_at(s), 0, 0))

    grid_spec = pltpu.PrefetchScalarGridSpec(
        num_scalar_prefetch=1,
        grid=(ROW_STEPS + PAIR_STEPS + 1,),
        in_specs=[
            slot_rows(width),
            pl.BlockSpec((4, ROWS // 2, gathered.shape[2]), lambda s, m: (0, row_at(s), 0)),
            fixed(out_weight.shape),
            fixed(gain.shape),
            fixed(router.shape),
            once((1, EXPERTS, SEQ_LEN), lambda s, m: (m[2], 0, 0)),
            once((1, SEQ_LEN, EXPERTS), lambda s, m: (m[2], 0, 0)),
            of_pairs(wg),
            of_pairs(wu),
            of_pairs(wd),
            fixed(wgs.shape),
            fixed(wus.shape),
            fixed(wds.shape),
        ]
        + [pl.BlockSpec(memory_space=pl.ANY)] * stored,
        out_specs=[
            fixed((SEQ_LEN, width)),
            slot_rows(width),
            slot_rows(width),
            slot_pair(width),
            slot_pair(hidden),
            slot_pair(hidden),
            slot_rows(hidden),
            slot_rows(hidden),
            pl.BlockSpec((1, EXPERTS, ROWS), lambda s, m: (m[1], 0, row_at(s))),
        ],
        scratch_shapes=[
            pltpu.VMEM((SEQ_LEN, width), F32),
            pltpu.VMEM((SEQ_LEN, width), BF16),
            pltpu.VMEM((EXPERTS, SEQ_LEN), F32),
            pltpu.VMEM((PAIR * CAPACITY, SEQ_LEN), BF16),
            pltpu.VMEM((SEQ_LEN, PAIR * SPAN), BF16),
            pltpu.VMEM((PAIR * CAPACITY, LANES), F32),
            pltpu.VMEM((PAIR * SPAN, width), BF16),
        ],
    )
    outs = pl.pallas_call(
        functools.partial(feed_forward_kernel, stored),
        grid_spec=grid_spec,
        out_shape=[shape_of((SEQ_LEN, width), BF16)] + saved,
        input_output_aliases={14 + k: 1 + k for k in range(stored)},
        compiler_params=pltpu.CompilerParams(vmem_limit_bytes=VMEM_BYTES),
        cost_estimate=cost(56),
        name="feed_forward",
    )(
        meta,
        layer_in,
        gathered,
        out_weight,
        gain,
        router,
        post,
        pos,
        wg,
        wu,
        wd,
        wgs,
        wus,
        wds,
        *(reserve(saved) if kept is None else kept),
    )
    return outs[0], outs[1:]


def pull(grad, weight, gate, lift):
    gate, lift = gate.astype(F32), lift.astype(F32)
    sigma = 1.0 / (1.0 + jnp.exp(-gate))
    swish = gate * sigma
    hidden = (swish * lift).astype(BF16)
    inner = None
    if weight is not None:
        inner = jnp.sum(hidden.astype(F32) * grad, axis=1, keepdims=True)
        grad = grad * weight
    grad_gate = (grad * lift * (sigma + swish * (1.0 - sigma))).astype(BF16)
    return hidden, grad_gate, (grad * swish).astype(BF16), inner


def feed_backward_kernel(
    stored,
    meta,
    cot_ref,
    rec_ref,
    post_ref,
    pos_ref,
    g_ref,
    u_ref,
    gs_ref,
    us_ref,
    probs_ref,
    wg_ref,
    wu_ref,
    wd_ref,
    wgs_ref,
    wus_ref,
    wds_ref,
    *rest,
):
    rest = rest[stored:]
    part_ref, dy_ref, hid_ref, dg_ref, du_ref, de_ref, hids_ref, dgs_ref, dus_ref = rest[:9]
    total, given, pick, put, gates, slots, choice = rest[9:]
    step = pl.program_id(0)
    pair = jnp.maximum(step - ROW_STEPS, 0)

    @pl.when(step < ROW_STEPS)
    def _():
        dy = jnp.where(meta[0] == 1, cot_ref[...], rec_ref[...])
        dy = jnp.where(meta[0] == 0, jnp.zeros_like(dy), dy)
        dy_ref[0] = dy
        here = rows_of(step, ROWS)
        given[here, :] = dy
        hidden, grad_gate, grad_lift, unused = pull(
            dot_nt(dy, wds_ref[...]), None, gs_ref[0], us_ref[0]
        )
        hids_ref[0] = hidden
        dgs_ref[0] = grad_gate
        dus_ref[0] = grad_lift
        total[here, :] = dot_nt(grad_gate, wgs_ref[...]) + dot_nt(grad_lift, wus_ref[...])

    @pl.when(step == 0)
    def _():
        build_pick(0, ALL_CHUNKS, post_ref, None, pick, gates)
        slots[...] = jnp.zeros_like(slots)

    def experts(combine):
        for start in range(0, SEQ_LEN, ROWS):
            rows = pl.ds(start, ROWS)
            if combine:
                total[rows, :] += dot(put[rows, :], slots[...])
            build_put(pair * PAIR, rows, pos_ref, put)
        picked = dot(pick[...], given[...]).astype(BF16)
        build_gates(pair * PAIR, post_ref, probs_ref.at[0], gates)
        build_pick(
            jnp.minimum(pair + 1, PAIR_STEPS - 1) * PAIR, ALL_CHUNKS, post_ref, None, pick, gates
        )
        for which in range(PAIR):
            rows = picked[of_pair(which), :]
            weight = gates[of_pair(which), 0:1]
            hidden, grad_gate, grad_lift, inner = pull(
                dot_nt(rows, wd_ref[which]), weight, g_ref[0, which], u_ref[0, which]
            )
            hid_ref[0, which] = hidden
            dg_ref[0, which] = grad_gate
            du_ref[0, which] = grad_lift
            de_ref[0, which] = (weight * rows.astype(F32)).astype(BF16)
            row = pl.ds(pair * PAIR + which, 1)
            chosen = jnp.zeros((1, SEQ_LEN), F32)
            for chunk in range(CAPACITY // CHUNK):
                slot_at = chunk * CHUNK + lax.broadcasted_iota(jnp.int32, (CHUNK, SEQ_LEN), 0)
                here = slot_at == post_ref[0, row, :]
                chosen += jnp.sum(
                    jnp.where(here, inner[chunk * CHUNK : (chunk + 1) * CHUNK], 0.0),
                    axis=0,
                    keepdims=True,
                )
            choice[row, :] = chosen
            slots[which * SPAN : which * SPAN + CAPACITY, :] = (
                dot_nt(grad_gate, wg_ref[which]) + dot_nt(grad_lift, wu_ref[which])
            ).astype(BF16)

    @pl.when(step == ROW_STEPS)
    def _():
        experts(False)

    @pl.when((step > ROW_STEPS) & (step < ROW_STEPS + PAIR_STEPS))
    def _():
        experts(True)

    @pl.when(step == ROW_STEPS + PAIR_STEPS)
    def _():
        for start in range(0, SEQ_LEN, ROWS):
            rows = pl.ds(start, ROWS)
            part_ref[rows, :] = (total[rows, :] + dot(put[rows, :], slots[...])).astype(BF16)
        half = SEQ_LEN // 2
        blank = jnp.zeros((8, half), F32)
        part_ref[SEQ_LEN:, :] = jnp.concatenate(
            [choice[:, :half], blank, choice[:, half:], blank], axis=0
        ).astype(BF16)


def feed_backward(meta, cotangent, received, post, pos, forward_kept, weights, kept):
    width = cotangent.shape[1]
    wg, wu, wd, wgs, wus, wds = weights
    hidden = wg.shape[2]
    stored = 8
    unused_h, unused_b, unused_x, gate, lift, gate_sh, lift_sh, probs = forward_kept
    saved = [
        shape_of((SLOTS, SEQ_LEN, width), BF16),
        shape_of((SLOTS, EXPERTS, CAPACITY, hidden), BF16),
        shape_of((SLOTS, EXPERTS, CAPACITY, hidden), BF16),
        shape_of((SLOTS, EXPERTS, CAPACITY, hidden), BF16),
        shape_of((SLOTS, EXPERTS, CAPACITY, width), BF16),
        shape_of((SLOTS, SEQ_LEN, hidden), BF16),
        shape_of((SLOTS, SEQ_LEN, hidden), BF16),
        shape_of((SLOTS, SEQ_LEN, hidden), BF16),
    ]
    row_at, pair_at = step_specs()

    def slot_rows(columns, which):
        return pl.BlockSpec((1, ROWS, columns), lambda s, m: (m[which], row_at(s), 0))

    def slot_pair(columns, which):
        return pl.BlockSpec(
            (1, PAIR, CAPACITY, columns), lambda s, m: (m[which], pair_at(s), 0, 0)
        )

    def fixed(shape):
        return once(shape, lambda s, m: (0,) * len(shape))

    def of_pairs(array):
        return pl.BlockSpec((PAIR,) + array.shape[1:], lambda s, m: (pair_at(s), 0, 0))

    grid_spec = pltpu.PrefetchScalarGridSpec(
        num_scalar_prefetch=1,
        grid=(ROW_STEPS + PAIR_STEPS + 1,),
        in_specs=[
            pl.BlockSpec((ROWS, width), lambda s, m: (m[2] * ROW_STEPS + row_at(s), 0)),
            pl.BlockSpec((ROWS, width), lambda s, m: (row_at(s), 0)),
            once((1, EXPERTS, SEQ_LEN), lambda s, m: (m[2], 0, 0)),
            once((1, SEQ_LEN, EXPERTS), lambda s, m: (m[2], 0, 0)),
            slot_pair(hidden, 3),
            slot_pair(hidden, 3),
            slot_rows(hidden, 3),
            slot_rows(hidden, 3),
            once((1, EXPERTS, SEQ_LEN), lambda s, m: (m[3], 0, 0)),
            of_pairs(wg),
            of_pairs(wu),
            of_pairs(wd),
            fixed(wgs.shape),
            fixed(wus.shape),
            fixed(wds.shape),
        ]
        + [pl.BlockSpec(memory_space=pl.ANY)] * stored,
        out_specs=[
            fixed((SEQ_LEN + 32, width)),
            slot_rows(width, 1),
            slot_pair(hidden, 1),
            slot_pair(hidden, 1),
            slot_pair(hidden, 1),
            slot_pair(width, 1),
            slot_rows(hidden, 1),
            slot_rows(hidden, 1),
            slot_rows(hidden, 1),
        ],
        scratch_shapes=[
            pltpu.VMEM((SEQ_LEN, width), F32),
            pltpu.VMEM((SEQ_LEN, width), BF16),
            pltpu.VMEM((PAIR * CAPACITY, SEQ_LEN), BF16),
            pltpu.VMEM((SEQ_LEN, PAIR * SPAN), BF16),
            pltpu.VMEM((PAIR * CAPACITY, LANES), F32),
            pltpu.VMEM((PAIR * SPAN, width), BF16),
            pltpu.VMEM((EXPERTS, SEQ_LEN), F32),
        ],
    )
    outs = pl.pallas_call(
        functools.partial(feed_backward_kernel, stored),
        grid_spec=grid_spec,
        out_shape=[shape_of((SEQ_LEN + 32, width), BF16)] + saved,
        input_output_aliases={16 + k: 1 + k for k in range(stored)},
        compiler_params=pltpu.CompilerParams(vmem_limit_bytes=VMEM_BYTES),
        cost_estimate=cost(60),
        name="feed_backward",
    )(
        meta,
        cotangent,
        received,
        post,
        pos,
        gate,
        lift,
        gate_sh,
        lift_sh,
        probs,
        wg,
        wu,
        wd,
        wgs,
        wus,
        wds,
        *(reserve(saved) if kept is None else kept),
    )
    return outs[0], outs[1:]


def attention_backward_kernel(
    stored,
    meta,
    first_block,
    sum_ref,
    choice_ref,
    probs_ref,
    dy_ref,
    h_ref,
    b_ref,
    gain_ref,
    router_ref,
    wall_ref,
    wo_ref,
    cos_ref,
    sin_ref,
    qkv_ref,
    o_ref,
    lse_ref,
    low_ref,
    *rest,
):
    rest = rest[stored:]
    part_ref, dh_ref, gain_grad_ref, router_grad_ref, dqkv_ref, dattn_ref = rest[:6]
    dk_all, dv_all, dq_all, do_all, inner_all = rest[6:]
    step = pl.program_id(0)
    index = BACK_BLOCKS - 1 - step
    heads = wo_ref.shape[0] // LANES
    wide = heads * LANES

    @pl.when(step == 0)
    def _():
        gain_grad_ref[...] = jnp.zeros_like(gain_grad_ref)
        router_grad_ref[...] = jnp.zeros_like(router_grad_ref)
        dk_all[...] = jnp.zeros_like(dk_all)
        dv_all[...] = jnp.zeros_like(dv_all)

    probs = probs_ref[0]
    chosen = choice_ref[0:8, :].astype(F32)
    logit_grads = probs * (chosen - jnp.sum(probs * chosen, axis=0, keepdims=True))
    logit_grads = logit_grads.astype(BF16)
    router_grad_ref[...] += dot(logit_grads, b_ref[0])
    grad_normed = sum_ref[...].astype(F32) + dot_tn(logit_grads, router_ref[...])
    state = h_ref[0]
    scale = lax.rsqrt(jnp.mean(state * state, axis=-1, keepdims=True) + 1e-06)
    normed = state * scale
    gain_grad_ref[...] += jnp.sum(grad_normed * normed, axis=0, keepdims=True)
    scaled = gain_ref[...] * grad_normed
    inner = jnp.mean(normed * scaled, axis=-1, keepdims=True)
    grad_state = dy_ref[0].astype(F32) + scale * (scaled - normed * inner)
    dh_ref[...] = grad_state
    dattn = grad_state.astype(BF16)
    dattn_ref[0] = dattn
    do = dot_nt(dattn, wo_ref[...]).astype(BF16)
    do_all[...] = do
    products = do.astype(F32) * o_ref[0].astype(F32)
    for head in range(heads):
        columns = slice(head * LANES, (head + 1) * LANES)
        row = jnp.sum(products[:, columns], axis=1, keepdims=True)
        inner_all[head : head + 1, :] = jnp.broadcast_to(row, (BACK_BLOCK, LANES)).T[0:1, :]
    dq_all[...] = jnp.zeros_like(dq_all)
    here = rows_of(index, BACK_BLOCK)
    low = low_ref[0]
    query_at = index * BACK_BLOCK + lax.broadcasted_iota(jnp.int32, (BACK_KEYS, BACK_BLOCK), 1)
    key_at = lax.broadcasted_iota(jnp.int32, (BACK_KEYS, BACK_BLOCK), 0)

    def body(block, none):
        at = key_at + block * BACK_KEYS
        valid = (at >= low) & (at <= query_at)
        there = rows_of(block, BACK_KEYS)
        for head in range(heads):
            columns = slice(head * LANES, (head + 1) * LANES)
            key_columns = slice(wide + head * LANES, wide + (head + 1) * LANES)
            value_columns = slice(2 * wide + head * LANES, 2 * wide + (head + 1) * LANES)
            query = qkv_ref[0, here, columns]
            keys = qkv_ref[0, there, key_columns]
            scores = jnp.where(valid, dot_nt(keys, query), -1e30)
            probs = jnp.exp(scores - lse_ref[0, head : head + 1, :])
            grad_probs = dot_nt(qkv_ref[0, there, value_columns], do_all[:, columns])
            grad_scores = (probs * (grad_probs - inner_all[head : head + 1, :])).astype(BF16)
            dv_all[there, columns] += dot(probs.astype(BF16), do_all[:, columns])
            dk_all[there, columns] += dot(grad_scores, query)
            dq_all[:, columns] += dot_tn(grad_scores, keys)
        return none

    lax.fori_loop(
        first_block[meta[2] * BACK_BLOCKS + index], ((index + 1) * BACK_BLOCK - 1) // BACK_KEYS + 1, body, 0
    )
    cosine, sine = cos_ref[...], sin_ref[...]
    for head in range(heads):
        columns = slice(head * LANES, (head + 1) * LANES)
        key_columns = slice(wide + head * LANES, wide + (head + 1) * LANES)
        value_columns = slice(2 * wide + head * LANES, 2 * wide + (head + 1) * LANES)
        dq = dq_all[:, columns] * 0.0625
        dk = dk_all[here, columns]
        dqkv_ref[0, :, columns] = (dq * cosine - pltpu.roll(dq, HEAD_DIM, 1) * sine).astype(BF16)
        dqkv_ref[0, :, key_columns] = (
            dk * cosine - pltpu.roll(dk, HEAD_DIM, 1) * sine
        ).astype(BF16)
        dqkv_ref[0, :, value_columns] = dv_all[here, columns].astype(BF16)
    part_ref[...] = dot_nt(dqkv_ref[0], wall_ref[...]).astype(BF16)


def attention_backward(
    meta, first_block, summed, forward_kept, attention_kept, dy, gain, router, wall, wo, cosine, sine, low, kept
):
    width = summed.shape[1]
    wide = wo.shape[0]
    stored = 0 if kept is None else 2
    h, b, probs = forward_kept[0], forward_kept[1], forward_kept[7]
    unused_x, unused_a, qkv, o, lse = attention_kept
    saved = [
        shape_of((SLOTS, SEQ_LEN, 3 * wide), BF16),
        shape_of((SLOTS, SEQ_LEN, width), BF16),
    ]

    def at(step):
        return BACK_BLOCKS - 1 - step

    def slot_rows(columns, which):
        return pl.BlockSpec((1, BACK_BLOCK, columns), lambda s, m, f: (m[which], at(s), 0))

    def fixed(shape):
        return once(shape, lambda s, m, f: (0,) * len(shape))

    halves_of = BACK_BLOCKS // 2
    grid_spec = pltpu.PrefetchScalarGridSpec(
        num_scalar_prefetch=2,
        grid=(BACK_BLOCKS,),
        in_specs=[
            pl.BlockSpec((BACK_BLOCK, width), lambda s, m, f: (at(s), 0)),
            pl.BlockSpec(
                (16, BACK_BLOCK), lambda s, m, f: (SEQ_LEN // 16 + at(s) // halves_of, at(s) % halves_of)
            ),
            pl.BlockSpec((1, EXPERTS, BACK_BLOCK), lambda s, m, f: (m[3], 0, at(s))),
            slot_rows(width, 1),
            slot_rows(width, 3),
            slot_rows(width, 3),
            fixed(gain.shape),
            fixed(router.shape),
            fixed(wall.shape),
            fixed(wo.shape),
            pl.BlockSpec((BACK_BLOCK, LANES), lambda s, m, f: (at(s), 0)),
            pl.BlockSpec((BACK_BLOCK, LANES), lambda s, m, f: (at(s), 0)),
            once((1, SEQ_LEN, 3 * wide), lambda s, m, f: (m[3], 0, 0)),
            slot_rows(wide, 3),
            pl.BlockSpec((1, 8, BACK_BLOCK), lambda s, m, f: (m[3], 0, at(s))),
            pl.BlockSpec((1, 1, BACK_BLOCK), lambda s, m, f: (m[2], 0, at(s))),
        ]
        + [pl.BlockSpec(memory_space=pl.ANY)] * stored,
        out_specs=[
            pl.BlockSpec((BACK_BLOCK, width), lambda s, m, f: (at(s), 0)),
            pl.BlockSpec((BACK_BLOCK, width), lambda s, m, f: (at(s), 0)),
            fixed((1, width)),
            fixed((8, width)),
            slot_rows(3 * wide, 1),
            slot_rows(width, 1),
        ],
        scratch_shapes=[
            pltpu.VMEM((SEQ_LEN, wide), F32),
            pltpu.VMEM((SEQ_LEN, wide), F32),
            pltpu.VMEM((BACK_BLOCK, wide), F32),
            pltpu.VMEM((BACK_BLOCK, wide), BF16),
            pltpu.VMEM((8, BACK_BLOCK), F32),
        ],
    )
    outs = pl.pallas_call(
        functools.partial(attention_backward_kernel, stored),
        grid_spec=grid_spec,
        out_shape=[
            shape_of((SEQ_LEN, width), BF16),
            shape_of((SEQ_LEN, width), F32),
            shape_of((1, width), F32),
            shape_of((8, width), F32),
        ]
        + saved,
        input_output_aliases={18 + k: 4 + k for k in range(stored)},
        compiler_params=pltpu.CompilerParams(vmem_limit_bytes=VMEM_BYTES),
        cost_estimate=cost(37),
        name="attention_backward",
    )(
        meta,
        first_block,
        summed,
        summed,
        probs,
        dy,
        h,
        b,
        gain,
        router,
        wall,
        wo,
        cosine,
        sine,
        qkv,
        o,
        lse,
        low,
        *(kept or ()),
    )
    return outs[:4], outs[4:]


def expert_grads_kernel(*refs):
    ins, out_ref = refs[:-1], refs[-1]
    (xa, xb), (ga, gb), (ua, ub), (ea, eb), (ha, hb) = (ins[2 * k : 2 * k + 2] for k in range(5))
    devices, unused, rows, unused = out_ref.shape
    pairs = [((xa, xb), (ga, gb)), ((xa, xb), (ua, ub)), ((ea, eb), (ha, hb))]
    for number, (left, right) in enumerate(pairs):
        for device in range(devices):
            columns = slice(device * rows, (device + 1) * rows)
            out_ref[device, number] = (
                dot_tn(left[0][0, 0, :, columns], right[0][0, 0])
                + dot_tn(left[1][0, 0, :, columns], right[1][0, 0])
            ).astype(BF16)


def expert_grads(first, count, extra, devices, picked, hid, grad_gate, grad_lift, grad_expert):
    width, hidden = picked.shape[3], hid.shape[3]
    rows = width // devices

    def pair(columns):
        return [
            pl.BlockSpec(
                (1, 1, CAPACITY, columns),
                functools.partial(lambda slot, e: (slot, first + e, 0, 0), slot),
            )
            for slot in (1, 2)
        ]

    return pl.pallas_call(
        expert_grads_kernel,
        grid=(count,),
        in_specs=pair(width) + pair(hidden) + pair(hidden) + pair(width) + pair(hidden),
        out_specs=pl.BlockSpec((devices, 3, rows, hidden), lambda e: (0, e, 0, 0)),
        out_shape=shape_of((devices, 3 * count + extra, rows, hidden), BF16),
        compiler_params=pltpu.CompilerParams(vmem_limit_bytes=VMEM_BYTES),
        cost_estimate=cost(6 * count),
        name="expert_grads",
    )(
        *(picked, picked, grad_gate, grad_gate, grad_lift, grad_lift),
        *(grad_expert, grad_expert, hid, hid),
    )


def lead_grads_kernel(
    meta,
    cot_ref,
    rec_ref,
    post_ref,
    probs_ref,
    g_ref,
    u_ref,
    wd_ref,
    xa_ref,
    xb_ref,
    ga_ref,
    ua_ref,
    ea_ref,
    ha_ref,
    out_ref,
    given,
    pick,
    gates,
    rows_in,
    grad_gate,
    grad_lift,
    grad_rows,
    hidden,
):
    step = pl.program_id(0)

    @pl.when(step == 0)
    def _():
        given[...] = jnp.where(meta[0] == 1, cot_ref[...], rec_ref[...])

    @pl.when(step > 0)
    def _():
        chunks = [(0, chunk) for chunk in range(CAPACITY // CHUNK)]
        build_pick(step - 1, chunks, post_ref, probs_ref.at[0], pick, gates)
        rows_in[...] = dot(pick[...], given[...]).astype(BF16)
        weight = gates[:, 0:1]
        grad_rows[...] = (weight * rows_in[...].astype(F32)).astype(BF16)
        hidden[...], grad_gate[...], grad_lift[...], unused = pull(
            dot_nt(rows_in[...], wd_ref[0]), weight, g_ref[0, 0], u_ref[0, 0]
        )
        devices, unused, rows, unused = out_ref.shape
        pairs = [
            (xa_ref.at[0, 0], ga_ref.at[0, 0], xb_ref.at[0, 0], grad_gate),
            (xa_ref.at[0, 0], ua_ref.at[0, 0], xb_ref.at[0, 0], grad_lift),
            (ea_ref.at[0, 0], ha_ref.at[0, 0], grad_rows, hidden),
        ]
        for number, (left, right, left_last, right_last) in enumerate(pairs):
            for device in range(devices):
                columns = slice(device * rows, (device + 1) * rows)
                out_ref[device, number] = (
                    dot_tn(left[:, columns], right[...])
                    + dot_tn(left_last[:, columns], right_last[...])
                ).astype(BF16)


def lead_grads(count, devices, meta, cotangent, received, post, forward_kept, kept, down):
    unused_h, unused_b, picked, gate, lift, unused_gate, unused_lift, probs = forward_kept
    unused_dy, hid, grad_gate, grad_lift, grad_expert = kept[:5]
    width, inner = picked.shape[3], gate.shape[3]
    rows = width // devices

    def at(step):
        return jnp.maximum(step - 1, 0)

    def of_slot(columns, which):
        return pl.BlockSpec((1, 1, CAPACITY, columns), lambda s, m: (m[which], at(s), 0, 0))

    grid_spec = pltpu.PrefetchScalarGridSpec(
        num_scalar_prefetch=1,
        grid=(count + 1,),
        in_specs=[
            once((SEQ_LEN, width), lambda s, m: (m[1], 0)),
            once((SEQ_LEN, width), lambda s, m: (0, 0)),
            once((1, EXPERTS, SEQ_LEN), lambda s, m: (m[1], 0, 0)),
            once((1, EXPERTS, SEQ_LEN), lambda s, m: (m[2], 0, 0)),
            of_slot(inner, 2),
            of_slot(inner, 2),
            pl.BlockSpec((1,) + down.shape[1:], lambda s, m: (at(s), 0, 0)),
            of_slot(width, 3),
            of_slot(width, 2),
            of_slot(inner, 3),
            of_slot(inner, 3),
            of_slot(width, 3),
            of_slot(inner, 3),
        ],
        out_specs=pl.BlockSpec((devices, 3, rows, inner), lambda s, m: (0, at(s), 0, 0)),
        scratch_shapes=[
            pltpu.VMEM((SEQ_LEN, width), BF16),
            pltpu.VMEM((CAPACITY, SEQ_LEN), BF16),
            pltpu.VMEM((CAPACITY, LANES), F32),
            pltpu.VMEM((CAPACITY, width), BF16),
            pltpu.VMEM((CAPACITY, inner), BF16),
            pltpu.VMEM((CAPACITY, inner), BF16),
            pltpu.VMEM((CAPACITY, width), BF16),
            pltpu.VMEM((CAPACITY, inner), BF16),
        ],
    )
    return pl.pallas_call(
        lead_grads_kernel,
        grid_spec=grid_spec,
        out_shape=shape_of((devices, 3 * count, rows, inner), BF16),
        compiler_params=pltpu.CompilerParams(vmem_limit_bytes=VMEM_BYTES),
        cost_estimate=cost(20),
        name="lead_grads",
    )(
        meta,
        cotangent,
        received,
        post,
        probs,
        gate,
        lift,
        down,
        picked,
        picked,
        grad_gate,
        grad_lift,
        grad_expert,
        hid,
    )


def shared_grads_kernel(b_ref, dy_ref, gate_ref, lift_ref, hid_ref, before_ref, out_ref, *totals):
    step = pl.program_id(0)
    pairs = [(b_ref, gate_ref), (b_ref, lift_ref), (dy_ref, hid_ref)]

    @pl.when(step == 0)
    def _():
        for total in totals:
            total[...] = jnp.zeros_like(total)

    for (left, right), total in zip(pairs, totals):
        total[...] += dot_tn(left[0], right[0])

    @pl.when(step == pl.num_programs(0) - 1)
    def _():
        devices, unused, rows, unused = out_ref.shape
        for number, total in enumerate(totals):
            for device in range(devices):
                out_ref[device, number] = total[device * rows : (device + 1) * rows, :].astype(
                    BF16
                )


def shared_grads(before, b, dy, grad_gate, grad_lift, hid):
    devices, matrices, width, hidden = before.shape
    rows = ROWS
    steps = SEQ_LEN // rows

    def spec(array):
        return pl.BlockSpec((1, rows, array.shape[2]), lambda s: (1 + s // steps, s % steps, 0))

    return pl.pallas_call(
        shared_grads_kernel,
        grid=(2 * steps,),
        in_specs=[spec(array) for array in (b, dy, grad_gate, grad_lift, hid)]
        + [pl.BlockSpec(memory_space=pl.ANY)],
        out_specs=once((devices, 3, width, hidden), lambda s: (0, matrices // 3 - 1, 0, 0)),
        out_shape=shape_of(before.shape, BF16),
        scratch_shapes=[pltpu.VMEM((devices * width, hidden), F32)] * 3,
        input_output_aliases={5: 0},
        compiler_params=pltpu.CompilerParams(vmem_limit_bytes=VMEM_BYTES),
        cost_estimate=cost(13),
        name="shared_grads",
    )(b, dy, grad_gate, grad_lift, hid, before)


def token_grads_kernel(count, *refs):
    lefts, rights = refs[:count], refs[count : 2 * count]
    outs, totals = refs[2 * count : 3 * count], refs[3 * count :]
    step = pl.program_id(0)

    @pl.when(step == 0)
    def _():
        for total in totals:
            total[...] = jnp.zeros_like(total)

    for left, right, total in zip(lefts, rights, totals):
        total[...] += dot_tn(left[0], right[0])

    @pl.when(step == pl.num_programs(0) - 1)
    def _():
        for out, total in zip(outs, totals):
            out[...] = total[...].astype(BF16)


def token_grads(lefts, rights):
    count = len(lefts)
    rows = ROWS
    steps = SEQ_LEN // rows

    def spec(array):
        return pl.BlockSpec((1, rows, array.shape[2]), lambda s: (1 + s // steps, s % steps, 0))

    shapes = [(left.shape[2], right.shape[2]) for left, right in zip(lefts, rights)]
    return pl.pallas_call(
        functools.partial(token_grads_kernel, count),
        grid=(2 * steps,),
        in_specs=[spec(a) for a in lefts] + [spec(a) for a in rights],
        out_specs=[once(shape, lambda s: (0, 0)) for shape in shapes],
        out_shape=[shape_of(shape, BF16) for shape in shapes],
        scratch_shapes=[pltpu.VMEM(shape, F32) for shape in shapes],
        compiler_params=pltpu.CompilerParams(vmem_limit_bytes=VMEM_BYTES),
        cost_estimate=cost(14),
        name="token_grads",
    )(*lefts, *rights)


def rotary_tables():
    half = HEAD_DIM // 2
    rates = np.exp(-np.log(10000.0) * np.arange(half) * 2.0 / HEAD_DIM)
    angles = np.arange(SEQ_LEN)[:, None] * rates[None, :]
    cosine, sine = np.cos(angles), np.sin(angles)
    cosine = np.concatenate([cosine] * 4, axis=1)
    sine = np.concatenate([sine, sine, -sine, -sine], axis=1)
    return jnp.asarray(cosine, F32), jnp.asarray(sine, F32)


def paired(weight):
    rows = weight.shape[0]
    heads = weight.shape[1] // HEAD_DIM
    half = HEAD_DIM // 2
    split = weight.reshape(rows, heads, HEAD_DIM)
    swapped = jnp.concatenate([-split[:, :, half:], split[:, :, :half]], axis=2)
    return jnp.concatenate([split, swapped], axis=2).reshape(rows, heads * LANES)


def padded(weight):
    rows = weight.shape[0]
    heads = weight.shape[1] // HEAD_DIM
    split = weight.reshape(rows, heads, HEAD_DIM)
    return jnp.concatenate([split, jnp.zeros_like(split)], axis=2).reshape(rows, heads * LANES)


def unpadded(grads):
    rows = grads.shape[0]
    return grads.reshape(rows, -1, LANES)[:, :, :HEAD_DIM].reshape(rows, -1)


def places(routes):
    experts = jnp.arange(EXPERTS, dtype=jnp.int32)
    named = jnp.any(routes[:, :, :, None] == experts, axis=2)
    before = (
        jnp.arange(SEQ_LEN, dtype=jnp.int32)[:, None] > jnp.arange(SEQ_LEN, dtype=jnp.int32)
    ).astype(BF16)
    rank = jnp.einsum("ts,nse->nte", before, named.astype(BF16), preferred_element_type=F32)
    by_token = jnp.where(named, rank.astype(jnp.int32), -1)
    return by_token, jnp.swapaxes(by_token, 1, 2)


def first_allowed(lengths):
    ends = jnp.cumsum(lengths, axis=1)
    at = jnp.arange(SEQ_LEN, dtype=jnp.int32)
    starts = jnp.max(jnp.where(ends[:, None, :] <= at[None, :, None], ends[:, None, :], 0), axis=2)
    return jnp.maximum(starts, at[None, :] - (WINDOW - 1)).astype(jnp.int32)


def on_device(
    tokens,
    doc_lengths,
    routes,
    gain_attn,
    w_query,
    w_key,
    w_value,
    w_output,
    gain_ffn,
    w_router,
    w_gate_exp,
    w_up_exp,
    w_down_exp,
    w_gate_sh,
    w_up_sh,
    w_down_sh,
    cotangent,
):
    section = lax.axis_index("section")
    devices = lax.axis_size("dp")
    count = doc_lengths.shape[0]
    width = tokens.shape[1]
    cosine, sine = rotary_tables()
    wall = jnp.concatenate([paired(w_query[0]), paired(w_key[0]), padded(w_value[0])], axis=1)
    wo = padded(w_output[0].T).T
    out_weight = lax.all_gather(w_output[0], "tensor", axis=0, tiled=True)
    router = w_router[0].T
    gain_a, gain_f = gain_attn.astype(F32), gain_ffn.astype(F32)
    feed_weights = (
        w_gate_exp[0],
        w_up_exp[0],
        w_down_exp[0],
        w_gate_sh[0],
        w_up_sh[0],
        w_down_sh[0],
    )
    pos, post = places(routes[0].reshape(count, SEQ_LEN, 2))
    low = first_allowed(doc_lengths)
    first_block = (low[:, ::BLOCK] // KEYS).reshape(-1)
    back_first = (low[:, ::BACK_BLOCK] // BACK_KEYS).reshape(-1)
    low_column, low_row = low[:, :, None], low[:, None, :]

    received = jnp.zeros((SEQ_LEN, width), BF16)
    attention_kept, feed_kept, results = None, None, []
    grads_kept, attention_grads_kept, inputs = None, None, []
    small = jnp.zeros((10, width), F32)

    def spread(array):
        return lax.psum_scatter(array, "dp", scatter_dimension=0, tiled=False)

    def after(meta, array):
        return lax.optimization_barrier((meta, array))

    def forward_meta(tick):
        raw = tick - section
        active = (raw >= 0) & (raw < count)
        sequence = jnp.clip(raw, 0, count - 1)
        return jnp.stack([section, jnp.where(active, sequence + 1, 0), sequence]).astype(jnp.int32)

    def backward_meta(tick):
        raw = tick - 1 + section
        active = (raw >= 0) & (raw < count)
        sequence = jnp.clip(raw, 0, count - 1)
        source = jnp.where(active, 2 - section, 0)
        return jnp.stack(
            [source, jnp.where(active, sequence + 1, 0), sequence, sequence + 1]
        ).astype(jnp.int32)

    def attend(meta, received, kept):
        return attention_forward(
            meta, first_block, tokens, received, gain_a, wall, cosine, sine, low_column, kept
        )

    def feed(meta, gathered, kept):
        return feed_forward(
            meta,
            attention_kept[0],
            gathered,
            out_weight,
            gain_f,
            router,
            post,
            pos,
            feed_weights,
            kept,
        )

    def feed_back(meta, received):
        return feed_backward(
            meta, cotangent, received, post, pos, feed_kept, feed_weights, grads_kept
        )

    def attend_back(meta, summed):
        return attention_backward(
            meta,
            back_first,
            summed,
            feed_kept,
            attention_kept,
            grads_kept[0],
            gain_f,
            router,
            wall,
            wo,
            cosine,
            sine,
            low_row,
            attention_grads_kept,
        )

    for tick in range(count):
        meta = forward_meta(tick)
        own, attention_kept = attend(meta, received, attention_kept)
        gathered = lax.all_gather(own, "tensor") if tick == 0 else tensor_gather(own, 0)
        part, feed_kept = feed(meta, gathered, feed_kept)
        result, received = output_relay(part, feed_kept[0], tick, 4 + tick)
        results.append(result)

    blank = jnp.zeros((SEQ_LEN, width), BF16)
    meta, back_meta = forward_meta(count), backward_meta(0)
    own, attention_kept = attend(meta, received, attention_kept)
    back_meta, own = after(back_meta, own)
    gathered = lax.all_gather(own, "tensor")
    part, grads_kept = feed_back(back_meta, blank)
    meta, part = after(meta, part)
    summed = lax.psum(part, "tensor")
    last_part, feed_kept = feed(meta, gathered, feed_kept)
    back_meta, last_part = after(back_meta, last_part)

    for tick in range(count + 1):
        if tick > 0:
            back_meta = backward_meta(tick)
        if tick == count:
            lead, middle = 2, 3
            lead_meta = jnp.stack(
                [2 - section, jnp.full_like(section, count - 1), jnp.full_like(section, count)]
                + [jnp.full_like(section, count - 1)]
            ).astype(jnp.int32)
            lead_part = lead_grads(
                lead,
                devices,
                lead_meta,
                cotangent,
                received,
                post,
                feed_kept,
                grads_kept,
                feed_weights[2],
            )
            back_meta, lead_part = after(back_meta, lead_part)
        if tick > 0:
            part, grads_kept = feed_back(back_meta, received)
        if tick == count:
            dy, hid, grad_gate, grad_lift, grad_expert, hid_sh, grad_gate_sh, grad_lift_sh = (
                grads_kept
            )
            picked = feed_kept[2]
            middle_part = expert_grads(
                lead, middle, 0, devices, picked, hid, grad_gate, grad_lift, grad_expert
            )
            middle_part, picked, grad_gate = lax.optimization_barrier(
                (middle_part, picked, grad_gate)
            )
            first = lead + middle
            last_grads = expert_grads(
                first,
                EXPERTS - first,
                3,
                devices,
                picked,
                hid,
                grad_gate,
                grad_lift,
                grad_expert,
            )
            last_grads = shared_grads(
                last_grads, feed_kept[1], dy, grad_gate_sh, grad_lift_sh, hid_sh
            )
            part, last_grads = lax.optimization_barrier((part, last_grads))
            parts = [spread(lead_part), spread(middle_part), spread(last_grads)]
        if tick > 0:
            summed = tensor_sum(part, 2, 7)
        (part, grad_state, gain_grad, router_grad), attention_grads_kept = attend_back(
            back_meta, summed
        )
        grad_input, received, gain_attn_grad = input_relay(
            part, attention_kept[0], grad_state, gain_a, tick, 4 + count + 1 + tick
        )
        inputs.append(grad_input)
        small = small + jnp.concatenate([gain_attn_grad, gain_grad, router_grad], axis=0)
    result, unused = output_relay(last_part, feed_kept[0], count, 4 + count)
    results.append(result)

    projections, outward = token_grads(
        [attention_kept[1], attention_grads_kept[1]], [attention_grads_kept[0], attention_kept[3]]
    )
    wide = wo.shape[0]
    rows = width // devices
    columns = w_query.shape[2]
    packed = jnp.concatenate(
        [
            2.0 * unpadded(projections[:, : 2 * wide]),
            unpadded(projections[:, 2 * wide :]),
            unpadded(outward),
            jnp.pad(small, ((0, 6), (0, 0))).T.astype(BF16),
        ],
        axis=1,
    )
    packed, *parts = lax.optimization_barrier((packed, *parts))
    packed = spread(packed.reshape(devices, rows, -1)).astype(F32)
    shared = parts[2][-3:].astype(F32)
    experts = jnp.concatenate([parts[0], parts[1], parts[2][:-3]], axis=0).astype(F32)
    experts = experts.reshape(EXPERTS, 3, rows, -1)

    def choose(items):
        return jnp.concatenate(
            [jnp.where(section == 0, items[k], items[k + 1]) for k in range(count)], axis=0
        )

    layer_out = choose(results)
    input_grad = jnp.concatenate(
        [jnp.where(section == 0, inputs[k + 1], inputs[k]) for k in range(count)], axis=0
    )
    extra = 4 * columns
    return (
        layer_out[None],
        input_grad[None],
        packed[None, :, extra],
        packed[None, :, :columns],
        packed[None, :, columns : 2 * columns],
        packed[None, :, 2 * columns : 3 * columns],
        packed[:, 3 * columns : extra].T[None],
        packed[None, :, extra + 1],
        packed[None, :, extra + 2 : extra + 10],
        experts[None, :, 0],
        experts[None, :, 1],
        jnp.swapaxes(experts[:, 2], 1, 2)[None],
        shared[None, 0],
        shared[None, 1],
        shared[2].T[None],
    )


def solution(mesh):
    return jax.shard_map(
        on_device,
        mesh=mesh,
        in_specs=(
            P("dp", None),
            P("dp", None),
            P("section", "dp", None),
            P("section", None),
            P("section", None, "tensor"),
            P("section", None, "tensor"),
            P("section", None, "tensor"),
            P("section", "tensor", None),
            P("section", None),
            P("section", None, None),
            P("section", None, None, "tensor"),
            P("section", None, None, "tensor"),
            P("section", None, "tensor", None),
            P("section", None, "tensor"),
            P("section", None, "tensor"),
            P("section", "tensor", None),
            P("dp", None),
        ),
        out_specs=(
            P("section", "dp", None),
            P("section", "dp", None),
            P("section", "dp"),
            P("section", "dp", "tensor"),
            P("section", "dp", "tensor"),
            P("section", "dp", "tensor"),
            P("section", "tensor", "dp"),
            P("section", "dp"),
            P("section", "dp", None),
            P("section", None, "dp", "tensor"),
            P("section", None, "dp", "tensor"),
            P("section", None, "tensor", "dp"),
            P("section", "dp", "tensor"),
            P("section", "dp", "tensor"),
            P("section", "tensor", "dp"),
        ),
        check_vma=False,
    )
```

```python
import functools

import jax
import jax.numpy as jnp
import numpy as np
from jax import lax
from jax.experimental import pallas as pl
from jax.experimental.pallas import tpu as pltpu
from jax.sharding import PartitionSpec as P

HEAD_DIM = 64
EXPERTS = 8
SEQ_LEN = 1536
WINDOW = 1024
CAPACITY = 480
BLOCK = 512
PACK = 256
BLOCKS = SEQ_LEN // BLOCK
KEYS = 256
BACK_BLOCK = 384
BACK_BLOCKS = SEQ_LEN // BACK_BLOCK
BACK_KEYS = 384
LANES = 128
SLOTS = 3
VMEM_BYTES = 60 * 2**20
MESH = pl.DeviceIdType.MESH
F32 = jnp.float32
BF16 = jnp.bfloat16
NT = (((1,), (1,)), ((), ()))
TN = (((0,), (0,)), ((), ()))


def shape_of(shape, dtype):
    return jax.ShapeDtypeStruct(shape, dtype)


def cost(micros):
    return pl.CostEstimate(
        flops=int(micros * 1.15e9), bytes_accessed=int(micros * 3.6e6), transcendentals=0
    )


def dot(left, right):
    return jnp.dot(left, right, preferred_element_type=F32)


def dot_nt(left, right):
    return lax.dot_general(left, right, NT, preferred_element_type=F32)


def dot_tn(left, right):
    return lax.dot_general(left, right, TN, preferred_element_type=F32)


def once(shape, index):
    return pl.BlockSpec(shape, index, pipeline_mode=pl.Buffered(1))


def loop(count, body):
    lax.fori_loop(0, count, lambda step, none: (body(step), none)[1], 0)


def rows_of(step, size):
    return pl.ds(pl.multiple_of(step * size, size), size)


def greet(partners):
    barrier = pltpu.get_barrier_semaphore()
    for partner in partners:
        pl.semaphore_signal(barrier, inc=1, device_id=partner, device_id_type=MESH)
    pl.semaphore_wait(barrier, len(partners))


def remote(source, target, send, recv, device):
    return pltpu.make_async_remote_copy(
        src_ref=source,
        dst_ref=target,
        send_sem=send,
        recv_sem=recv,
        device_id=device,
        device_id_type=MESH,
    )


def partners_of():
    place = lax.axis_index("tensor")
    core = lax.rem(place, 2)
    return {"tensor": place + 1 - 2 * core}, {"tensor": lax.rem(place + 2, 4)}


def sides(rows):
    core = lax.rem(lax.axis_index("tensor"), 2)
    half = rows // 2
    return core * half, (1 - core) * half


def piece_rows(side, step, size):
    return pl.ds(pl.multiple_of(side + step * size, 16), size)


def cross_kernel(pieces, part_ref, mine, first, kept, second, sends, recvs, loaded, use):
    near, far = partners_of()
    own, other = sides(part_ref.shape[0])
    size = mine.shape[0] // pieces
    copies = []
    for step in range(pieces):
        local = pl.ds(step * size, size)
        copies.append(
            remote(
                part_ref.at[piece_rows(other, step, size)],
                first.at[local],
                sends.at[0, step],
                recvs.at[0, step],
                near,
            )
        )
        copies[-1].start()
    load = pltpu.make_async_copy(
        part_ref.at[pl.ds(pl.multiple_of(own, 16), mine.shape[0])], mine, loaded
    )
    load.start()
    load.wait()
    for step in range(pieces):
        local = pl.ds(step * size, size)
        copies[step].wait_recv()
        kept[local, :] = (mine[local, :].astype(F32) + first[local, :].astype(F32)).astype(BF16)
        copies.append(
            remote(
                kept.at[local], second.at[local], sends.at[1, step], recvs.at[1, step], far
            )
        )
        copies[-1].start()
    for step in range(pieces):
        local = pl.ds(step * size, size)
        copies[pieces + step].wait_recv()
        use(step, local, kept[local, :].astype(F32) + second[local, :].astype(F32))
    return copies


def sum_kernel(
    pieces, part_ref, out_ref, mine, first, kept, second, done, sends, recvs, loaded, stored
):
    near, far = partners_of()
    greet([near, far])
    own, other = sides(part_ref.shape[0])
    size = mine.shape[0] // pieces
    back, local_copies = [], []

    def use(step, local, total):
        done[local, :] = total.astype(BF16)
        rows = piece_rows(own, step, size)
        back.append(
            remote(done.at[local], out_ref.at[rows], sends.at[2, step], recvs.at[2, step], near)
        )
        back[-1].start()
        local_copies.append(
            pltpu.make_async_copy(done.at[local], out_ref.at[rows], stored.at[step])
        )
        local_copies[-1].start()

    copies = cross_kernel(
        pieces, part_ref, mine, first, kept, second, sends, recvs, loaded, use
    )
    for copy in back:
        copy.wait_recv()
    for copy in copies + back:
        copy.wait_send()
    for copy in local_copies:
        copy.wait()


def tensor_sum(part, identity, pieces):
    rows, width = part.shape
    hbm = pl.BlockSpec(memory_space=pl.ANY)
    return pl.pallas_call(
        functools.partial(sum_kernel, pieces),
        out_shape=shape_of((rows, width), BF16),
        in_specs=[hbm],
        out_specs=hbm,
        scratch_shapes=[pltpu.VMEM((rows // 2, width), BF16)] * 5
        + [pltpu.SemaphoreType.DMA((3, pieces))] * 2
        + [pltpu.SemaphoreType.DMA, pltpu.SemaphoreType.DMA((pieces,))],
        compiler_params=pltpu.CompilerParams(
            collective_id=identity, has_side_effects=True, vmem_limit_bytes=VMEM_BYTES
        ),
        cost_estimate=cost(32),
        name="tensor_sum",
    )(part)


def gather_kernel(pieces, own_ref, out_ref, sends, recvs, stored):
    place = lax.axis_index("tensor")
    near, far = partners_of()
    greet([near, far])
    far_place = lax.rem(place + 2, 4)
    size = own_ref.shape[0] // pieces
    first, crossing, passed = [], [], []
    for group, copies, partner in ((0, crossing, far), (1, first, near)):
        for piece in range(pieces):
            rows = pl.ds(piece * size, size)
            copies.append(
                remote(
                    own_ref.at[rows],
                    out_ref.at[place, rows],
                    sends.at[group, piece],
                    recvs.at[group, piece],
                    partner,
                )
            )
            copies[-1].start()
    local = pltpu.make_async_copy(own_ref, out_ref.at[place], stored)
    local.start()
    for piece in range(pieces):
        rows = pl.ds(piece * size, size)
        crossing[piece].wait_recv()
        passed.append(
            remote(
                out_ref.at[far_place, rows],
                out_ref.at[far_place, rows],
                sends.at[2, piece],
                recvs.at[2, piece],
                near,
            )
        )
        passed[-1].start()
    for copy in first + passed:
        copy.wait_recv()
    for copy in first + crossing + passed:
        copy.wait_send()
    local.wait()


def tensor_gather(own, identity, pieces=6):
    hbm = pl.BlockSpec(memory_space=pl.ANY)
    return pl.pallas_call(
        functools.partial(gather_kernel, pieces),
        out_shape=shape_of((4,) + own.shape, BF16),
        in_specs=[hbm],
        out_specs=hbm,
        scratch_shapes=[pltpu.SemaphoreType.DMA((3, pieces))] * 2 + [pltpu.SemaphoreType.DMA],
        compiler_params=pltpu.CompilerParams(
            collective_id=identity, has_side_effects=True, vmem_limit_bytes=VMEM_BYTES
        ),
        cost_estimate=cost(18),
        name="tensor_gather",
    )(own)


def pass_on(step, source, rows, next_ref, sends, recvs, across):
    copy = remote(source, next_ref.at[rows], sends.at[3, step], recvs.at[3, step], across)
    copy.start()
    return copy


LAG = 3


def spread_on(step, passed, rows, next_ref, sends, recvs, near):
    passed[step].wait_recv()
    copy = remote(next_ref.at[rows], next_ref.at[rows], sends.at[4, step], recvs.at[4, step], near)
    copy.start()
    return copy


def output_kernel(
    pieces,
    tick,
    part_ref,
    states_ref,
    out_ref,
    next_ref,
    mine,
    first,
    kept,
    second,
    done,
    state,
    sends,
    recvs,
    loaded,
    state_loaded,
    stored,
):
    near, far = partners_of()
    section = lax.axis_index("section")
    across = {"section": 1 - section}
    slot = lax.rem(tick + 1 - section, states_ref.shape[0])
    own, other = sides(part_ref.shape[0])
    size = mine.shape[0] // pieces
    load = pltpu.make_async_copy(
        states_ref.at[slot, pl.ds(pl.multiple_of(own, 16), mine.shape[0])], state, state_loaded
    )
    load.start()
    greet([near, far, across])
    back, passed, spread, local_copies = [], [], [], []

    def forward(step):
        rows = piece_rows(own, step, size)
        spread.append(spread_on(step, passed, rows, next_ref, sends, recvs, near))

    def use(step, local, total):
        if step == 0:
            load.wait()
        done[local, :] = (state[local, :] + total.astype(BF16).astype(F32)).astype(BF16)
        rows = piece_rows(own, step, size)
        passed.append(pass_on(step, done.at[local], rows, next_ref, sends, recvs, across))
        back.append(
            remote(done.at[local], out_ref.at[rows], sends.at[2, step], recvs.at[2, step], near)
        )
        back[-1].start()
        local_copies.append(
            pltpu.make_async_copy(done.at[local], out_ref.at[rows], stored.at[step])
        )
        local_copies[-1].start()
        if step >= LAG:
            forward(step - LAG)

    copies = cross_kernel(
        pieces, part_ref, mine, first, kept, second, sends, recvs, loaded, use
    )
    for step in range(pieces - LAG, pieces):
        forward(step)
    for copy in back + spread:
        copy.wait_recv()
    for copy in copies + back + passed + spread:
        copy.wait_send()
    for copy in local_copies:
        copy.wait()


def output_relay(part, states, tick, identity, pieces=16):
    rows, width = part.shape
    hbm = pl.BlockSpec(memory_space=pl.ANY)
    return pl.pallas_call(
        functools.partial(output_kernel, pieces, tick),
        out_shape=[shape_of((rows, width), BF16)] * 2,
        in_specs=[hbm] * 2,
        out_specs=[hbm] * 2,
        scratch_shapes=[pltpu.VMEM((rows // 2, width), BF16)] * 5
        + [pltpu.VMEM((rows // 2, width), F32)]
        + [pltpu.SemaphoreType.DMA((5, pieces))] * 2
        + [pltpu.SemaphoreType.DMA] * 2
        + [pltpu.SemaphoreType.DMA((pieces,))],
        compiler_params=pltpu.CompilerParams(
            collective_id=identity, has_side_effects=True, vmem_limit_bytes=VMEM_BYTES
        ),
        cost_estimate=cost(38),
        name="output_relay",
    )(part, states)


def input_kernel(
    pieces,
    tick,
    part_ref,
    layers_ref,
    grad_state_ref,
    gain_ref,
    grad_ref,
    next_ref,
    grad_gain_ref,
    mine,
    first,
    kept,
    second,
    given,
    full,
    layer_in,
    grad_state,
    grad,
    gains,
    sends,
    recvs,
    loaded,
    inputs_loaded,
    stored,
):
    near, far = partners_of()
    section = lax.axis_index("section")
    across = {"section": 1 - section}
    slot = lax.rem(tick + section, layers_ref.shape[0])
    rows = part_ref.shape[0]
    own, other = sides(rows)
    half = rows // 2
    size = half // pieces
    loads = []
    for side, start in ((0, own), (1, other)):
        there = pl.ds(pl.multiple_of(start, 16), half)
        loads.append(
            [
                pltpu.make_async_copy(
                    layers_ref.at[slot, there], layer_in.at[there], inputs_loaded.at[side, 0]
                ),
                pltpu.make_async_copy(
                    grad_state_ref.at[there], grad_state.at[there], inputs_loaded.at[side, 1]
                ),
            ]
        )
        for load in loads[-1]:
            load.start()
    greet([near, far, across])
    gains[...] = jnp.zeros_like(gains)
    back, passed, spread, local_copies = [], [], [], []

    def rows_back(here, side, step):
        grad_normed = full[here, :].astype(F32)
        values = layer_in[here, :].astype(F32)
        scale = lax.rsqrt(jnp.mean(values * values, axis=-1, keepdims=True) + 1e-06)
        normed = values * scale
        scaled = gain_ref[...] * grad_normed
        inner = jnp.mean(normed * scaled, axis=-1, keepdims=True)
        result = grad_state[here, :] + scale * (scaled - normed * inner)
        grad[here, :] = result
        gains[side : side + 1, :] += jnp.sum(grad_normed * normed, axis=0, keepdims=True)
        local_copies.append(
            pltpu.make_async_copy(grad.at[here], grad_ref.at[here], stored.at[side, step])
        )
        local_copies[-1].start()
        return result

    def partner_rows(step):
        if step == 0:
            for load in loads[1]:
                load.wait()
        back[step].wait_recv()
        rows_back(piece_rows(other, step, size), 1, step)

    def forward(step):
        here = piece_rows(own, step, size)
        spread.append(spread_on(step, passed, here, next_ref, sends, recvs, near))

    def use(step, local, total):
        if step == 0:
            for load in loads[0]:
                load.wait()
        here = piece_rows(own, step, size)
        full[here, :] = total.astype(BF16)
        back.append(
            remote(full.at[here], full.at[here], sends.at[2, step], recvs.at[2, step], near)
        )
        back[-1].start()
        given[local, :] = rows_back(here, 0, step).astype(BF16)
        passed.append(pass_on(step, given.at[local], here, next_ref, sends, recvs, across))
        if step > 0:
            partner_rows(step - 1)
        if step >= LAG:
            forward(step - LAG)

    copies = cross_kernel(
        pieces, part_ref, mine, first, kept, second, sends, recvs, loaded, use
    )
    partner_rows(pieces - 1)
    for step in range(pieces - LAG, pieces):
        forward(step)
    grad_gain_ref[...] = gains[0:1, :] + gains[1:2, :]
    for copy in spread:
        copy.wait_recv()
    for copy in copies + back + passed + spread:
        copy.wait_send()
    for copy in local_copies:
        copy.wait()


def input_relay(part, layers, grad_state, gain, tick, identity, pieces=16):
    rows, width = part.shape
    hbm = pl.BlockSpec(memory_space=pl.ANY)
    whole = pl.BlockSpec(memory_space=pltpu.VMEM)
    return pl.pallas_call(
        functools.partial(input_kernel, pieces, tick),
        out_shape=[
            shape_of((rows, width), F32),
            shape_of((rows, width), BF16),
            shape_of((1, width), F32),
        ],
        in_specs=[hbm] * 3 + [whole],
        out_specs=[hbm] * 2 + [whole],
        scratch_shapes=[pltpu.VMEM((rows // 2, width), BF16)] * 5
        + [pltpu.VMEM((rows, width), BF16)] * 2
        + [pltpu.VMEM((rows, width), F32)] * 2
        + [pltpu.VMEM((8, width), F32)]
        + [pltpu.SemaphoreType.DMA((5, pieces))] * 2
        + [pltpu.SemaphoreType.DMA]
        + [pltpu.SemaphoreType.DMA((2, 2)), pltpu.SemaphoreType.DMA((2, pieces))],
        compiler_params=pltpu.CompilerParams(
            collective_id=identity, has_side_effects=True, vmem_limit_bytes=VMEM_BYTES
        ),
        cost_estimate=cost(42),
        name="input_relay",
    )(part, layers, grad_state, gain)


def attention_forward_kernel(
    stored,
    meta,
    first_block,
    tok_ref,
    rec_ref,
    gain_ref,
    wall_ref,
    cos_ref,
    sin_ref,
    low_ref,
    *rest,
):
    rest = rest[stored:]
    packed_ref, x_ref, a_ref, qkv_ref, o_ref, lse_ref = rest[:6]
    keys, values, scores, tops, sums, mixed = rest[6:]
    index = pl.program_id(0)
    heads = wall_ref.shape[1] // (3 * LANES)
    wide = heads * LANES
    x = jnp.where(meta[0] == 0, tok_ref[...], rec_ref[...])
    x_ref[0] = x
    x = x.astype(F32)
    normed = gain_ref[...] * x * lax.rsqrt(jnp.mean(x * x, axis=-1, keepdims=True) + 1e-06)
    normed = normed.astype(BF16)
    a_ref[0] = normed
    cosine, sine = cos_ref[...], sin_ref[...]
    here = rows_of(index, BLOCK)
    projected = dot(normed, wall_ref[...])
    for group in range(2 * heads):
        columns = slice(group * LANES, (group + 1) * LANES)
        pre = projected[:, columns]
        turned = pre * cosine + pltpu.roll(pre, HEAD_DIM, 1) * sine
        if group < heads:
            turned = turned * 0.0625
        qkv_ref[0, :, columns] = turned.astype(BF16)
    qkv_ref[0, :, 2 * wide :] = projected[:, 2 * wide :].astype(BF16)
    keys[here, :] = qkv_ref[0, :, wide : 2 * wide]
    low = low_ref[0]
    query_at = index * BLOCK + lax.broadcasted_iota(jnp.int32, (BLOCK, KEYS), 0)
    key_at = lax.broadcasted_iota(jnp.int32, (BLOCK, KEYS), 1)

    @pl.when(index * BLOCK % KEYS == 0)
    def _():
        values[rows_of(index * BLOCK // KEYS, KEYS), :] = jnp.zeros((KEYS, wide), BF16)

    values[here, :] = qkv_ref[0, :, 2 * wide :]
    tops[...] = jnp.full_like(tops, -1e30)
    sums[...] = jnp.zeros_like(sums)
    mixed[...] = jnp.zeros_like(mixed)
    begin = first_block[meta[2] * BLOCKS + index]

    def score(block, none):
        at = key_at + block * KEYS
        valid = (at >= low) & (at <= query_at)
        there = rows_of(block, KEYS)
        for head in range(heads):
            columns = slice(head * LANES, (head + 1) * LANES)
            raw = dot_nt(qkv_ref[0, :, columns], keys[there, columns])
            raw = jnp.where(valid, raw, -1e30)
            scores[head, block] = raw
            best = tops[head]
            for start in range(0, KEYS, LANES):
                best = jnp.maximum(best, raw[:, start : start + LANES])
            tops[head] = best
        return none

    end = ((index + 1) * BLOCK - 1) // KEYS + 1
    lax.fori_loop(begin, end, score, 0)
    top = [jnp.max(tops[head], axis=1, keepdims=True) for head in range(heads)]

    def mix(block, none):
        there = rows_of(block, KEYS)
        for head in range(heads):
            columns = slice(head * LANES, (head + 1) * LANES)
            weights = jnp.exp(scores[head, block] - top[head])
            part = weights[:, :LANES]
            for start in range(LANES, KEYS, LANES):
                part = part + weights[:, start : start + LANES]
            sums[head] += part
            mixed[:, columns] += dot(weights.astype(BF16), values[there, columns])
        return none

    lax.fori_loop(begin, end, mix, 0)
    for head in range(heads):
        columns = slice(head * LANES, (head + 1) * LANES)
        total = jnp.sum(sums[head], axis=1, keepdims=True)
        o_ref[0, :, columns] = (mixed[:, columns] / total).astype(BF16)
        logsum = jnp.broadcast_to(top[head] + jnp.log(total), (BLOCK, LANES))
        lse_ref[0, head : head + 1, :] = logsum.T[0:1, :]
    half = PACK // 2
    for start in range(0, BLOCK, PACK):
        packed_ref[start // 2 : start // 2 + half, :] = jnp.concatenate(
            [
                o_ref[
                    0,
                    start + side * half : start + (side + 1) * half,
                    head * LANES : head * LANES + HEAD_DIM,
                ]
                for side in range(2)
                for head in range(heads)
            ],
            axis=1,
        )


def attention_forward(meta, first_block, tokens, received, gain, wall, cosine, sine, low, kept):
    width = tokens.shape[1]
    wide = wall.shape[1] // 3
    heads = wide // LANES
    stored = 0 if kept is None else 5
    saved = [
        shape_of((SLOTS, SEQ_LEN, width), BF16),
        shape_of((SLOTS, SEQ_LEN, width), BF16),
        shape_of((SLOTS, SEQ_LEN, 3 * wide), BF16),
        shape_of((SLOTS, SEQ_LEN, wide), BF16),
        shape_of((SLOTS, 8, SEQ_LEN), F32),
    ]

    def slot_rows(columns):
        return pl.BlockSpec((1, BLOCK, columns), lambda i, m, f: (m[1], i, 0))

    grid_spec = pltpu.PrefetchScalarGridSpec(
        num_scalar_prefetch=2,
        grid=(BLOCKS,),
        in_specs=[
            pl.BlockSpec((BLOCK, width), lambda i, m, f: (m[2] * BLOCKS + i, 0)),
            pl.BlockSpec((BLOCK, width), lambda i, m, f: (i, 0)),
            once((1, width), lambda i, m, f: (0, 0)),
            once(wall.shape, lambda i, m, f: (0, 0)),
            pl.BlockSpec((BLOCK, LANES), lambda i, m, f: (i, 0)),
            pl.BlockSpec((BLOCK, LANES), lambda i, m, f: (i, 0)),
            pl.BlockSpec((1, BLOCK, 1), lambda i, m, f: (m[2], i, 0)),
        ]
        + [pl.BlockSpec(memory_space=pl.ANY)] * stored,
        out_specs=[
            pl.BlockSpec((BLOCK // 2, wide), lambda i, m, f: (i, 0)),
            slot_rows(width),
            slot_rows(width),
            slot_rows(3 * wide),
            slot_rows(wide),
            pl.BlockSpec((1, 8, BLOCK), lambda i, m, f: (m[1], 0, i)),
        ],
        scratch_shapes=[
            pltpu.VMEM((SEQ_LEN, wide), BF16),
            pltpu.VMEM((SEQ_LEN, wide), BF16),
            pltpu.VMEM((heads, SEQ_LEN // KEYS, BLOCK, KEYS), F32),
            pltpu.VMEM((heads, BLOCK, LANES), F32),
            pltpu.VMEM((heads, BLOCK, LANES), F32),
            pltpu.VMEM((BLOCK, wide), F32),
        ],
    )
    outs = pl.pallas_call(
        functools.partial(attention_forward_kernel, stored),
        grid_spec=grid_spec,
        out_shape=[shape_of((SEQ_LEN // 2, wide), BF16)] + saved,
        input_output_aliases={9 + k: 1 + k for k in range(stored)},
        compiler_params=pltpu.CompilerParams(vmem_limit_bytes=VMEM_BYTES),
        cost_estimate=cost(24),
        name="attention_forward",
    )(
        meta,
        first_block,
        tokens,
        received,
        gain,
        wall,
        cosine,
        sine,
        low,
        *(kept or ()),
    )
    return outs[0], outs[1:]


def reserve(shapes):
    return pl.pallas_call(
        lambda *refs: None,
        out_shape=shapes,
        out_specs=[pl.BlockSpec(memory_space=pl.ANY)] * len(shapes),
        compiler_params=pltpu.CompilerParams(has_side_effects=True),
        cost_estimate=cost(1),
        name="reserve",
    )()


PAIR = 2
ROWS = 512
ROW_STEPS = SEQ_LEN // ROWS
PAIR_STEPS = EXPERTS // PAIR
SPAN = 512
CHUNK = 96


def build_pick(first, chunks, post_ref, probs, pick, gates):
    for which, step in chunks:
        row = pl.ds(first + which, 1)
        slot_at = step * CHUNK + lax.broadcasted_iota(jnp.int32, (CHUNK, SEQ_LEN), 0)
        here = slot_at == post_ref[0, row, :]
        rows = slice(which * CAPACITY + step * CHUNK, which * CAPACITY + (step + 1) * CHUNK)
        pick[rows, :] = jnp.where(here, 1.0, 0.0).astype(BF16)
        if probs is not None:
            chosen = jnp.sum(jnp.where(here, probs[row, :], 0.0), axis=1, keepdims=True)
            gates[rows, :] = jnp.broadcast_to(chosen, (CHUNK, LANES))


def build_gates(first, post_ref, probs, gates):
    for which in range(PAIR):
        row = pl.ds(first + which, 1)
        for step in range(CAPACITY // CHUNK):
            slot_at = step * CHUNK + lax.broadcasted_iota(jnp.int32, (CHUNK, SEQ_LEN), 0)
            here = slot_at == post_ref[0, row, :]
            rows = slice(which * CAPACITY + step * CHUNK, which * CAPACITY + (step + 1) * CHUNK)
            chosen = jnp.sum(jnp.where(here, probs[row, :], 0.0), axis=1, keepdims=True)
            gates[rows, :] = jnp.broadcast_to(chosen, (CHUNK, LANES))


WINDOW_SLOTS = 256


def is_narrow(starts, sequence):
    return starts[starts.shape[0] - SLOTS + 1 + sequence] > 0


def window_at(starts, sequence, expert, chunk):
    place = starts[(sequence * EXPERTS + expert) * (ROW_STEPS + 1) + chunk]
    return jnp.minimum(place // 16 * 16, SPAN - WINDOW_SLOTS)


def chunk_rows(chunk):
    return pl.ds(chunk * ROWS, ROWS)


def token_places(expert, rows, pos_ref):
    places = pos_ref[0, rows, :]
    lane = lax.broadcasted_iota(jnp.int32, places.shape, 1)
    return jnp.sum(jnp.where(lane == expert, places, 0), axis=1, keepdims=True)


def build_put(starts, sequence, pair, chunk, pos_ref, put):
    rows = chunk_rows(chunk)
    slot_at = lax.broadcasted_iota(jnp.int32, (ROWS, WINDOW_SLOTS), 1)
    for which in range(PAIR):
        expert = pair * PAIR + which
        begin = jnp.where(
            is_narrow(starts, sequence), window_at(starts, sequence, expert, chunk), -SEQ_LEN
        )
        put[rows, which * WINDOW_SLOTS : (which + 1) * WINDOW_SLOTS] = jnp.where(
            slot_at == token_places(expert, rows, pos_ref) - begin, 1.0, 0.0
        ).astype(BF16)


def put_back(starts, sequence, pair, chunk, put, slots, window):
    for which in range(PAIR):
        begin = window_at(starts, sequence, pair * PAIR + which, chunk)
        there = pl.ds(pl.multiple_of(which * SPAN + begin, 16), WINDOW_SLOTS)
        window[which * WINDOW_SLOTS : (which + 1) * WINDOW_SLOTS, :] = slots[there, :]
    return dot(put[chunk_rows(chunk), : PAIR * WINDOW_SLOTS], window[...])


def put_back_wide(pair, pos_ref, put, slots, total):
    def body(step):
        which, chunk = step // ROW_STEPS, step % ROW_STEPS
        rows = rows_of(chunk, ROWS)
        slot_at = lax.broadcasted_iota(jnp.int32, (ROWS, SPAN), 1)
        place = token_places(pair * PAIR + which, rows, pos_ref)
        put[rows, SPAN:] = jnp.where(slot_at == place, 1.0, 0.0).astype(BF16)
        total[rows, :] += dot(put[rows, SPAN:], slots[rows_of(which, SPAN), :])

    loop(PAIR * ROW_STEPS, body)


ALL_CHUNKS = [(which, step) for which in range(PAIR) for step in range(CAPACITY // CHUNK)]


def of_pair(which):
    return slice(which * CAPACITY, (which + 1) * CAPACITY)


def feed_forward_kernel(
    stored,
    meta,
    starts,
    x_ref,
    ag_ref,
    wo_ref,
    gain_ref,
    router_ref,
    post_ref,
    pos_ref,
    wg_ref,
    wu_ref,
    wd_ref,
    wgs_ref,
    wus_ref,
    wds_ref,
    *rest,
):
    rest = rest[stored:]
    part_ref, h_ref, b_ref, xe_ref, g_ref, u_ref, gs_ref, us_ref, probs_ref = rest[:9]
    total, normed, probs, pick, put, gates, scaled, window = rest[9:]
    step = pl.program_id(0)
    pair = jnp.maximum(step - ROW_STEPS, 0)

    def activate(gate, lift, gate_out, lift_out):
        gate_out[...] = gate.astype(BF16)
        lift_out[...] = lift.astype(BF16)
        return (gate / (1.0 + jnp.exp(-gate)) * lift).astype(BF16)

    @pl.when(step < ROW_STEPS)
    def _():
        half = PACK // 2
        columns = ag_ref.shape[2] // 2
        mixed = jnp.concatenate(
            [
                jnp.concatenate(
                    [
                        ag_ref[device, block : block + half, side * columns : (side + 1) * columns]
                        for device in range(4)
                    ],
                    axis=1,
                )
                for block in range(0, ROWS // 2, half)
                for side in range(2)
            ],
            axis=0,
        )
        state = x_ref[0].astype(F32) + dot(mixed, wo_ref[...])
        h_ref[0] = state
        scale = lax.rsqrt(jnp.mean(state * state, axis=-1, keepdims=True) + 1e-06)
        b = (gain_ref[...] * state * scale).astype(BF16)
        b_ref[0] = b
        here = rows_of(step, ROWS)
        normed[here, :] = b
        logits = dot_nt(router_ref[...], b)
        weights = jnp.exp(logits - jnp.max(logits, axis=0, keepdims=True))
        weights = weights / jnp.sum(weights, axis=0, keepdims=True)
        probs_ref[0] = weights
        probs[:, here] = weights
        hidden = activate(dot(b, wgs_ref[...]), dot(b, wus_ref[...]), gs_ref.at[0], us_ref.at[0])
        total[here, :] = dot(hidden, wds_ref[...])

    @pl.when(step == 0)
    def _():
        build_pick(0, ALL_CHUNKS, post_ref, None, pick, gates)
        scaled[...] = jnp.zeros_like(scaled)
        put[:, : PAIR * WINDOW_SLOTS] = jnp.zeros((SEQ_LEN, PAIR * WINDOW_SLOTS), BF16)

    before = jnp.maximum(pair - 1, 0)

    @pl.when((step > ROW_STEPS) & jnp.logical_not(is_narrow(starts, meta[2])))
    def _():
        put_back_wide(before, pos_ref, put, scaled, total)

    @pl.when(step == ROW_STEPS + PAIR_STEPS)
    def _():
        for chunk in range(ROW_STEPS):
            rows = chunk_rows(chunk)
            values = put_back(starts, meta[2], before, chunk, put, scaled, window)
            part_ref[rows, :] = (total[rows, :] + values).astype(BF16)

    @pl.when((step >= ROW_STEPS) & (step < ROW_STEPS + PAIR_STEPS))
    def _():
        for chunk in range(ROW_STEPS):
            total[chunk_rows(chunk), :] += put_back(
                starts, meta[2], before, chunk, put, scaled, window
            )
            build_put(starts, meta[2], pair, chunk, pos_ref, put)
        picked = dot(pick[...], normed[...]).astype(BF16)
        build_gates(pair * PAIR, post_ref, probs, gates)
        build_pick(
            jnp.minimum(pair + 1, PAIR_STEPS - 1) * PAIR, ALL_CHUNKS, post_ref, None, pick, gates
        )
        for which in range(PAIR):
            rows = picked[of_pair(which), :]
            xe_ref[0, which] = rows
            hidden = activate(
                dot(rows, wg_ref[which]), dot(rows, wu_ref[which]), g_ref.at[0, which], u_ref.at[0, which]
            )
            scaled[which * SPAN : which * SPAN + CAPACITY, :] = (
                dot(hidden, wd_ref[which]) * gates[of_pair(which), 0:1]
            ).astype(BF16)


def step_specs():
    def row_at(step):
        return jnp.minimum(step, ROW_STEPS - 1)

    def pair_at(step):
        return jnp.clip(step - ROW_STEPS, 0, PAIR_STEPS - 1)

    return row_at, pair_at


def feed_forward(
    meta, starts, layer_in, gathered, out_weight, gain, router, post, pos, weights, kept
):
    width = layer_in.shape[2]
    wg, wu, wd, wgs, wus, wds = weights
    hidden = wg.shape[2]
    stored = 8
    saved = [
        shape_of((SLOTS, SEQ_LEN, width), F32),
        shape_of((SLOTS, SEQ_LEN, width), BF16),
        shape_of((SLOTS, EXPERTS, CAPACITY, width), BF16),
        shape_of((SLOTS, EXPERTS, CAPACITY, hidden), BF16),
        shape_of((SLOTS, EXPERTS, CAPACITY, hidden), BF16),
        shape_of((SLOTS, SEQ_LEN, hidden), BF16),
        shape_of((SLOTS, SEQ_LEN, hidden), BF16),
        shape_of((SLOTS, EXPERTS, SEQ_LEN), F32),
    ]
    row_at, pair_at = step_specs()

    def slot_rows(columns):
        return pl.BlockSpec((1, ROWS, columns), lambda s, m, f: (m[1], row_at(s), 0))

    def slot_pair(columns):
        return pl.BlockSpec((1, PAIR, CAPACITY, columns), lambda s, m, f: (m[1], pair_at(s), 0, 0))

    def fixed(shape):
        return once(shape, lambda s, m, f: (0,) * len(shape))

    def of_pairs(array):
        return pl.BlockSpec((PAIR,) + array.shape[1:], lambda s, m, f: (pair_at(s), 0, 0))

    grid_spec = pltpu.PrefetchScalarGridSpec(
        num_scalar_prefetch=2,
        grid=(ROW_STEPS + PAIR_STEPS + 1,),
        in_specs=[
            slot_rows(width),
            pl.BlockSpec((4, ROWS // 2, gathered.shape[2]), lambda s, m, f: (0, row_at(s), 0)),
            fixed(out_weight.shape),
            fixed(gain.shape),
            fixed(router.shape),
            once((1, EXPERTS, SEQ_LEN), lambda s, m, f: (m[2], 0, 0)),
            once((1, SEQ_LEN, EXPERTS), lambda s, m, f: (m[2], 0, 0)),
            of_pairs(wg),
            of_pairs(wu),
            of_pairs(wd),
            fixed(wgs.shape),
            fixed(wus.shape),
            fixed(wds.shape),
        ]
        + [pl.BlockSpec(memory_space=pl.ANY)] * stored,
        out_specs=[
            fixed((SEQ_LEN, width)),
            slot_rows(width),
            slot_rows(width),
            slot_pair(width),
            slot_pair(hidden),
            slot_pair(hidden),
            slot_rows(hidden),
            slot_rows(hidden),
            pl.BlockSpec((1, EXPERTS, ROWS), lambda s, m, f: (m[1], 0, row_at(s))),
        ],
        scratch_shapes=[
            pltpu.VMEM((SEQ_LEN, width), F32),
            pltpu.VMEM((SEQ_LEN, width), BF16),
            pltpu.VMEM((EXPERTS, SEQ_LEN), F32),
            pltpu.VMEM((PAIR * CAPACITY, SEQ_LEN), BF16),
            pltpu.VMEM((SEQ_LEN, PAIR * SPAN), BF16),
            pltpu.VMEM((PAIR * CAPACITY, LANES), F32),
            pltpu.VMEM((PAIR * SPAN, width), BF16),
            pltpu.VMEM((PAIR * WINDOW_SLOTS, width), BF16),
        ],
    )
    outs = pl.pallas_call(
        functools.partial(feed_forward_kernel, stored),
        grid_spec=grid_spec,
        out_shape=[shape_of((SEQ_LEN, width), BF16)] + saved,
        input_output_aliases={15 + k: 1 + k for k in range(stored)},
        compiler_params=pltpu.CompilerParams(vmem_limit_bytes=VMEM_BYTES),
        cost_estimate=cost(56),
        name="feed_forward",
    )(
        meta,
        starts,
        layer_in,
        gathered,
        out_weight,
        gain,
        router,
        post,
        pos,
        wg,
        wu,
        wd,
        wgs,
        wus,
        wds,
        *(reserve(saved) if kept is None else kept),
    )
    return outs[0], outs[1:]


def pull(grad, weight, gate, lift):
    gate, lift = gate.astype(F32), lift.astype(F32)
    sigma = 1.0 / (1.0 + jnp.exp(-gate))
    swish = gate * sigma
    hidden = (swish * lift).astype(BF16)
    inner = None
    if weight is not None:
        inner = jnp.sum(hidden.astype(F32) * grad, axis=1, keepdims=True)
        grad = grad * weight
    grad_gate = (grad * lift * (sigma + swish * (1.0 - sigma))).astype(BF16)
    return hidden, grad_gate, (grad * swish).astype(BF16), inner


def feed_backward_kernel(
    stored,
    meta,
    starts,
    cot_ref,
    rec_ref,
    post_ref,
    pos_ref,
    g_ref,
    u_ref,
    gs_ref,
    us_ref,
    probs_ref,
    wg_ref,
    wu_ref,
    wd_ref,
    wgs_ref,
    wus_ref,
    wds_ref,
    *rest,
):
    rest = rest[stored:]
    part_ref, dy_ref, hid_ref, dg_ref, du_ref, de_ref, hids_ref, dgs_ref, dus_ref = rest[:9]
    total, given, pick, put, gates, slots, choice, window = rest[9:]
    step = pl.program_id(0)
    pair = jnp.maximum(step - ROW_STEPS, 0)

    @pl.when(step < ROW_STEPS)
    def _():
        dy = jnp.where(meta[0] == 1, cot_ref[...], rec_ref[...])
        dy = jnp.where(meta[0] == 0, jnp.zeros_like(dy), dy)
        dy_ref[0] = dy
        here = rows_of(step, ROWS)
        given[here, :] = dy
        hidden, grad_gate, grad_lift, unused = pull(
            dot_nt(dy, wds_ref[...]), None, gs_ref[0], us_ref[0]
        )
        hids_ref[0] = hidden
        dgs_ref[0] = grad_gate
        dus_ref[0] = grad_lift
        total[here, :] = dot_nt(grad_gate, wgs_ref[...]) + dot_nt(grad_lift, wus_ref[...])

    @pl.when(step == 0)
    def _():
        build_pick(0, ALL_CHUNKS, post_ref, None, pick, gates)
        slots[...] = jnp.zeros_like(slots)
        put[:, : PAIR * WINDOW_SLOTS] = jnp.zeros((SEQ_LEN, PAIR * WINDOW_SLOTS), BF16)

    before = jnp.maximum(pair - 1, 0)

    @pl.when((step > ROW_STEPS) & jnp.logical_not(is_narrow(starts, meta[2])))
    def _():
        put_back_wide(before, pos_ref, put, slots, total)

    @pl.when(step == ROW_STEPS + PAIR_STEPS)
    def _():
        for chunk in range(ROW_STEPS):
            rows = chunk_rows(chunk)
            values = put_back(starts, meta[2], before, chunk, put, slots, window)
            part_ref[rows, :] = (total[rows, :] + values).astype(BF16)

    @pl.when((step >= ROW_STEPS) & (step < ROW_STEPS + PAIR_STEPS))
    def _():
        for chunk in range(ROW_STEPS):
            total[chunk_rows(chunk), :] += put_back(
                starts, meta[2], before, chunk, put, slots, window
            )
            build_put(starts, meta[2], pair, chunk, pos_ref, put)
        picked = dot(pick[...], given[...]).astype(BF16)
        build_gates(pair * PAIR, post_ref, probs_ref.at[0], gates)
        build_pick(
            jnp.minimum(pair + 1, PAIR_STEPS - 1) * PAIR, ALL_CHUNKS, post_ref, None, pick, gates
        )
        for which in range(PAIR):
            rows = picked[of_pair(which), :]
            weight = gates[of_pair(which), 0:1]
            hidden, grad_gate, grad_lift, inner = pull(
                dot_nt(rows, wd_ref[which]), weight, g_ref[0, which], u_ref[0, which]
            )
            hid_ref[0, which] = hidden
            dg_ref[0, which] = grad_gate
            du_ref[0, which] = grad_lift
            de_ref[0, which] = (weight * rows.astype(F32)).astype(BF16)
            row = pl.ds(pair * PAIR + which, 1)
            chosen = jnp.zeros((1, SEQ_LEN), F32)
            for chunk in range(CAPACITY // CHUNK):
                slot_at = chunk * CHUNK + lax.broadcasted_iota(jnp.int32, (CHUNK, SEQ_LEN), 0)
                here = slot_at == post_ref[0, row, :]
                chosen += jnp.sum(
                    jnp.where(here, inner[chunk * CHUNK : (chunk + 1) * CHUNK], 0.0),
                    axis=0,
                    keepdims=True,
                )
            choice[row, :] = chosen
            slots[which * SPAN : which * SPAN + CAPACITY, :] = (
                dot_nt(grad_gate, wg_ref[which]) + dot_nt(grad_lift, wu_ref[which])
            ).astype(BF16)

    @pl.when(step == ROW_STEPS + PAIR_STEPS)
    def _():
        half = SEQ_LEN // 2
        blank = jnp.zeros((8, half), F32)
        part_ref[SEQ_LEN:, :] = jnp.concatenate(
            [choice[:, :half], blank, choice[:, half:], blank], axis=0
        ).astype(BF16)


def feed_backward(meta, starts, cotangent, received, post, pos, forward_kept, weights, kept):
    width = cotangent.shape[1]
    wg, wu, wd, wgs, wus, wds = weights
    hidden = wg.shape[2]
    stored = 8
    unused_h, unused_b, unused_x, gate, lift, gate_sh, lift_sh, probs = forward_kept
    saved = [
        shape_of((SLOTS, SEQ_LEN, width), BF16),
        shape_of((SLOTS, EXPERTS, CAPACITY, hidden), BF16),
        shape_of((SLOTS, EXPERTS, CAPACITY, hidden), BF16),
        shape_of((SLOTS, EXPERTS, CAPACITY, hidden), BF16),
        shape_of((SLOTS, EXPERTS, CAPACITY, width), BF16),
        shape_of((SLOTS, SEQ_LEN, hidden), BF16),
        shape_of((SLOTS, SEQ_LEN, hidden), BF16),
        shape_of((SLOTS, SEQ_LEN, hidden), BF16),
    ]
    row_at, pair_at = step_specs()

    def slot_rows(columns, which):
        return pl.BlockSpec((1, ROWS, columns), lambda s, m, f: (m[which], row_at(s), 0))

    def slot_pair(columns, which):
        return pl.BlockSpec(
            (1, PAIR, CAPACITY, columns), lambda s, m, f: (m[which], pair_at(s), 0, 0)
        )

    def fixed(shape):
        return once(shape, lambda s, m, f: (0,) * len(shape))

    def of_pairs(array):
        return pl.BlockSpec((PAIR,) + array.shape[1:], lambda s, m, f: (pair_at(s), 0, 0))

    grid_spec = pltpu.PrefetchScalarGridSpec(
        num_scalar_prefetch=2,
        grid=(ROW_STEPS + PAIR_STEPS + 1,),
        in_specs=[
            pl.BlockSpec((ROWS, width), lambda s, m, f: (m[2] * ROW_STEPS + row_at(s), 0)),
            pl.BlockSpec((ROWS, width), lambda s, m, f: (row_at(s), 0)),
            once((1, EXPERTS, SEQ_LEN), lambda s, m, f: (m[2], 0, 0)),
            once((1, SEQ_LEN, EXPERTS), lambda s, m, f: (m[2], 0, 0)),
            slot_pair(hidden, 3),
            slot_pair(hidden, 3),
            slot_rows(hidden, 3),
            slot_rows(hidden, 3),
            once((1, EXPERTS, SEQ_LEN), lambda s, m, f: (m[3], 0, 0)),
            of_pairs(wg),
            of_pairs(wu),
            of_pairs(wd),
            fixed(wgs.shape),
            fixed(wus.shape),
            fixed(wds.shape),
        ]
        + [pl.BlockSpec(memory_space=pl.ANY)] * stored,
        out_specs=[
            fixed((SEQ_LEN + 32, width)),
            slot_rows(width, 1),
            slot_pair(hidden, 1),
            slot_pair(hidden, 1),
            slot_pair(hidden, 1),
            slot_pair(width, 1),
            slot_rows(hidden, 1),
            slot_rows(hidden, 1),
            slot_rows(hidden, 1),
        ],
        scratch_shapes=[
            pltpu.VMEM((SEQ_LEN, width), F32),
            pltpu.VMEM((SEQ_LEN, width), BF16),
            pltpu.VMEM((PAIR * CAPACITY, SEQ_LEN), BF16),
            pltpu.VMEM((SEQ_LEN, PAIR * SPAN), BF16),
            pltpu.VMEM((PAIR * CAPACITY, LANES), F32),
            pltpu.VMEM((PAIR * SPAN, width), BF16),
            pltpu.VMEM((EXPERTS, SEQ_LEN), F32),
            pltpu.VMEM((PAIR * WINDOW_SLOTS, width), BF16),
        ],
    )
    outs = pl.pallas_call(
        functools.partial(feed_backward_kernel, stored),
        grid_spec=grid_spec,
        out_shape=[shape_of((SEQ_LEN + 32, width), BF16)] + saved,
        input_output_aliases={17 + k: 1 + k for k in range(stored)},
        compiler_params=pltpu.CompilerParams(vmem_limit_bytes=VMEM_BYTES),
        cost_estimate=cost(60),
        name="feed_backward",
    )(
        meta,
        starts,
        cotangent,
        received,
        post,
        pos,
        gate,
        lift,
        gate_sh,
        lift_sh,
        probs,
        wg,
        wu,
        wd,
        wgs,
        wus,
        wds,
        *(reserve(saved) if kept is None else kept),
    )
    return outs[0], outs[1:]


def attention_backward_kernel(
    stored,
    meta,
    first_block,
    sum_ref,
    choice_ref,
    probs_ref,
    dy_ref,
    h_ref,
    b_ref,
    gain_ref,
    router_ref,
    wall_ref,
    wo_ref,
    cos_ref,
    sin_ref,
    qkv_ref,
    o_ref,
    lse_ref,
    low_ref,
    *rest,
):
    rest = rest[stored:]
    part_ref, dh_ref, gain_grad_ref, router_grad_ref, dqkv_ref, dattn_ref = rest[:6]
    dk_all, dv_all, dq_all, do_all, inner_all = rest[6:]
    step = pl.program_id(0)
    index = BACK_BLOCKS - 1 - step
    heads = wo_ref.shape[0] // LANES
    wide = heads * LANES

    @pl.when(step == 0)
    def _():
        gain_grad_ref[...] = jnp.zeros_like(gain_grad_ref)
        router_grad_ref[...] = jnp.zeros_like(router_grad_ref)
        dk_all[...] = jnp.zeros_like(dk_all)
        dv_all[...] = jnp.zeros_like(dv_all)

    probs = probs_ref[0]
    chosen = choice_ref[0:8, :].astype(F32)
    logit_grads = probs * (chosen - jnp.sum(probs * chosen, axis=0, keepdims=True))
    logit_grads = logit_grads.astype(BF16)
    router_grad_ref[...] += dot(logit_grads, b_ref[0])
    grad_normed = sum_ref[...].astype(F32) + dot_tn(logit_grads, router_ref[...])
    state = h_ref[0]
    scale = lax.rsqrt(jnp.mean(state * state, axis=-1, keepdims=True) + 1e-06)
    normed = state * scale
    gain_grad_ref[...] += jnp.sum(grad_normed * normed, axis=0, keepdims=True)
    scaled = gain_ref[...] * grad_normed
    inner = jnp.mean(normed * scaled, axis=-1, keepdims=True)
    grad_state = dy_ref[0].astype(F32) + scale * (scaled - normed * inner)
    dh_ref[...] = grad_state
    dattn = grad_state.astype(BF16)
    dattn_ref[0] = dattn
    do = dot_nt(dattn, wo_ref[...]).astype(BF16)
    do_all[...] = do
    products = do.astype(F32) * o_ref[0].astype(F32)
    for head in range(heads):
        columns = slice(head * LANES, (head + 1) * LANES)
        row = jnp.sum(products[:, columns], axis=1, keepdims=True)
        inner_all[head : head + 1, :] = jnp.broadcast_to(row, (BACK_BLOCK, LANES)).T[0:1, :]
    dq_all[...] = jnp.zeros_like(dq_all)
    here = rows_of(index, BACK_BLOCK)
    low = low_ref[0]
    query_at = index * BACK_BLOCK + lax.broadcasted_iota(jnp.int32, (BACK_KEYS, BACK_BLOCK), 1)
    key_at = lax.broadcasted_iota(jnp.int32, (BACK_KEYS, BACK_BLOCK), 0)

    def body(block, none):
        at = key_at + block * BACK_KEYS
        valid = (at >= low) & (at <= query_at)
        there = rows_of(block, BACK_KEYS)
        for head in range(heads):
            columns = slice(head * LANES, (head + 1) * LANES)
            key_columns = slice(wide + head * LANES, wide + (head + 1) * LANES)
            value_columns = slice(2 * wide + head * LANES, 2 * wide + (head + 1) * LANES)
            query = qkv_ref[0, here, columns]
            keys = qkv_ref[0, there, key_columns]
            scores = jnp.where(valid, dot_nt(keys, query), -1e30)
            probs = jnp.exp(scores - lse_ref[0, head : head + 1, :])
            grad_probs = dot_nt(qkv_ref[0, there, value_columns], do_all[:, columns])
            grad_scores = (probs * (grad_probs - inner_all[head : head + 1, :])).astype(BF16)
            dv_all[there, columns] += dot(probs.astype(BF16), do_all[:, columns])
            dk_all[there, columns] += dot(grad_scores, query)
            dq_all[:, columns] += dot_tn(grad_scores, keys)
        return none

    lax.fori_loop(
        first_block[meta[2] * BACK_BLOCKS + index], ((index + 1) * BACK_BLOCK - 1) // BACK_KEYS + 1, body, 0
    )
    cosine, sine = cos_ref[...], sin_ref[...]
    for head in range(heads):
        columns = slice(head * LANES, (head + 1) * LANES)
        key_columns = slice(wide + head * LANES, wide + (head + 1) * LANES)
        value_columns = slice(2 * wide + head * LANES, 2 * wide + (head + 1) * LANES)
        dq = dq_all[:, columns] * 0.0625
        dk = dk_all[here, columns]
        dqkv_ref[0, :, columns] = (dq * cosine - pltpu.roll(dq, HEAD_DIM, 1) * sine).astype(BF16)
        dqkv_ref[0, :, key_columns] = (
            dk * cosine - pltpu.roll(dk, HEAD_DIM, 1) * sine
        ).astype(BF16)
        dqkv_ref[0, :, value_columns] = dv_all[here, columns].astype(BF16)
    part_ref[...] = dot_nt(dqkv_ref[0], wall_ref[...]).astype(BF16)


def attention_backward(
    meta, first_block, summed, forward_kept, attention_kept, dy, gain, router, wall, wo, cosine, sine, low, kept
):
    width = summed.shape[1]
    wide = wo.shape[0]
    stored = 0 if kept is None else 2
    h, b, probs = forward_kept[0], forward_kept[1], forward_kept[7]
    unused_x, unused_a, qkv, o, lse = attention_kept
    saved = [
        shape_of((SLOTS, SEQ_LEN, 3 * wide), BF16),
        shape_of((SLOTS, SEQ_LEN, width), BF16),
    ]

    def at(step):
        return BACK_BLOCKS - 1 - step

    def slot_rows(columns, which):
        return pl.BlockSpec((1, BACK_BLOCK, columns), lambda s, m, f: (m[which], at(s), 0))

    def fixed(shape):
        return once(shape, lambda s, m, f: (0,) * len(shape))

    halves_of = BACK_BLOCKS // 2
    grid_spec = pltpu.PrefetchScalarGridSpec(
        num_scalar_prefetch=2,
        grid=(BACK_BLOCKS,),
        in_specs=[
            pl.BlockSpec((BACK_BLOCK, width), lambda s, m, f: (at(s), 0)),
            pl.BlockSpec(
                (16, BACK_BLOCK), lambda s, m, f: (SEQ_LEN // 16 + at(s) // halves_of, at(s) % halves_of)
            ),
            pl.BlockSpec((1, EXPERTS, BACK_BLOCK), lambda s, m, f: (m[3], 0, at(s))),
            slot_rows(width, 1),
            slot_rows(width, 3),
            slot_rows(width, 3),
            fixed(gain.shape),
            fixed(router.shape),
            fixed(wall.shape),
            fixed(wo.shape),
            pl.BlockSpec((BACK_BLOCK, LANES), lambda s, m, f: (at(s), 0)),
            pl.BlockSpec((BACK_BLOCK, LANES), lambda s, m, f: (at(s), 0)),
            once((1, SEQ_LEN, 3 * wide), lambda s, m, f: (m[3], 0, 0)),
            slot_rows(wide, 3),
            pl.BlockSpec((1, 8, BACK_BLOCK), lambda s, m, f: (m[3], 0, at(s))),
            pl.BlockSpec((1, 1, BACK_BLOCK), lambda s, m, f: (m[2], 0, at(s))),
        ]
        + [pl.BlockSpec(memory_space=pl.ANY)] * stored,
        out_specs=[
            pl.BlockSpec((BACK_BLOCK, width), lambda s, m, f: (at(s), 0)),
            pl.BlockSpec((BACK_BLOCK, width), lambda s, m, f: (at(s), 0)),
            fixed((1, width)),
            fixed((8, width)),
            slot_rows(3 * wide, 1),
            slot_rows(width, 1),
        ],
        scratch_shapes=[
            pltpu.VMEM((SEQ_LEN, wide), F32),
            pltpu.VMEM((SEQ_LEN, wide), F32),
            pltpu.VMEM((BACK_BLOCK, wide), F32),
            pltpu.VMEM((BACK_BLOCK, wide), BF16),
            pltpu.VMEM((8, BACK_BLOCK), F32),
        ],
    )
    outs = pl.pallas_call(
        functools.partial(attention_backward_kernel, stored),
        grid_spec=grid_spec,
        out_shape=[
            shape_of((SEQ_LEN, width), BF16),
            shape_of((SEQ_LEN, width), F32),
            shape_of((1, width), F32),
            shape_of((8, width), F32),
        ]
        + saved,
        input_output_aliases={18 + k: 4 + k for k in range(stored)},
        compiler_params=pltpu.CompilerParams(vmem_limit_bytes=VMEM_BYTES),
        cost_estimate=cost(37),
        name="attention_backward",
    )(
        meta,
        first_block,
        summed,
        summed,
        probs,
        dy,
        h,
        b,
        gain,
        router,
        wall,
        wo,
        cosine,
        sine,
        qkv,
        o,
        lse,
        low,
        *(kept or ()),
    )
    return outs[:4], outs[4:]


def expert_grads_kernel(*refs):
    ins, out_ref = refs[:-1], refs[-1]
    (xa, xb), (ga, gb), (ua, ub), (ea, eb), (ha, hb) = (ins[2 * k : 2 * k + 2] for k in range(5))
    devices, unused, rows, unused = out_ref.shape
    pairs = [((xa, xb), (ga, gb)), ((xa, xb), (ua, ub)), ((ea, eb), (ha, hb))]
    for number, (left, right) in enumerate(pairs):
        for device in range(devices):
            columns = slice(device * rows, (device + 1) * rows)
            out_ref[device, number] = (
                dot_tn(left[0][0, 0, :, columns], right[0][0, 0])
                + dot_tn(left[1][0, 0, :, columns], right[1][0, 0])
            ).astype(BF16)


def expert_grads(first, count, extra, devices, picked, hid, grad_gate, grad_lift, grad_expert):
    width, hidden = picked.shape[3], hid.shape[3]
    rows = width // devices

    def pair(columns):
        return [
            pl.BlockSpec(
                (1, 1, CAPACITY, columns),
                functools.partial(lambda slot, e: (slot, first + e, 0, 0), slot),
            )
            for slot in (1, 2)
        ]

    return pl.pallas_call(
        expert_grads_kernel,
        grid=(count,),
        in_specs=pair(width) + pair(hidden) + pair(hidden) + pair(width) + pair(hidden),
        out_specs=pl.BlockSpec((devices, 3, rows, hidden), lambda e: (0, e, 0, 0)),
        out_shape=shape_of((devices, 3 * count + extra, rows, hidden), BF16),
        compiler_params=pltpu.CompilerParams(vmem_limit_bytes=VMEM_BYTES),
        cost_estimate=cost(6 * count),
        name="expert_grads",
    )(
        *(picked, picked, grad_gate, grad_gate, grad_lift, grad_lift),
        *(grad_expert, grad_expert, hid, hid),
    )


def lead_grads_kernel(
    meta,
    cot_ref,
    rec_ref,
    post_ref,
    probs_ref,
    g_ref,
    u_ref,
    wd_ref,
    xa_ref,
    xb_ref,
    ga_ref,
    ua_ref,
    ea_ref,
    ha_ref,
    out_ref,
    given,
    pick,
    gates,
    rows_in,
    grad_gate,
    grad_lift,
    grad_rows,
    hidden,
):
    step = pl.program_id(0)

    @pl.when(step == 0)
    def _():
        given[...] = jnp.where(meta[0] == 1, cot_ref[...], rec_ref[...])

    @pl.when(step > 0)
    def _():
        chunks = [(0, chunk) for chunk in range(CAPACITY // CHUNK)]
        build_pick(step - 1, chunks, post_ref, probs_ref.at[0], pick, gates)
        rows_in[...] = dot(pick[...], given[...]).astype(BF16)
        weight = gates[:, 0:1]
        grad_rows[...] = (weight * rows_in[...].astype(F32)).astype(BF16)
        hidden[...], grad_gate[...], grad_lift[...], unused = pull(
            dot_nt(rows_in[...], wd_ref[0]), weight, g_ref[0, 0], u_ref[0, 0]
        )
        devices, unused, rows, unused = out_ref.shape
        pairs = [
            (xa_ref.at[0, 0], ga_ref.at[0, 0], xb_ref.at[0, 0], grad_gate),
            (xa_ref.at[0, 0], ua_ref.at[0, 0], xb_ref.at[0, 0], grad_lift),
            (ea_ref.at[0, 0], ha_ref.at[0, 0], grad_rows, hidden),
        ]
        for number, (left, right, left_last, right_last) in enumerate(pairs):
            for device in range(devices):
                columns = slice(device * rows, (device + 1) * rows)
                out_ref[device, number] = (
                    dot_tn(left[:, columns], right[...])
                    + dot_tn(left_last[:, columns], right_last[...])
                ).astype(BF16)


def lead_grads(count, devices, meta, cotangent, received, post, forward_kept, kept, down):
    unused_h, unused_b, picked, gate, lift, unused_gate, unused_lift, probs = forward_kept
    unused_dy, hid, grad_gate, grad_lift, grad_expert = kept[:5]
    width, inner = picked.shape[3], gate.shape[3]
    rows = width // devices

    def at(step):
        return jnp.maximum(step - 1, 0)

    def of_slot(columns, which):
        return pl.BlockSpec((1, 1, CAPACITY, columns), lambda s, m: (m[which], at(s), 0, 0))

    grid_spec = pltpu.PrefetchScalarGridSpec(
        num_scalar_prefetch=1,
        grid=(count + 1,),
        in_specs=[
            once((SEQ_LEN, width), lambda s, m: (m[1], 0)),
            once((SEQ_LEN, width), lambda s, m: (0, 0)),
            once((1, EXPERTS, SEQ_LEN), lambda s, m: (m[1], 0, 0)),
            once((1, EXPERTS, SEQ_LEN), lambda s, m: (m[2], 0, 0)),
            of_slot(inner, 2),
            of_slot(inner, 2),
            pl.BlockSpec((1,) + down.shape[1:], lambda s, m: (at(s), 0, 0)),
            of_slot(width, 3),
            of_slot(width, 2),
            of_slot(inner, 3),
            of_slot(inner, 3),
            of_slot(width, 3),
            of_slot(inner, 3),
        ],
        out_specs=pl.BlockSpec((devices, 3, rows, inner), lambda s, m: (0, at(s), 0, 0)),
        scratch_shapes=[
            pltpu.VMEM((SEQ_LEN, width), BF16),
            pltpu.VMEM((CAPACITY, SEQ_LEN), BF16),
            pltpu.VMEM((CAPACITY, LANES), F32),
            pltpu.VMEM((CAPACITY, width), BF16),
            pltpu.VMEM((CAPACITY, inner), BF16),
            pltpu.VMEM((CAPACITY, inner), BF16),
            pltpu.VMEM((CAPACITY, width), BF16),
            pltpu.VMEM((CAPACITY, inner), BF16),
        ],
    )
    return pl.pallas_call(
        lead_grads_kernel,
        grid_spec=grid_spec,
        out_shape=shape_of((devices, 3 * count, rows, inner), BF16),
        compiler_params=pltpu.CompilerParams(vmem_limit_bytes=VMEM_BYTES),
        cost_estimate=cost(20),
        name="lead_grads",
    )(
        meta,
        cotangent,
        received,
        post,
        probs,
        gate,
        lift,
        down,
        picked,
        picked,
        grad_gate,
        grad_lift,
        grad_expert,
        hid,
    )


def shared_grads_kernel(b_ref, dy_ref, gate_ref, lift_ref, hid_ref, before_ref, out_ref, *totals):
    step = pl.program_id(0)
    pairs = [(b_ref, gate_ref), (b_ref, lift_ref), (dy_ref, hid_ref)]

    @pl.when(step == 0)
    def _():
        for total in totals:
            total[...] = jnp.zeros_like(total)

    for (left, right), total in zip(pairs, totals):
        total[...] += dot_tn(left[0], right[0])

    @pl.when(step == pl.num_programs(0) - 1)
    def _():
        devices, unused, rows, unused = out_ref.shape
        for number, total in enumerate(totals):
            for device in range(devices):
                out_ref[device, number] = total[device * rows : (device + 1) * rows, :].astype(
                    BF16
                )


def shared_grads(before, b, dy, grad_gate, grad_lift, hid):
    devices, matrices, width, hidden = before.shape
    rows = ROWS
    steps = SEQ_LEN // rows

    def spec(array):
        return pl.BlockSpec((1, rows, array.shape[2]), lambda s: (1 + s // steps, s % steps, 0))

    return pl.pallas_call(
        shared_grads_kernel,
        grid=(2 * steps,),
        in_specs=[spec(array) for array in (b, dy, grad_gate, grad_lift, hid)]
        + [pl.BlockSpec(memory_space=pl.ANY)],
        out_specs=once((devices, 3, width, hidden), lambda s: (0, matrices // 3 - 1, 0, 0)),
        out_shape=shape_of(before.shape, BF16),
        scratch_shapes=[pltpu.VMEM((devices * width, hidden), F32)] * 3,
        input_output_aliases={5: 0},
        compiler_params=pltpu.CompilerParams(vmem_limit_bytes=VMEM_BYTES),
        cost_estimate=cost(13),
        name="shared_grads",
    )(b, dy, grad_gate, grad_lift, hid, before)


def token_grads_kernel(count, *refs):
    lefts, rights = refs[:count], refs[count : 2 * count]
    outs, totals = refs[2 * count : 3 * count], refs[3 * count :]
    step = pl.program_id(0)

    @pl.when(step == 0)
    def _():
        for total in totals:
            total[...] = jnp.zeros_like(total)

    for left, right, total in zip(lefts, rights, totals):
        total[...] += dot_tn(left[0], right[0])

    @pl.when(step == pl.num_programs(0) - 1)
    def _():
        for out, total in zip(outs, totals):
            out[...] = total[...].astype(BF16)


def token_grads(lefts, rights):
    count = len(lefts)
    rows = ROWS
    steps = SEQ_LEN // rows

    def spec(array):
        return pl.BlockSpec((1, rows, array.shape[2]), lambda s: (1 + s // steps, s % steps, 0))

    shapes = [(left.shape[2], right.shape[2]) for left, right in zip(lefts, rights)]
    return pl.pallas_call(
        functools.partial(token_grads_kernel, count),
        grid=(2 * steps,),
        in_specs=[spec(a) for a in lefts] + [spec(a) for a in rights],
        out_specs=[once(shape, lambda s: (0, 0)) for shape in shapes],
        out_shape=[shape_of(shape, BF16) for shape in shapes],
        scratch_shapes=[pltpu.VMEM(shape, F32) for shape in shapes],
        compiler_params=pltpu.CompilerParams(vmem_limit_bytes=VMEM_BYTES),
        cost_estimate=cost(14),
        name="token_grads",
    )(*lefts, *rights)


def rotary_tables():
    half = HEAD_DIM // 2
    rates = np.exp(-np.log(10000.0) * np.arange(half) * 2.0 / HEAD_DIM)
    angles = np.arange(SEQ_LEN)[:, None] * rates[None, :]
    cosine, sine = np.cos(angles), np.sin(angles)
    cosine = np.concatenate([cosine] * 4, axis=1)
    sine = np.concatenate([sine, sine, -sine, -sine], axis=1)
    return jnp.asarray(cosine, F32), jnp.asarray(sine, F32)


def paired(weight):
    rows = weight.shape[0]
    heads = weight.shape[1] // HEAD_DIM
    half = HEAD_DIM // 2
    split = weight.reshape(rows, heads, HEAD_DIM)
    swapped = jnp.concatenate([-split[:, :, half:], split[:, :, :half]], axis=2)
    return jnp.concatenate([split, swapped], axis=2).reshape(rows, heads * LANES)


def padded(weight):
    rows = weight.shape[0]
    heads = weight.shape[1] // HEAD_DIM
    split = weight.reshape(rows, heads, HEAD_DIM)
    return jnp.concatenate([split, jnp.zeros_like(split)], axis=2).reshape(rows, heads * LANES)


def unpadded(grads):
    rows = grads.shape[0]
    return grads.reshape(rows, -1, LANES)[:, :, :HEAD_DIM].reshape(rows, -1)


def places(routes):
    experts = jnp.arange(EXPERTS, dtype=jnp.int32)
    named = jnp.any(routes[:, :, :, None] == experts, axis=2)
    before = (
        jnp.arange(SEQ_LEN, dtype=jnp.int32)[:, None] > jnp.arange(SEQ_LEN, dtype=jnp.int32)
    ).astype(BF16)
    rank = jnp.einsum("ts,nse->nte", before, named.astype(BF16), preferred_element_type=F32)
    by_token = jnp.where(named, rank.astype(jnp.int32), -1)
    counts = jnp.sum(named.reshape(-1, ROW_STEPS, ROWS, EXPERTS).astype(jnp.int32), axis=2)
    before = jnp.cumsum(jnp.pad(counts, ((0, 0), (1, 0), (0, 0))), axis=1)
    starts = jnp.swapaxes(before, 1, 2)
    held = starts[:, :, 1:] <= starts[:, :, :-1] // 16 * 16 + WINDOW_SLOTS
    narrow = jnp.all(held, axis=(1, 2)).astype(jnp.int32)
    starts = jnp.concatenate([starts.reshape(-1), narrow])
    return by_token, jnp.swapaxes(by_token, 1, 2), starts


def first_allowed(lengths):
    ends = jnp.cumsum(lengths, axis=1)
    at = jnp.arange(SEQ_LEN, dtype=jnp.int32)
    starts = jnp.max(jnp.where(ends[:, None, :] <= at[None, :, None], ends[:, None, :], 0), axis=2)
    return jnp.maximum(starts, at[None, :] - (WINDOW - 1)).astype(jnp.int32)


def on_device(
    tokens,
    doc_lengths,
    routes,
    gain_attn,
    w_query,
    w_key,
    w_value,
    w_output,
    gain_ffn,
    w_router,
    w_gate_exp,
    w_up_exp,
    w_down_exp,
    w_gate_sh,
    w_up_sh,
    w_down_sh,
    cotangent,
):
    section = lax.axis_index("section")
    devices = lax.axis_size("dp")
    count = doc_lengths.shape[0]
    width = tokens.shape[1]
    cosine, sine = rotary_tables()
    wall = jnp.concatenate([paired(w_query[0]), paired(w_key[0]), padded(w_value[0])], axis=1)
    wo = padded(w_output[0].T).T
    out_weight = lax.all_gather(w_output[0], "tensor", axis=0, tiled=True)
    router = w_router[0].T
    gain_a, gain_f = gain_attn.astype(F32), gain_ffn.astype(F32)
    feed_weights = (
        w_gate_exp[0],
        w_up_exp[0],
        w_down_exp[0],
        w_gate_sh[0],
        w_up_sh[0],
        w_down_sh[0],
    )
    pos, post, starts = places(routes[0].reshape(count, SEQ_LEN, 2))
    low = first_allowed(doc_lengths)
    first_block = (low[:, ::BLOCK] // KEYS).reshape(-1)
    back_first = (low[:, ::BACK_BLOCK] // BACK_KEYS).reshape(-1)
    low_column, low_row = low[:, :, None], low[:, None, :]

    received = jnp.zeros((SEQ_LEN, width), BF16)
    attention_kept, feed_kept, results = None, None, []
    grads_kept, attention_grads_kept, inputs = None, None, []
    small = jnp.zeros((10, width), F32)

    def spread(array):
        return lax.psum_scatter(array, "dp", scatter_dimension=0, tiled=False)

    def after(meta, array):
        return lax.optimization_barrier((meta, array))

    def forward_meta(tick):
        raw = tick - section
        active = (raw >= 0) & (raw < count)
        sequence = jnp.clip(raw, 0, count - 1)
        return jnp.stack([section, jnp.where(active, sequence + 1, 0), sequence]).astype(jnp.int32)

    def backward_meta(tick):
        raw = tick - 1 + section
        active = (raw >= 0) & (raw < count)
        sequence = jnp.clip(raw, 0, count - 1)
        source = jnp.where(active, 2 - section, 0)
        return jnp.stack(
            [source, jnp.where(active, sequence + 1, 0), sequence, sequence + 1]
        ).astype(jnp.int32)

    def attend(meta, received, kept):
        return attention_forward(
            meta, first_block, tokens, received, gain_a, wall, cosine, sine, low_column, kept
        )

    def feed(meta, gathered, kept):
        return feed_forward(
            meta,
            starts,
            attention_kept[0],
            gathered,
            out_weight,
            gain_f,
            router,
            post,
            pos,
            feed_weights,
            kept,
        )

    def feed_back(meta, received):
        return feed_backward(
            meta, starts, cotangent, received, post, pos, feed_kept, feed_weights, grads_kept
        )

    def attend_back(meta, summed):
        return attention_backward(
            meta,
            back_first,
            summed,
            feed_kept,
            attention_kept,
            grads_kept[0],
            gain_f,
            router,
            wall,
            wo,
            cosine,
            sine,
            low_row,
            attention_grads_kept,
        )

    for tick in range(count):
        meta = forward_meta(tick)
        own, attention_kept = attend(meta, received, attention_kept)
        gathered = lax.all_gather(own, "tensor") if tick == 0 else tensor_gather(own, 0)
        part, feed_kept = feed(meta, gathered, feed_kept)
        result, received = output_relay(part, feed_kept[0], tick, 4 + tick)
        results.append(result)

    blank = jnp.zeros((SEQ_LEN, width), BF16)
    meta, back_meta = forward_meta(count), backward_meta(0)
    own, attention_kept = attend(meta, received, attention_kept)
    back_meta, own = after(back_meta, own)
    gathered = lax.all_gather(own, "tensor")
    part, grads_kept = feed_back(back_meta, blank)
    meta, part = after(meta, part)
    summed = lax.psum(part, "tensor")
    last_part, feed_kept = feed(meta, gathered, feed_kept)
    back_meta, last_part = after(back_meta, last_part)

    for tick in range(count + 1):
        if tick > 0:
            back_meta = backward_meta(tick)
        if tick == count:
            lead, middle = 2, 3
            lead_meta = jnp.stack(
                [2 - section, jnp.full_like(section, count - 1), jnp.full_like(section, count)]
                + [jnp.full_like(section, count - 1)]
            ).astype(jnp.int32)
            lead_part = lead_grads(
                lead,
                devices,
                lead_meta,
                cotangent,
                received,
                post,
                feed_kept,
                grads_kept,
                feed_weights[2],
            )
            back_meta, lead_part = after(back_meta, lead_part)
        if tick > 0:
            part, grads_kept = feed_back(back_meta, received)
        if tick == count:
            dy, hid, grad_gate, grad_lift, grad_expert, hid_sh, grad_gate_sh, grad_lift_sh = (
                grads_kept
            )
            picked = feed_kept[2]
            middle_part = expert_grads(
                lead, middle, 0, devices, picked, hid, grad_gate, grad_lift, grad_expert
            )
            middle_part, picked, grad_gate = lax.optimization_barrier(
                (middle_part, picked, grad_gate)
            )
            first = lead + middle
            last_grads = expert_grads(
                first,
                EXPERTS - first,
                3,
                devices,
                picked,
                hid,
                grad_gate,
                grad_lift,
                grad_expert,
            )
            last_grads = shared_grads(
                last_grads, feed_kept[1], dy, grad_gate_sh, grad_lift_sh, hid_sh
            )
            part, last_grads = lax.optimization_barrier((part, last_grads))
            parts = [spread(lead_part), spread(middle_part), spread(last_grads)]
        if tick > 0:
            summed = tensor_sum(part, 2, 7)
        (part, grad_state, gain_grad, router_grad), attention_grads_kept = attend_back(
            back_meta, summed
        )
        grad_input, received, gain_attn_grad = input_relay(
            part, attention_kept[0], grad_state, gain_a, tick, 4 + count + 1 + tick
        )
        inputs.append(grad_input)
        small = small + jnp.concatenate([gain_attn_grad, gain_grad, router_grad], axis=0)
    result, unused = output_relay(last_part, feed_kept[0], count, 4 + count)
    results.append(result)

    projections, outward = token_grads(
        [attention_kept[1], attention_grads_kept[1]], [attention_grads_kept[0], attention_kept[3]]
    )
    wide = wo.shape[0]
    rows = width // devices
    columns = w_query.shape[2]
    packed = jnp.concatenate(
        [
            2.0 * unpadded(projections[:, : 2 * wide]),
            unpadded(projections[:, 2 * wide :]),
            unpadded(outward),
            jnp.pad(small, ((0, 6), (0, 0))).T.astype(BF16),
        ],
        axis=1,
    )
    packed, *parts = lax.optimization_barrier((packed, *parts))
    packed = spread(packed.reshape(devices, rows, -1)).astype(F32)
    shared = parts[2][-3:].astype(F32)
    experts = jnp.concatenate([parts[0], parts[1], parts[2][:-3]], axis=0).astype(F32)
    experts = experts.reshape(EXPERTS, 3, rows, -1)

    def choose(items):
        return jnp.concatenate(
            [jnp.where(section == 0, items[k], items[k + 1]) for k in range(count)], axis=0
        )

    layer_out = choose(results)
    input_grad = jnp.concatenate(
        [jnp.where(section == 0, inputs[k + 1], inputs[k]) for k in range(count)], axis=0
    )
    extra = 4 * columns
    return (
        layer_out[None],
        input_grad[None],
        packed[None, :, extra],
        packed[None, :, :columns],
        packed[None, :, columns : 2 * columns],
        packed[None, :, 2 * columns : 3 * columns],
        packed[:, 3 * columns : extra].T[None],
        packed[None, :, extra + 1],
        packed[None, :, extra + 2 : extra + 10],
        experts[None, :, 0],
        experts[None, :, 1],
        jnp.swapaxes(experts[:, 2], 1, 2)[None],
        shared[None, 0],
        shared[None, 1],
        shared[2].T[None],
    )


def solution(mesh):
    return jax.shard_map(
        on_device,
        mesh=mesh,
        in_specs=(
            P("dp", None),
            P("dp", None),
            P("section", "dp", None),
            P("section", None),
            P("section", None, "tensor"),
            P("section", None, "tensor"),
            P("section", None, "tensor"),
            P("section", "tensor", None),
            P("section", None),
            P("section", None, None),
            P("section", None, None, "tensor"),
            P("section", None, None, "tensor"),
            P("section", None, "tensor", None),
            P("section", None, "tensor"),
            P("section", None, "tensor"),
            P("section", "tensor", None),
            P("dp", None),
        ),
        out_specs=(
            P("section", "dp", None),
            P("section", "dp", None),
            P("section", "dp"),
            P("section", "dp", "tensor"),
            P("section", "dp", "tensor"),
            P("section", "dp", "tensor"),
            P("section", "tensor", "dp"),
            P("section", "dp"),
            P("section", "dp", None),
            P("section", None, "dp", "tensor"),
            P("section", None, "dp", "tensor"),
            P("section", None, "tensor", "dp"),
            P("section", "dp", "tensor"),
            P("section", "dp", "tensor"),
            P("section", "tensor", "dp"),
        ),
        check_vma=False,
    )
```

```python
import functools

import jax
import jax.numpy as jnp
import numpy as np
from jax import lax
from jax.experimental import pallas as pl
from jax.experimental.pallas import tpu as pltpu
from jax.sharding import PartitionSpec as P

HEAD_DIM = 64
EXPERTS = 8
SEQ_LEN = 1536
WINDOW = 1024
CAPACITY = 480
BLOCK = 512
PACK = 256
BLOCKS = SEQ_LEN // BLOCK
KEYS = 256
BACK_BLOCK = 384
BACK_BLOCKS = SEQ_LEN // BACK_BLOCK
BACK_KEYS = 384
LANES = 128
SLOTS = 3
VMEM_BYTES = 60 * 2**20
MESH = pl.DeviceIdType.MESH
F32 = jnp.float32
BF16 = jnp.bfloat16
NT = (((1,), (1,)), ((), ()))
TN = (((0,), (0,)), ((), ()))


def shape_of(shape, dtype):
    return jax.ShapeDtypeStruct(shape, dtype)


def cost(micros):
    return pl.CostEstimate(
        flops=int(micros * 1.15e9), bytes_accessed=int(micros * 3.6e6), transcendentals=0
    )


def dot(left, right):
    return jnp.dot(left, right, preferred_element_type=F32)


def dot_nt(left, right):
    return lax.dot_general(left, right, NT, preferred_element_type=F32)


def dot_tn(left, right):
    return lax.dot_general(left, right, TN, preferred_element_type=F32)


def once(shape, index):
    return pl.BlockSpec(shape, index, pipeline_mode=pl.Buffered(1))


def loop(count, body):
    lax.fori_loop(0, count, lambda step, none: (body(step), none)[1], 0)


def rows_of(step, size):
    return pl.ds(pl.multiple_of(step * size, size), size)


def greet(partners):
    barrier = pltpu.get_barrier_semaphore()
    for partner in partners:
        pl.semaphore_signal(barrier, inc=1, device_id=partner, device_id_type=MESH)
    pl.semaphore_wait(barrier, len(partners))


def remote(source, target, send, recv, device):
    return pltpu.make_async_remote_copy(
        src_ref=source,
        dst_ref=target,
        send_sem=send,
        recv_sem=recv,
        device_id=device,
        device_id_type=MESH,
    )


def partners_of():
    place = lax.axis_index("tensor")
    core = lax.rem(place, 2)
    return {"tensor": place + 1 - 2 * core}, {"tensor": lax.rem(place + 2, 4)}


def sides(rows):
    core = lax.rem(lax.axis_index("tensor"), 2)
    half = rows // 2
    return core * half, (1 - core) * half


def piece_rows(side, step, size):
    return pl.ds(pl.multiple_of(side + step * size, 16), size)


def cross_kernel(pieces, part_ref, mine, first, kept, second, sends, recvs, loaded, use):
    near, far = partners_of()
    own, other = sides(part_ref.shape[0])
    size = mine.shape[0] // pieces
    copies = []
    for step in range(pieces):
        local = pl.ds(step * size, size)
        copies.append(
            remote(
                part_ref.at[piece_rows(other, step, size)],
                first.at[local],
                sends.at[0, step],
                recvs.at[0, step],
                near,
            )
        )
        copies[-1].start()
    load = pltpu.make_async_copy(
        part_ref.at[pl.ds(pl.multiple_of(own, 16), mine.shape[0])], mine, loaded
    )
    load.start()
    load.wait()
    for step in range(pieces):
        local = pl.ds(step * size, size)
        copies[step].wait_recv()
        kept[local, :] = (mine[local, :].astype(F32) + first[local, :].astype(F32)).astype(BF16)
        copies.append(
            remote(
                kept.at[local], second.at[local], sends.at[1, step], recvs.at[1, step], far
            )
        )
        copies[-1].start()
    for step in range(pieces):
        local = pl.ds(step * size, size)
        copies[pieces + step].wait_recv()
        use(step, local, kept[local, :].astype(F32) + second[local, :].astype(F32))
    return copies


def sum_kernel(
    pieces, part_ref, out_ref, mine, first, kept, second, done, sends, recvs, loaded, stored
):
    near, far = partners_of()
    greet([near, far])
    own, other = sides(part_ref.shape[0])
    size = mine.shape[0] // pieces
    back, local_copies = [], []

    def use(step, local, total):
        done[local, :] = total.astype(BF16)
        rows = piece_rows(own, step, size)
        back.append(
            remote(done.at[local], out_ref.at[rows], sends.at[2, step], recvs.at[2, step], near)
        )
        back[-1].start()
        local_copies.append(
            pltpu.make_async_copy(done.at[local], out_ref.at[rows], stored.at[step])
        )
        local_copies[-1].start()

    copies = cross_kernel(
        pieces, part_ref, mine, first, kept, second, sends, recvs, loaded, use
    )
    for copy in back:
        copy.wait_recv()
    for copy in copies + back:
        copy.wait_send()
    for copy in local_copies:
        copy.wait()


def tensor_sum(part, identity, pieces):
    rows, width = part.shape
    hbm = pl.BlockSpec(memory_space=pl.ANY)
    return pl.pallas_call(
        functools.partial(sum_kernel, pieces),
        out_shape=shape_of((rows, width), BF16),
        in_specs=[hbm],
        out_specs=hbm,
        scratch_shapes=[pltpu.VMEM((rows // 2, width), BF16)] * 5
        + [pltpu.SemaphoreType.DMA((3, pieces))] * 2
        + [pltpu.SemaphoreType.DMA, pltpu.SemaphoreType.DMA((pieces,))],
        compiler_params=pltpu.CompilerParams(
            collective_id=identity, has_side_effects=True, vmem_limit_bytes=VMEM_BYTES
        ),
        cost_estimate=cost(32),
        name="tensor_sum",
    )(part)


def gather_kernel(pieces, own_ref, out_ref, sends, recvs, stored):
    place = lax.axis_index("tensor")
    near, far = partners_of()
    greet([near, far])
    far_place = lax.rem(place + 2, 4)
    size = own_ref.shape[0] // pieces
    first, crossing, passed = [], [], []
    for group, copies, partner in ((0, crossing, far), (1, first, near)):
        for piece in range(pieces):
            rows = pl.ds(piece * size, size)
            copies.append(
                remote(
                    own_ref.at[rows],
                    out_ref.at[place, rows],
                    sends.at[group, piece],
                    recvs.at[group, piece],
                    partner,
                )
            )
            copies[-1].start()
    local = pltpu.make_async_copy(own_ref, out_ref.at[place], stored)
    local.start()
    for piece in range(pieces):
        rows = pl.ds(piece * size, size)
        crossing[piece].wait_recv()
        passed.append(
            remote(
                out_ref.at[far_place, rows],
                out_ref.at[far_place, rows],
                sends.at[2, piece],
                recvs.at[2, piece],
                near,
            )
        )
        passed[-1].start()
    for copy in first + passed:
        copy.wait_recv()
    for copy in first + crossing + passed:
        copy.wait_send()
    local.wait()


def tensor_gather(own, identity, pieces=6):
    hbm = pl.BlockSpec(memory_space=pl.ANY)
    return pl.pallas_call(
        functools.partial(gather_kernel, pieces),
        out_shape=shape_of((4,) + own.shape, BF16),
        in_specs=[hbm],
        out_specs=hbm,
        scratch_shapes=[pltpu.SemaphoreType.DMA((3, pieces))] * 2 + [pltpu.SemaphoreType.DMA],
        compiler_params=pltpu.CompilerParams(
            collective_id=identity, has_side_effects=True, vmem_limit_bytes=VMEM_BYTES
        ),
        cost_estimate=cost(18),
        name="tensor_gather",
    )(own)


def pass_on(step, source, rows, next_ref, sends, recvs, across):
    copy = remote(source, next_ref.at[rows], sends.at[3, step], recvs.at[3, step], across)
    copy.start()
    return copy


LAG = 3


def spread_on(step, passed, rows, next_ref, sends, recvs, near):
    passed[step].wait_recv()
    copy = remote(next_ref.at[rows], next_ref.at[rows], sends.at[4, step], recvs.at[4, step], near)
    copy.start()
    return copy


def output_kernel(
    pieces,
    tick,
    part_ref,
    states_ref,
    out_ref,
    next_ref,
    mine,
    first,
    kept,
    second,
    done,
    state,
    sends,
    recvs,
    loaded,
    state_loaded,
    stored,
):
    near, far = partners_of()
    section = lax.axis_index("section")
    across = {"section": 1 - section}
    slot = lax.rem(tick + 1 - section, states_ref.shape[0])
    own, other = sides(part_ref.shape[0])
    size = mine.shape[0] // pieces
    load = pltpu.make_async_copy(
        states_ref.at[slot, pl.ds(pl.multiple_of(own, 16), mine.shape[0])], state, state_loaded
    )
    load.start()
    greet([near, far, across])
    back, passed, spread, local_copies = [], [], [], []

    def forward(step):
        rows = piece_rows(own, step, size)
        spread.append(spread_on(step, passed, rows, next_ref, sends, recvs, near))

    def use(step, local, total):
        if step == 0:
            load.wait()
        done[local, :] = (state[local, :] + total.astype(BF16).astype(F32)).astype(BF16)
        rows = piece_rows(own, step, size)
        passed.append(pass_on(step, done.at[local], rows, next_ref, sends, recvs, across))
        back.append(
            remote(done.at[local], out_ref.at[rows], sends.at[2, step], recvs.at[2, step], near)
        )
        back[-1].start()
        local_copies.append(
            pltpu.make_async_copy(done.at[local], out_ref.at[rows], stored.at[step])
        )
        local_copies[-1].start()
        if step >= LAG:
            forward(step - LAG)

    copies = cross_kernel(
        pieces, part_ref, mine, first, kept, second, sends, recvs, loaded, use
    )
    for step in range(pieces - LAG, pieces):
        forward(step)
    for copy in back + spread:
        copy.wait_recv()
    for copy in copies + back + passed + spread:
        copy.wait_send()
    for copy in local_copies:
        copy.wait()


def output_relay(part, states, tick, identity, pieces=16):
    rows, width = part.shape
    hbm = pl.BlockSpec(memory_space=pl.ANY)
    return pl.pallas_call(
        functools.partial(output_kernel, pieces, tick),
        out_shape=[shape_of((rows, width), BF16)] * 2,
        in_specs=[hbm] * 2,
        out_specs=[hbm] * 2,
        scratch_shapes=[pltpu.VMEM((rows // 2, width), BF16)] * 5
        + [pltpu.VMEM((rows // 2, width), F32)]
        + [pltpu.SemaphoreType.DMA((5, pieces))] * 2
        + [pltpu.SemaphoreType.DMA] * 2
        + [pltpu.SemaphoreType.DMA((pieces,))],
        compiler_params=pltpu.CompilerParams(
            collective_id=identity, has_side_effects=True, vmem_limit_bytes=VMEM_BYTES
        ),
        cost_estimate=cost(38),
        name="output_relay",
    )(part, states)


def input_kernel(
    pieces,
    tick,
    part_ref,
    layers_ref,
    grad_state_ref,
    gain_ref,
    grad_ref,
    next_ref,
    grad_gain_ref,
    mine,
    first,
    kept,
    second,
    given,
    full,
    layer_in,
    grad_state,
    grad,
    gains,
    sends,
    recvs,
    loaded,
    inputs_loaded,
    stored,
):
    near, far = partners_of()
    section = lax.axis_index("section")
    across = {"section": 1 - section}
    slot = lax.rem(tick + section, layers_ref.shape[0])
    rows = part_ref.shape[0]
    own, other = sides(rows)
    half = rows // 2
    size = half // pieces
    loads = []
    for side, start in ((0, own), (1, other)):
        there = pl.ds(pl.multiple_of(start, 16), half)
        loads.append(
            [
                pltpu.make_async_copy(
                    layers_ref.at[slot, there], layer_in.at[there], inputs_loaded.at[side, 0]
                ),
                pltpu.make_async_copy(
                    grad_state_ref.at[there], grad_state.at[there], inputs_loaded.at[side, 1]
                ),
            ]
        )
        for load in loads[-1]:
            load.start()
    greet([near, far, across])
    gains[...] = jnp.zeros_like(gains)
    back, passed, spread, local_copies = [], [], [], []

    def rows_back(here, side, step):
        grad_normed = full[here, :].astype(F32)
        values = layer_in[here, :].astype(F32)
        scale = lax.rsqrt(jnp.mean(values * values, axis=-1, keepdims=True) + 1e-06)
        normed = values * scale
        scaled = gain_ref[...] * grad_normed
        inner = jnp.mean(normed * scaled, axis=-1, keepdims=True)
        result = grad_state[here, :] + scale * (scaled - normed * inner)
        grad[here, :] = result
        gains[side : side + 1, :] += jnp.sum(grad_normed * normed, axis=0, keepdims=True)
        local_copies.append(
            pltpu.make_async_copy(grad.at[here], grad_ref.at[here], stored.at[side, step])
        )
        local_copies[-1].start()
        return result

    def partner_rows(step):
        if step == 0:
            for load in loads[1]:
                load.wait()
        back[step].wait_recv()
        rows_back(piece_rows(other, step, size), 1, step)

    def forward(step):
        here = piece_rows(own, step, size)
        spread.append(spread_on(step, passed, here, next_ref, sends, recvs, near))

    def use(step, local, total):
        if step == 0:
            for load in loads[0]:
                load.wait()
        here = piece_rows(own, step, size)
        full[here, :] = total.astype(BF16)
        back.append(
            remote(full.at[here], full.at[here], sends.at[2, step], recvs.at[2, step], near)
        )
        back[-1].start()
        given[local, :] = rows_back(here, 0, step).astype(BF16)
        passed.append(pass_on(step, given.at[local], here, next_ref, sends, recvs, across))
        if step > 0:
            partner_rows(step - 1)
        if step >= LAG:
            forward(step - LAG)

    copies = cross_kernel(
        pieces, part_ref, mine, first, kept, second, sends, recvs, loaded, use
    )
    partner_rows(pieces - 1)
    for step in range(pieces - LAG, pieces):
        forward(step)
    grad_gain_ref[...] = gains[0:1, :] + gains[1:2, :]
    for copy in spread:
        copy.wait_recv()
    for copy in copies + back + passed + spread:
        copy.wait_send()
    for copy in local_copies:
        copy.wait()


def input_relay(part, layers, grad_state, gain, tick, identity, pieces=16):
    rows, width = part.shape
    hbm = pl.BlockSpec(memory_space=pl.ANY)
    whole = pl.BlockSpec(memory_space=pltpu.VMEM)
    return pl.pallas_call(
        functools.partial(input_kernel, pieces, tick),
        out_shape=[
            shape_of((rows, width), F32),
            shape_of((rows, width), BF16),
            shape_of((1, width), F32),
        ],
        in_specs=[hbm] * 3 + [whole],
        out_specs=[hbm] * 2 + [whole],
        scratch_shapes=[pltpu.VMEM((rows // 2, width), BF16)] * 5
        + [pltpu.VMEM((rows, width), BF16)] * 2
        + [pltpu.VMEM((rows, width), F32)] * 2
        + [pltpu.VMEM((8, width), F32)]
        + [pltpu.SemaphoreType.DMA((5, pieces))] * 2
        + [pltpu.SemaphoreType.DMA]
        + [pltpu.SemaphoreType.DMA((2, 2)), pltpu.SemaphoreType.DMA((2, pieces))],
        compiler_params=pltpu.CompilerParams(
            collective_id=identity, has_side_effects=True, vmem_limit_bytes=VMEM_BYTES
        ),
        cost_estimate=cost(42),
        name="input_relay",
    )(part, layers, grad_state, gain)


def attention_forward_kernel(
    stored,
    meta,
    first_block,
    tok_ref,
    rec_ref,
    gain_ref,
    wall_ref,
    cos_ref,
    sin_ref,
    low_ref,
    *rest,
):
    rest = rest[stored:]
    packed_ref, x_ref, a_ref, qkv_ref, o_ref, lse_ref = rest[:6]
    keys, values, scores, tops, sums, mixed = rest[6:]
    index = pl.program_id(0)
    heads = wall_ref.shape[1] // (3 * LANES)
    wide = heads * LANES
    x = jnp.where(meta[0] == 0, tok_ref[...], rec_ref[...])
    x_ref[0] = x
    x = x.astype(F32)
    normed = gain_ref[...] * x * lax.rsqrt(jnp.mean(x * x, axis=-1, keepdims=True) + 1e-06)
    normed = normed.astype(BF16)
    a_ref[0] = normed
    cosine, sine = cos_ref[...], sin_ref[...]
    here = rows_of(index, BLOCK)
    projected = dot(normed, wall_ref[...])
    for group in range(2 * heads):
        columns = slice(group * LANES, (group + 1) * LANES)
        pre = projected[:, columns]
        turned = pre * cosine + pltpu.roll(pre, HEAD_DIM, 1) * sine
        if group < heads:
            turned = turned * 0.0625
        qkv_ref[0, :, columns] = turned.astype(BF16)
    qkv_ref[0, :, 2 * wide :] = projected[:, 2 * wide :].astype(BF16)
    keys[here, :] = qkv_ref[0, :, wide : 2 * wide]
    low = low_ref[0]
    query_at = index * BLOCK + lax.broadcasted_iota(jnp.int32, (BLOCK, KEYS), 0)
    key_at = lax.broadcasted_iota(jnp.int32, (BLOCK, KEYS), 1)

    @pl.when(index * BLOCK % KEYS == 0)
    def _():
        values[rows_of(index * BLOCK // KEYS, KEYS), :] = jnp.zeros((KEYS, wide), BF16)

    values[here, :] = qkv_ref[0, :, 2 * wide :]
    tops[...] = jnp.full_like(tops, -1e30)
    sums[...] = jnp.zeros_like(sums)
    mixed[...] = jnp.zeros_like(mixed)
    begin = first_block[meta[2] * BLOCKS + index]

    def score(block, none):
        at = key_at + block * KEYS
        valid = (at >= low) & (at <= query_at)
        there = rows_of(block, KEYS)
        for head in range(heads):
            columns = slice(head * LANES, (head + 1) * LANES)
            raw = dot_nt(qkv_ref[0, :, columns], keys[there, columns])
            raw = jnp.where(valid, raw, -1e30)
            scores[head, block] = raw
            best = tops[head]
            for start in range(0, KEYS, LANES):
                best = jnp.maximum(best, raw[:, start : start + LANES])
            tops[head] = best
        return none

    end = ((index + 1) * BLOCK - 1) // KEYS + 1
    lax.fori_loop(begin, end, score, 0)
    top = [jnp.max(tops[head], axis=1, keepdims=True) for head in range(heads)]

    def mix(block, none):
        there = rows_of(block, KEYS)
        for head in range(heads):
            columns = slice(head * LANES, (head + 1) * LANES)
            weights = jnp.exp(scores[head, block] - top[head])
            part = weights[:, :LANES]
            for start in range(LANES, KEYS, LANES):
                part = part + weights[:, start : start + LANES]
            sums[head] += part
            mixed[:, columns] += dot(weights.astype(BF16), values[there, columns])
        return none

    lax.fori_loop(begin, end, mix, 0)
    for head in range(heads):
        columns = slice(head * LANES, (head + 1) * LANES)
        total = jnp.sum(sums[head], axis=1, keepdims=True)
        o_ref[0, :, columns] = (mixed[:, columns] / total).astype(BF16)
        logsum = jnp.broadcast_to(top[head] + jnp.log(total), (BLOCK, LANES))
        lse_ref[0, head : head + 1, :] = logsum.T[0:1, :]
    half = PACK // 2
    for start in range(0, BLOCK, PACK):
        packed_ref[start // 2 : start // 2 + half, :] = jnp.concatenate(
            [
                o_ref[
                    0,
                    start + side * half : start + (side + 1) * half,
                    head * LANES : head * LANES + HEAD_DIM,
                ]
                for side in range(2)
                for head in range(heads)
            ],
            axis=1,
        )


def attention_forward(meta, first_block, tokens, received, gain, wall, cosine, sine, low, kept):
    width = tokens.shape[1]
    wide = wall.shape[1] // 3
    heads = wide // LANES
    stored = 0 if kept is None else 5
    saved = [
        shape_of((SLOTS, SEQ_LEN, width), BF16),
        shape_of((SLOTS, SEQ_LEN, width), BF16),
        shape_of((SLOTS, SEQ_LEN, 3 * wide), BF16),
        shape_of((SLOTS, SEQ_LEN, wide), BF16),
        shape_of((SLOTS, 8, SEQ_LEN), F32),
    ]

    def slot_rows(columns):
        return pl.BlockSpec((1, BLOCK, columns), lambda i, m, f: (m[1], i, 0))

    grid_spec = pltpu.PrefetchScalarGridSpec(
        num_scalar_prefetch=2,
        grid=(BLOCKS,),
        in_specs=[
            pl.BlockSpec((BLOCK, width), lambda i, m, f: (m[2] * BLOCKS + i, 0)),
            pl.BlockSpec((BLOCK, width), lambda i, m, f: (i, 0)),
            once((1, width), lambda i, m, f: (0, 0)),
            once(wall.shape, lambda i, m, f: (0, 0)),
            pl.BlockSpec((BLOCK, LANES), lambda i, m, f: (i, 0)),
            pl.BlockSpec((BLOCK, LANES), lambda i, m, f: (i, 0)),
            pl.BlockSpec((1, BLOCK, 1), lambda i, m, f: (m[2], i, 0)),
        ]
        + [pl.BlockSpec(memory_space=pl.ANY)] * stored,
        out_specs=[
            pl.BlockSpec((BLOCK // 2, wide), lambda i, m, f: (i, 0)),
            slot_rows(width),
            slot_rows(width),
            slot_rows(3 * wide),
            slot_rows(wide),
            pl.BlockSpec((1, 8, BLOCK), lambda i, m, f: (m[1], 0, i)),
        ],
        scratch_shapes=[
            pltpu.VMEM((SEQ_LEN, wide), BF16),
            pltpu.VMEM((SEQ_LEN, wide), BF16),
            pltpu.VMEM((heads, SEQ_LEN // KEYS, BLOCK, KEYS), F32),
            pltpu.VMEM((heads, BLOCK, LANES), F32),
            pltpu.VMEM((heads, BLOCK, LANES), F32),
            pltpu.VMEM((BLOCK, wide), F32),
        ],
    )
    outs = pl.pallas_call(
        functools.partial(attention_forward_kernel, stored),
        grid_spec=grid_spec,
        out_shape=[shape_of((SEQ_LEN // 2, wide), BF16)] + saved,
        input_output_aliases={9 + k: 1 + k for k in range(stored)},
        compiler_params=pltpu.CompilerParams(vmem_limit_bytes=VMEM_BYTES),
        cost_estimate=cost(24),
        name="attention_forward",
    )(
        meta,
        first_block,
        tokens,
        received,
        gain,
        wall,
        cosine,
        sine,
        low,
        *(kept or ()),
    )
    return outs[0], outs[1:]


def touch_kernel(*refs):
    outs, zeros, semaphores = refs[:-2], refs[-2], refs[-1]
    zeros[...] = jnp.zeros_like(zeros)
    copies = []
    for out in outs:
        if out.dtype != BF16 or out.shape[-1] > zeros.shape[-1]:
            continue
        source = zeros.at[:, : out.shape[-1]]
        for slot in range(out.shape[0]):
            if len(out.shape) == 3:
                places = [out.at[slot, row : row + 16] for row in range(0, out.shape[1], 512)]
            else:
                places = [out.at[slot, step, 0:16] for step in range(0, out.shape[1], 2)]
            for place in places:
                copies.append(pltpu.make_async_copy(source, place, semaphores.at[len(copies)]))
    for copy in copies:
        copy.start()
    for copy in copies:
        copy.wait()


def reserve(shapes):
    width = max(shape.shape[-1] for shape in shapes if shape.dtype == BF16)
    return pl.pallas_call(
        touch_kernel,
        out_shape=shapes,
        out_specs=[pl.BlockSpec(memory_space=pl.ANY)] * len(shapes),
        scratch_shapes=[pltpu.VMEM((16, width), BF16), pltpu.SemaphoreType.DMA((128,))],
        compiler_params=pltpu.CompilerParams(has_side_effects=True),
        cost_estimate=cost(3),
        name="reserve",
    )()


PAIR = 2
ROWS = 512
ROW_STEPS = SEQ_LEN // ROWS
PAIR_STEPS = EXPERTS // PAIR
SPAN = 512
CHUNK = 96


def build_pick(first, chunks, post_ref, probs, pick, gates):
    for which, step in chunks:
        row = pl.ds(first + which, 1)
        slot_at = step * CHUNK + lax.broadcasted_iota(jnp.int32, (CHUNK, SEQ_LEN), 0)
        here = slot_at == post_ref[0, row, :]
        rows = slice(which * CAPACITY + step * CHUNK, which * CAPACITY + (step + 1) * CHUNK)
        pick[rows, :] = jnp.where(here, 1.0, 0.0).astype(BF16)
        if probs is not None:
            chosen = jnp.sum(jnp.where(here, probs[row, :], 0.0), axis=1, keepdims=True)
            gates[rows, :] = jnp.broadcast_to(chosen, (CHUNK, LANES))


def build_gates(first, post_ref, probs, gates):
    for which in range(PAIR):
        row = pl.ds(first + which, 1)
        for step in range(CAPACITY // CHUNK):
            slot_at = step * CHUNK + lax.broadcasted_iota(jnp.int32, (CHUNK, SEQ_LEN), 0)
            here = slot_at == post_ref[0, row, :]
            rows = slice(which * CAPACITY + step * CHUNK, which * CAPACITY + (step + 1) * CHUNK)
            chosen = jnp.sum(jnp.where(here, probs[row, :], 0.0), axis=1, keepdims=True)
            gates[rows, :] = jnp.broadcast_to(chosen, (CHUNK, LANES))


WINDOW_SLOTS = 256


def is_narrow(starts, sequence):
    return starts[starts.shape[0] - SLOTS + 1 + sequence] > 0


def window_at(starts, sequence, expert, chunk):
    place = starts[(sequence * EXPERTS + expert) * (ROW_STEPS + 1) + chunk]
    return jnp.minimum(place // 16 * 16, SPAN - WINDOW_SLOTS)


def chunk_rows(chunk):
    return pl.ds(chunk * ROWS, ROWS)


def token_places(expert, rows, pos_ref):
    places = pos_ref[0, rows, :]
    lane = lax.broadcasted_iota(jnp.int32, places.shape, 1)
    return jnp.sum(jnp.where(lane == expert, places, 0), axis=1, keepdims=True)


def build_put(starts, sequence, pair, chunk, pos_ref, put):
    rows = chunk_rows(chunk)
    slot_at = lax.broadcasted_iota(jnp.int32, (ROWS, WINDOW_SLOTS), 1)
    for which in range(PAIR):
        expert = pair * PAIR + which
        begin = jnp.where(
            is_narrow(starts, sequence), window_at(starts, sequence, expert, chunk), -SEQ_LEN
        )
        put[rows, which * WINDOW_SLOTS : (which + 1) * WINDOW_SLOTS] = jnp.where(
            slot_at == token_places(expert, rows, pos_ref) - begin, 1.0, 0.0
        ).astype(BF16)


def put_back(starts, sequence, pair, chunk, put, slots, window):
    for which in range(PAIR):
        begin = window_at(starts, sequence, pair * PAIR + which, chunk)
        there = pl.ds(pl.multiple_of(which * SPAN + begin, 16), WINDOW_SLOTS)
        window[which * WINDOW_SLOTS : (which + 1) * WINDOW_SLOTS, :] = slots[there, :]
    return dot(put[chunk_rows(chunk), : PAIR * WINDOW_SLOTS], window[...])


def put_back_wide(pair, pos_ref, put, slots, total):
    def body(step):
        which, chunk = step // ROW_STEPS, step % ROW_STEPS
        rows = rows_of(chunk, ROWS)
        slot_at = lax.broadcasted_iota(jnp.int32, (ROWS, SPAN), 1)
        place = token_places(pair * PAIR + which, rows, pos_ref)
        put[rows, SPAN:] = jnp.where(slot_at == place, 1.0, 0.0).astype(BF16)
        total[rows, :] += dot(put[rows, SPAN:], slots[rows_of(which, SPAN), :])

    loop(PAIR * ROW_STEPS, body)


ALL_CHUNKS = [(which, step) for which in range(PAIR) for step in range(CAPACITY // CHUNK)]


def of_pair(which):
    return slice(which * CAPACITY, (which + 1) * CAPACITY)


def feed_forward_kernel(
    stored,
    meta,
    starts,
    x_ref,
    ag_ref,
    wo_ref,
    gain_ref,
    router_ref,
    post_ref,
    pos_ref,
    wg_ref,
    wu_ref,
    wd_ref,
    wgs_ref,
    wus_ref,
    wds_ref,
    *rest,
):
    rest = rest[stored:]
    part_ref, h_ref, b_ref, xe_ref, g_ref, u_ref, gs_ref, us_ref, probs_ref = rest[:9]
    total, normed, probs, pick, put, gates, scaled, window = rest[9:]
    step = pl.program_id(0)
    pair = jnp.maximum(step - ROW_STEPS, 0)

    def activate(gate, lift, gate_out, lift_out):
        gate_out[...] = gate.astype(BF16)
        lift_out[...] = lift.astype(BF16)
        return (gate / (1.0 + jnp.exp(-gate)) * lift).astype(BF16)

    @pl.when(step < ROW_STEPS)
    def _():
        half = PACK // 2
        columns = ag_ref.shape[2] // 2
        mixed = jnp.concatenate(
            [
                jnp.concatenate(
                    [
                        ag_ref[device, block : block + half, side * columns : (side + 1) * columns]
                        for device in range(4)
                    ],
                    axis=1,
                )
                for block in range(0, ROWS // 2, half)
                for side in range(2)
            ],
            axis=0,
        )
        state = x_ref[0].astype(F32) + dot(mixed, wo_ref[...])
        h_ref[0] = state
        scale = lax.rsqrt(jnp.mean(state * state, axis=-1, keepdims=True) + 1e-06)
        b = (gain_ref[...] * state * scale).astype(BF16)
        b_ref[0] = b
        here = rows_of(step, ROWS)
        normed[here, :] = b
        logits = dot_nt(router_ref[...], b)
        weights = jnp.exp(logits - jnp.max(logits, axis=0, keepdims=True))
        weights = weights / jnp.sum(weights, axis=0, keepdims=True)
        probs_ref[0] = weights
        probs[:, here] = weights
        hidden = activate(dot(b, wgs_ref[...]), dot(b, wus_ref[...]), gs_ref.at[0], us_ref.at[0])
        total[here, :] = dot(hidden, wds_ref[...])

    @pl.when(step == 0)
    def _():
        build_pick(0, ALL_CHUNKS, post_ref, None, pick, gates)
        scaled[...] = jnp.zeros_like(scaled)
        put[:, : PAIR * WINDOW_SLOTS] = jnp.zeros((SEQ_LEN, PAIR * WINDOW_SLOTS), BF16)

    before = jnp.maximum(pair - 1, 0)

    @pl.when((step > ROW_STEPS) & jnp.logical_not(is_narrow(starts, meta[2])))
    def _():
        put_back_wide(before, pos_ref, put, scaled, total)

    @pl.when(step == ROW_STEPS + PAIR_STEPS)
    def _():
        for chunk in range(ROW_STEPS):
            rows = chunk_rows(chunk)
            values = put_back(starts, meta[2], before, chunk, put, scaled, window)
            part_ref[rows, :] = (total[rows, :] + values).astype(BF16)

    @pl.when((step >= ROW_STEPS) & (step < ROW_STEPS + PAIR_STEPS))
    def _():
        for chunk in range(ROW_STEPS):
            total[chunk_rows(chunk), :] += put_back(
                starts, meta[2], before, chunk, put, scaled, window
            )
            build_put(starts, meta[2], pair, chunk, pos_ref, put)
        picked = dot(pick[...], normed[...]).astype(BF16)
        build_gates(pair * PAIR, post_ref, probs, gates)
        build_pick(
            jnp.minimum(pair + 1, PAIR_STEPS - 1) * PAIR, ALL_CHUNKS, post_ref, None, pick, gates
        )
        for which in range(PAIR):
            rows = picked[of_pair(which), :]
            xe_ref[0, which] = rows
            hidden = activate(
                dot(rows, wg_ref[which]), dot(rows, wu_ref[which]), g_ref.at[0, which], u_ref.at[0, which]
            )
            scaled[which * SPAN : which * SPAN + CAPACITY, :] = (
                dot(hidden, wd_ref[which]) * gates[of_pair(which), 0:1]
            ).astype(BF16)


def step_specs():
    def row_at(step):
        return jnp.minimum(step, ROW_STEPS - 1)

    def pair_at(step):
        return jnp.clip(step - ROW_STEPS, 0, PAIR_STEPS - 1)

    return row_at, pair_at


def feed_forward(
    meta, starts, layer_in, gathered, out_weight, gain, router, post, pos, weights, kept
):
    width = layer_in.shape[2]
    wg, wu, wd, wgs, wus, wds = weights
    hidden = wg.shape[2]
    stored = 8
    saved = [
        shape_of((SLOTS, SEQ_LEN, width), F32),
        shape_of((SLOTS, SEQ_LEN, width), BF16),
        shape_of((SLOTS, EXPERTS, CAPACITY, width), BF16),
        shape_of((SLOTS, EXPERTS, CAPACITY, hidden), BF16),
        shape_of((SLOTS, EXPERTS, CAPACITY, hidden), BF16),
        shape_of((SLOTS, SEQ_LEN, hidden), BF16),
        shape_of((SLOTS, SEQ_LEN, hidden), BF16),
        shape_of((SLOTS, EXPERTS, SEQ_LEN), F32),
    ]
    row_at, pair_at = step_specs()

    def slot_rows(columns):
        return pl.BlockSpec((1, ROWS, columns), lambda s, m, f: (m[1], row_at(s), 0))

    def slot_pair(columns):
        return pl.BlockSpec((1, PAIR, CAPACITY, columns), lambda s, m, f: (m[1], pair_at(s), 0, 0))

    def fixed(shape):
        return once(shape, lambda s, m, f: (0,) * len(shape))

    def of_pairs(array):
        return pl.BlockSpec((PAIR,) + array.shape[1:], lambda s, m, f: (pair_at(s), 0, 0))

    grid_spec = pltpu.PrefetchScalarGridSpec(
        num_scalar_prefetch=2,
        grid=(ROW_STEPS + PAIR_STEPS + 1,),
        in_specs=[
            slot_rows(width),
            pl.BlockSpec((4, ROWS // 2, gathered.shape[2]), lambda s, m, f: (0, row_at(s), 0)),
            fixed(out_weight.shape),
            fixed(gain.shape),
            fixed(router.shape),
            once((1, EXPERTS, SEQ_LEN), lambda s, m, f: (m[2], 0, 0)),
            once((1, SEQ_LEN, EXPERTS), lambda s, m, f: (m[2], 0, 0)),
            of_pairs(wg),
            of_pairs(wu),
            of_pairs(wd),
            fixed(wgs.shape),
            fixed(wus.shape),
            fixed(wds.shape),
        ]
        + [pl.BlockSpec(memory_space=pl.ANY)] * stored,
        out_specs=[
            fixed((SEQ_LEN, width)),
            slot_rows(width),
            slot_rows(width),
            slot_pair(width),
            slot_pair(hidden),
            slot_pair(hidden),
            slot_rows(hidden),
            slot_rows(hidden),
            pl.BlockSpec((1, EXPERTS, ROWS), lambda s, m, f: (m[1], 0, row_at(s))),
        ],
        scratch_shapes=[
            pltpu.VMEM((SEQ_LEN, width), F32),
            pltpu.VMEM((SEQ_LEN, width), BF16),
            pltpu.VMEM((EXPERTS, SEQ_LEN), F32),
            pltpu.VMEM((PAIR * CAPACITY, SEQ_LEN), BF16),
            pltpu.VMEM((SEQ_LEN, PAIR * SPAN), BF16),
            pltpu.VMEM((PAIR * CAPACITY, LANES), F32),
            pltpu.VMEM((PAIR * SPAN, width), BF16),
            pltpu.VMEM((PAIR * WINDOW_SLOTS, width), BF16),
        ],
    )
    outs = pl.pallas_call(
        functools.partial(feed_forward_kernel, stored),
        grid_spec=grid_spec,
        out_shape=[shape_of((SEQ_LEN, width), BF16)] + saved,
        input_output_aliases={15 + k: 1 + k for k in range(stored)},
        compiler_params=pltpu.CompilerParams(vmem_limit_bytes=VMEM_BYTES),
        cost_estimate=cost(56),
        name="feed_forward",
    )(
        meta,
        starts,
        layer_in,
        gathered,
        out_weight,
        gain,
        router,
        post,
        pos,
        wg,
        wu,
        wd,
        wgs,
        wus,
        wds,
        *(reserve(saved) if kept is None else kept),
    )
    return outs[0], outs[1:]


def pull(grad, weight, gate, lift):
    gate, lift = gate.astype(F32), lift.astype(F32)
    sigma = 1.0 / (1.0 + jnp.exp(-gate))
    swish = gate * sigma
    hidden = (swish * lift).astype(BF16)
    inner = None
    if weight is not None:
        inner = jnp.sum(hidden.astype(F32) * grad, axis=1, keepdims=True)
        grad = grad * weight
    grad_gate = (grad * lift * (sigma + swish * (1.0 - sigma))).astype(BF16)
    return hidden, grad_gate, (grad * swish).astype(BF16), inner


def feed_backward_kernel(
    stored,
    meta,
    starts,
    cot_ref,
    rec_ref,
    post_ref,
    pos_ref,
    g_ref,
    u_ref,
    gs_ref,
    us_ref,
    probs_ref,
    wg_ref,
    wu_ref,
    wd_ref,
    wgs_ref,
    wus_ref,
    wds_ref,
    *rest,
):
    rest = rest[stored:]
    part_ref, dy_ref, hid_ref, dg_ref, du_ref, de_ref, hids_ref, dgs_ref, dus_ref = rest[:9]
    total, given, pick, put, gates, slots, choice, window = rest[9:]
    step = pl.program_id(0)
    pair = jnp.maximum(step - ROW_STEPS, 0)

    @pl.when(step < ROW_STEPS)
    def _():
        dy = jnp.where(meta[0] == 1, cot_ref[...], rec_ref[...])
        dy = jnp.where(meta[0] == 0, jnp.zeros_like(dy), dy)
        dy_ref[0] = dy
        here = rows_of(step, ROWS)
        given[here, :] = dy
        hidden, grad_gate, grad_lift, unused = pull(
            dot_nt(dy, wds_ref[...]), None, gs_ref[0], us_ref[0]
        )
        hids_ref[0] = hidden
        dgs_ref[0] = grad_gate
        dus_ref[0] = grad_lift
        total[here, :] = dot_nt(grad_gate, wgs_ref[...]) + dot_nt(grad_lift, wus_ref[...])

    @pl.when(step == 0)
    def _():
        build_pick(0, ALL_CHUNKS, post_ref, None, pick, gates)
        slots[...] = jnp.zeros_like(slots)
        put[:, : PAIR * WINDOW_SLOTS] = jnp.zeros((SEQ_LEN, PAIR * WINDOW_SLOTS), BF16)

    before = jnp.maximum(pair - 1, 0)

    @pl.when((step > ROW_STEPS) & jnp.logical_not(is_narrow(starts, meta[2])))
    def _():
        put_back_wide(before, pos_ref, put, slots, total)

    @pl.when(step == ROW_STEPS + PAIR_STEPS)
    def _():
        for chunk in range(ROW_STEPS):
            rows = chunk_rows(chunk)
            values = put_back(starts, meta[2], before, chunk, put, slots, window)
            part_ref[rows, :] = (total[rows, :] + values).astype(BF16)

    @pl.when((step >= ROW_STEPS) & (step < ROW_STEPS + PAIR_STEPS))
    def _():
        for chunk in range(ROW_STEPS):
            total[chunk_rows(chunk), :] += put_back(
                starts, meta[2], before, chunk, put, slots, window
            )
            build_put(starts, meta[2], pair, chunk, pos_ref, put)
        picked = dot(pick[...], given[...]).astype(BF16)
        build_gates(pair * PAIR, post_ref, probs_ref.at[0], gates)
        build_pick(
            jnp.minimum(pair + 1, PAIR_STEPS - 1) * PAIR, ALL_CHUNKS, post_ref, None, pick, gates
        )
        for which in range(PAIR):
            rows = picked[of_pair(which), :]
            weight = gates[of_pair(which), 0:1]
            hidden, grad_gate, grad_lift, inner = pull(
                dot_nt(rows, wd_ref[which]), weight, g_ref[0, which], u_ref[0, which]
            )
            hid_ref[0, which] = hidden
            dg_ref[0, which] = grad_gate
            du_ref[0, which] = grad_lift
            de_ref[0, which] = (weight * rows.astype(F32)).astype(BF16)
            row = pl.ds(pair * PAIR + which, 1)
            chosen = jnp.zeros((1, SEQ_LEN), F32)
            for chunk in range(CAPACITY // CHUNK):
                slot_at = chunk * CHUNK + lax.broadcasted_iota(jnp.int32, (CHUNK, SEQ_LEN), 0)
                here = slot_at == post_ref[0, row, :]
                chosen += jnp.sum(
                    jnp.where(here, inner[chunk * CHUNK : (chunk + 1) * CHUNK], 0.0),
                    axis=0,
                    keepdims=True,
                )
            choice[row, :] = chosen
            slots[which * SPAN : which * SPAN + CAPACITY, :] = (
                dot_nt(grad_gate, wg_ref[which]) + dot_nt(grad_lift, wu_ref[which])
            ).astype(BF16)

    @pl.when(step == ROW_STEPS + PAIR_STEPS)
    def _():
        half = SEQ_LEN // 2
        blank = jnp.zeros((8, half), F32)
        part_ref[SEQ_LEN:, :] = jnp.concatenate(
            [choice[:, :half], blank, choice[:, half:], blank], axis=0
        ).astype(BF16)


def feed_backward(meta, starts, cotangent, received, post, pos, forward_kept, weights, kept):
    width = cotangent.shape[1]
    wg, wu, wd, wgs, wus, wds = weights
    hidden = wg.shape[2]
    stored = 8
    unused_h, unused_b, unused_x, gate, lift, gate_sh, lift_sh, probs = forward_kept
    saved = [
        shape_of((SLOTS, SEQ_LEN, width), BF16),
        shape_of((SLOTS, EXPERTS, CAPACITY, hidden), BF16),
        shape_of((SLOTS, EXPERTS, CAPACITY, hidden), BF16),
        shape_of((SLOTS, EXPERTS, CAPACITY, hidden), BF16),
        shape_of((SLOTS, EXPERTS, CAPACITY, width), BF16),
        shape_of((SLOTS, SEQ_LEN, hidden), BF16),
        shape_of((SLOTS, SEQ_LEN, hidden), BF16),
        shape_of((SLOTS, SEQ_LEN, hidden), BF16),
    ]
    row_at, pair_at = step_specs()

    def slot_rows(columns, which):
        return pl.BlockSpec((1, ROWS, columns), lambda s, m, f: (m[which], row_at(s), 0))

    def slot_pair(columns, which):
        return pl.BlockSpec(
            (1, PAIR, CAPACITY, columns), lambda s, m, f: (m[which], pair_at(s), 0, 0)
        )

    def fixed(shape):
        return once(shape, lambda s, m, f: (0,) * len(shape))

    def of_pairs(array):
        return pl.BlockSpec((PAIR,) + array.shape[1:], lambda s, m, f: (pair_at(s), 0, 0))

    grid_spec = pltpu.PrefetchScalarGridSpec(
        num_scalar_prefetch=2,
        grid=(ROW_STEPS + PAIR_STEPS + 1,),
        in_specs=[
            pl.BlockSpec((ROWS, width), lambda s, m, f: (m[2] * ROW_STEPS + row_at(s), 0)),
            pl.BlockSpec((ROWS, width), lambda s, m, f: (row_at(s), 0)),
            once((1, EXPERTS, SEQ_LEN), lambda s, m, f: (m[2], 0, 0)),
            once((1, SEQ_LEN, EXPERTS), lambda s, m, f: (m[2], 0, 0)),
            slot_pair(hidden, 3),
            slot_pair(hidden, 3),
            slot_rows(hidden, 3),
            slot_rows(hidden, 3),
            once((1, EXPERTS, SEQ_LEN), lambda s, m, f: (m[3], 0, 0)),
            of_pairs(wg),
            of_pairs(wu),
            of_pairs(wd),
            fixed(wgs.shape),
            fixed(wus.shape),
            fixed(wds.shape),
        ]
        + [pl.BlockSpec(memory_space=pl.ANY)] * stored,
        out_specs=[
            fixed((SEQ_LEN + 32, width)),
            slot_rows(width, 1),
            slot_pair(hidden, 1),
            slot_pair(hidden, 1),
            slot_pair(hidden, 1),
            slot_pair(width, 1),
            slot_rows(hidden, 1),
            slot_rows(hidden, 1),
            slot_rows(hidden, 1),
        ],
        scratch_shapes=[
            pltpu.VMEM((SEQ_LEN, width), F32),
            pltpu.VMEM((SEQ_LEN, width), BF16),
            pltpu.VMEM((PAIR * CAPACITY, SEQ_LEN), BF16),
            pltpu.VMEM((SEQ_LEN, PAIR * SPAN), BF16),
            pltpu.VMEM((PAIR * CAPACITY, LANES), F32),
            pltpu.VMEM((PAIR * SPAN, width), BF16),
            pltpu.VMEM((EXPERTS, SEQ_LEN), F32),
            pltpu.VMEM((PAIR * WINDOW_SLOTS, width), BF16),
        ],
    )
    outs = pl.pallas_call(
        functools.partial(feed_backward_kernel, stored),
        grid_spec=grid_spec,
        out_shape=[shape_of((SEQ_LEN + 32, width), BF16)] + saved,
        input_output_aliases={17 + k: 1 + k for k in range(stored)},
        compiler_params=pltpu.CompilerParams(vmem_limit_bytes=VMEM_BYTES),
        cost_estimate=cost(60),
        name="feed_backward",
    )(
        meta,
        starts,
        cotangent,
        received,
        post,
        pos,
        gate,
        lift,
        gate_sh,
        lift_sh,
        probs,
        wg,
        wu,
        wd,
        wgs,
        wus,
        wds,
        *(reserve(saved) if kept is None else kept),
    )
    return outs[0], outs[1:]


def attention_backward_kernel(
    stored,
    meta,
    first_block,
    sum_ref,
    choice_ref,
    probs_ref,
    dy_ref,
    h_ref,
    b_ref,
    gain_ref,
    router_ref,
    wall_ref,
    wo_ref,
    cos_ref,
    sin_ref,
    qkv_ref,
    o_ref,
    lse_ref,
    low_ref,
    *rest,
):
    rest = rest[stored:]
    part_ref, dh_ref, gain_grad_ref, router_grad_ref, dqkv_ref, dattn_ref = rest[:6]
    dk_all, dv_all, dq_all, do_all, inner_all = rest[6:]
    step = pl.program_id(0)
    index = BACK_BLOCKS - 1 - step
    heads = wo_ref.shape[0] // LANES
    wide = heads * LANES

    @pl.when(step == 0)
    def _():
        gain_grad_ref[...] = jnp.zeros_like(gain_grad_ref)
        router_grad_ref[...] = jnp.zeros_like(router_grad_ref)
        dk_all[...] = jnp.zeros_like(dk_all)
        dv_all[...] = jnp.zeros_like(dv_all)

    probs = probs_ref[0]
    chosen = choice_ref[0:8, :].astype(F32)
    logit_grads = probs * (chosen - jnp.sum(probs * chosen, axis=0, keepdims=True))
    logit_grads = logit_grads.astype(BF16)
    router_grad_ref[...] += dot(logit_grads, b_ref[0])
    grad_normed = sum_ref[...].astype(F32) + dot_tn(logit_grads, router_ref[...])
    state = h_ref[0]
    scale = lax.rsqrt(jnp.mean(state * state, axis=-1, keepdims=True) + 1e-06)
    normed = state * scale
    gain_grad_ref[...] += jnp.sum(grad_normed * normed, axis=0, keepdims=True)
    scaled = gain_ref[...] * grad_normed
    inner = jnp.mean(normed * scaled, axis=-1, keepdims=True)
    grad_state = dy_ref[0].astype(F32) + scale * (scaled - normed * inner)
    dh_ref[...] = grad_state
    dattn = grad_state.astype(BF16)
    dattn_ref[0] = dattn
    do = dot_nt(dattn, wo_ref[...]).astype(BF16)
    do_all[...] = do
    products = do.astype(F32) * o_ref[0].astype(F32)
    for head in range(heads):
        columns = slice(head * LANES, (head + 1) * LANES)
        row = jnp.sum(products[:, columns], axis=1, keepdims=True)
        inner_all[head : head + 1, :] = jnp.broadcast_to(row, (BACK_BLOCK, LANES)).T[0:1, :]
    dq_all[...] = jnp.zeros_like(dq_all)
    here = rows_of(index, BACK_BLOCK)
    low = low_ref[0]
    query_at = index * BACK_BLOCK + lax.broadcasted_iota(jnp.int32, (BACK_KEYS, BACK_BLOCK), 1)
    key_at = lax.broadcasted_iota(jnp.int32, (BACK_KEYS, BACK_BLOCK), 0)

    def body(block, none):
        at = key_at + block * BACK_KEYS
        valid = (at >= low) & (at <= query_at)
        there = rows_of(block, BACK_KEYS)
        for head in range(heads):
            columns = slice(head * LANES, (head + 1) * LANES)
            key_columns = slice(wide + head * LANES, wide + (head + 1) * LANES)
            value_columns = slice(2 * wide + head * LANES, 2 * wide + (head + 1) * LANES)
            query = qkv_ref[0, here, columns]
            keys = qkv_ref[0, there, key_columns]
            scores = jnp.where(valid, dot_nt(keys, query), -1e30)
            probs = jnp.exp(scores - lse_ref[0, head : head + 1, :])
            grad_probs = dot_nt(qkv_ref[0, there, value_columns], do_all[:, columns])
            grad_scores = (probs * (grad_probs - inner_all[head : head + 1, :])).astype(BF16)
            dv_all[there, columns] += dot(probs.astype(BF16), do_all[:, columns])
            dk_all[there, columns] += dot(grad_scores, query)
            dq_all[:, columns] += dot_tn(grad_scores, keys)
        return none

    lax.fori_loop(
        first_block[meta[2] * BACK_BLOCKS + index], ((index + 1) * BACK_BLOCK - 1) // BACK_KEYS + 1, body, 0
    )
    cosine, sine = cos_ref[...], sin_ref[...]
    for head in range(heads):
        columns = slice(head * LANES, (head + 1) * LANES)
        key_columns = slice(wide + head * LANES, wide + (head + 1) * LANES)
        value_columns = slice(2 * wide + head * LANES, 2 * wide + (head + 1) * LANES)
        dq = dq_all[:, columns] * 0.0625
        dk = dk_all[here, columns]
        dqkv_ref[0, :, columns] = (dq * cosine - pltpu.roll(dq, HEAD_DIM, 1) * sine).astype(BF16)
        dqkv_ref[0, :, key_columns] = (
            dk * cosine - pltpu.roll(dk, HEAD_DIM, 1) * sine
        ).astype(BF16)
        dqkv_ref[0, :, value_columns] = dv_all[here, columns].astype(BF16)
    part_ref[...] = dot_nt(dqkv_ref[0], wall_ref[...]).astype(BF16)


def attention_backward(
    meta, first_block, summed, forward_kept, attention_kept, dy, gain, router, wall, wo, cosine, sine, low, kept
):
    width = summed.shape[1]
    wide = wo.shape[0]
    stored = 0 if kept is None else 2
    h, b, probs = forward_kept[0], forward_kept[1], forward_kept[7]
    unused_x, unused_a, qkv, o, lse = attention_kept
    saved = [
        shape_of((SLOTS, SEQ_LEN, 3 * wide), BF16),
        shape_of((SLOTS, SEQ_LEN, width), BF16),
    ]

    def at(step):
        return BACK_BLOCKS - 1 - step

    def slot_rows(columns, which):
        return pl.BlockSpec((1, BACK_BLOCK, columns), lambda s, m, f: (m[which], at(s), 0))

    def fixed(shape):
        return once(shape, lambda s, m, f: (0,) * len(shape))

    halves_of = BACK_BLOCKS // 2
    grid_spec = pltpu.PrefetchScalarGridSpec(
        num_scalar_prefetch=2,
        grid=(BACK_BLOCKS,),
        in_specs=[
            pl.BlockSpec((BACK_BLOCK, width), lambda s, m, f: (at(s), 0)),
            pl.BlockSpec(
                (16, BACK_BLOCK), lambda s, m, f: (SEQ_LEN // 16 + at(s) // halves_of, at(s) % halves_of)
            ),
            pl.BlockSpec((1, EXPERTS, BACK_BLOCK), lambda s, m, f: (m[3], 0, at(s))),
            slot_rows(width, 1),
            slot_rows(width, 3),
            slot_rows(width, 3),
            fixed(gain.shape),
            fixed(router.shape),
            fixed(wall.shape),
            fixed(wo.shape),
            pl.BlockSpec((BACK_BLOCK, LANES), lambda s, m, f: (at(s), 0)),
            pl.BlockSpec((BACK_BLOCK, LANES), lambda s, m, f: (at(s), 0)),
            once((1, SEQ_LEN, 3 * wide), lambda s, m, f: (m[3], 0, 0)),
            slot_rows(wide, 3),
            pl.BlockSpec((1, 8, BACK_BLOCK), lambda s, m, f: (m[3], 0, at(s))),
            pl.BlockSpec((1, 1, BACK_BLOCK), lambda s, m, f: (m[2], 0, at(s))),
        ]
        + [pl.BlockSpec(memory_space=pl.ANY)] * stored,
        out_specs=[
            pl.BlockSpec((BACK_BLOCK, width), lambda s, m, f: (at(s), 0)),
            pl.BlockSpec((BACK_BLOCK, width), lambda s, m, f: (at(s), 0)),
            fixed((1, width)),
            fixed((8, width)),
            slot_rows(3 * wide, 1),
            slot_rows(width, 1),
        ],
        scratch_shapes=[
            pltpu.VMEM((SEQ_LEN, wide), F32),
            pltpu.VMEM((SEQ_LEN, wide), F32),
            pltpu.VMEM((BACK_BLOCK, wide), F32),
            pltpu.VMEM((BACK_BLOCK, wide), BF16),
            pltpu.VMEM((8, BACK_BLOCK), F32),
        ],
    )
    outs = pl.pallas_call(
        functools.partial(attention_backward_kernel, stored),
        grid_spec=grid_spec,
        out_shape=[
            shape_of((SEQ_LEN, width), BF16),
            shape_of((SEQ_LEN, width), F32),
            shape_of((1, width), F32),
            shape_of((8, width), F32),
        ]
        + saved,
        input_output_aliases={18 + k: 4 + k for k in range(stored)},
        compiler_params=pltpu.CompilerParams(vmem_limit_bytes=VMEM_BYTES),
        cost_estimate=cost(37),
        name="attention_backward",
    )(
        meta,
        first_block,
        summed,
        summed,
        probs,
        dy,
        h,
        b,
        gain,
        router,
        wall,
        wo,
        cosine,
        sine,
        qkv,
        o,
        lse,
        low,
        *(kept or ()),
    )
    return outs[:4], outs[4:]


def expert_grads_kernel(*refs):
    ins, out_ref = refs[:-1], refs[-1]
    (xa, xb), (ga, gb), (ua, ub), (ea, eb), (ha, hb) = (ins[2 * k : 2 * k + 2] for k in range(5))
    devices, unused, rows, unused = out_ref.shape
    pairs = [((xa, xb), (ga, gb)), ((xa, xb), (ua, ub)), ((ea, eb), (ha, hb))]
    for number, (left, right) in enumerate(pairs):
        for device in range(devices):
            columns = slice(device * rows, (device + 1) * rows)
            out_ref[device, number] = (
                dot_tn(left[0][0, 0, :, columns], right[0][0, 0])
                + dot_tn(left[1][0, 0, :, columns], right[1][0, 0])
            ).astype(BF16)


def expert_grads(first, count, extra, devices, picked, hid, grad_gate, grad_lift, grad_expert):
    width, hidden = picked.shape[3], hid.shape[3]
    rows = width // devices

    def pair(columns):
        return [
            pl.BlockSpec(
                (1, 1, CAPACITY, columns),
                functools.partial(lambda slot, e: (slot, first + e, 0, 0), slot),
            )
            for slot in (1, 2)
        ]

    return pl.pallas_call(
        expert_grads_kernel,
        grid=(count,),
        in_specs=pair(width) + pair(hidden) + pair(hidden) + pair(width) + pair(hidden),
        out_specs=pl.BlockSpec((devices, 3, rows, hidden), lambda e: (0, e, 0, 0)),
        out_shape=shape_of((devices, 3 * count + extra, rows, hidden), BF16),
        compiler_params=pltpu.CompilerParams(vmem_limit_bytes=VMEM_BYTES),
        cost_estimate=cost(6 * count),
        name="expert_grads",
    )(
        *(picked, picked, grad_gate, grad_gate, grad_lift, grad_lift),
        *(grad_expert, grad_expert, hid, hid),
    )


def lead_grads_kernel(
    meta,
    cot_ref,
    rec_ref,
    post_ref,
    probs_ref,
    g_ref,
    u_ref,
    wd_ref,
    xa_ref,
    xb_ref,
    ga_ref,
    ua_ref,
    ea_ref,
    ha_ref,
    out_ref,
    given,
    pick,
    gates,
    rows_in,
    grad_gate,
    grad_lift,
    grad_rows,
    hidden,
):
    step = pl.program_id(0)

    @pl.when(step == 0)
    def _():
        given[...] = jnp.where(meta[0] == 1, cot_ref[...], rec_ref[...])

    @pl.when(step > 0)
    def _():
        chunks = [(0, chunk) for chunk in range(CAPACITY // CHUNK)]
        build_pick(step - 1, chunks, post_ref, probs_ref.at[0], pick, gates)
        rows_in[...] = dot(pick[...], given[...]).astype(BF16)
        weight = gates[:, 0:1]
        grad_rows[...] = (weight * rows_in[...].astype(F32)).astype(BF16)
        hidden[...], grad_gate[...], grad_lift[...], unused = pull(
            dot_nt(rows_in[...], wd_ref[0]), weight, g_ref[0, 0], u_ref[0, 0]
        )
        devices, unused, rows, unused = out_ref.shape
        pairs = [
            (xa_ref.at[0, 0], ga_ref.at[0, 0], xb_ref.at[0, 0], grad_gate),
            (xa_ref.at[0, 0], ua_ref.at[0, 0], xb_ref.at[0, 0], grad_lift),
            (ea_ref.at[0, 0], ha_ref.at[0, 0], grad_rows, hidden),
        ]
        for number, (left, right, left_last, right_last) in enumerate(pairs):
            for device in range(devices):
                columns = slice(device * rows, (device + 1) * rows)
                out_ref[device, number] = (
                    dot_tn(left[:, columns], right[...])
                    + dot_tn(left_last[:, columns], right_last[...])
                ).astype(BF16)


def lead_grads(count, devices, meta, cotangent, received, post, forward_kept, kept, down):
    unused_h, unused_b, picked, gate, lift, unused_gate, unused_lift, probs = forward_kept
    unused_dy, hid, grad_gate, grad_lift, grad_expert = kept[:5]
    width, inner = picked.shape[3], gate.shape[3]
    rows = width // devices

    def at(step):
        return jnp.maximum(step - 1, 0)

    def of_slot(columns, which):
        return pl.BlockSpec((1, 1, CAPACITY, columns), lambda s, m: (m[which], at(s), 0, 0))

    grid_spec = pltpu.PrefetchScalarGridSpec(
        num_scalar_prefetch=1,
        grid=(count + 1,),
        in_specs=[
            once((SEQ_LEN, width), lambda s, m: (m[1], 0)),
            once((SEQ_LEN, width), lambda s, m: (0, 0)),
            once((1, EXPERTS, SEQ_LEN), lambda s, m: (m[1], 0, 0)),
            once((1, EXPERTS, SEQ_LEN), lambda s, m: (m[2], 0, 0)),
            of_slot(inner, 2),
            of_slot(inner, 2),
            pl.BlockSpec((1,) + down.shape[1:], lambda s, m: (at(s), 0, 0)),
            of_slot(width, 3),
            of_slot(width, 2),
            of_slot(inner, 3),
            of_slot(inner, 3),
            of_slot(width, 3),
            of_slot(inner, 3),
        ],
        out_specs=pl.BlockSpec((devices, 3, rows, inner), lambda s, m: (0, at(s), 0, 0)),
        scratch_shapes=[
            pltpu.VMEM((SEQ_LEN, width), BF16),
            pltpu.VMEM((CAPACITY, SEQ_LEN), BF16),
            pltpu.VMEM((CAPACITY, LANES), F32),
            pltpu.VMEM((CAPACITY, width), BF16),
            pltpu.VMEM((CAPACITY, inner), BF16),
            pltpu.VMEM((CAPACITY, inner), BF16),
            pltpu.VMEM((CAPACITY, width), BF16),
            pltpu.VMEM((CAPACITY, inner), BF16),
        ],
    )
    return pl.pallas_call(
        lead_grads_kernel,
        grid_spec=grid_spec,
        out_shape=shape_of((devices, 3 * count, rows, inner), BF16),
        compiler_params=pltpu.CompilerParams(vmem_limit_bytes=VMEM_BYTES),
        cost_estimate=cost(20),
        name="lead_grads",
    )(
        meta,
        cotangent,
        received,
        post,
        probs,
        gate,
        lift,
        down,
        picked,
        picked,
        grad_gate,
        grad_lift,
        grad_expert,
        hid,
    )


def shared_grads_kernel(b_ref, dy_ref, gate_ref, lift_ref, hid_ref, before_ref, out_ref, *totals):
    step = pl.program_id(0)
    pairs = [(b_ref, gate_ref), (b_ref, lift_ref), (dy_ref, hid_ref)]

    @pl.when(step == 0)
    def _():
        for total in totals:
            total[...] = jnp.zeros_like(total)

    for (left, right), total in zip(pairs, totals):
        total[...] += dot_tn(left[0], right[0])

    @pl.when(step == pl.num_programs(0) - 1)
    def _():
        devices, unused, rows, unused = out_ref.shape
        for number, total in enumerate(totals):
            for device in range(devices):
                out_ref[device, number] = total[device * rows : (device + 1) * rows, :].astype(
                    BF16
                )


def shared_grads(before, b, dy, grad_gate, grad_lift, hid):
    devices, matrices, width, hidden = before.shape
    rows = ROWS
    steps = SEQ_LEN // rows

    def spec(array):
        return pl.BlockSpec((1, rows, array.shape[2]), lambda s: (1 + s // steps, s % steps, 0))

    return pl.pallas_call(
        shared_grads_kernel,
        grid=(2 * steps,),
        in_specs=[spec(array) for array in (b, dy, grad_gate, grad_lift, hid)]
        + [pl.BlockSpec(memory_space=pl.ANY)],
        out_specs=once((devices, 3, width, hidden), lambda s: (0, matrices // 3 - 1, 0, 0)),
        out_shape=shape_of(before.shape, BF16),
        scratch_shapes=[pltpu.VMEM((devices * width, hidden), F32)] * 3,
        input_output_aliases={5: 0},
        compiler_params=pltpu.CompilerParams(vmem_limit_bytes=VMEM_BYTES),
        cost_estimate=cost(13),
        name="shared_grads",
    )(b, dy, grad_gate, grad_lift, hid, before)


def token_grads_kernel(count, *refs):
    lefts, rights = refs[:count], refs[count : 2 * count]
    outs, totals = refs[2 * count : 3 * count], refs[3 * count :]
    step = pl.program_id(0)

    @pl.when(step == 0)
    def _():
        for total in totals:
            total[...] = jnp.zeros_like(total)

    for left, right, total in zip(lefts, rights, totals):
        total[...] += dot_tn(left[0], right[0])

    @pl.when(step == pl.num_programs(0) - 1)
    def _():
        for out, total in zip(outs, totals):
            out[...] = total[...].astype(BF16)


def token_grads(lefts, rights):
    count = len(lefts)
    rows = ROWS
    steps = SEQ_LEN // rows

    def spec(array):
        return pl.BlockSpec((1, rows, array.shape[2]), lambda s: (1 + s // steps, s % steps, 0))

    shapes = [(left.shape[2], right.shape[2]) for left, right in zip(lefts, rights)]
    return pl.pallas_call(
        functools.partial(token_grads_kernel, count),
        grid=(2 * steps,),
        in_specs=[spec(a) for a in lefts] + [spec(a) for a in rights],
        out_specs=[once(shape, lambda s: (0, 0)) for shape in shapes],
        out_shape=[shape_of(shape, BF16) for shape in shapes],
        scratch_shapes=[pltpu.VMEM(shape, F32) for shape in shapes],
        compiler_params=pltpu.CompilerParams(vmem_limit_bytes=VMEM_BYTES),
        cost_estimate=cost(14),
        name="token_grads",
    )(*lefts, *rights)


def rotary_tables():
    half = HEAD_DIM // 2
    rates = np.exp(-np.log(10000.0) * np.arange(half) * 2.0 / HEAD_DIM)
    angles = np.arange(SEQ_LEN)[:, None] * rates[None, :]
    cosine, sine = np.cos(angles), np.sin(angles)
    cosine = np.concatenate([cosine] * 4, axis=1)
    sine = np.concatenate([sine, sine, -sine, -sine], axis=1)
    return jnp.asarray(cosine, F32), jnp.asarray(sine, F32)


def paired(weight):
    rows = weight.shape[0]
    heads = weight.shape[1] // HEAD_DIM
    half = HEAD_DIM // 2
    split = weight.reshape(rows, heads, HEAD_DIM)
    swapped = jnp.concatenate([-split[:, :, half:], split[:, :, :half]], axis=2)
    return jnp.concatenate([split, swapped], axis=2).reshape(rows, heads * LANES)


def padded(weight):
    rows = weight.shape[0]
    heads = weight.shape[1] // HEAD_DIM
    split = weight.reshape(rows, heads, HEAD_DIM)
    return jnp.concatenate([split, jnp.zeros_like(split)], axis=2).reshape(rows, heads * LANES)


def unpadded(grads):
    rows = grads.shape[0]
    return grads.reshape(rows, -1, LANES)[:, :, :HEAD_DIM].reshape(rows, -1)


def places(routes):
    experts = jnp.arange(EXPERTS, dtype=jnp.int32)
    named = jnp.any(routes[:, :, :, None] == experts, axis=2)
    before = (
        jnp.arange(SEQ_LEN, dtype=jnp.int32)[:, None] > jnp.arange(SEQ_LEN, dtype=jnp.int32)
    ).astype(BF16)
    rank = jnp.einsum("ts,nse->nte", before, named.astype(BF16), preferred_element_type=F32)
    by_token = jnp.where(named, rank.astype(jnp.int32), -1)
    counts = jnp.sum(named.reshape(-1, ROW_STEPS, ROWS, EXPERTS).astype(jnp.int32), axis=2)
    before = jnp.cumsum(jnp.pad(counts, ((0, 0), (1, 0), (0, 0))), axis=1)
    starts = jnp.swapaxes(before, 1, 2)
    held = starts[:, :, 1:] <= starts[:, :, :-1] // 16 * 16 + WINDOW_SLOTS
    narrow = jnp.all(held, axis=(1, 2)).astype(jnp.int32)
    starts = jnp.concatenate([starts.reshape(-1), narrow])
    return by_token, jnp.swapaxes(by_token, 1, 2), starts


def first_allowed(lengths):
    ends = jnp.cumsum(lengths, axis=1)
    at = jnp.arange(SEQ_LEN, dtype=jnp.int32)
    starts = jnp.max(jnp.where(ends[:, None, :] <= at[None, :, None], ends[:, None, :], 0), axis=2)
    return jnp.maximum(starts, at[None, :] - (WINDOW - 1)).astype(jnp.int32)


def on_device(
    tokens,
    doc_lengths,
    routes,
    gain_attn,
    w_query,
    w_key,
    w_value,
    w_output,
    gain_ffn,
    w_router,
    w_gate_exp,
    w_up_exp,
    w_down_exp,
    w_gate_sh,
    w_up_sh,
    w_down_sh,
    cotangent,
):
    section = lax.axis_index("section")
    devices = lax.axis_size("dp")
    count = doc_lengths.shape[0]
    width = tokens.shape[1]
    cosine, sine = rotary_tables()
    wall = jnp.concatenate([paired(w_query[0]), paired(w_key[0]), padded(w_value[0])], axis=1)
    wo = padded(w_output[0].T).T
    out_weight = lax.all_gather(w_output[0], "tensor", axis=0, tiled=True)
    router = w_router[0].T
    gain_a, gain_f = gain_attn.astype(F32), gain_ffn.astype(F32)
    feed_weights = (
        w_gate_exp[0],
        w_up_exp[0],
        w_down_exp[0],
        w_gate_sh[0],
        w_up_sh[0],
        w_down_sh[0],
    )
    pos, post, starts = places(routes[0].reshape(count, SEQ_LEN, 2))
    low = first_allowed(doc_lengths)
    first_block = (low[:, ::BLOCK] // KEYS).reshape(-1)
    back_first = (low[:, ::BACK_BLOCK] // BACK_KEYS).reshape(-1)
    low_column, low_row = low[:, :, None], low[:, None, :]

    received = jnp.zeros((SEQ_LEN, width), BF16)
    attention_kept, feed_kept, results = None, None, []
    grads_kept, attention_grads_kept, inputs = None, None, []
    small = jnp.zeros((10, width), F32)

    def spread(array):
        return lax.psum_scatter(array, "dp", scatter_dimension=0, tiled=False)

    def after(meta, array):
        return lax.optimization_barrier((meta, array))

    def forward_meta(tick):
        raw = tick - section
        active = (raw >= 0) & (raw < count)
        sequence = jnp.clip(raw, 0, count - 1)
        return jnp.stack([section, jnp.where(active, sequence + 1, 0), sequence]).astype(jnp.int32)

    def backward_meta(tick):
        raw = tick - 1 + section
        active = (raw >= 0) & (raw < count)
        sequence = jnp.clip(raw, 0, count - 1)
        source = jnp.where(active, 2 - section, 0)
        return jnp.stack(
            [source, jnp.where(active, sequence + 1, 0), sequence, sequence + 1]
        ).astype(jnp.int32)

    def attend(meta, received, kept):
        return attention_forward(
            meta, first_block, tokens, received, gain_a, wall, cosine, sine, low_column, kept
        )

    def feed(meta, gathered, kept):
        return feed_forward(
            meta,
            starts,
            attention_kept[0],
            gathered,
            out_weight,
            gain_f,
            router,
            post,
            pos,
            feed_weights,
            kept,
        )

    def feed_back(meta, received):
        return feed_backward(
            meta, starts, cotangent, received, post, pos, feed_kept, feed_weights, grads_kept
        )

    def attend_back(meta, summed):
        return attention_backward(
            meta,
            back_first,
            summed,
            feed_kept,
            attention_kept,
            grads_kept[0],
            gain_f,
            router,
            wall,
            wo,
            cosine,
            sine,
            low_row,
            attention_grads_kept,
        )

    for tick in range(count):
        meta = forward_meta(tick)
        own, attention_kept = attend(meta, received, attention_kept)
        gathered = lax.all_gather(own, "tensor") if tick == 0 else tensor_gather(own, 0)
        part, feed_kept = feed(meta, gathered, feed_kept)
        result, received = output_relay(part, feed_kept[0], tick, 4 + tick)
        results.append(result)

    blank = jnp.zeros((SEQ_LEN, width), BF16)
    meta, back_meta = forward_meta(count), backward_meta(0)
    own, attention_kept = attend(meta, received, attention_kept)
    back_meta, own = after(back_meta, own)
    gathered = lax.all_gather(own, "tensor")
    part, grads_kept = feed_back(back_meta, blank)
    meta, part = after(meta, part)
    summed = lax.psum(part, "tensor")
    last_part, feed_kept = feed(meta, gathered, feed_kept)
    back_meta, last_part = after(back_meta, last_part)

    for tick in range(count + 1):
        if tick > 0:
            back_meta = backward_meta(tick)
        if tick == count:
            lead = 3
            lead_meta = jnp.stack(
                [2 - section, jnp.full_like(section, count - 1), jnp.full_like(section, count)]
                + [jnp.full_like(section, count - 1)]
            ).astype(jnp.int32)
            lead_part = lead_grads(
                lead,
                devices,
                lead_meta,
                cotangent,
                received,
                post,
                feed_kept,
                grads_kept,
                feed_weights[2],
            )
            back_meta, lead_part = after(back_meta, lead_part)
        if tick > 0:
            part, grads_kept = feed_back(back_meta, received)
        if tick == count:
            dy, hid, grad_gate, grad_lift, grad_expert, hid_sh, grad_gate_sh, grad_lift_sh = (
                grads_kept
            )
            last_grads = expert_grads(
                lead,
                EXPERTS - lead,
                3,
                devices,
                feed_kept[2],
                hid,
                grad_gate,
                grad_lift,
                grad_expert,
            )
            last_grads = shared_grads(
                last_grads, feed_kept[1], dy, grad_gate_sh, grad_lift_sh, hid_sh
            )
            part, last_grads = lax.optimization_barrier((part, last_grads))
            parts = [spread(lead_part), spread(last_grads)]
        if tick > 0:
            summed = tensor_sum(part, 2, 7)
        (part, grad_state, gain_grad, router_grad), attention_grads_kept = attend_back(
            back_meta, summed
        )
        grad_input, received, gain_attn_grad = input_relay(
            part, attention_kept[0], grad_state, gain_a, tick, 4 + count + 1 + tick
        )
        inputs.append(grad_input)
        small = small + jnp.concatenate([gain_attn_grad, gain_grad, router_grad], axis=0)
    result, unused = output_relay(last_part, feed_kept[0], count, 4 + count)
    results.append(result)

    projections, outward = token_grads(
        [attention_kept[1], attention_grads_kept[1]], [attention_grads_kept[0], attention_kept[3]]
    )
    wide = wo.shape[0]
    rows = width // devices
    columns = w_query.shape[2]
    packed = jnp.concatenate(
        [
            2.0 * unpadded(projections[:, : 2 * wide]),
            unpadded(projections[:, 2 * wide :]),
            unpadded(outward),
            jnp.pad(small, ((0, 6), (0, 0))).T.astype(BF16),
        ],
        axis=1,
    )
    packed, *parts = lax.optimization_barrier((packed, *parts))
    packed = spread(packed.reshape(devices, rows, -1)).astype(F32)
    shared = parts[1][-3:].astype(F32)
    experts = jnp.concatenate([parts[0], parts[1][:-3]], axis=0).astype(F32)
    experts = experts.reshape(EXPERTS, 3, rows, -1)

    def choose(items):
        return jnp.concatenate(
            [jnp.where(section == 0, items[k], items[k + 1]) for k in range(count)], axis=0
        )

    layer_out = choose(results)
    input_grad = jnp.concatenate(
        [jnp.where(section == 0, inputs[k + 1], inputs[k]) for k in range(count)], axis=0
    )
    extra = 4 * columns
    return (
        layer_out[None],
        input_grad[None],
        packed[None, :, extra],
        packed[None, :, :columns],
        packed[None, :, columns : 2 * columns],
        packed[None, :, 2 * columns : 3 * columns],
        packed[:, 3 * columns : extra].T[None],
        packed[None, :, extra + 1],
        packed[None, :, extra + 2 : extra + 10],
        experts[None, :, 0],
        experts[None, :, 1],
        jnp.swapaxes(experts[:, 2], 1, 2)[None],
        shared[None, 0],
        shared[None, 1],
        shared[2].T[None],
    )


def solution(mesh):
    return jax.shard_map(
        on_device,
        mesh=mesh,
        in_specs=(
            P("dp", None),
            P("dp", None),
            P("section", "dp", None),
            P("section", None),
            P("section", None, "tensor"),
            P("section", None, "tensor"),
            P("section", None, "tensor"),
            P("section", "tensor", None),
            P("section", None),
            P("section", None, None),
            P("section", None, None, "tensor"),
            P("section", None, None, "tensor"),
            P("section", None, "tensor", None),
            P("section", None, "tensor"),
            P("section", None, "tensor"),
            P("section", "tensor", None),
            P("dp", None),
        ),
        out_specs=(
            P("section", "dp", None),
            P("section", "dp", None),
            P("section", "dp"),
            P("section", "dp", "tensor"),
            P("section", "dp", "tensor"),
            P("section", "dp", "tensor"),
            P("section", "tensor", "dp"),
            P("section", "dp"),
            P("section", "dp", None),
            P("section", None, "dp", "tensor"),
            P("section", None, "dp", "tensor"),
            P("section", None, "tensor", "dp"),
            P("section", "dp", "tensor"),
            P("section", "dp", "tensor"),
            P("section", "tensor", "dp"),
        ),
        check_vma=False,
    )
```

```python
import functools

import jax
import jax.numpy as jnp
import numpy as np
from jax import lax
from jax.experimental import pallas as pl
from jax.experimental.pallas import tpu as pltpu
from jax.sharding import PartitionSpec as P

HEAD_DIM = 64
EXPERTS = 8
SEQ_LEN = 1536
WINDOW = 1024
CAPACITY = 480
BLOCK = 512
PACK = 256
BLOCKS = SEQ_LEN // BLOCK
KEYS = 256
BACK_BLOCK = 384
BACK_BLOCKS = SEQ_LEN // BACK_BLOCK
BACK_KEYS = 384
LANES = 128
SLOTS = 3
VMEM_BYTES = 60 * 2**20
MESH = pl.DeviceIdType.MESH
F32 = jnp.float32
BF16 = jnp.bfloat16
NT = (((1,), (1,)), ((), ()))
TN = (((0,), (0,)), ((), ()))


def shape_of(shape, dtype):
    return jax.ShapeDtypeStruct(shape, dtype)


def cost(micros):
    return pl.CostEstimate(
        flops=int(micros * 1.15e9), bytes_accessed=int(micros * 3.6e6), transcendentals=0
    )


def dot(left, right):
    return jnp.dot(left, right, preferred_element_type=F32)


def dot_nt(left, right):
    return lax.dot_general(left, right, NT, preferred_element_type=F32)


def dot_tn(left, right):
    return lax.dot_general(left, right, TN, preferred_element_type=F32)


def once(shape, index):
    return pl.BlockSpec(shape, index, pipeline_mode=pl.Buffered(1))


def loop(count, body):
    lax.fori_loop(0, count, lambda step, none: (body(step), none)[1], 0)


def rows_of(step, size):
    return pl.ds(pl.multiple_of(step * size, size), size)


def greet(partners):
    barrier = pltpu.get_barrier_semaphore()
    for partner in partners:
        pl.semaphore_signal(barrier, inc=1, device_id=partner, device_id_type=MESH)
    pl.semaphore_wait(barrier, len(partners))


def remote(source, target, send, recv, device):
    return pltpu.make_async_remote_copy(
        src_ref=source,
        dst_ref=target,
        send_sem=send,
        recv_sem=recv,
        device_id=device,
        device_id_type=MESH,
    )


def partners_of():
    place = lax.axis_index("tensor")
    core = lax.rem(place, 2)
    return {"tensor": place + 1 - 2 * core}, {"tensor": lax.rem(place + 2, 4)}


def sides(rows):
    core = lax.rem(lax.axis_index("tensor"), 2)
    half = rows // 2
    return core * half, (1 - core) * half


def piece_rows(side, step, size):
    return pl.ds(pl.multiple_of(side + step * size, 16), size)


def cross_kernel(pieces, part_ref, mine, first, kept, second, sends, recvs, loaded, use):
    near, far = partners_of()
    own, other = sides(part_ref.shape[0])
    size = mine.shape[0] // pieces
    copies = []
    for step in range(pieces):
        local = pl.ds(step * size, size)
        copies.append(
            remote(
                part_ref.at[piece_rows(other, step, size)],
                first.at[local],
                sends.at[0, step],
                recvs.at[0, step],
                near,
            )
        )
        copies[-1].start()
    load = pltpu.make_async_copy(
        part_ref.at[pl.ds(pl.multiple_of(own, 16), mine.shape[0])], mine, loaded
    )
    load.start()
    load.wait()
    for step in range(pieces):
        local = pl.ds(step * size, size)
        copies[step].wait_recv()
        kept[local, :] = (mine[local, :].astype(F32) + first[local, :].astype(F32)).astype(BF16)
        copies.append(
            remote(
                kept.at[local], second.at[local], sends.at[1, step], recvs.at[1, step], far
            )
        )
        copies[-1].start()
    for step in range(pieces):
        local = pl.ds(step * size, size)
        copies[pieces + step].wait_recv()
        use(step, local, kept[local, :].astype(F32) + second[local, :].astype(F32))
    return copies


def sum_kernel(
    pieces, part_ref, out_ref, mine, first, kept, second, done, sends, recvs, loaded, stored
):
    near, far = partners_of()
    greet([near, far])
    own, other = sides(part_ref.shape[0])
    size = mine.shape[0] // pieces
    back, local_copies = [], []

    def use(step, local, total):
        done[local, :] = total.astype(BF16)
        rows = piece_rows(own, step, size)
        back.append(
            remote(done.at[local], out_ref.at[rows], sends.at[2, step], recvs.at[2, step], near)
        )
        back[-1].start()
        local_copies.append(
            pltpu.make_async_copy(done.at[local], out_ref.at[rows], stored.at[step])
        )
        local_copies[-1].start()

    copies = cross_kernel(
        pieces, part_ref, mine, first, kept, second, sends, recvs, loaded, use
    )
    for copy in back:
        copy.wait_recv()
    for copy in copies + back:
        copy.wait_send()
    for copy in local_copies:
        copy.wait()


def tensor_sum(part, identity, pieces):
    rows, width = part.shape
    hbm = pl.BlockSpec(memory_space=pl.ANY)
    return pl.pallas_call(
        functools.partial(sum_kernel, pieces),
        out_shape=shape_of((rows, width), BF16),
        in_specs=[hbm],
        out_specs=hbm,
        scratch_shapes=[pltpu.VMEM((rows // 2, width), BF16)] * 5
        + [pltpu.SemaphoreType.DMA((3, pieces))] * 2
        + [pltpu.SemaphoreType.DMA, pltpu.SemaphoreType.DMA((pieces,))],
        compiler_params=pltpu.CompilerParams(
            collective_id=identity, has_side_effects=True, vmem_limit_bytes=VMEM_BYTES
        ),
        cost_estimate=cost(32),
        name="tensor_sum",
    )(part)


def gather_kernel(pieces, own_ref, out_ref, sends, recvs, stored):
    place = lax.axis_index("tensor")
    near, far = partners_of()
    greet([near, far])
    far_place = lax.rem(place + 2, 4)
    size = own_ref.shape[0] // pieces
    first, crossing, passed = [], [], []
    for group, copies, partner in ((0, crossing, far), (1, first, near)):
        for piece in range(pieces):
            rows = pl.ds(piece * size, size)
            copies.append(
                remote(
                    own_ref.at[rows],
                    out_ref.at[place, rows],
                    sends.at[group, piece],
                    recvs.at[group, piece],
                    partner,
                )
            )
            copies[-1].start()
    local = pltpu.make_async_copy(own_ref, out_ref.at[place], stored)
    local.start()
    for piece in range(pieces):
        rows = pl.ds(piece * size, size)
        crossing[piece].wait_recv()
        passed.append(
            remote(
                out_ref.at[far_place, rows],
                out_ref.at[far_place, rows],
                sends.at[2, piece],
                recvs.at[2, piece],
                near,
            )
        )
        passed[-1].start()
    for copy in first + passed:
        copy.wait_recv()
    for copy in first + crossing + passed:
        copy.wait_send()
    local.wait()


def tensor_gather(own, identity, pieces=6):
    hbm = pl.BlockSpec(memory_space=pl.ANY)
    return pl.pallas_call(
        functools.partial(gather_kernel, pieces),
        out_shape=shape_of((4,) + own.shape, BF16),
        in_specs=[hbm],
        out_specs=hbm,
        scratch_shapes=[pltpu.SemaphoreType.DMA((3, pieces))] * 2 + [pltpu.SemaphoreType.DMA],
        compiler_params=pltpu.CompilerParams(
            collective_id=identity, has_side_effects=True, vmem_limit_bytes=VMEM_BYTES
        ),
        cost_estimate=cost(18),
        name="tensor_gather",
    )(own)


def pass_on(step, source, rows, next_ref, sends, recvs, across):
    copy = remote(source, next_ref.at[rows], sends.at[3, step], recvs.at[3, step], across)
    copy.start()
    return copy


LAG = 3


def spread_on(step, passed, rows, next_ref, sends, recvs, near):
    passed[step].wait_recv()
    copy = remote(next_ref.at[rows], next_ref.at[rows], sends.at[4, step], recvs.at[4, step], near)
    copy.start()
    return copy


def output_kernel(
    pieces,
    tick,
    part_ref,
    states_ref,
    out_ref,
    next_ref,
    mine,
    first,
    kept,
    second,
    done,
    state,
    sends,
    recvs,
    loaded,
    state_loaded,
    stored,
):
    near, far = partners_of()
    section = lax.axis_index("section")
    across = {"section": 1 - section}
    slot = lax.rem(tick + 1 - section, states_ref.shape[0])
    own, other = sides(part_ref.shape[0])
    size = mine.shape[0] // pieces
    load = pltpu.make_async_copy(
        states_ref.at[slot, pl.ds(pl.multiple_of(own, 16), mine.shape[0])], state, state_loaded
    )
    load.start()
    greet([near, far, across])
    back, passed, spread, local_copies = [], [], [], []

    def forward(step):
        rows = piece_rows(own, step, size)
        spread.append(spread_on(step, passed, rows, next_ref, sends, recvs, near))

    def use(step, local, total):
        if step == 0:
            load.wait()
        done[local, :] = (state[local, :] + total.astype(BF16).astype(F32)).astype(BF16)
        rows = piece_rows(own, step, size)
        passed.append(pass_on(step, done.at[local], rows, next_ref, sends, recvs, across))
        back.append(
            remote(done.at[local], out_ref.at[rows], sends.at[2, step], recvs.at[2, step], near)
        )
        back[-1].start()
        local_copies.append(
            pltpu.make_async_copy(done.at[local], out_ref.at[rows], stored.at[step])
        )
        local_copies[-1].start()
        if step >= LAG:
            forward(step - LAG)

    copies = cross_kernel(
        pieces, part_ref, mine, first, kept, second, sends, recvs, loaded, use
    )
    for step in range(pieces - LAG, pieces):
        forward(step)
    for copy in back + spread:
        copy.wait_recv()
    for copy in copies + back + passed + spread:
        copy.wait_send()
    for copy in local_copies:
        copy.wait()


def output_relay(part, states, tick, identity, pieces=16):
    rows, width = part.shape
    hbm = pl.BlockSpec(memory_space=pl.ANY)
    return pl.pallas_call(
        functools.partial(output_kernel, pieces, tick),
        out_shape=[shape_of((rows, width), BF16)] * 2,
        in_specs=[hbm] * 2,
        out_specs=[hbm] * 2,
        scratch_shapes=[pltpu.VMEM((rows // 2, width), BF16)] * 5
        + [pltpu.VMEM((rows // 2, width), F32)]
        + [pltpu.SemaphoreType.DMA((5, pieces))] * 2
        + [pltpu.SemaphoreType.DMA] * 2
        + [pltpu.SemaphoreType.DMA((pieces,))],
        compiler_params=pltpu.CompilerParams(
            collective_id=identity, has_side_effects=True, vmem_limit_bytes=VMEM_BYTES
        ),
        cost_estimate=cost(38),
        name="output_relay",
    )(part, states)


def input_kernel(
    pieces,
    tick,
    part_ref,
    layers_ref,
    grad_state_ref,
    gain_ref,
    grad_ref,
    next_ref,
    grad_gain_ref,
    mine,
    first,
    kept,
    second,
    given,
    full,
    layer_in,
    grad_state,
    grad,
    gains,
    sends,
    recvs,
    loaded,
    inputs_loaded,
    stored,
):
    near, far = partners_of()
    section = lax.axis_index("section")
    across = {"section": 1 - section}
    slot = lax.rem(tick + section, layers_ref.shape[0])
    rows = part_ref.shape[0]
    own, other = sides(rows)
    half = rows // 2
    size = half // pieces
    loads = []
    for side, start in ((0, own), (1, other)):
        there = pl.ds(pl.multiple_of(start, 16), half)
        loads.append(
            [
                pltpu.make_async_copy(
                    layers_ref.at[slot, there], layer_in.at[there], inputs_loaded.at[side, 0]
                ),
                pltpu.make_async_copy(
                    grad_state_ref.at[there], grad_state.at[there], inputs_loaded.at[side, 1]
                ),
            ]
        )
        for load in loads[-1]:
            load.start()
    greet([near, far, across])
    gains[...] = jnp.zeros_like(gains)
    back, passed, spread, local_copies = [], [], [], []

    def rows_back(here, side, step):
        grad_normed = full[here, :].astype(F32)
        values = layer_in[here, :].astype(F32)
        scale = lax.rsqrt(jnp.mean(values * values, axis=-1, keepdims=True) + 1e-06)
        normed = values * scale
        scaled = gain_ref[...] * grad_normed
        inner = jnp.mean(normed * scaled, axis=-1, keepdims=True)
        result = grad_state[here, :] + scale * (scaled - normed * inner)
        grad[here, :] = result
        gains[side : side + 1, :] += jnp.sum(grad_normed * normed, axis=0, keepdims=True)
        local_copies.append(
            pltpu.make_async_copy(grad.at[here], grad_ref.at[here], stored.at[side, step])
        )
        local_copies[-1].start()
        return result

    def partner_rows(step):
        if step == 0:
            for load in loads[1]:
                load.wait()
        back[step].wait_recv()
        rows_back(piece_rows(other, step, size), 1, step)

    def forward(step):
        here = piece_rows(own, step, size)
        spread.append(spread_on(step, passed, here, next_ref, sends, recvs, near))

    def use(step, local, total):
        if step == 0:
            for load in loads[0]:
                load.wait()
        here = piece_rows(own, step, size)
        full[here, :] = total.astype(BF16)
        back.append(
            remote(full.at[here], full.at[here], sends.at[2, step], recvs.at[2, step], near)
        )
        back[-1].start()
        given[local, :] = rows_back(here, 0, step).astype(BF16)
        passed.append(pass_on(step, given.at[local], here, next_ref, sends, recvs, across))
        if step > 0:
            partner_rows(step - 1)
        if step >= LAG:
            forward(step - LAG)

    copies = cross_kernel(
        pieces, part_ref, mine, first, kept, second, sends, recvs, loaded, use
    )
    partner_rows(pieces - 1)
    for step in range(pieces - LAG, pieces):
        forward(step)
    grad_gain_ref[...] = gains[0:1, :] + gains[1:2, :]
    for copy in spread:
        copy.wait_recv()
    for copy in copies + back + passed + spread:
        copy.wait_send()
    for copy in local_copies:
        copy.wait()


def input_relay(part, layers, grad_state, gain, tick, identity, pieces=16):
    rows, width = part.shape
    hbm = pl.BlockSpec(memory_space=pl.ANY)
    whole = pl.BlockSpec(memory_space=pltpu.VMEM)
    return pl.pallas_call(
        functools.partial(input_kernel, pieces, tick),
        out_shape=[
            shape_of((rows, width), F32),
            shape_of((rows, width), BF16),
            shape_of((1, width), F32),
        ],
        in_specs=[hbm] * 3 + [whole],
        out_specs=[hbm] * 2 + [whole],
        scratch_shapes=[pltpu.VMEM((rows // 2, width), BF16)] * 5
        + [pltpu.VMEM((rows, width), BF16)] * 2
        + [pltpu.VMEM((rows, width), F32)] * 2
        + [pltpu.VMEM((8, width), F32)]
        + [pltpu.SemaphoreType.DMA((5, pieces))] * 2
        + [pltpu.SemaphoreType.DMA]
        + [pltpu.SemaphoreType.DMA((2, 2)), pltpu.SemaphoreType.DMA((2, pieces))],
        compiler_params=pltpu.CompilerParams(
            collective_id=identity, has_side_effects=True, vmem_limit_bytes=VMEM_BYTES
        ),
        cost_estimate=cost(42),
        name="input_relay",
    )(part, layers, grad_state, gain)


def attention_forward_kernel(
    stored,
    meta,
    first_block,
    tok_ref,
    rec_ref,
    gain_ref,
    wall_ref,
    cos_ref,
    sin_ref,
    low_ref,
    *rest,
):
    rest = rest[stored:]
    packed_ref, x_ref, a_ref, qkv_ref, o_ref, lse_ref = rest[:6]
    keys, values, scores, tops, sums, mixed = rest[6:]
    index = pl.program_id(0)
    heads = wall_ref.shape[1] // (3 * LANES)
    wide = heads * LANES
    x = jnp.where(meta[0] == 0, tok_ref[...], rec_ref[...])
    x_ref[0] = x
    x = x.astype(F32)
    normed = gain_ref[...] * x * lax.rsqrt(jnp.mean(x * x, axis=-1, keepdims=True) + 1e-06)
    normed = normed.astype(BF16)
    a_ref[0] = normed
    cosine, sine = cos_ref[...], sin_ref[...]
    here = rows_of(index, BLOCK)
    projected = dot(normed, wall_ref[...])
    for group in range(2 * heads):
        columns = slice(group * LANES, (group + 1) * LANES)
        pre = projected[:, columns]
        turned = pre * cosine + pltpu.roll(pre, HEAD_DIM, 1) * sine
        if group < heads:
            turned = turned * 0.0625
        qkv_ref[0, :, columns] = turned.astype(BF16)
    qkv_ref[0, :, 2 * wide :] = projected[:, 2 * wide :].astype(BF16)
    keys[here, :] = qkv_ref[0, :, wide : 2 * wide]
    low = low_ref[0]
    query_at = index * BLOCK + lax.broadcasted_iota(jnp.int32, (BLOCK, KEYS), 0)
    key_at = lax.broadcasted_iota(jnp.int32, (BLOCK, KEYS), 1)

    @pl.when(index * BLOCK % KEYS == 0)
    def _():
        values[rows_of(index * BLOCK // KEYS, KEYS), :] = jnp.zeros((KEYS, wide), BF16)

    values[here, :] = qkv_ref[0, :, 2 * wide :]
    tops[...] = jnp.full_like(tops, -1e30)
    sums[...] = jnp.zeros_like(sums)
    mixed[...] = jnp.zeros_like(mixed)
    begin = first_block[meta[2] * BLOCKS + index]

    def score(block, none):
        at = key_at + block * KEYS
        valid = (at >= low) & (at <= query_at)
        there = rows_of(block, KEYS)
        for head in range(heads):
            columns = slice(head * LANES, (head + 1) * LANES)
            raw = dot_nt(qkv_ref[0, :, columns], keys[there, columns])
            raw = jnp.where(valid, raw, -1e30)
            scores[head, block] = raw
            best = tops[head]
            for start in range(0, KEYS, LANES):
                best = jnp.maximum(best, raw[:, start : start + LANES])
            tops[head] = best
        return none

    end = ((index + 1) * BLOCK - 1) // KEYS + 1
    lax.fori_loop(begin, end, score, 0)
    top = [jnp.max(tops[head], axis=1, keepdims=True) for head in range(heads)]

    def mix(block, none):
        there = rows_of(block, KEYS)
        for head in range(heads):
            columns = slice(head * LANES, (head + 1) * LANES)
            weights = jnp.exp(scores[head, block] - top[head])
            part = weights[:, :LANES]
            for start in range(LANES, KEYS, LANES):
                part = part + weights[:, start : start + LANES]
            sums[head] += part
            mixed[:, columns] += dot(weights.astype(BF16), values[there, columns])
        return none

    lax.fori_loop(begin, end, mix, 0)
    for head in range(heads):
        columns = slice(head * LANES, (head + 1) * LANES)
        total = jnp.sum(sums[head], axis=1, keepdims=True)
        o_ref[0, :, columns] = (mixed[:, columns] / total).astype(BF16)
        logsum = jnp.broadcast_to(top[head] + jnp.log(total), (BLOCK, LANES))
        lse_ref[0, head : head + 1, :] = logsum.T[0:1, :]
    half = PACK // 2
    for start in range(0, BLOCK, PACK):
        packed_ref[start // 2 : start // 2 + half, :] = jnp.concatenate(
            [
                o_ref[
                    0,
                    start + side * half : start + (side + 1) * half,
                    head * LANES : head * LANES + HEAD_DIM,
                ]
                for side in range(2)
                for head in range(heads)
            ],
            axis=1,
        )


def attention_forward(meta, first_block, tokens, received, gain, wall, cosine, sine, low, kept):
    width = tokens.shape[1]
    wide = wall.shape[1] // 3
    heads = wide // LANES
    stored = 0 if kept is None else 5
    saved = [
        shape_of((SLOTS, SEQ_LEN, width), BF16),
        shape_of((SLOTS, SEQ_LEN, width), BF16),
        shape_of((SLOTS, SEQ_LEN, 3 * wide), BF16),
        shape_of((SLOTS, SEQ_LEN, wide), BF16),
        shape_of((SLOTS, 8, SEQ_LEN), F32),
    ]

    def slot_rows(columns):
        return pl.BlockSpec((1, BLOCK, columns), lambda i, m, f: (m[1], i, 0))

    grid_spec = pltpu.PrefetchScalarGridSpec(
        num_scalar_prefetch=2,
        grid=(BLOCKS,),
        in_specs=[
            pl.BlockSpec((BLOCK, width), lambda i, m, f: (m[2] * BLOCKS + i, 0)),
            pl.BlockSpec((BLOCK, width), lambda i, m, f: (i, 0)),
            once((1, width), lambda i, m, f: (0, 0)),
            once(wall.shape, lambda i, m, f: (0, 0)),
            pl.BlockSpec((BLOCK, LANES), lambda i, m, f: (i, 0)),
            pl.BlockSpec((BLOCK, LANES), lambda i, m, f: (i, 0)),
            pl.BlockSpec((1, BLOCK, 1), lambda i, m, f: (m[2], i, 0)),
        ]
        + [pl.BlockSpec(memory_space=pl.ANY)] * stored,
        out_specs=[
            pl.BlockSpec((BLOCK // 2, wide), lambda i, m, f: (i, 0)),
            slot_rows(width),
            slot_rows(width),
            slot_rows(3 * wide),
            slot_rows(wide),
            pl.BlockSpec((1, 8, BLOCK), lambda i, m, f: (m[1], 0, i)),
        ],
        scratch_shapes=[
            pltpu.VMEM((SEQ_LEN, wide), BF16),
            pltpu.VMEM((SEQ_LEN, wide), BF16),
            pltpu.VMEM((heads, SEQ_LEN // KEYS, BLOCK, KEYS), F32),
            pltpu.VMEM((heads, BLOCK, LANES), F32),
            pltpu.VMEM((heads, BLOCK, LANES), F32),
            pltpu.VMEM((BLOCK, wide), F32),
        ],
    )
    outs = pl.pallas_call(
        functools.partial(attention_forward_kernel, stored),
        grid_spec=grid_spec,
        out_shape=[shape_of((SEQ_LEN // 2, wide), BF16)] + saved,
        input_output_aliases={9 + k: 1 + k for k in range(stored)},
        compiler_params=pltpu.CompilerParams(vmem_limit_bytes=VMEM_BYTES),
        cost_estimate=cost(24),
        name="attention_forward",
    )(
        meta,
        first_block,
        tokens,
        received,
        gain,
        wall,
        cosine,
        sine,
        low,
        *(kept or ()),
    )
    return outs[0], outs[1:]


def touch_kernel(*refs):
    outs, zeros, semaphores = refs[:-2], refs[-2], refs[-1]
    zeros[...] = jnp.zeros_like(zeros)
    copies = []
    for out in outs:
        if out.dtype != BF16 or out.shape[-1] > zeros.shape[-1]:
            continue
        source = zeros.at[:, : out.shape[-1]]
        for slot in range(out.shape[0]):
            if len(out.shape) == 3:
                places = [out.at[slot, row : row + 16] for row in range(0, out.shape[1], 512)]
            else:
                places = [out.at[slot, step, 0:16] for step in range(0, out.shape[1], 2)]
            for place in places:
                copies.append(pltpu.make_async_copy(source, place, semaphores.at[len(copies)]))
    for copy in copies:
        copy.start()
    for copy in copies:
        copy.wait()


def reserve(shapes):
    width = max(shape.shape[-1] for shape in shapes if shape.dtype == BF16)
    return pl.pallas_call(
        touch_kernel,
        out_shape=shapes,
        out_specs=[pl.BlockSpec(memory_space=pl.ANY)] * len(shapes),
        scratch_shapes=[pltpu.VMEM((16, width), BF16), pltpu.SemaphoreType.DMA((128,))],
        compiler_params=pltpu.CompilerParams(has_side_effects=True),
        cost_estimate=cost(3),
        name="reserve",
    )()


PAIR = 2
ROWS = 512
ROW_STEPS = SEQ_LEN // ROWS
PAIR_STEPS = EXPERTS // PAIR
SPAN = 512
CHUNK = 96


def build_pick(first, chunks, post_ref, probs, pick, gates):
    for which, step in chunks:
        row = pl.ds(first + which, 1)
        slot_at = step * CHUNK + lax.broadcasted_iota(jnp.int32, (CHUNK, SEQ_LEN), 0)
        here = slot_at == post_ref[0, row, :]
        rows = slice(which * CAPACITY + step * CHUNK, which * CAPACITY + (step + 1) * CHUNK)
        pick[rows, :] = jnp.where(here, 1.0, 0.0).astype(BF16)
        if probs is not None:
            chosen = jnp.sum(jnp.where(here, probs[row, :], 0.0), axis=1, keepdims=True)
            gates[rows, :] = jnp.broadcast_to(chosen, (CHUNK, LANES))


def build_gates(first, post_ref, probs, gates):
    for which in range(PAIR):
        row = pl.ds(first + which, 1)
        for step in range(CAPACITY // CHUNK):
            slot_at = step * CHUNK + lax.broadcasted_iota(jnp.int32, (CHUNK, SEQ_LEN), 0)
            here = slot_at == post_ref[0, row, :]
            rows = slice(which * CAPACITY + step * CHUNK, which * CAPACITY + (step + 1) * CHUNK)
            chosen = jnp.sum(jnp.where(here, probs[row, :], 0.0), axis=1, keepdims=True)
            gates[rows, :] = jnp.broadcast_to(chosen, (CHUNK, LANES))


WINDOW_SLOTS = 256


def is_narrow(starts, sequence):
    return starts[starts.shape[0] - SLOTS + 1 + sequence] > 0


def window_at(starts, sequence, expert, chunk):
    place = starts[(sequence * EXPERTS + expert) * (ROW_STEPS + 1) + chunk]
    return jnp.minimum(place // 16 * 16, SPAN - WINDOW_SLOTS)


def chunk_rows(chunk):
    return pl.ds(chunk * ROWS, ROWS)


def token_places(expert, rows, pos_ref):
    places = pos_ref[0, rows, :]
    lane = lax.broadcasted_iota(jnp.int32, places.shape, 1)
    return jnp.sum(jnp.where(lane == expert, places, 0), axis=1, keepdims=True)


def build_put(starts, sequence, pair, chunk, pos_ref, put):
    rows = chunk_rows(chunk)
    slot_at = lax.broadcasted_iota(jnp.int32, (ROWS, WINDOW_SLOTS), 1)
    for which in range(PAIR):
        expert = pair * PAIR + which
        begin = jnp.where(
            is_narrow(starts, sequence), window_at(starts, sequence, expert, chunk), -SEQ_LEN
        )
        put[rows, which * WINDOW_SLOTS : (which + 1) * WINDOW_SLOTS] = jnp.where(
            slot_at == token_places(expert, rows, pos_ref) - begin, 1.0, 0.0
        ).astype(BF16)


def put_back(starts, sequence, pair, chunk, put, slots, window):
    for which in range(PAIR):
        begin = window_at(starts, sequence, pair * PAIR + which, chunk)
        there = pl.ds(pl.multiple_of(which * SPAN + begin, 16), WINDOW_SLOTS)
        window[which * WINDOW_SLOTS : (which + 1) * WINDOW_SLOTS, :] = slots[there, :]
    return dot(put[chunk_rows(chunk), : PAIR * WINDOW_SLOTS], window[...])


def put_back_wide(pair, pos_ref, put, slots, total):
    def body(step):
        which, chunk = step // ROW_STEPS, step % ROW_STEPS
        rows = rows_of(chunk, ROWS)
        slot_at = lax.broadcasted_iota(jnp.int32, (ROWS, SPAN), 1)
        place = token_places(pair * PAIR + which, rows, pos_ref)
        put[rows, SPAN:] = jnp.where(slot_at == place, 1.0, 0.0).astype(BF16)
        total[rows, :] += dot(put[rows, SPAN:], slots[rows_of(which, SPAN), :])

    loop(PAIR * ROW_STEPS, body)


ALL_CHUNKS = [(which, step) for which in range(PAIR) for step in range(CAPACITY // CHUNK)]


def of_pair(which):
    return slice(which * CAPACITY, (which + 1) * CAPACITY)


def feed_forward_kernel(
    stored,
    meta,
    starts,
    x_ref,
    ag_ref,
    wo_ref,
    gain_ref,
    router_ref,
    post_ref,
    pos_ref,
    wg_ref,
    wu_ref,
    wd_ref,
    wgs_ref,
    wus_ref,
    wds_ref,
    *rest,
):
    rest = rest[stored:]
    part_ref, h_ref, b_ref, xe_ref, g_ref, u_ref, gs_ref, us_ref, probs_ref = rest[:9]
    total, normed, probs, pick, put, gates, scaled, window = rest[9:]
    step = pl.program_id(0)
    pair = jnp.maximum(step - ROW_STEPS, 0)

    def activate(gate, lift, gate_out, lift_out):
        gate_out[...] = gate.astype(BF16)
        lift_out[...] = lift.astype(BF16)
        return (gate / (1.0 + jnp.exp(-gate)) * lift).astype(BF16)

    @pl.when(step < ROW_STEPS)
    def _():
        half = PACK // 2
        columns = ag_ref.shape[2] // 2
        mixed = jnp.concatenate(
            [
                jnp.concatenate(
                    [
                        ag_ref[device, block : block + half, side * columns : (side + 1) * columns]
                        for device in range(4)
                    ],
                    axis=1,
                )
                for block in range(0, ROWS // 2, half)
                for side in range(2)
            ],
            axis=0,
        )
        state = x_ref[0].astype(F32) + dot(mixed, wo_ref[...])
        h_ref[0] = state
        scale = lax.rsqrt(jnp.mean(state * state, axis=-1, keepdims=True) + 1e-06)
        b = (gain_ref[...] * state * scale).astype(BF16)
        b_ref[0] = b
        here = rows_of(step, ROWS)
        normed[here, :] = b
        logits = dot_nt(router_ref[...], b)
        weights = jnp.exp(logits - jnp.max(logits, axis=0, keepdims=True))
        weights = weights / jnp.sum(weights, axis=0, keepdims=True)
        probs_ref[0] = weights
        probs[:, here] = weights
        hidden = activate(dot(b, wgs_ref[...]), dot(b, wus_ref[...]), gs_ref.at[0], us_ref.at[0])
        total[here, :] = dot(hidden, wds_ref[...])

    @pl.when(step == 0)
    def _():
        build_pick(0, ALL_CHUNKS, post_ref, None, pick, gates)
        scaled[...] = jnp.zeros_like(scaled)
        put[:, : PAIR * WINDOW_SLOTS] = jnp.zeros((SEQ_LEN, PAIR * WINDOW_SLOTS), BF16)

    before = jnp.maximum(pair - 1, 0)

    @pl.when((step > ROW_STEPS) & jnp.logical_not(is_narrow(starts, meta[2])))
    def _():
        put_back_wide(before, pos_ref, put, scaled, total)

    @pl.when(step == ROW_STEPS + PAIR_STEPS)
    def _():
        for chunk in range(ROW_STEPS):
            rows = chunk_rows(chunk)
            values = put_back(starts, meta[2], before, chunk, put, scaled, window)
            part_ref[rows, :] = (total[rows, :] + values).astype(BF16)

    @pl.when((step >= ROW_STEPS) & (step < ROW_STEPS + PAIR_STEPS))
    def _():
        for chunk in range(ROW_STEPS):
            total[chunk_rows(chunk), :] += put_back(
                starts, meta[2], before, chunk, put, scaled, window
            )
            build_put(starts, meta[2], pair, chunk, pos_ref, put)
        picked = dot(pick[...], normed[...]).astype(BF16)
        build_gates(pair * PAIR, post_ref, probs, gates)
        build_pick(
            jnp.minimum(pair + 1, PAIR_STEPS - 1) * PAIR, ALL_CHUNKS, post_ref, None, pick, gates
        )
        for which in range(PAIR):
            rows = picked[of_pair(which), :]
            xe_ref[0, which] = rows
            hidden = activate(
                dot(rows, wg_ref[which]), dot(rows, wu_ref[which]), g_ref.at[0, which], u_ref.at[0, which]
            )
            scaled[which * SPAN : which * SPAN + CAPACITY, :] = (
                dot(hidden, wd_ref[which]) * gates[of_pair(which), 0:1]
            ).astype(BF16)


def step_specs():
    def row_at(step):
        return jnp.minimum(step, ROW_STEPS - 1)

    def pair_at(step):
        return jnp.clip(step - ROW_STEPS, 0, PAIR_STEPS - 1)

    return row_at, pair_at


def feed_forward(
    meta, starts, layer_in, gathered, out_weight, gain, router, post, pos, weights, kept
):
    width = layer_in.shape[2]
    wg, wu, wd, wgs, wus, wds = weights
    hidden = wg.shape[2]
    stored = 8
    saved = [
        shape_of((SLOTS, SEQ_LEN, width), F32),
        shape_of((SLOTS, SEQ_LEN, width), BF16),
        shape_of((SLOTS, EXPERTS, CAPACITY, width), BF16),
        shape_of((SLOTS, EXPERTS, CAPACITY, hidden), BF16),
        shape_of((SLOTS, EXPERTS, CAPACITY, hidden), BF16),
        shape_of((SLOTS, SEQ_LEN, hidden), BF16),
        shape_of((SLOTS, SEQ_LEN, hidden), BF16),
        shape_of((SLOTS, EXPERTS, SEQ_LEN), F32),
    ]
    row_at, pair_at = step_specs()

    def slot_rows(columns):
        return pl.BlockSpec((1, ROWS, columns), lambda s, m, f: (m[1], row_at(s), 0))

    def slot_pair(columns):
        return pl.BlockSpec((1, PAIR, CAPACITY, columns), lambda s, m, f: (m[1], pair_at(s), 0, 0))

    def fixed(shape):
        return once(shape, lambda s, m, f: (0,) * len(shape))

    def of_pairs(array):
        return pl.BlockSpec((PAIR,) + array.shape[1:], lambda s, m, f: (pair_at(s), 0, 0))

    grid_spec = pltpu.PrefetchScalarGridSpec(
        num_scalar_prefetch=2,
        grid=(ROW_STEPS + PAIR_STEPS + 1,),
        in_specs=[
            slot_rows(width),
            pl.BlockSpec((4, ROWS // 2, gathered.shape[2]), lambda s, m, f: (0, row_at(s), 0)),
            fixed(out_weight.shape),
            fixed(gain.shape),
            fixed(router.shape),
            once((1, EXPERTS, SEQ_LEN), lambda s, m, f: (m[2], 0, 0)),
            once((1, SEQ_LEN, EXPERTS), lambda s, m, f: (m[2], 0, 0)),
            of_pairs(wg),
            of_pairs(wu),
            of_pairs(wd),
            fixed(wgs.shape),
            fixed(wus.shape),
            fixed(wds.shape),
        ]
        + [pl.BlockSpec(memory_space=pl.ANY)] * stored,
        out_specs=[
            fixed((SEQ_LEN, width)),
            slot_rows(width),
            slot_rows(width),
            slot_pair(width),
            slot_pair(hidden),
            slot_pair(hidden),
            slot_rows(hidden),
            slot_rows(hidden),
            pl.BlockSpec((1, EXPERTS, ROWS), lambda s, m, f: (m[1], 0, row_at(s))),
        ],
        scratch_shapes=[
            pltpu.VMEM((SEQ_LEN, width), F32),
            pltpu.VMEM((SEQ_LEN, width), BF16),
            pltpu.VMEM((EXPERTS, SEQ_LEN), F32),
            pltpu.VMEM((PAIR * CAPACITY, SEQ_LEN), BF16),
            pltpu.VMEM((SEQ_LEN, PAIR * SPAN), BF16),
            pltpu.VMEM((PAIR * CAPACITY, LANES), F32),
            pltpu.VMEM((PAIR * SPAN, width), BF16),
            pltpu.VMEM((PAIR * WINDOW_SLOTS, width), BF16),
        ],
    )
    outs = pl.pallas_call(
        functools.partial(feed_forward_kernel, stored),
        grid_spec=grid_spec,
        out_shape=[shape_of((SEQ_LEN, width), BF16)] + saved,
        input_output_aliases={15 + k: 1 + k for k in range(stored)},
        compiler_params=pltpu.CompilerParams(vmem_limit_bytes=VMEM_BYTES),
        cost_estimate=cost(56),
        name="feed_forward",
    )(
        meta,
        starts,
        layer_in,
        gathered,
        out_weight,
        gain,
        router,
        post,
        pos,
        wg,
        wu,
        wd,
        wgs,
        wus,
        wds,
        *(reserve(saved) if kept is None else kept),
    )
    return outs[0], outs[1:]


def pull(grad, weight, gate, lift):
    gate, lift = gate.astype(F32), lift.astype(F32)
    sigma = 1.0 / (1.0 + jnp.exp(-gate))
    swish = gate * sigma
    hidden = (swish * lift).astype(BF16)
    inner = None
    if weight is not None:
        inner = jnp.sum(hidden.astype(F32) * grad, axis=1, keepdims=True)
        grad = grad * weight
    grad_gate = (grad * lift * (sigma + swish * (1.0 - sigma))).astype(BF16)
    return hidden, grad_gate, (grad * swish).astype(BF16), inner


def feed_backward_kernel(
    stored,
    meta,
    starts,
    cot_ref,
    rec_ref,
    post_ref,
    pos_ref,
    g_ref,
    u_ref,
    gs_ref,
    us_ref,
    probs_ref,
    wg_ref,
    wu_ref,
    wd_ref,
    wgs_ref,
    wus_ref,
    wds_ref,
    *rest,
):
    rest = rest[stored:]
    part_ref, dy_ref, hid_ref, dg_ref, du_ref, de_ref, hids_ref, dgs_ref, dus_ref = rest[:9]
    total, given, pick, put, gates, slots, choice, window = rest[9:]
    step = pl.program_id(0)
    pair = jnp.maximum(step - ROW_STEPS, 0)

    @pl.when(step < ROW_STEPS)
    def _():
        dy = jnp.where(meta[0] == 1, cot_ref[...], rec_ref[...])
        dy = jnp.where(meta[0] == 0, jnp.zeros_like(dy), dy)
        dy_ref[0] = dy
        here = rows_of(step, ROWS)
        given[here, :] = dy
        hidden, grad_gate, grad_lift, unused = pull(
            dot_nt(dy, wds_ref[...]), None, gs_ref[0], us_ref[0]
        )
        hids_ref[0] = hidden
        dgs_ref[0] = grad_gate
        dus_ref[0] = grad_lift
        total[here, :] = dot_nt(grad_gate, wgs_ref[...]) + dot_nt(grad_lift, wus_ref[...])

    @pl.when(step == 0)
    def _():
        build_pick(0, ALL_CHUNKS, post_ref, None, pick, gates)
        slots[...] = jnp.zeros_like(slots)
        put[:, : PAIR * WINDOW_SLOTS] = jnp.zeros((SEQ_LEN, PAIR * WINDOW_SLOTS), BF16)

    before = jnp.maximum(pair - 1, 0)

    @pl.when((step > ROW_STEPS) & jnp.logical_not(is_narrow(starts, meta[2])))
    def _():
        put_back_wide(before, pos_ref, put, slots, total)

    @pl.when(step == ROW_STEPS + PAIR_STEPS)
    def _():
        for chunk in range(ROW_STEPS):
            rows = chunk_rows(chunk)
            values = put_back(starts, meta[2], before, chunk, put, slots, window)
            part_ref[rows, :] = (total[rows, :] + values).astype(BF16)

    @pl.when((step >= ROW_STEPS) & (step < ROW_STEPS + PAIR_STEPS))
    def _():
        for chunk in range(ROW_STEPS):
            total[chunk_rows(chunk), :] += put_back(
                starts, meta[2], before, chunk, put, slots, window
            )
            build_put(starts, meta[2], pair, chunk, pos_ref, put)
        picked = dot(pick[...], given[...]).astype(BF16)
        build_gates(pair * PAIR, post_ref, probs_ref.at[0], gates)
        build_pick(
            jnp.minimum(pair + 1, PAIR_STEPS - 1) * PAIR, ALL_CHUNKS, post_ref, None, pick, gates
        )
        for which in range(PAIR):
            rows = picked[of_pair(which), :]
            weight = gates[of_pair(which), 0:1]
            hidden, grad_gate, grad_lift, inner = pull(
                dot_nt(rows, wd_ref[which]), weight, g_ref[0, which], u_ref[0, which]
            )
            hid_ref[0, which] = hidden
            dg_ref[0, which] = grad_gate
            du_ref[0, which] = grad_lift
            de_ref[0, which] = (weight * rows.astype(F32)).astype(BF16)
            row = pl.ds(pair * PAIR + which, 1)
            chosen = jnp.zeros((1, SEQ_LEN), F32)
            for chunk in range(CAPACITY // CHUNK):
                slot_at = chunk * CHUNK + lax.broadcasted_iota(jnp.int32, (CHUNK, SEQ_LEN), 0)
                here = slot_at == post_ref[0, row, :]
                chosen += jnp.sum(
                    jnp.where(here, inner[chunk * CHUNK : (chunk + 1) * CHUNK], 0.0),
                    axis=0,
                    keepdims=True,
                )
            choice[row, :] = chosen
            slots[which * SPAN : which * SPAN + CAPACITY, :] = (
                dot_nt(grad_gate, wg_ref[which]) + dot_nt(grad_lift, wu_ref[which])
            ).astype(BF16)

    @pl.when(step == ROW_STEPS + PAIR_STEPS)
    def _():
        half = SEQ_LEN // 2
        blank = jnp.zeros((8, half), F32)
        part_ref[SEQ_LEN:, :] = jnp.concatenate(
            [choice[:, :half], blank, choice[:, half:], blank], axis=0
        ).astype(BF16)


def feed_backward(meta, starts, cotangent, received, post, pos, forward_kept, weights, kept):
    width = cotangent.shape[1]
    wg, wu, wd, wgs, wus, wds = weights
    hidden = wg.shape[2]
    stored = 8
    unused_h, unused_b, unused_x, gate, lift, gate_sh, lift_sh, probs = forward_kept
    saved = [
        shape_of((SLOTS, SEQ_LEN, width), BF16),
        shape_of((SLOTS, EXPERTS, CAPACITY, hidden), BF16),
        shape_of((SLOTS, EXPERTS, CAPACITY, hidden), BF16),
        shape_of((SLOTS, EXPERTS, CAPACITY, hidden), BF16),
        shape_of((SLOTS, EXPERTS, CAPACITY, width), BF16),
        shape_of((SLOTS, SEQ_LEN, hidden), BF16),
        shape_of((SLOTS, SEQ_LEN, hidden), BF16),
        shape_of((SLOTS, SEQ_LEN, hidden), BF16),
    ]
    row_at, pair_at = step_specs()

    def slot_rows(columns, which):
        return pl.BlockSpec((1, ROWS, columns), lambda s, m, f: (m[which], row_at(s), 0))

    def slot_pair(columns, which):
        return pl.BlockSpec(
            (1, PAIR, CAPACITY, columns), lambda s, m, f: (m[which], pair_at(s), 0, 0)
        )

    def fixed(shape):
        return once(shape, lambda s, m, f: (0,) * len(shape))

    def of_pairs(array):
        return pl.BlockSpec((PAIR,) + array.shape[1:], lambda s, m, f: (pair_at(s), 0, 0))

    grid_spec = pltpu.PrefetchScalarGridSpec(
        num_scalar_prefetch=2,
        grid=(ROW_STEPS + PAIR_STEPS + 1,),
        in_specs=[
            pl.BlockSpec((ROWS, width), lambda s, m, f: (m[2] * ROW_STEPS + row_at(s), 0)),
            pl.BlockSpec((ROWS, width), lambda s, m, f: (row_at(s), 0)),
            once((1, EXPERTS, SEQ_LEN), lambda s, m, f: (m[2], 0, 0)),
            once((1, SEQ_LEN, EXPERTS), lambda s, m, f: (m[2], 0, 0)),
            slot_pair(hidden, 3),
            slot_pair(hidden, 3),
            slot_rows(hidden, 3),
            slot_rows(hidden, 3),
            once((1, EXPERTS, SEQ_LEN), lambda s, m, f: (m[3], 0, 0)),
            of_pairs(wg),
            of_pairs(wu),
            of_pairs(wd),
            fixed(wgs.shape),
            fixed(wus.shape),
            fixed(wds.shape),
        ]
        + [pl.BlockSpec(memory_space=pl.ANY)] * stored,
        out_specs=[
            fixed((SEQ_LEN + 32, width)),
            slot_rows(width, 1),
            slot_pair(hidden, 1),
            slot_pair(hidden, 1),
            slot_pair(hidden, 1),
            slot_pair(width, 1),
            slot_rows(hidden, 1),
            slot_rows(hidden, 1),
            slot_rows(hidden, 1),
        ],
        scratch_shapes=[
            pltpu.VMEM((SEQ_LEN, width), F32),
            pltpu.VMEM((SEQ_LEN, width), BF16),
            pltpu.VMEM((PAIR * CAPACITY, SEQ_LEN), BF16),
            pltpu.VMEM((SEQ_LEN, PAIR * SPAN), BF16),
            pltpu.VMEM((PAIR * CAPACITY, LANES), F32),
            pltpu.VMEM((PAIR * SPAN, width), BF16),
            pltpu.VMEM((EXPERTS, SEQ_LEN), F32),
            pltpu.VMEM((PAIR * WINDOW_SLOTS, width), BF16),
        ],
    )
    outs = pl.pallas_call(
        functools.partial(feed_backward_kernel, stored),
        grid_spec=grid_spec,
        out_shape=[shape_of((SEQ_LEN + 32, width), BF16)] + saved,
        input_output_aliases={17 + k: 1 + k for k in range(stored)},
        compiler_params=pltpu.CompilerParams(vmem_limit_bytes=VMEM_BYTES),
        cost_estimate=cost(60),
        name="feed_backward",
    )(
        meta,
        starts,
        cotangent,
        received,
        post,
        pos,
        gate,
        lift,
        gate_sh,
        lift_sh,
        probs,
        wg,
        wu,
        wd,
        wgs,
        wus,
        wds,
        *(reserve(saved) if kept is None else kept),
    )
    return outs[0], outs[1:]


def attention_backward_kernel(
    stored,
    meta,
    first_block,
    sum_ref,
    choice_ref,
    probs_ref,
    dy_ref,
    h_ref,
    b_ref,
    gain_ref,
    router_ref,
    wall_ref,
    wo_ref,
    cos_ref,
    sin_ref,
    qkv_ref,
    o_ref,
    lse_ref,
    low_ref,
    *rest,
):
    rest = rest[stored:]
    part_ref, dh_ref, gain_grad_ref, router_grad_ref, dqkv_ref, dattn_ref = rest[:6]
    dk_all, dv_all, dq_all, do_all, inner_all = rest[6:]
    step = pl.program_id(0)
    index = BACK_BLOCKS - 1 - step
    heads = wo_ref.shape[0] // LANES
    wide = heads * LANES

    @pl.when(step == 0)
    def _():
        gain_grad_ref[...] = jnp.zeros_like(gain_grad_ref)
        router_grad_ref[...] = jnp.zeros_like(router_grad_ref)
        dk_all[...] = jnp.zeros_like(dk_all)
        dv_all[...] = jnp.zeros_like(dv_all)

    probs = probs_ref[0]
    chosen = choice_ref[0:8, :].astype(F32)
    logit_grads = probs * (chosen - jnp.sum(probs * chosen, axis=0, keepdims=True))
    logit_grads = logit_grads.astype(BF16)
    router_grad_ref[...] += dot(logit_grads, b_ref[0])
    grad_normed = sum_ref[...].astype(F32) + dot_tn(logit_grads, router_ref[...])
    state = h_ref[0]
    scale = lax.rsqrt(jnp.mean(state * state, axis=-1, keepdims=True) + 1e-06)
    normed = state * scale
    gain_grad_ref[...] += jnp.sum(grad_normed * normed, axis=0, keepdims=True)
    scaled = gain_ref[...] * grad_normed
    inner = jnp.mean(normed * scaled, axis=-1, keepdims=True)
    grad_state = dy_ref[0].astype(F32) + scale * (scaled - normed * inner)
    dh_ref[...] = grad_state
    dattn = grad_state.astype(BF16)
    dattn_ref[0] = dattn
    do = dot_nt(dattn, wo_ref[...]).astype(BF16)
    do_all[...] = do
    products = do.astype(F32) * o_ref[0].astype(F32)
    for head in range(heads):
        columns = slice(head * LANES, (head + 1) * LANES)
        row = jnp.sum(products[:, columns], axis=1, keepdims=True)
        inner_all[head : head + 1, :] = jnp.broadcast_to(row, (BACK_BLOCK, LANES)).T[0:1, :]
    dq_all[...] = jnp.zeros_like(dq_all)
    here = rows_of(index, BACK_BLOCK)
    low = low_ref[0]
    query_at = index * BACK_BLOCK + lax.broadcasted_iota(jnp.int32, (BACK_KEYS, BACK_BLOCK), 1)
    key_at = lax.broadcasted_iota(jnp.int32, (BACK_KEYS, BACK_BLOCK), 0)

    def body(block, none):
        at = key_at + block * BACK_KEYS
        valid = (at >= low) & (at <= query_at)
        there = rows_of(block, BACK_KEYS)
        for head in range(heads):
            columns = slice(head * LANES, (head + 1) * LANES)
            key_columns = slice(wide + head * LANES, wide + (head + 1) * LANES)
            value_columns = slice(2 * wide + head * LANES, 2 * wide + (head + 1) * LANES)
            query = qkv_ref[0, here, columns]
            keys = qkv_ref[0, there, key_columns]
            scores = jnp.where(valid, dot_nt(keys, query), -1e30)
            probs = jnp.exp(scores - lse_ref[0, head : head + 1, :])
            grad_probs = dot_nt(qkv_ref[0, there, value_columns], do_all[:, columns])
            grad_scores = (probs * (grad_probs - inner_all[head : head + 1, :])).astype(BF16)
            dv_all[there, columns] += dot(probs.astype(BF16), do_all[:, columns])
            dk_all[there, columns] += dot(grad_scores, query)
            dq_all[:, columns] += dot_tn(grad_scores, keys)
        return none

    lax.fori_loop(
        first_block[meta[2] * BACK_BLOCKS + index], ((index + 1) * BACK_BLOCK - 1) // BACK_KEYS + 1, body, 0
    )
    cosine, sine = cos_ref[...], sin_ref[...]
    for head in range(heads):
        columns = slice(head * LANES, (head + 1) * LANES)
        key_columns = slice(wide + head * LANES, wide + (head + 1) * LANES)
        value_columns = slice(2 * wide + head * LANES, 2 * wide + (head + 1) * LANES)
        dq = dq_all[:, columns] * 0.0625
        dk = dk_all[here, columns]
        dqkv_ref[0, :, columns] = (dq * cosine - pltpu.roll(dq, HEAD_DIM, 1) * sine).astype(BF16)
        dqkv_ref[0, :, key_columns] = (
            dk * cosine - pltpu.roll(dk, HEAD_DIM, 1) * sine
        ).astype(BF16)
        dqkv_ref[0, :, value_columns] = dv_all[here, columns].astype(BF16)
    part_ref[...] = dot_nt(dqkv_ref[0], wall_ref[...]).astype(BF16)


def attention_backward(
    meta, first_block, summed, forward_kept, attention_kept, dy, gain, router, wall, wo, cosine, sine, low, kept
):
    width = summed.shape[1]
    wide = wo.shape[0]
    stored = 0 if kept is None else 2
    h, b, probs = forward_kept[0], forward_kept[1], forward_kept[7]
    unused_x, unused_a, qkv, o, lse = attention_kept
    saved = [
        shape_of((SLOTS, SEQ_LEN, 3 * wide), BF16),
        shape_of((SLOTS, SEQ_LEN, width), BF16),
    ]

    def at(step):
        return BACK_BLOCKS - 1 - step

    def slot_rows(columns, which):
        return pl.BlockSpec((1, BACK_BLOCK, columns), lambda s, m, f: (m[which], at(s), 0))

    def fixed(shape):
        return once(shape, lambda s, m, f: (0,) * len(shape))

    halves_of = BACK_BLOCKS // 2
    grid_spec = pltpu.PrefetchScalarGridSpec(
        num_scalar_prefetch=2,
        grid=(BACK_BLOCKS,),
        in_specs=[
            pl.BlockSpec((BACK_BLOCK, width), lambda s, m, f: (at(s), 0)),
            pl.BlockSpec(
                (16, BACK_BLOCK), lambda s, m, f: (SEQ_LEN // 16 + at(s) // halves_of, at(s) % halves_of)
            ),
            pl.BlockSpec((1, EXPERTS, BACK_BLOCK), lambda s, m, f: (m[3], 0, at(s))),
            slot_rows(width, 1),
            slot_rows(width, 3),
            slot_rows(width, 3),
            fixed(gain.shape),
            fixed(router.shape),
            fixed(wall.shape),
            fixed(wo.shape),
            pl.BlockSpec((BACK_BLOCK, LANES), lambda s, m, f: (at(s), 0)),
            pl.BlockSpec((BACK_BLOCK, LANES), lambda s, m, f: (at(s), 0)),
            once((1, SEQ_LEN, 3 * wide), lambda s, m, f: (m[3], 0, 0)),
            slot_rows(wide, 3),
            pl.BlockSpec((1, 8, BACK_BLOCK), lambda s, m, f: (m[3], 0, at(s))),
            pl.BlockSpec((1, 1, BACK_BLOCK), lambda s, m, f: (m[2], 0, at(s))),
        ]
        + [pl.BlockSpec(memory_space=pl.ANY)] * stored,
        out_specs=[
            pl.BlockSpec((BACK_BLOCK, width), lambda s, m, f: (at(s), 0)),
            pl.BlockSpec((BACK_BLOCK, width), lambda s, m, f: (at(s), 0)),
            fixed((1, width)),
            fixed((8, width)),
            slot_rows(3 * wide, 1),
            slot_rows(width, 1),
        ],
        scratch_shapes=[
            pltpu.VMEM((SEQ_LEN, wide), F32),
            pltpu.VMEM((SEQ_LEN, wide), F32),
            pltpu.VMEM((BACK_BLOCK, wide), F32),
            pltpu.VMEM((BACK_BLOCK, wide), BF16),
            pltpu.VMEM((8, BACK_BLOCK), F32),
        ],
    )
    outs = pl.pallas_call(
        functools.partial(attention_backward_kernel, stored),
        grid_spec=grid_spec,
        out_shape=[
            shape_of((SEQ_LEN, width), BF16),
            shape_of((SEQ_LEN, width), F32),
            shape_of((1, width), F32),
            shape_of((8, width), F32),
        ]
        + saved,
        input_output_aliases={18 + k: 4 + k for k in range(stored)},
        compiler_params=pltpu.CompilerParams(vmem_limit_bytes=VMEM_BYTES),
        cost_estimate=cost(37),
        name="attention_backward",
    )(
        meta,
        first_block,
        summed,
        summed,
        probs,
        dy,
        h,
        b,
        gain,
        router,
        wall,
        wo,
        cosine,
        sine,
        qkv,
        o,
        lse,
        low,
        *(kept or ()),
    )
    return outs[:4], outs[4:]


def expert_grads_kernel(*refs):
    ins, out_ref = refs[:-1], refs[-1]
    (xa, xb), (ga, gb), (ua, ub), (ea, eb), (ha, hb) = (ins[2 * k : 2 * k + 2] for k in range(5))
    devices, unused, rows, unused = out_ref.shape
    pairs = [((xa, xb), (ga, gb)), ((xa, xb), (ua, ub)), ((ea, eb), (ha, hb))]
    for number, (left, right) in enumerate(pairs):
        grads = dot_tn(left[0][0, 0], right[0][0, 0]) + dot_tn(left[1][0, 0], right[1][0, 0])
        for device in range(devices):
            out_ref[device, number] = grads[device * rows : (device + 1) * rows].astype(BF16)


def expert_grads(first, count, extra, devices, picked, hid, grad_gate, grad_lift, grad_expert):
    width, hidden = picked.shape[3], hid.shape[3]
    rows = width // devices

    def pair(columns):
        return [
            pl.BlockSpec(
                (1, 1, CAPACITY, columns),
                functools.partial(lambda slot, e: (slot, first + e, 0, 0), slot),
            )
            for slot in (1, 2)
        ]

    return pl.pallas_call(
        expert_grads_kernel,
        grid=(count,),
        in_specs=pair(width) + pair(hidden) + pair(hidden) + pair(width) + pair(hidden),
        out_specs=pl.BlockSpec((devices, 3, rows, hidden), lambda e: (0, e, 0, 0)),
        out_shape=shape_of((devices, 3 * count + extra, rows, hidden), BF16),
        compiler_params=pltpu.CompilerParams(vmem_limit_bytes=VMEM_BYTES),
        cost_estimate=cost(6 * count),
        name="expert_grads",
    )(
        *(picked, picked, grad_gate, grad_gate, grad_lift, grad_lift),
        *(grad_expert, grad_expert, hid, hid),
    )


def lead_grads_kernel(
    meta,
    cot_ref,
    rec_ref,
    post_ref,
    probs_ref,
    g_ref,
    u_ref,
    wd_ref,
    xa_ref,
    xb_ref,
    ga_ref,
    ua_ref,
    ea_ref,
    ha_ref,
    out_ref,
    given,
    pick,
    gates,
    rows_in,
    grad_gate,
    grad_lift,
    grad_rows,
    hidden,
):
    step = pl.program_id(0)

    @pl.when(step == 0)
    def _():
        given[...] = jnp.where(meta[0] == 1, cot_ref[...], rec_ref[...])

    @pl.when(step > 0)
    def _():
        chunks = [(0, chunk) for chunk in range(CAPACITY // CHUNK)]
        build_pick(step - 1, chunks, post_ref, probs_ref.at[0], pick, gates)
        rows_in[...] = dot(pick[...], given[...]).astype(BF16)
        weight = gates[:, 0:1]
        grad_rows[...] = (weight * rows_in[...].astype(F32)).astype(BF16)
        hidden[...], grad_gate[...], grad_lift[...], unused = pull(
            dot_nt(rows_in[...], wd_ref[0]), weight, g_ref[0, 0], u_ref[0, 0]
        )
        devices, unused, rows, unused = out_ref.shape
        pairs = [
            (xa_ref.at[0, 0], ga_ref.at[0, 0], xb_ref.at[0, 0], grad_gate),
            (xa_ref.at[0, 0], ua_ref.at[0, 0], xb_ref.at[0, 0], grad_lift),
            (ea_ref.at[0, 0], ha_ref.at[0, 0], grad_rows, hidden),
        ]
        for number, (left, right, left_last, right_last) in enumerate(pairs):
            grads = dot_tn(left[...], right[...]) + dot_tn(left_last[...], right_last[...])
            for device in range(devices):
                out_ref[device, number] = grads[device * rows : (device + 1) * rows].astype(BF16)


def lead_grads(count, devices, meta, cotangent, received, post, forward_kept, kept, down):
    unused_h, unused_b, picked, gate, lift, unused_gate, unused_lift, probs = forward_kept
    unused_dy, hid, grad_gate, grad_lift, grad_expert = kept[:5]
    width, inner = picked.shape[3], gate.shape[3]
    rows = width // devices

    def at(step):
        return jnp.maximum(step - 1, 0)

    def of_slot(columns, which):
        return pl.BlockSpec((1, 1, CAPACITY, columns), lambda s, m: (m[which], at(s), 0, 0))

    grid_spec = pltpu.PrefetchScalarGridSpec(
        num_scalar_prefetch=1,
        grid=(count + 1,),
        in_specs=[
            once((SEQ_LEN, width), lambda s, m: (m[1], 0)),
            once((SEQ_LEN, width), lambda s, m: (0, 0)),
            once((1, EXPERTS, SEQ_LEN), lambda s, m: (m[1], 0, 0)),
            once((1, EXPERTS, SEQ_LEN), lambda s, m: (m[2], 0, 0)),
            of_slot(inner, 2),
            of_slot(inner, 2),
            pl.BlockSpec((1,) + down.shape[1:], lambda s, m: (at(s), 0, 0)),
            of_slot(width, 3),
            of_slot(width, 2),
            of_slot(inner, 3),
            of_slot(inner, 3),
            of_slot(width, 3),
            of_slot(inner, 3),
        ],
        out_specs=pl.BlockSpec((devices, 3, rows, inner), lambda s, m: (0, at(s), 0, 0)),
        scratch_shapes=[
            pltpu.VMEM((SEQ_LEN, width), BF16),
            pltpu.VMEM((CAPACITY, SEQ_LEN), BF16),
            pltpu.VMEM((CAPACITY, LANES), F32),
            pltpu.VMEM((CAPACITY, width), BF16),
            pltpu.VMEM((CAPACITY, inner), BF16),
            pltpu.VMEM((CAPACITY, inner), BF16),
            pltpu.VMEM((CAPACITY, width), BF16),
            pltpu.VMEM((CAPACITY, inner), BF16),
        ],
    )
    return pl.pallas_call(
        lead_grads_kernel,
        grid_spec=grid_spec,
        out_shape=shape_of((devices, 3 * count, rows, inner), BF16),
        compiler_params=pltpu.CompilerParams(vmem_limit_bytes=VMEM_BYTES),
        cost_estimate=cost(20),
        name="lead_grads",
    )(
        meta,
        cotangent,
        received,
        post,
        probs,
        gate,
        lift,
        down,
        picked,
        picked,
        grad_gate,
        grad_lift,
        grad_expert,
        hid,
    )


def shared_grads_kernel(b_ref, dy_ref, gate_ref, lift_ref, hid_ref, before_ref, out_ref, *totals):
    step = pl.program_id(0)
    pairs = [(b_ref, gate_ref), (b_ref, lift_ref), (dy_ref, hid_ref)]

    @pl.when(step == 0)
    def _():
        for total in totals:
            total[...] = jnp.zeros_like(total)

    for (left, right), total in zip(pairs, totals):
        total[...] += dot_tn(left[0], right[0])

    @pl.when(step == pl.num_programs(0) - 1)
    def _():
        devices, unused, rows, unused = out_ref.shape
        for number, total in enumerate(totals):
            for device in range(devices):
                out_ref[device, number] = total[device * rows : (device + 1) * rows, :].astype(
                    BF16
                )


def shared_grads(before, b, dy, grad_gate, grad_lift, hid):
    devices, matrices, width, hidden = before.shape
    rows = ROWS
    steps = SEQ_LEN // rows

    def spec(array):
        return pl.BlockSpec((1, rows, array.shape[2]), lambda s: (1 + s // steps, s % steps, 0))

    return pl.pallas_call(
        shared_grads_kernel,
        grid=(2 * steps,),
        in_specs=[spec(array) for array in (b, dy, grad_gate, grad_lift, hid)]
        + [pl.BlockSpec(memory_space=pl.ANY)],
        out_specs=once((devices, 3, width, hidden), lambda s: (0, matrices // 3 - 1, 0, 0)),
        out_shape=shape_of(before.shape, BF16),
        scratch_shapes=[pltpu.VMEM((devices * width, hidden), F32)] * 3,
        input_output_aliases={5: 0},
        compiler_params=pltpu.CompilerParams(vmem_limit_bytes=VMEM_BYTES),
        cost_estimate=cost(13),
        name="shared_grads",
    )(b, dy, grad_gate, grad_lift, hid, before)


def token_grads_kernel(count, *refs):
    lefts, rights = refs[:count], refs[count : 2 * count]
    outs, totals = refs[2 * count : 3 * count], refs[3 * count :]
    step = pl.program_id(0)

    @pl.when(step == 0)
    def _():
        for total in totals:
            total[...] = jnp.zeros_like(total)

    for left, right, total in zip(lefts, rights, totals):
        total[...] += dot_tn(left[0], right[0])

    @pl.when(step == pl.num_programs(0) - 1)
    def _():
        for out, total in zip(outs, totals):
            out[...] = total[...].astype(BF16)


def token_grads(lefts, rights):
    count = len(lefts)
    rows = ROWS
    steps = SEQ_LEN // rows

    def spec(array):
        return pl.BlockSpec((1, rows, array.shape[2]), lambda s: (1 + s // steps, s % steps, 0))

    shapes = [(left.shape[2], right.shape[2]) for left, right in zip(lefts, rights)]
    return pl.pallas_call(
        functools.partial(token_grads_kernel, count),
        grid=(2 * steps,),
        in_specs=[spec(a) for a in lefts] + [spec(a) for a in rights],
        out_specs=[once(shape, lambda s: (0, 0)) for shape in shapes],
        out_shape=[shape_of(shape, BF16) for shape in shapes],
        scratch_shapes=[pltpu.VMEM(shape, F32) for shape in shapes],
        compiler_params=pltpu.CompilerParams(vmem_limit_bytes=VMEM_BYTES),
        cost_estimate=cost(14),
        name="token_grads",
    )(*lefts, *rights)


def rotary_tables():
    half = HEAD_DIM // 2
    rates = np.exp(-np.log(10000.0) * np.arange(half) * 2.0 / HEAD_DIM)
    angles = np.arange(SEQ_LEN)[:, None] * rates[None, :]
    cosine, sine = np.cos(angles), np.sin(angles)
    cosine = np.concatenate([cosine] * 4, axis=1)
    sine = np.concatenate([sine, sine, -sine, -sine], axis=1)
    return jnp.asarray(cosine, F32), jnp.asarray(sine, F32)


def paired(weight):
    rows = weight.shape[0]
    heads = weight.shape[1] // HEAD_DIM
    half = HEAD_DIM // 2
    split = weight.reshape(rows, heads, HEAD_DIM)
    swapped = jnp.concatenate([-split[:, :, half:], split[:, :, :half]], axis=2)
    return jnp.concatenate([split, swapped], axis=2).reshape(rows, heads * LANES)


def padded(weight):
    rows = weight.shape[0]
    heads = weight.shape[1] // HEAD_DIM
    split = weight.reshape(rows, heads, HEAD_DIM)
    return jnp.concatenate([split, jnp.zeros_like(split)], axis=2).reshape(rows, heads * LANES)


def unpadded(grads):
    rows = grads.shape[0]
    return grads.reshape(rows, -1, LANES)[:, :, :HEAD_DIM].reshape(rows, -1)


def places(routes):
    experts = jnp.arange(EXPERTS, dtype=jnp.int32)
    named = jnp.any(routes[:, :, :, None] == experts, axis=2)
    before = (
        jnp.arange(SEQ_LEN, dtype=jnp.int32)[:, None] > jnp.arange(SEQ_LEN, dtype=jnp.int32)
    ).astype(BF16)
    rank = jnp.einsum("ts,nse->nte", before, named.astype(BF16), preferred_element_type=F32)
    by_token = jnp.where(named, rank.astype(jnp.int32), -1)
    counts = jnp.sum(named.reshape(-1, ROW_STEPS, ROWS, EXPERTS).astype(jnp.int32), axis=2)
    before = jnp.cumsum(jnp.pad(counts, ((0, 0), (1, 0), (0, 0))), axis=1)
    starts = jnp.swapaxes(before, 1, 2)
    held = starts[:, :, 1:] <= starts[:, :, :-1] // 16 * 16 + WINDOW_SLOTS
    narrow = jnp.all(held, axis=(1, 2)).astype(jnp.int32)
    starts = jnp.concatenate([starts.reshape(-1), narrow])
    return by_token, jnp.swapaxes(by_token, 1, 2), starts


def first_allowed(lengths):
    ends = jnp.cumsum(lengths, axis=1)
    at = jnp.arange(SEQ_LEN, dtype=jnp.int32)
    starts = jnp.max(jnp.where(ends[:, None, :] <= at[None, :, None], ends[:, None, :], 0), axis=2)
    return jnp.maximum(starts, at[None, :] - (WINDOW - 1)).astype(jnp.int32)


def on_device(
    tokens,
    doc_lengths,
    routes,
    gain_attn,
    w_query,
    w_key,
    w_value,
    w_output,
    gain_ffn,
    w_router,
    w_gate_exp,
    w_up_exp,
    w_down_exp,
    w_gate_sh,
    w_up_sh,
    w_down_sh,
    cotangent,
):
    section = lax.axis_index("section")
    devices = lax.axis_size("dp")
    count = doc_lengths.shape[0]
    width = tokens.shape[1]
    cosine, sine = rotary_tables()
    wall = jnp.concatenate([paired(w_query[0]), paired(w_key[0]), padded(w_value[0])], axis=1)
    wo = padded(w_output[0].T).T
    out_weight = lax.all_gather(w_output[0], "tensor", axis=0, tiled=True)
    router = w_router[0].T
    gain_a, gain_f = gain_attn.astype(F32), gain_ffn.astype(F32)
    feed_weights = (
        w_gate_exp[0],
        w_up_exp[0],
        w_down_exp[0],
        w_gate_sh[0],
        w_up_sh[0],
        w_down_sh[0],
    )
    pos, post, starts = places(routes[0].reshape(count, SEQ_LEN, 2))
    low = first_allowed(doc_lengths)
    first_block = (low[:, ::BLOCK] // KEYS).reshape(-1)
    back_first = (low[:, ::BACK_BLOCK] // BACK_KEYS).reshape(-1)
    low_column, low_row = low[:, :, None], low[:, None, :]

    received = tokens
    attention_kept, feed_kept, results = None, None, []
    grads_kept, attention_grads_kept, inputs = None, None, []
    small = jnp.zeros((10, width), F32)

    def spread(array):
        return lax.psum_scatter(array, "dp", scatter_dimension=0, tiled=False)

    def after(meta, array):
        return lax.optimization_barrier((meta, array))

    def forward_meta(tick):
        raw = tick - section
        active = (raw >= 0) & (raw < count)
        sequence = jnp.clip(raw, 0, count - 1)
        return jnp.stack([section, jnp.where(active, sequence + 1, 0), sequence]).astype(jnp.int32)

    def backward_meta(tick):
        raw = tick - 1 + section
        active = (raw >= 0) & (raw < count)
        sequence = jnp.clip(raw, 0, count - 1)
        source = jnp.where(active, 2 - section, 0)
        return jnp.stack(
            [source, jnp.where(active, sequence + 1, 0), sequence, sequence + 1]
        ).astype(jnp.int32)

    def attend(meta, received, kept):
        return attention_forward(
            meta, first_block, tokens, received, gain_a, wall, cosine, sine, low_column, kept
        )

    def feed(meta, gathered, kept):
        return feed_forward(
            meta,
            starts,
            attention_kept[0],
            gathered,
            out_weight,
            gain_f,
            router,
            post,
            pos,
            feed_weights,
            kept,
        )

    def feed_back(meta, received):
        return feed_backward(
            meta, starts, cotangent, received, post, pos, feed_kept, feed_weights, grads_kept
        )

    def attend_back(meta, summed):
        return attention_backward(
            meta,
            back_first,
            summed,
            feed_kept,
            attention_kept,
            grads_kept[0],
            gain_f,
            router,
            wall,
            wo,
            cosine,
            sine,
            low_row,
            attention_grads_kept,
        )

    for tick in range(count):
        meta = forward_meta(tick)
        own, attention_kept = attend(meta, received, attention_kept)
        gathered = lax.all_gather(own, "tensor") if tick == 0 else tensor_gather(own, 0)
        part, feed_kept = feed(meta, gathered, feed_kept)
        result, received = output_relay(part, feed_kept[0], tick, 4 + tick)
        results.append(result)

    blank = cotangent
    meta, back_meta = forward_meta(count), backward_meta(0)
    own, attention_kept = attend(meta, received, attention_kept)
    back_meta, own = after(back_meta, own)
    gathered = lax.all_gather(own, "tensor")
    part, grads_kept = feed_back(back_meta, blank)
    meta, part = after(meta, part)
    summed = lax.psum(part, "tensor")
    last_part, feed_kept = feed(meta, gathered, feed_kept)
    back_meta, last_part = after(back_meta, last_part)

    for tick in range(count + 1):
        if tick > 0:
            back_meta = backward_meta(tick)
        if tick == count:
            lead = 3
            lead_meta = jnp.stack(
                [2 - section, jnp.full_like(section, count - 1), jnp.full_like(section, count)]
                + [jnp.full_like(section, count - 1)]
            ).astype(jnp.int32)
            lead_part = lead_grads(
                lead,
                devices,
                lead_meta,
                cotangent,
                received,
                post,
                feed_kept,
                grads_kept,
                feed_weights[2],
            )
            back_meta, lead_part = after(back_meta, lead_part)
        if tick > 0:
            part, grads_kept = feed_back(back_meta, received)
        if tick == count:
            dy, hid, grad_gate, grad_lift, grad_expert, hid_sh, grad_gate_sh, grad_lift_sh = (
                grads_kept
            )
            last_grads = expert_grads(
                lead,
                EXPERTS - lead,
                3,
                devices,
                feed_kept[2],
                hid,
                grad_gate,
                grad_lift,
                grad_expert,
            )
            last_grads = shared_grads(
                last_grads, feed_kept[1], dy, grad_gate_sh, grad_lift_sh, hid_sh
            )
            part, last_grads = lax.optimization_barrier((part, last_grads))
            parts = [spread(lead_part), spread(last_grads)]
        if tick > 0:
            summed = tensor_sum(part, 2, 7)
        (part, grad_state, gain_grad, router_grad), attention_grads_kept = attend_back(
            back_meta, summed
        )
        grad_input, received, gain_attn_grad = input_relay(
            part, attention_kept[0], grad_state, gain_a, tick, 4 + count + 1 + tick
        )
        inputs.append(grad_input)
        small = small + jnp.concatenate([gain_attn_grad, gain_grad, router_grad], axis=0)
    result, unused = output_relay(last_part, feed_kept[0], count, 4 + count)
    results.append(result)

    projections, outward = token_grads(
        [attention_kept[1], attention_grads_kept[1]], [attention_grads_kept[0], attention_kept[3]]
    )
    wide = wo.shape[0]
    rows = width // devices
    columns = w_query.shape[2]
    packed = jnp.concatenate(
        [
            2.0 * unpadded(projections[:, : 2 * wide]),
            unpadded(projections[:, 2 * wide :]),
            unpadded(outward),
            jnp.pad(small, ((0, 6), (0, 0))).T.astype(BF16),
        ],
        axis=1,
    )
    packed, *parts = lax.optimization_barrier((packed, *parts))
    packed = spread(packed.reshape(devices, rows, -1)).astype(F32)
    shared = parts[1][-3:].astype(F32)
    experts = jnp.concatenate([parts[0], parts[1][:-3]], axis=0).astype(F32)
    experts = experts.reshape(EXPERTS, 3, rows, -1)

    def choose(items):
        return jnp.concatenate(
            [jnp.where(section == 0, items[k], items[k + 1]) for k in range(count)], axis=0
        )

    layer_out = choose(results)
    input_grad = jnp.concatenate(
        [jnp.where(section == 0, inputs[k + 1], inputs[k]) for k in range(count)], axis=0
    )
    extra = 4 * columns
    return (
        layer_out[None],
        input_grad[None],
        packed[None, :, extra],
        packed[None, :, :columns],
        packed[None, :, columns : 2 * columns],
        packed[None, :, 2 * columns : 3 * columns],
        packed[:, 3 * columns : extra].T[None],
        packed[None, :, extra + 1],
        packed[None, :, extra + 2 : extra + 10],
        experts[None, :, 0],
        experts[None, :, 1],
        jnp.swapaxes(experts[:, 2], 1, 2)[None],
        shared[None, 0],
        shared[None, 1],
        shared[2].T[None],
    )


def solution(mesh):
    return jax.shard_map(
        on_device,
        mesh=mesh,
        in_specs=(
            P("dp", None),
            P("dp", None),
            P("section", "dp", None),
            P("section", None),
            P("section", None, "tensor"),
            P("section", None, "tensor"),
            P("section", None, "tensor"),
            P("section", "tensor", None),
            P("section", None),
            P("section", None, None),
            P("section", None, None, "tensor"),
            P("section", None, None, "tensor"),
            P("section", None, "tensor", None),
            P("section", None, "tensor"),
            P("section", None, "tensor"),
            P("section", "tensor", None),
            P("dp", None),
        ),
        out_specs=(
            P("section", "dp", None),
            P("section", "dp", None),
            P("section", "dp"),
            P("section", "dp", "tensor"),
            P("section", "dp", "tensor"),
            P("section", "dp", "tensor"),
            P("section", "tensor", "dp"),
            P("section", "dp"),
            P("section", "dp", None),
            P("section", None, "dp", "tensor"),
            P("section", None, "dp", "tensor"),
            P("section", None, "tensor", "dp"),
            P("section", "dp", "tensor"),
            P("section", "dp", "tensor"),
            P("section", "tensor", "dp"),
        ),
        check_vma=False,
    )
```
